32 devices in a mesh: grp: 2 (over y), gx: 16 (over z, x, core).
Axes of the slice: x: 2, y: 2, z: 4, core: 2. Of those that a mesh axis runs over, the one named last changes fastest.
Arguments:
- mesh_feature_array: bfloat16 [128, 32, 32, 512], P(('grp', 'gx')), parts along dimension 0, may hold values from -6 to 6
- stencil_coefficients: float32 [27, 512], replicated, may hold values from -1.25 to 1.25
- partition_affinity_matrix: bfloat16 [512, 512], replicated, may hold values from -16 to 16
- softness_mapping_matrix: float32 [512], replicated, may hold values from -0.25 to 0.25
- content_mapping_matrix: bfloat16 [512, 512], replicated, may hold values from -0.25 to 0.25
- layernorm_multiplier: float32 [512], replicated, may hold values from 0.1 to 1.9
- widening_matrix: bfloat16 [512, 1024], replicated, may hold values from -0.25 to 0.25
- narrowing_matrix: bfloat16 [1024, 512], replicated, may hold values from -0.1875 to 0.1875
- final_mapping_matrix: bfloat16 [512, 512], replicated, may hold values from -0.25 to 0.25
Outputs:
- updated: bfloat16 [128, 32, 32, 512], P(('grp', 'gx')), parts along dimension 0
- slice_out: bfloat16 [1024, 512], P(('grp', 'gx')), parts along dimension 0
The draws below stay inside these ranges and needn't reach their ends.
There are 2 independent parts, one for each index of `grp`. The reference program is written for one: setup_inputs(seed, part) draws one part's arguments, and reference() takes and returns one part's arrays. A program takes and returns all parts, laid end to end along the dimension named above; an argument that names none is the same for every part. Nothing has to cross between parts.
All inputs are finite; a program needn't handle non-finite values.
Results may differ from the reference program's by a relative error of at most 0.0056.
Values may be sent and summed in bfloat16 or wider, within the bound.
No kernel may reach another device: no remote copies, remote signals or barrier semaphores. Data moves between devices by JAX's collectives and lax.ppermute only.
A program may use at most 128 MiB of HBM per device.

```python
import math
import jax
import jax.numpy as jnp
from jax import lax

CHANNEL_COUNT = 512
M = 512
HID = 1024
NY = 32
NZ = 32
NX = 64


def draw_partition_affinity_matrix(key, part):
    key = jax.random.fold_in(key, 7)
    key_base = jax.random.fold_in(key, 0)
    base = jax.random.normal(key_base, (CHANNEL_COUNT, M), jnp.float32) * (3.0 / math.sqrt(CHANNEL_COUNT))
    return jnp.clip(base, -16.0, 16.0).astype(jnp.bfloat16)


def block_scale(rng, shape, cuts, low, top_value):
    loudness = 1.0
    for dim, blocks in cuts:
        steps = jax.random.uniform(jax.random.fold_in(jax.random.fold_in(rng, 6), dim), (blocks,), jnp.float32, low / len(cuts), top_value / len(cuts))
        loudness = loudness * jnp.repeat(jnp.exp(steps), shape[dim] // blocks).reshape((-1,) + (1,) * (len(shape) - 1 - dim))
    return loudness


def gaussian(rng, dims, width, most, pieces=(), dtype=jnp.bfloat16):
    loudness = block_scale(rng, dims, pieces, -0.22, 0.18) if pieces else 1.0
    drawn = jax.random.normal(rng, dims, jnp.float32) * width * loudness
    return jnp.minimum(jnp.maximum(drawn, -most), most).astype(dtype)


def setup_inputs(seed: int = 0, part: int = 0) -> dict:
    arg_keys = jax.random.split(jax.random.key(seed), 10)
    part_splits = jax.random.split(jax.random.fold_in(arg_keys[9], part), 10)
    mesh_feature_array = gaussian(part_splits[0], (NX, NY, NZ, CHANNEL_COUNT), 1.0, 6.0, ((0, 16),))
    stencil_coefficients = gaussian(arg_keys[1], (27, CHANNEL_COUNT), 27 ** -0.5, 1.25, (), jnp.float32)
    partition_affinity_matrix = draw_partition_affinity_matrix(jax.random.fold_in(arg_keys[9], 71), part)
    softness_mapping_matrix = gaussian(arg_keys[3], (CHANNEL_COUNT,), CHANNEL_COUNT ** -0.5, 0.25, (), jnp.float32)
    content_mapping_matrix = gaussian(arg_keys[4], (CHANNEL_COUNT, CHANNEL_COUNT), CHANNEL_COUNT ** -0.5, 0.25)
    layernorm_multiplier = jnp.clip(1.0 + 0.18 * jax.random.normal(arg_keys[5], (CHANNEL_COUNT,), jnp.float32), 0.1, 1.9)
    widening_matrix = gaussian(arg_keys[6], (CHANNEL_COUNT, HID), CHANNEL_COUNT ** -0.5, 0.25)
    narrowing_matrix = gaussian(arg_keys[7], (HID, CHANNEL_COUNT), HID ** -0.5, 0.1875)
    final_mapping_matrix = gaussian(arg_keys[8], (CHANNEL_COUNT, CHANNEL_COUNT), CHANNEL_COUNT ** -0.5, 0.25)
    return {"mesh_feature_array": mesh_feature_array, "stencil_coefficients": stencil_coefficients, "partition_affinity_matrix": partition_affinity_matrix, "softness_mapping_matrix": softness_mapping_matrix, "content_mapping_matrix": content_mapping_matrix, "layernorm_multiplier": layernorm_multiplier, "widening_matrix": widening_matrix, "narrowing_matrix": narrowing_matrix, "final_mapping_matrix": final_mapping_matrix}


epsilon = 1e-05

def conv_gelu(padded, stencil_coefficients, size_x, size_y, size_z):
    total = jnp.zeros((size_x, size_y, size_z, stencil_coefficients.shape[1]), jnp.float32)
    for offset_a in range(3):
        for offset_b in range(3):
            for offset_c in range(3):
                window = padded[offset_a:offset_a + size_x, offset_b:offset_b + size_y, offset_c:offset_c + size_z]
                total = total + window.astype(jnp.float32) * stencil_coefficients[9 * offset_a + 3 * offset_b + offset_c]
    return jax.nn.gelu(total).astype(jnp.bfloat16)

def owner_mlp(tokens, layernorm_multiplier, widening_matrix, narrowing_matrix):
    center = lax.optimization_barrier(jnp.mean(tokens, axis=-1, keepdims=True))
    spread = lax.optimization_barrier(jnp.mean((tokens - center) ** 2, axis=-1, keepdims=True))
    normed = ((tokens - center) * lax_rsqrt(spread + epsilon) * layernorm_multiplier).astype(jnp.bfloat16)
    inner = jax.nn.gelu(jnp.dot(normed, widening_matrix, preferred_element_type=jnp.float32)).astype(jnp.bfloat16)
    return (tokens + jnp.dot(inner, narrowing_matrix, preferred_element_type=jnp.float32)).astype(jnp.bfloat16)

def lax_rsqrt(value):
    return 1.0 / jnp.sqrt(value)

def reference(mesh_feature_array, stencil_coefficients, partition_affinity_matrix, softness_mapping_matrix, content_mapping_matrix, layernorm_multiplier, widening_matrix, narrowing_matrix, final_mapping_matrix):
    padded = jnp.pad(mesh_feature_array, ((1, 1), (1, 1), (1, 1), (0, 0)))
    intermediate_response = conv_gelu(padded, stencil_coefficients, NX, NY, NZ).reshape(-1, CHANNEL_COUNT)
    local_softness_factor = 0.25 + jax.nn.softplus(jnp.dot(intermediate_response, softness_mapping_matrix.astype(jnp.bfloat16), preferred_element_type=jnp.float32))
    partition_affinity_raw = jnp.dot(intermediate_response, partition_affinity_matrix, preferred_element_type=jnp.float32) / local_softness_factor[:, None]
    slice_probs = jax.nn.softmax(partition_affinity_raw, axis=-1).astype(jnp.bfloat16)
    values = jnp.dot(intermediate_response, content_mapping_matrix, preferred_element_type=jnp.float32).astype(jnp.bfloat16)
    weighted_tokens = jax.lax.dot_general(slice_probs, values, (((0,), (0,)), ((), ())), preferred_element_type=jnp.float32)
    mass = lax.optimization_barrier(jnp.sum(slice_probs.astype(jnp.float32), axis=0))
    tokens = weighted_tokens / (mass[:, None] + epsilon)
    slice_out = owner_mlp(tokens, layernorm_multiplier, widening_matrix, narrowing_matrix)
    desliced = jnp.dot(slice_probs, slice_out, preferred_element_type=jnp.float32).astype(jnp.bfloat16)
    flat = mesh_feature_array.reshape(-1, CHANNEL_COUNT).astype(jnp.float32)
    updated = (flat + jnp.dot(desliced, final_mapping_matrix, preferred_element_type=jnp.float32)).astype(jnp.bfloat16)
    return (updated.reshape(NX, NY, NZ, CHANNEL_COUNT), slice_out)
```

```python
import functools
import math

import jax
import jax.numpy as jnp
from jax import lax
from jax.experimental import pallas as pl
from jax.experimental.pallas import tpu as pltpu
from jax.sharding import PartitionSpec as P

epsilon = 1e-05
LANES = 128
F32, BF16 = jnp.float32, jnp.bfloat16


def gelu(x):
    inner = x * (x * x * (0.044715 * math.sqrt(2 / math.pi)) + math.sqrt(2 / math.pi))
    half = 0.5 * x
    return half + half * jnp.tanh(inner)


def conv_rows(planes, k8_ref, y, rows, lanes, height):
    depth = planes[0].shape[-2]
    sums = [[None] * 3 for _ in range(rows)]
    for role, plane in enumerate(planes):
        for j in range(rows + 2):
            if isinstance(y, int) and not 0 <= y + j - 1 < height:
                continue
            row = plane[0, y + j - 1, :, lanes].astype(F32).reshape(depth // 8, 8, LANES)
            for out in range(rows):
                b = j - out
                if not 0 <= b < 3:
                    continue
                for c in range(3):
                    term = row * k8_ref[9 * role + 3 * b + c, :, lanes]
                    sums[out][c] = term if sums[out][c] is None else sums[out][c] + term
    position = lax.broadcasted_iota(jnp.int32, (depth, LANES), 0)
    results = []
    for out in range(rows):
        before, here, after = (s.reshape(depth, LANES) for s in sums[out])
        before = jnp.where(position == 0, 0.0, pltpu.roll(before, 1, 0))
        after = jnp.where(position == depth - 1, 0.0, pltpu.roll(after, depth - 1, 0))
        results.append(gelu(here + before + after).astype(BF16))
    return results


def conv_plane(planes, k8_ref, hid_ref):
    height, depth, channels = planes[0].shape[1:]
    for block in range(channels // LANES):
        lanes = slice(block * LANES, (block + 1) * LANES)

        def put(y, rows):
            for out, value in enumerate(conv_rows(planes, k8_ref, y, rows, lanes, height)):
                start = (y + out) * depth
                if not isinstance(start, int):
                    start = pl.multiple_of(start, depth)
                hid_ref[pl.ds(start, depth), lanes] = value

        put(0, 1)

        def pair(i, carry):
            put(1 + 2 * i, 2)
            return carry

        lax.fori_loop(0, (height - 2) // 2, pair, 0)
        put(height - 1, 1)


def assign(hid_ref, affinity_ref, softness_ref, probs_ref, chunk):
    cells, width = hid_ref.shape[0], affinity_ref.shape[1]
    channels = affinity_ref.shape[0]
    for first in range(0, cells, chunk):
        hid = hid_ref[first : first + chunk, :channels]
        raw = jnp.dot(hid, affinity_ref[...], preferred_element_type=F32)
        soft = jnp.dot(hid, softness_ref[...], preferred_element_type=F32)
        temperature = 0.25 + jnp.maximum(soft, 0.0) + jnp.log1p(jnp.exp(-jnp.abs(soft)))
        scale = (1.0 / math.log(2.0)) / temperature
        top = jnp.max(raw, axis=1, keepdims=True)
        scale = jnp.concatenate([scale] * (width // LANES), axis=1)
        powers = jnp.exp2((raw - top) * scale)
        probs = powers * (1.0 / jnp.sum(powers, axis=1, keepdims=True))
        probs_ref[0, first : first + chunk, :] = probs.astype(BF16)


def plane_kernel(first, last, chunk, meta_ref, a_ref, s_ref, b_ref, k_ref, affinity_ref,
                 softness_ref, *rest):
    if first:
        probs_ref, sums_ref, *rest = rest
    else:
        _, sums_in_ref, probs_ref, sums_ref, *rest = rest
    k8_ref, hid_ref = rest
    channels = affinity_ref.shape[0]

    @pl.when(pl.program_id(0) == 0)
    def _():
        for role in range(3):
            for tap in range(9):
                row = k_ref[meta_ref[2 + role], tap : tap + 1, :]
                k8_ref[9 * role + tap] = jnp.broadcast_to(row, k8_ref.shape[1:])
        hid_ref[:, channels:] = jnp.ones((hid_ref.shape[0], LANES), BF16)

    conv_plane((a_ref, s_ref, b_ref), k8_ref, hid_ref)
    assign(hid_ref, affinity_ref, softness_ref, probs_ref, chunk)
    share = lax.dot_general(
        probs_ref[0], hid_ref[...], (((0,), (0,)), ((), ())), preferred_element_type=F32
    )
    if first:
        @pl.when(pl.program_id(0) == 0)
        def _():
            sums_ref[...] = share

        @pl.when(pl.program_id(0) > 0)
        def _():
            sums_ref[...] += share
    else:
        total = sums_in_ref[...] + share
        if last:
            mass = total[:, channels:]
            high = mass.astype(BF16)
            low = (mass - high.astype(F32)).astype(BF16)
            lane = lax.broadcasted_iota(jnp.int32, mass.shape, 1)
            sums_ref[:, :channels] = total[:, :channels].astype(BF16)
            sums_ref[:, channels:] = jnp.where(
                lane < LANES // 2, high.astype(F32), low.astype(F32)
            ).astype(BF16)
        else:
            sums_ref[...] = total


def planes_call(mesh_x, halo, meta, taps, affinity, softness, carry, last):
    planes, height, depth, channels = mesh_x.shape
    slices = affinity.shape[1]
    cells = height * depth
    first = carry is None
    block = (1, height, depth, channels)
    whole = lambda shape: pl.BlockSpec(shape, lambda i, meta: (0,) * len(shape))
    if halo is None:
        steps = planes - 2
        sources = (mesh_x, mesh_x, mesh_x)
        maps = [lambda i, meta, o=o: (i + o, 0, 0, 0) for o in range(3)]
        out_map = lambda i, meta: (i + 1, 0, 0)
    else:
        steps = 1
        sources = (halo, mesh_x, mesh_x)
        maps = [lambda i, meta: (0, 0, 0, 0), lambda i, meta: (meta[0], 0, 0, 0),
                lambda i, meta: (meta[1], 0, 0, 0)]
        out_map = lambda i, meta: (meta[0], 0, 0)
    sums_shape = (slices, channels + LANES)
    in_specs = [pl.BlockSpec(block, m) for m in maps] + [
        whole(taps.shape), whole(affinity.shape), whole(softness.shape)]
    operands = [meta, *sources, taps, affinity, softness]
    aliases = {}
    if not first:
        in_specs += [pl.BlockSpec(memory_space=pl.ANY), whole(sums_shape)]
        aliases = {len(operands): 0}
        operands += list(carry)
    flops = steps * cells * (channels * 70 + 2 * channels * slices * 2)
    return pl.pallas_call(
        functools.partial(plane_kernel, first, last, 256),
        grid_spec=pltpu.PrefetchScalarGridSpec(
            num_scalar_prefetch=1,
            grid=(steps,),
            in_specs=in_specs,
            out_specs=[pl.BlockSpec((1, cells, slices), out_map), whole(sums_shape)],
            scratch_shapes=[
                pltpu.VMEM((27, 8, channels), F32),
                pltpu.VMEM((cells, channels + LANES), BF16),
            ],
        ),
        out_shape=[
            jax.ShapeDtypeStruct((planes, cells, slices), BF16),
            jax.ShapeDtypeStruct(sums_shape, BF16 if last else F32),
        ],
        input_output_aliases=aliases,
        cost_estimate=pl.CostEstimate(
            flops=flops * 8, bytes_accessed=steps * 3 * 2**20, transcendentals=steps * cells * channels * 2
        ),
        compiler_params=pltpu.CompilerParams(vmem_limit_bytes=32 * 2**20),
        name="planes",
    )(*operands)


def owner_kernel(parts_ref, content_ref, gain_ref, widening_ref, narrowing_ref, final_ref,
                 out_ref, spread_ref):
    channels = content_ref.shape[0]
    total = jnp.sum(parts_ref[...].astype(F32), axis=0)
    mass = total[:, channels : channels + 1] + total[:, channels + LANES // 2 : channels + LANES // 2 + 1]
    pooled = total[:, :channels] / (mass + epsilon)
    high = pooled.astype(BF16)
    low = (pooled - high.astype(F32)).astype(BF16)
    dot = functools.partial(jnp.dot, preferred_element_type=F32)
    tokens = dot(high, content_ref[...]) + dot(low, content_ref[...])
    center = jnp.mean(tokens, axis=-1, keepdims=True)
    spread = jnp.mean((tokens - center) ** 2, axis=-1, keepdims=True)
    normed = ((tokens - center) * (1.0 / jnp.sqrt(spread + epsilon)) * gain_ref[...]).astype(BF16)
    inner = gelu(dot(normed, widening_ref[...])).astype(BF16)
    out = (tokens + dot(inner, narrowing_ref[...])).astype(BF16)
    out_ref[...] = out
    mapped = dot(out, final_ref[...]).astype(BF16)
    spread_ref[...] = jnp.broadcast_to(mapped[None], spread_ref.shape)


def owner_call(parts, content, gain, widening, narrowing, final):
    n, rows, _ = parts.shape
    channels = content.shape[0]
    return pl.pallas_call(
        owner_kernel,
        out_shape=[
            jax.ShapeDtypeStruct((rows, channels), BF16),
            jax.ShapeDtypeStruct((n, rows, channels), BF16),
        ],
        compiler_params=pltpu.CompilerParams(vmem_limit_bytes=24 * 2**20),
        name="owner",
    )(parts, content, gain, widening, narrowing, final)


def update_kernel(x_ref, probs_ref, mapped_ref, out_ref):
    out_ref[...] = (
        x_ref[...].astype(F32)
        + jnp.dot(probs_ref[...], mapped_ref[...], preferred_element_type=F32)
    ).astype(BF16)


def update_call(x, probs, mapped):
    cells, channels = x.shape
    slices = probs.shape[1]
    rows = math.gcd(cells, 512)
    return pl.pallas_call(
        update_kernel,
        grid=(cells // rows,),
        in_specs=[
            pl.BlockSpec((rows, channels), lambda i: (i, 0)),
            pl.BlockSpec((rows, slices), lambda i: (i, 0)),
            pl.BlockSpec((slices, channels), lambda i: (0, 0)),
        ],
        out_specs=pl.BlockSpec((rows, channels), lambda i: (i, 0)),
        out_shape=jax.ShapeDtypeStruct(x.shape, BF16),
        compiler_params=pltpu.CompilerParams(vmem_limit_bytes=24 * 2**20),
        name="update",
    )(x, probs, mapped)


def per_device(
    mesh_feature_array,
    stencil_coefficients,
    partition_affinity_matrix,
    softness_mapping_matrix,
    content_mapping_matrix,
    layernorm_multiplier,
    widening_matrix,
    narrowing_matrix,
    final_mapping_matrix,
):
    x = mesh_feature_array
    planes, height, depth, channels = x.shape
    slices = partition_affinity_matrix.shape[1]
    n, me = lax.axis_size("gx"), lax.axis_index("gx")
    odd = lax.rem(me, 2)
    near = (planes - 1) * (1 - odd)
    far = (planes - 1) * odd
    pick = lambda index: lax.dynamic_slice_in_dim(x, index, 1, axis=0)
    far_pairs = [p for i in range(1, n - 1, 2) for p in ((i, i + 1), (i + 1, i))]
    near_pairs = [p for i in range(0, n, 2) for p in ((i, i + 1), (i + 1, i))]
    far_halo = lax.ppermute(pick(far), "gx", far_pairs)
    near_halo = lax.ppermute(pick(near), "gx", near_pairs)

    taps = stencil_coefficients.reshape(3, 9, channels)
    softness = jnp.broadcast_to(softness_mapping_matrix.astype(BF16)[:, None], (channels, LANES))
    args = (taps, partition_affinity_matrix, softness)
    meta_of = lambda index, low: jnp.stack([
        index, jnp.where(low, 1, planes - 2), jnp.where(low, 0, 2), 1, jnp.where(low, 2, 0)
    ]).astype(jnp.int32)
    inside = jnp.array([0, 0, 0, 1, 2], jnp.int32)
    carry = planes_call(x, None, inside, *args, None, False)
    carry = planes_call(x, near_halo, meta_of(near, odd == 1), *args, carry, False)
    probs, share = planes_call(x, far_halo, meta_of(far, odd == 0), *args, carry, True)

    parts = lax.all_to_all(share.reshape(n, slices // n, -1), "gx", 0, 0)
    own_out, mapped = owner_call(
        parts, content_mapping_matrix, layernorm_multiplier[None], widening_matrix,
        narrowing_matrix, final_mapping_matrix,
    )
    mapped = lax.all_to_all(mapped, "gx", 0, 0).reshape(slices, channels)
    cells = planes * height * depth
    updated = update_call(x.reshape(cells, channels), probs.reshape(cells, slices), mapped)
    return updated.reshape(x.shape), own_out


def solution(mesh):
    return jax.shard_map(
        per_device,
        mesh=mesh,
        in_specs=(P(("grp", "gx"), None, None, None), P(), P(), P(), P(), P(), P(), P(), P()),
        out_specs=(P(("grp", "gx"), None, None, None), P(("grp", "gx"), None)),
        check_vma=False,
    )
```

```python
import functools
import math

import jax
import jax.numpy as jnp
from jax import lax
from jax.experimental import pallas as pl
from jax.experimental.pallas import tpu as pltpu
from jax.sharding import PartitionSpec as P

epsilon = 1e-05
LANES = 128
BLOCK = 256
GROUP = 8
TILE = 16
F32, BF16 = jnp.float32, jnp.bfloat16
CONV = BF16
VMEM = pl.BlockSpec(memory_space=pltpu.VMEM)
SMEM = pl.BlockSpec(memory_space=pltpu.SMEM)
HBM = pl.BlockSpec(memory_space=pltpu.HBM)


def dot(a, b):
    return jnp.dot(a, b, preferred_element_type=F32)


def gelu(x):
    inner = x * (x * x * (0.044715 * math.sqrt(2 / math.pi)) + math.sqrt(2 / math.pi))
    half = 0.5 * x
    return half + half * jnp.tanh(inner)


def spread_taps(k_ref, planes, taps_ref):
    for role, plane in enumerate(planes):
        for tap in range(9):
            row = k_ref[plane, tap : tap + 1, :]
            taps_ref[9 * role + tap] = jnp.broadcast_to(row, taps_ref.shape[1:]).astype(CONV)


def conv_row(sources, taps_ref, lanes):
    sums = [None] * 3
    for role, rows in sources:
        for b, row in enumerate(rows):
            if row is None:
                continue
            depth, width = row.shape
            row = row.astype(CONV).reshape(depth // TILE, TILE, width)
            for c in range(3):
                term = row * taps_ref[9 * role + 3 * b + c, :, lanes]
                sums[c] = term if sums[c] is None else sums[c] + term
    before, here, after = (s.astype(F32).reshape(depth, width) for s in sums)
    position = lax.broadcasted_iota(jnp.int32, (depth, width), 0)
    before = jnp.where(position == 0, 0.0, pltpu.roll(before, 1, 0))
    after = jnp.where(position == depth - 1, 0.0, pltpu.roll(after, depth - 1, 0))
    return here + before + after


def padded_rows(ref, plane, y, lanes):
    return [ref[plane, y + b, :, lanes] for b in range(3)]


def channel_blocks(channels):
    return [slice(i, i + BLOCK) for i in range(0, channels, BLOCK)]


def assign(pre, affinity_ref, softness_ref, probs_ref, where, sums_ref, mass_ref):
    width = affinity_ref.shape[1]
    hid = gelu(pre).astype(BF16)
    raw = dot(hid, affinity_ref[...])
    soft = dot(hid, softness_ref[...])
    temperature = 0.25 + jnp.maximum(soft, 0.0) + jnp.log1p(jnp.exp(-jnp.abs(soft)))
    scale = (1.0 / math.log(2.0)) / temperature
    top = jnp.max(raw, axis=1, keepdims=True)
    scale = jnp.concatenate([scale] * (width // LANES), axis=1)
    powers = jnp.exp2((raw - top) * scale)
    probs = (powers * (1.0 / jnp.sum(powers, axis=1, keepdims=True))).astype(BF16)
    probs_ref[where] = probs
    sums_ref[...] += lax.dot_general(
        probs, hid, (((0,), (0,)), ((), ())), preferred_element_type=F32
    )
    mass_ref[...] += jnp.sum(probs.astype(F32).reshape(-1, 8, width), axis=0)


def pack_kernel(meta_ref, x_ref, far_ref, near_ref, sem):
    far = pltpu.make_async_copy(x_ref.at[pl.ds(meta_ref[0], 1)], far_ref, sem.at[0])
    near = pltpu.make_async_copy(x_ref.at[pl.ds(meta_ref[1], 1)], near_ref, sem.at[1])
    far.start()
    near.start()
    far.wait()
    near.wait()


def pack_call(x, meta):
    plane = jax.ShapeDtypeStruct((1, *x.shape[1:]), BF16)
    return pl.pallas_call(
        pack_kernel,
        in_specs=[SMEM, HBM],
        out_specs=[VMEM, VMEM],
        out_shape=[plane, plane],
        scratch_shapes=[pltpu.SemaphoreType.DMA((2,))],
        cost_estimate=pl.CostEstimate(flops=0, bytes_accessed=2**22, transcendentals=0),
        compiler_params=pltpu.CompilerParams(vmem_limit_bytes=16 * 2**20),
        name="pack",
    )(meta, x)


def inside_kernel(x_ref, k_ref, affinity_ref, softness_ref, probs_ref, partial_ref, sums_ref,
                  mass_ref, taps_ref, held_ref, even_ref, odd_ref, sem):
    planes, height, depth, channels = x_ref.shape
    loads = [
        pltpu.make_async_copy(x_ref.at[p], held_ref.at[p, pl.ds(1, height)], sem.at[p])
        for p in range(planes)
    ]
    for load in loads:
        load.start()
    spread_taps(k_ref, range(3), taps_ref)
    held_ref[:, 0] = jnp.zeros((planes, depth, channels), BF16)
    held_ref[:, height + 1] = jnp.zeros((planes, depth, channels), BF16)
    sums_ref[...] = jnp.zeros(sums_ref.shape, F32)
    mass_ref[...] = jnp.zeros(mass_ref.shape, F32)

    def partial(which, pairs):
        for lanes in channel_blocks(channels):
            def rows(i, carry):
                for j in range(2):
                    y = 2 * i + j
                    sources = [(role, padded_rows(held_ref, p, y, lanes)) for p, role in pairs]
                    total = conv_row(sources, taps_ref, lanes)
                    start = pl.multiple_of(y * depth, depth)
                    partial_ref[which, pl.ds(start, depth), lanes] = total.astype(BF16)
                return carry

            lax.fori_loop(0, height // 2, rows, 0)

    loads[0].wait()
    loads[1].wait()
    partial(0, ((0, 1), (1, 2)))
    for load in loads[2:]:
        load.wait()
    partial(1, ((planes - 2, 0), (planes - 1, 1)))

    groups = height // GROUP
    cells = GROUP * depth

    def conv(t, pre_ref):
        plane = t // groups
        for lanes in channel_blocks(channels):
            for j in range(GROUP):
                y = lax.rem(t, groups) * GROUP + j
                sources = [(role, padded_rows(held_ref, plane + role, y, lanes)) for role in range(3)]
                pre_ref[j * depth : (j + 1) * depth, lanes] = conv_row(sources, taps_ref, lanes)

    def slices(t, pre_ref):
        where = (t // groups, pl.ds(pl.multiple_of(lax.rem(t, groups) * cells, cells), cells))
        assign(pre_ref[...], affinity_ref, softness_ref, probs_ref, where, sums_ref, mass_ref)

    count = (planes - 2) * groups
    conv(jnp.int32(0), even_ref)

    def pair(s, carry):
        t = 2 * s
        slices(t, even_ref)
        conv(t + 1, odd_ref)
        slices(t + 1, odd_ref)
        conv(jnp.minimum(t + 2, count - 1), even_ref)
        return carry

    lax.fori_loop(0, count // 2, pair, 0)


def inside_call(x, taps, affinity, softness):
    planes, height, depth, channels = x.shape
    slices = affinity.shape[1]
    cells = height * depth
    work = planes * cells * channels
    return pl.pallas_call(
        inside_kernel,
        in_specs=[HBM, VMEM, VMEM, VMEM],
        out_specs=[VMEM] * 4,
        out_shape=[
            jax.ShapeDtypeStruct((planes - 2, cells, slices), BF16),
            jax.ShapeDtypeStruct((2, cells, channels), BF16),
            jax.ShapeDtypeStruct((slices, channels), F32),
            jax.ShapeDtypeStruct((8, slices), F32),
        ],
        scratch_shapes=[
            pltpu.VMEM((27, TILE, channels), CONV),
            pltpu.VMEM((planes, height + 2, depth, channels), BF16),
            pltpu.VMEM((GROUP * depth, channels), F32),
            pltpu.VMEM((GROUP * depth, channels), F32),
            pltpu.SemaphoreType.DMA((planes,)),
        ],
        cost_estimate=pl.CostEstimate(
            flops=work * 5000, bytes_accessed=2 * work, transcendentals=2 * work
        ),
        compiler_params=pltpu.CompilerParams(vmem_limit_bytes=32 * 2**20),
        name="inside",
    )(x, taps, affinity, softness)


def edge_kernel(last, meta_ref, halo_ref, partial_ref, k_ref, affinity_ref, softness_ref,
                sums_in_ref, mass_in_ref, probs_ref, sums_ref, mass_ref, taps_ref, pre_ref, *rest):
    _, height, depth, channels = halo_ref.shape
    if last:
        share_ref, (sums_ref, mass_ref) = sums_ref, rest
    spread_taps(k_ref, [meta_ref[1]], taps_ref)
    sums_ref[...] = sums_in_ref[...]
    mass_ref[...] = mass_in_ref[...]
    cells = GROUP * depth
    which = meta_ref[0]
    for first in range(0, height, GROUP):
        group = slice(first * depth, (first + GROUP) * depth)
        for lanes in channel_blocks(channels):
            for y in range(first, first + GROUP):
                rows = [halo_ref[0, y + b, :, lanes] if 0 <= y + b < height else None
                        for b in (-1, 0, 1)]
                at = slice(y * depth, (y + 1) * depth)
                total = conv_row([(0, rows)], taps_ref, lanes)
                pre_ref[at, lanes] = total + partial_ref[which, at, lanes].astype(F32)
        assign(pre_ref[group], affinity_ref, softness_ref, probs_ref, (0, group), sums_ref, mass_ref)
    if last:
        owners, rows, _ = share_ref.shape
        held = channels // LANES
        rows = (rows - 8) // held
        for i in range(held):
            part = sums_ref[:, i * LANES : (i + 1) * LANES].astype(BF16)
            share_ref[:, i * rows : (i + 1) * rows, :] = part.reshape(owners, rows, LANES)
        mass = jnp.sum(mass_ref[...], axis=0, keepdims=True)
        high = mass.astype(BF16).astype(F32)
        row = lax.broadcasted_iota(jnp.int32, (8, mass.shape[1]), 0)
        both = jnp.where(row == 0, high, jnp.where(row == 1, mass - high, 0.0)).astype(BF16)
        for owner in range(owners):
            start = owner * rows // LANES * LANES
            share_ref[owner, held * rows :, :] = both[:, start : start + LANES]


def edge_call(halo, meta, taps, affinity, softness, partial, sums, mass, owners, last):
    _, height, depth, channels = halo.shape
    slices = affinity.shape[1]
    cells = height * depth
    if last:
        rows = channels // LANES * (slices // owners) + 8
        outs = [jax.ShapeDtypeStruct((owners, rows, LANES), BF16)]
    else:
        outs = [jax.ShapeDtypeStruct(s.shape, F32) for s in (sums, mass)]
    scratch = [
        pltpu.VMEM((9, TILE, channels), CONV),
        pltpu.VMEM((cells, channels), F32),
    ]
    if last:
        scratch += [pltpu.VMEM(sums.shape, F32), pltpu.VMEM(mass.shape, F32)]
        kernel = lambda *refs: edge_kernel(True, *refs[:10], None, *refs[10:])
    else:
        kernel = functools.partial(edge_kernel, False)
    return pl.pallas_call(
        kernel,
        in_specs=[SMEM] + [VMEM] * 7,
        out_specs=[VMEM] * (1 + len(outs)),
        out_shape=[jax.ShapeDtypeStruct((1, cells, slices), BF16)] + outs,
        scratch_shapes=scratch,
        cost_estimate=pl.CostEstimate(
            flops=cells * channels * 5000, bytes_accessed=4 * cells * channels,
            transcendentals=2 * cells * channels,
        ),
        compiler_params=pltpu.CompilerParams(vmem_limit_bytes=24 * 2**20),
        name="edge",
    )(meta, halo, partial, taps, affinity, softness, sums, mass)


def owner_kernel(meta_ref, parts_ref, content_ref, gain_ref, widening_ref, narrowing_ref, final_ref,
                 out_ref, spread_ref):
    channels = content_ref.shape[0]
    held = channels // LANES
    rows = out_ref.shape[0]
    total = jnp.sum(parts_ref[...].astype(F32), axis=0)
    pooled = jnp.concatenate([total[i * rows : (i + 1) * rows] for i in range(held)], axis=1)
    mass = total[held * rows : held * rows + 1] + total[held * rows + 1 : held * rows + 2]
    lane = lax.broadcasted_iota(jnp.int32, (rows, LANES), 1)
    row = lax.broadcasted_iota(jnp.int32, (rows, LANES), 0)
    mass = jnp.sum(jnp.where(lane == row + meta_ref[0], mass, 0.0), axis=1, keepdims=True)
    pooled = pooled / (mass + epsilon)
    high = pooled.astype(BF16)
    low = (pooled - high.astype(F32)).astype(BF16)
    tokens = dot(high, content_ref[...]) + dot(low, content_ref[...])
    center = jnp.mean(tokens, axis=-1, keepdims=True)
    spread = jnp.mean((tokens - center) ** 2, axis=-1, keepdims=True)
    normed = ((tokens - center) * (1.0 / jnp.sqrt(spread + epsilon)) * gain_ref[...]).astype(BF16)
    inner = gelu(dot(normed, widening_ref[...])).astype(BF16)
    out = (tokens + dot(inner, narrowing_ref[...])).astype(BF16)
    out_ref[...] = out
    mapped = dot(out, final_ref[...]).astype(BF16)
    spread_ref[...] = jnp.broadcast_to(mapped[None], spread_ref.shape)


def owner_call(meta, parts, content, gain, widening, narrowing, final):
    channels = content.shape[0]
    owners = parts.shape[0]
    rows = (parts.shape[1] - 8) // (channels // LANES)
    return pl.pallas_call(
        owner_kernel,
        in_specs=[SMEM] + [VMEM] * 6,
        out_specs=[VMEM, VMEM],
        out_shape=[
            jax.ShapeDtypeStruct((rows, channels), BF16),
            jax.ShapeDtypeStruct((owners, rows, channels), BF16),
        ],
        compiler_params=pltpu.CompilerParams(vmem_limit_bytes=24 * 2**20),
        name="owner",
    )(meta, parts, content, gain, widening, narrowing, final)


def update_kernel(meta_ref, x_ref, inside_ref, near_ref, far_ref, mapped_ref, out_ref, done_ref, sem):
    planes, cells, channels = x_ref.shape
    rows = done_ref.shape[1]
    pieces = cells // rows
    copies = []
    for step in range(planes * pieces):
        part, piece = divmod(step, pieces)
        at = slice(piece * rows, (piece + 1) * rows)
        if part < planes - 2:
            plane, probs = part + 1, inside_ref[part, at]
        elif part == planes - 2:
            plane, probs = meta_ref[1], near_ref[0, at]
        else:
            plane, probs = meta_ref[0], far_ref[0, at]
        slot = step % 2
        if step >= 2:
            copies[step - 2].wait()
        done_ref[slot] = (x_ref[plane, at].astype(F32) + dot(probs, mapped_ref[...])).astype(BF16)
        copies.append(pltpu.make_async_copy(done_ref.at[slot], out_ref.at[plane, at], sem.at[slot]))
        copies[-1].start()
    for copy in copies[-2:]:
        copy.wait()


def update_call(meta, x, inside, near, far, mapped):
    channels = x.shape[2]
    return pl.pallas_call(
        update_kernel,
        in_specs=[SMEM] + [VMEM] * 5,
        out_specs=HBM,
        out_shape=jax.ShapeDtypeStruct(x.shape, BF16),
        scratch_shapes=[
            pltpu.VMEM((2, math.gcd(x.shape[1], 512), channels), BF16),
            pltpu.SemaphoreType.DMA((2,)),
        ],
        compiler_params=pltpu.CompilerParams(vmem_limit_bytes=16 * 2**20),
        name="update",
    )(meta, x, inside, near, far, mapped)


def per_device(
    mesh_feature_array,
    stencil_coefficients,
    partition_affinity_matrix,
    softness_mapping_matrix,
    content_mapping_matrix,
    layernorm_multiplier,
    widening_matrix,
    narrowing_matrix,
    final_mapping_matrix,
):
    x = mesh_feature_array
    planes, height, depth, channels = x.shape
    slices = partition_affinity_matrix.shape[1]
    n, me = lax.axis_size("gx"), lax.axis_index("gx")
    odd = lax.rem(me, 2)
    near = (planes - 1) * (1 - odd)
    far = (planes - 1) * odd
    ends = jnp.stack([far, near]).astype(jnp.int32)
    far_pairs = [p for i in range(1, n - 1, 2) for p in ((i, i + 1), (i + 1, i))]
    near_pairs = [p for i in range(0, n, 2) for p in ((i, i + 1), (i + 1, i))]
    far_plane, near_plane = pack_call(x, ends)
    far_halo = lax.ppermute(far_plane, "gx", far_pairs)
    near_halo = lax.ppermute(near_plane, "gx", near_pairs)

    taps = stencil_coefficients.reshape(3, 9, channels)
    softness = jnp.broadcast_to(softness_mapping_matrix.astype(BF16)[:, None], (channels, LANES))
    args = (taps, partition_affinity_matrix, softness)
    near_meta = jnp.stack([1 - odd, 2 * (1 - odd)]).astype(jnp.int32)
    far_meta = jnp.stack([odd, 2 * odd]).astype(jnp.int32)

    owners = min(n, slices // TILE)
    share = n // owners
    groups = [[s + share * j for j in range(owners)] for s in range(share)]
    owner = me // share
    inside_probs, partial, sums, mass = inside_call(x, *args)
    near_probs, sums, mass = edge_call(near_halo, near_meta, *args, partial, sums, mass, owners, False)
    far_probs, parts = edge_call(far_halo, far_meta, *args, partial, sums, mass, owners, True)

    parts = lax.all_to_all(parts, "gx", 0, 0, axis_index_groups=groups)
    if share > 1:
        sharers = [[share * j + s for s in range(share)] for j in range(owners)]
        parts = lax.psum(parts, "gx", axis_index_groups=sharers)
    own_out, mapped = owner_call(
        lax.rem(owner * (slices // owners), LANES).astype(jnp.int32)[None], parts,
        content_mapping_matrix, layernorm_multiplier[None], widening_matrix, narrowing_matrix,
        final_mapping_matrix,
    )
    if share > 1:
        own_out = lax.dynamic_slice_in_dim(own_out, lax.rem(me, share) * (slices // n), slices // n)
    mapped = lax.all_to_all(mapped, "gx", 0, 0, axis_index_groups=groups).reshape(slices, channels)
    updated = update_call(
        ends, x.reshape(planes, height * depth, channels), inside_probs, near_probs, far_probs, mapped
    )
    return updated.reshape(x.shape), own_out


def solution(mesh):
    return jax.shard_map(
        per_device,
        mesh=mesh,
        in_specs=(P(("grp", "gx"), None, None, None), P(), P(), P(), P(), P(), P(), P(), P()),
        out_specs=(P(("grp", "gx"), None, None, None), P(("grp", "gx"), None)),
        check_vma=False,
    )
```

```python
import functools
import math

import jax
import jax.numpy as jnp
from jax import lax
from jax.experimental import pallas as pl
from jax.experimental.pallas import tpu as pltpu
from jax.sharding import PartitionSpec as P

epsilon = 1e-05
LANES = 128
BLOCK = 256
GROUP = 8
TILE = 16
MIB = 2**20
F32, BF16 = jnp.float32, jnp.bfloat16
CONV = BF16
VMEM = pl.BlockSpec(memory_space=pltpu.VMEM)
SMEM = pl.BlockSpec(memory_space=pltpu.SMEM)
HBM = pl.BlockSpec(memory_space=pltpu.HBM)


def dot(a, b):
    return jnp.dot(a, b, preferred_element_type=F32)


def gelu(x):
    inner = x * (x * x * (0.044715 * math.sqrt(2 / math.pi)) + math.sqrt(2 / math.pi))
    half = 0.5 * x
    return half + half * jnp.tanh(inner)


def spread_taps(k_ref, planes, taps_ref):
    for role, plane in enumerate(planes):
        for tap in range(9):
            row = k_ref[plane, tap : tap + 1, :]
            taps_ref[9 * role + tap] = jnp.broadcast_to(row, taps_ref.shape[1:]).astype(CONV)


def conv_row(sources, taps_ref, lanes):
    sums = [None] * 3
    for role, rows in sources:
        for b, row in enumerate(rows):
            if row is None:
                continue
            depth, width = row.shape
            row = row.astype(CONV).reshape(depth // TILE, TILE, width)
            for c in range(3):
                term = row * taps_ref[9 * role + 3 * b + c, :, lanes]
                sums[c] = term if sums[c] is None else sums[c] + term
    before, here, after = (s.astype(F32).reshape(depth, width) for s in sums)
    position = lax.broadcasted_iota(jnp.int32, (depth, width), 0)
    before = jnp.where(position == 0, 0.0, pltpu.roll(before, 1, 0))
    after = jnp.where(position == depth - 1, 0.0, pltpu.roll(after, depth - 1, 0))
    return here + before + after


def padded_rows(ref, plane, y, lanes):
    return [ref[plane, y + b, :, lanes] for b in range(3)]


def channel_blocks(channels):
    return [slice(i, i + BLOCK) for i in range(0, channels, BLOCK)]


def nt_dot(a, b):
    return lax.dot_general(a, b, (((1,), (1,)), ((), ())), preferred_element_type=F32)


def identity(size):
    row = lax.broadcasted_iota(jnp.int32, (size, size), 0)
    return (row == lax.broadcasted_iota(jnp.int32, (size, size), 1)).astype(BF16)


def assign(pre, map_ref, mass_ref):
    cells = pre.shape[0]
    slices = map_ref.shape[0] - TILE
    hid = gelu(pre).astype(BF16)
    raw = nt_dot(map_ref[...], hid)
    soft = raw[slices : slices + 8]
    temperature = 0.25 + jnp.maximum(soft, 0.0) + jnp.log(1.0 + jnp.exp(-jnp.abs(soft)))
    scale = (1.0 / math.log(2.0)) / temperature
    raw = raw[:slices].reshape(slices // 8, 8, cells)
    top = jnp.max(jnp.max(raw, axis=0), axis=0, keepdims=True)
    powers = jnp.exp2((raw - top[None]) * scale[None])
    total = jnp.sum(jnp.sum(powers, axis=0), axis=0, keepdims=True)
    probs = (powers * (1.0 / total)[None]).reshape(slices, cells)
    mass = probs[:, :LANES]
    for start in range(LANES, cells, LANES):
        mass = mass + probs[:, start : start + LANES]
    mass_ref[...] += mass
    by_slice = probs.astype(BF16)
    by_cell = nt_dot(identity(cells), by_slice).astype(BF16)
    return hid, by_slice, by_cell


def pack_kernel(meta_ref, x_ref, far_ref, near_ref, sem):
    far = pltpu.make_async_copy(x_ref.at[pl.ds(meta_ref[0], 1)], far_ref, sem.at[0])
    near = pltpu.make_async_copy(x_ref.at[pl.ds(meta_ref[1], 1)], near_ref, sem.at[1])
    far.start()
    near.start()
    far.wait()
    near.wait()


def pack_call(x, meta):
    plane = jax.ShapeDtypeStruct((1, *x.shape[1:]), BF16)
    return pl.pallas_call(
        pack_kernel,
        in_specs=[SMEM, HBM],
        out_specs=[HBM, HBM],
        out_shape=[plane, plane],
        scratch_shapes=[pltpu.SemaphoreType.DMA((2,))],
        cost_estimate=pl.CostEstimate(flops=0, bytes_accessed=2**22, transcendentals=0),
        compiler_params=pltpu.CompilerParams(vmem_limit_bytes=58 * MIB),
        name="pack",
    )(meta, x)


def inside_kernel(run, x_ref, k_ref, affinity_ref, softness_ref, probs_ref, partial_ref, sums_ref,
                  mass_ref, map_ref, taps_ref, held_ref, even_ref, odd_ref, hid_ref, by_slice_ref, sem):
    planes, height, depth, channels = x_ref.shape
    slices = affinity_ref.shape[1]
    loads = [
        pltpu.make_async_copy(x_ref.at[p], held_ref.at[p, pl.ds(1, height)], sem.at[p])
        for p in range(planes)
    ]
    for load in loads:
        load.start()
    spread_taps(k_ref, range(3), taps_ref)
    held_ref[:, 0] = jnp.zeros((planes, depth, channels), BF16)
    held_ref[:, height + 1] = jnp.zeros((planes, depth, channels), BF16)
    sums_ref[...] = jnp.zeros(sums_ref.shape, F32)
    mass_ref[...] = jnp.zeros(mass_ref.shape, F32)
    new = lax.broadcasted_iota(jnp.int32, (slices, slices), 0)
    old = lax.broadcasted_iota(jnp.int32, (slices, slices), 1)
    half = (new >= slices // 2).astype(jnp.int32)
    rest = new - half * (slices // 2)
    place = rest & (run - 1)
    order = (old == 2 * (rest - place) + half * run + place).astype(BF16)
    map_ref[:slices] = nt_dot(order, affinity_ref[...]).astype(BF16)
    map_ref[slices:] = jnp.broadcast_to(softness_ref[...], (TILE, channels)).astype(BF16)

    def partial(which, pairs):
        for lanes in channel_blocks(channels):
            def rows(i, carry):
                for j in range(2):
                    y = 2 * i + j
                    sources = [(role, padded_rows(held_ref, p, y, lanes)) for p, role in pairs]
                    total = conv_row(sources, taps_ref, lanes)
                    start = pl.multiple_of(y * depth, depth)
                    partial_ref[which, pl.ds(start, depth), lanes] = total.astype(BF16)
                return carry

            lax.fori_loop(0, height // 2, rows, 0)

    loads[0].wait()
    loads[1].wait()
    partial(0, ((0, 1), (1, 2)))
    for load in loads[2:]:
        load.wait()
    partial(1, ((planes - 2, 0), (planes - 1, 1)))

    groups = height // GROUP
    cells = GROUP * depth

    def conv(t, pre_ref):
        plane = t // groups
        for lanes in channel_blocks(channels):
            for j in range(GROUP):
                y = lax.rem(t, groups) * GROUP + j
                sources = [(role, padded_rows(held_ref, plane + role, y, lanes)) for role in range(3)]
                pre_ref[j * depth : (j + 1) * depth, lanes] = conv_row(sources, taps_ref, lanes)

    def share(t, pre_ref, at):
        hid, by_slice, by_cell = assign(pre_ref[...], map_ref, mass_ref)
        start = pl.multiple_of(lax.rem(t, groups) * cells, cells)
        probs_ref[t // groups, pl.ds(start, cells), :] = by_cell
        hid_ref[at, :] = hid
        by_slice_ref[:, at] = by_slice

    count = (planes - 2) * groups
    conv(jnp.int32(0), even_ref)

    def pair(s, carry):
        t = 2 * s
        share(t, even_ref, slice(0, cells))
        conv(t + 1, odd_ref)
        share(t + 1, odd_ref, slice(cells, 2 * cells))
        sums_ref[...] += dot(by_slice_ref[...], hid_ref[...])
        conv(jnp.minimum(t + 2, count - 1), even_ref)
        return carry

    lax.fori_loop(0, count // 2, pair, 0)


def inside_call(x, taps, affinity, softness, run):
    planes, height, depth, channels = x.shape
    slices = affinity.shape[1]
    cells = height * depth
    work = planes * cells * channels
    return pl.pallas_call(
        functools.partial(inside_kernel, run),
        in_specs=[HBM, VMEM, VMEM, VMEM],
        out_specs=[VMEM] * 5,
        out_shape=[
            jax.ShapeDtypeStruct((planes - 2, cells, slices), BF16),
            jax.ShapeDtypeStruct((2, cells, channels), BF16),
            jax.ShapeDtypeStruct((slices, channels), F32),
            jax.ShapeDtypeStruct((slices, LANES), F32),
            jax.ShapeDtypeStruct((slices + TILE, channels), BF16),
        ],
        scratch_shapes=[
            pltpu.VMEM((27, TILE, channels), CONV),
            pltpu.VMEM((planes, height + 2, depth, channels), BF16),
            pltpu.VMEM((GROUP * depth, channels), F32),
            pltpu.VMEM((GROUP * depth, channels), F32),
            pltpu.VMEM((2 * GROUP * depth, channels), BF16),
            pltpu.VMEM((slices, 2 * GROUP * depth), BF16),
            pltpu.SemaphoreType.DMA((planes,)),
        ],
        cost_estimate=pl.CostEstimate(
            flops=work * 9000, bytes_accessed=2 * work, transcendentals=2 * work
        ),
        compiler_params=pltpu.CompilerParams(vmem_limit_bytes=56 * MIB),
        name="inside",
    )(x, taps, affinity, softness)


def edge_kernel(meta_ref, halo_ref, partial_ref, k_ref, map_ref, sums_in_ref, mass_in_ref,
                probs_ref, *rest):
    last = len(rest) == 10
    if last:
        send_ref, keep_ref, *rest = rest
    sums_ref, mass_ref, taps_ref, pre_ref, hid_ref, by_slice_ref, *rest = rest
    _, height, depth, channels = halo_ref.shape
    slices = sums_in_ref.shape[0]
    spread_taps(k_ref, [meta_ref[1]], taps_ref)
    mass_ref[...] = mass_in_ref[...]
    cells = GROUP * depth
    which = meta_ref[0]
    for first in range(0, height, GROUP):
        group = slice(first * depth, first * depth + cells)
        for lanes in channel_blocks(channels):
            for y in range(first, first + GROUP):
                rows = [halo_ref[0, y + b, :, lanes] if 0 <= y + b < height else None
                        for b in (-1, 0, 1)]
                at = slice(y * depth, (y + 1) * depth)
                total = conv_row([(0, rows)], taps_ref, lanes)
                pre_ref[at, lanes] = total + partial_ref[which, at, lanes].astype(F32)
        hid, by_slice, by_cell = assign(pre_ref[group], map_ref, mass_ref)
        probs_ref[0, group] = by_cell
        hid_ref[group] = hid
        by_slice_ref[:, group] = by_slice
    sums_ref[...] = sums_in_ref[...] + dot(by_slice_ref[...], hid_ref[...])
    if not last:
        return
    split_ref, lane_ref = rest
    mass = lax.dot_general(
        jnp.ones((8, LANES), F32), mass_ref[...], (((1,), (1,)), ((), ())),
        preferred_element_type=F32, precision=lax.Precision.HIGHEST,
    )
    split_ref[...] = split(mass)
    owners, rows, _ = send_ref.shape
    held = channels // LANES
    rows = (rows - 8) // held
    odd = meta_ref[2]
    for ref, half in ((send_ref, 1 - odd), (keep_ref, odd)):
        start = pl.multiple_of(half * (slices // 2), slices // 2)
        for i in range(held):
            part = sums_ref[pl.ds(start, slices // 2), i * LANES : (i + 1) * LANES].astype(BF16)
            ref[:, i * rows : (i + 1) * rows, :] = part.reshape(owners, rows, LANES)
        for owner in range(owners):
            lane = pl.multiple_of(start + owner * rows // LANES * LANES, LANES)
            ref[owner, held * rows :, :] = split_ref[:, pl.ds(lane, LANES)].astype(BF16)


def split(mass):
    high = mass.astype(BF16).astype(F32)
    row = lax.broadcasted_iota(jnp.int32, mass.shape, mass.ndim - 2)
    return jnp.where(row == 0, high, jnp.where(row == 1, mass - high, 0.0))


def edge_call(halo, meta, taps, maps, partial, sums, mass, owners, last):
    _, height, depth, channels = halo.shape
    slices = sums.shape[0]
    cells = height * depth
    carry = [(s.shape, F32) for s in (sums, mass)]
    scratch = [
        pltpu.VMEM((9, TILE, channels), CONV),
        pltpu.VMEM((cells, channels), F32),
        pltpu.VMEM((cells, channels), BF16),
        pltpu.VMEM((slices, cells), BF16),
    ]
    if last:
        rows = channels // LANES * (slices // 2 // owners) + 8
        outs = [((owners, rows, LANES), BF16)] * 2
        scratch = [pltpu.VMEM(*c) for c in carry] + scratch + [
            pltpu.VMEM((8, slices), F32), pltpu.VMEM((8, LANES), F32)]
    else:
        outs = carry
    return pl.pallas_call(
        edge_kernel,
        in_specs=[SMEM] + [VMEM] * 6,
        out_specs=[VMEM] * (1 + len(outs)),
        out_shape=[jax.ShapeDtypeStruct((1, cells, slices), BF16)]
        + [jax.ShapeDtypeStruct(*o) for o in outs],
        scratch_shapes=scratch,
        cost_estimate=pl.CostEstimate(
            flops=cells * channels * 16000, bytes_accessed=4 * cells * channels,
            transcendentals=2 * cells * channels,
        ),
        compiler_params=pltpu.CompilerParams(vmem_limit_bytes=46 * MIB),
        name="edge",
    )(meta, halo, partial, taps, maps, sums, mass)


def merge_kernel(keep_ref, other_ref, out_ref):
    total = keep_ref[...].astype(F32) + other_ref[...].astype(F32)
    rows = total.shape[1] - 8
    out_ref[:, :rows] = total[:, :rows].astype(BF16)
    tail = total[:, rows:]
    mass = jnp.broadcast_to(tail[:, 0:1] + tail[:, 1:2], tail.shape)
    out_ref[:, rows:] = split(mass).astype(BF16)


def merge_call(keep, other):
    return pl.pallas_call(
        merge_kernel,
        in_specs=[VMEM, VMEM],
        out_specs=VMEM,
        out_shape=jax.ShapeDtypeStruct(keep.shape, BF16),
        compiler_params=pltpu.CompilerParams(vmem_limit_bytes=46 * MIB),
        name="merge",
    )(keep, other)


def owner_kernel(meta_ref, parts_ref, gain_ref, content_ref, widening_ref, narrowing_ref, final_ref,
                 out_ref, spread_ref, content, widening, narrowing, final, sem):
    loads = [
        pltpu.make_async_copy(src, dst, sem.at[i])
        for i, (src, dst) in enumerate(((content_ref, content), (widening_ref, widening),
                                        (narrowing_ref, narrowing), (final_ref, final)))
    ]
    for load in loads:
        load.start()
    channels = content.shape[0]
    held = channels // LANES
    rows = out_ref.shape[0]
    total = jnp.sum(parts_ref[...].astype(F32), axis=0)
    pooled = jnp.concatenate([total[i * rows : (i + 1) * rows] for i in range(held)], axis=1)
    mass = total[held * rows : held * rows + 1] + total[held * rows + 1 : held * rows + 2]
    lane = lax.broadcasted_iota(jnp.int32, (rows, LANES), 1)
    row = lax.broadcasted_iota(jnp.int32, (rows, LANES), 0)
    mass = jnp.sum(jnp.where(lane == row + meta_ref[0], mass, 0.0), axis=1, keepdims=True)
    pooled = pooled / (mass + epsilon)
    high = pooled.astype(BF16)
    low = (pooled - high.astype(F32)).astype(BF16)
    loads[0].wait()
    tokens = dot(high, content[...]) + dot(low, content[...])
    center = jnp.mean(tokens, axis=-1, keepdims=True)
    spread = jnp.mean((tokens - center) ** 2, axis=-1, keepdims=True)
    normed = ((tokens - center) * (1.0 / jnp.sqrt(spread + epsilon)) * gain_ref[...]).astype(BF16)
    loads[1].wait()
    inner = gelu(dot(normed, widening[...])).astype(BF16)
    loads[2].wait()
    out = (tokens + dot(inner, narrowing[...])).astype(BF16)
    out_ref[...] = out
    loads[3].wait()
    mapped = dot(out, final[...]).astype(BF16)
    spread_ref[...] = jnp.broadcast_to(mapped[None], spread_ref.shape)


def owner_call(meta, parts, gain, *weights):
    channels = weights[0].shape[0]
    owners = parts.shape[0]
    rows = (parts.shape[1] - 8) // (channels // LANES)
    return pl.pallas_call(
        owner_kernel,
        in_specs=[SMEM] + [VMEM] * 2 + [HBM] * 4,
        out_specs=[VMEM, VMEM],
        out_shape=[
            jax.ShapeDtypeStruct((rows, channels), BF16),
            jax.ShapeDtypeStruct((owners, rows, channels), BF16),
        ],
        scratch_shapes=[pltpu.VMEM(w.shape, BF16) for w in weights] + [pltpu.SemaphoreType.DMA((4,))],
        compiler_params=pltpu.CompilerParams(vmem_limit_bytes=46 * MIB),
        name="owner",
    )(meta, parts, gain, *weights)


def update_kernel(meta_ref, x_ref, inside_ref, near_ref, far_ref, own_ref, other_ref, out_ref,
                  held_ref, done_ref, mapped_ref, load_sem, store_sem):
    planes, cells, channels = x_ref.shape
    half = own_ref.shape[0]
    rows = math.gcd(cells, 512)
    steps = []
    for part in range(planes):
        plane = part + 1 if part < planes - 2 else meta_ref[planes - 1 - part]
        for start in range(0, cells, rows):
            steps.append((part, plane, slice(start, start + rows)))
    loads = [
        pltpu.make_async_copy(x_ref.at[plane, at], held_ref.at[part, at], load_sem.at[i])
        for i, (part, plane, at) in enumerate(steps)
    ]
    for load in loads:
        load.start()
    odd = meta_ref[2]
    mapped_ref[pl.ds(pl.multiple_of(odd * half, half), half)] = own_ref[...]
    mapped_ref[pl.ds(pl.multiple_of((1 - odd) * half, half), half)] = other_ref[...]
    stores = []
    for i, (part, plane, at) in enumerate(steps):
        if part < planes - 2:
            probs = inside_ref[part, at]
        else:
            probs = (near_ref if part == planes - 2 else far_ref)[0, at]
        change = dot(probs, mapped_ref[...])
        loads[i].wait()
        done_ref[part, at] = (held_ref[part, at].astype(F32) + change).astype(BF16)
        stores.append(
            pltpu.make_async_copy(done_ref.at[part, at], out_ref.at[plane, at], store_sem.at[i])
        )
        stores[-1].start()
    for store in stores:
        store.wait()


def update_call(meta, x, inside, near, far, own, other):
    planes, cells, channels = x.shape
    steps = planes * cells // math.gcd(cells, 512)
    return pl.pallas_call(
        update_kernel,
        in_specs=[SMEM, HBM] + [VMEM] * 5,
        out_specs=HBM,
        out_shape=jax.ShapeDtypeStruct(x.shape, BF16),
        scratch_shapes=[
            pltpu.VMEM(x.shape, BF16),
            pltpu.VMEM(x.shape, BF16),
            pltpu.VMEM((2 * own.shape[0], channels), BF16),
            pltpu.SemaphoreType.DMA((steps,)),
            pltpu.SemaphoreType.DMA((steps,)),
        ],
        compiler_params=pltpu.CompilerParams(vmem_limit_bytes=46 * MIB),
        name="update",
    )(meta, x, inside, near, far, own, other)


def per_device(
    mesh_feature_array,
    stencil_coefficients,
    partition_affinity_matrix,
    softness_mapping_matrix,
    content_mapping_matrix,
    layernorm_multiplier,
    widening_matrix,
    narrowing_matrix,
    final_mapping_matrix,
):
    x = mesh_feature_array
    planes, height, depth, channels = x.shape
    slices = partition_affinity_matrix.shape[1]
    n, me = lax.axis_size("gx"), lax.axis_index("gx")
    odd = lax.rem(me, 2)
    near = (planes - 1) * (1 - odd)
    far = (planes - 1) * odd
    ends = jnp.stack([far, near, odd]).astype(jnp.int32)
    far_pairs = [p for i in range(1, n - 1, 2) for p in ((i, i + 1), (i + 1, i))]
    near_pairs = [p for i in range(0, n, 2) for p in ((i, i + 1), (i + 1, i))]
    far_plane, near_plane = pack_call(x, ends)
    far_halo = lax.ppermute(far_plane, "gx", far_pairs)
    near_halo = lax.ppermute(near_plane, "gx", near_pairs)

    taps = stencil_coefficients.reshape(3, 9, channels)
    near_meta = jnp.stack([1 - odd, 2 * (1 - odd), odd]).astype(jnp.int32)
    far_meta = jnp.stack([odd, 2 * odd, odd]).astype(jnp.int32)

    owners = min(n // 2, slices // 2 // TILE)
    share = n // 2 // owners
    groups = [[2 * (share * j + s) + h for j in range(owners)] for h in range(2) for s in range(share)]
    owner = me // 2 // share
    rows = slices // 2 // owners
    inside_probs, partial, sums, mass, maps = inside_call(
        x, taps, partition_affinity_matrix, softness_mapping_matrix[None], slices // n
    )
    near_probs, sums, mass = edge_call(
        near_halo, near_meta, taps, maps, partial, sums, mass, owners, False
    )
    far_probs, send, keep = edge_call(
        far_halo, far_meta, taps, maps, partial, sums, mass, owners, True
    )

    parts = merge_call(keep, lax.ppermute(send, "gx", near_pairs))
    parts = lax.all_to_all(parts, "gx", 0, 0, axis_index_groups=groups)
    if share > 1:
        sharers = [[2 * (share * j + s) + h for s in range(share)]
                   for h in range(2) for j in range(owners)]
        parts = lax.psum(parts, "gx", axis_index_groups=sharers)
    own_out, mapped = owner_call(
        lax.rem(owner * rows, LANES).astype(jnp.int32)[None], parts, layernorm_multiplier[None],
        content_mapping_matrix, widening_matrix, narrowing_matrix, final_mapping_matrix,
    )
    if share > 1:
        place = lax.rem(me // 2, share) * (slices // n)
        own_out = lax.dynamic_slice_in_dim(own_out, place, slices // n)
    mapped = lax.all_to_all(mapped, "gx", 0, 0, axis_index_groups=groups)
    mapped = mapped.reshape(slices // 2, channels)
    updated = update_call(
        ends, x.reshape(planes, height * depth, channels), inside_probs, near_probs, far_probs,
        mapped, lax.ppermute(mapped, "gx", near_pairs),
    )
    return updated.reshape(x.shape), own_out


def solution(mesh):
    return jax.shard_map(
        per_device,
        mesh=mesh,
        in_specs=(P(("grp", "gx"), None, None, None), P(), P(), P(), P(), P(), P(), P(), P()),
        out_specs=(P(("grp", "gx"), None, None, None), P(("grp", "gx"), None)),
        check_vma=False,
    )
```

```python
import functools
import math

import jax
import jax.numpy as jnp
from jax import lax
from jax.experimental import pallas as pl
from jax.experimental.pallas import tpu as pltpu
from jax.sharding import PartitionSpec as P

epsilon = 1e-05
LANES = 128
BLOCK = 256
GROUP = 256
TILE = 16
MIB = 2**20
LIMIT = 32 * MIB
F32, BF16 = jnp.float32, jnp.bfloat16
CONV = BF16
VMEM = pl.BlockSpec(memory_space=pltpu.VMEM)
SMEM = pl.BlockSpec(memory_space=pltpu.SMEM)
HBM = pl.BlockSpec(memory_space=pltpu.HBM)


def dot(a, b):
    return jnp.dot(a, b, preferred_element_type=F32)


def gelu(x):
    inner = x * (x * x * (0.044715 * math.sqrt(2 / math.pi)) + math.sqrt(2 / math.pi))
    half = 0.5 * x
    return half + half * jnp.tanh(inner)


def spread_taps(k_ref, planes, taps_ref):
    for role, plane in enumerate(planes):
        for tap in range(9):
            row = k_ref[plane, tap : tap + 1, :]
            taps_ref[9 * role + tap] = jnp.broadcast_to(row, taps_ref.shape[1:]).astype(CONV)


def conv_row(sources, taps_ref, lanes):
    sums = [None] * 3
    for role, rows in sources:
        for b, row in enumerate(rows):
            if row is None:
                continue
            depth, width = row.shape
            row = row.astype(CONV).reshape(depth // TILE, TILE, width)
            for c in range(3):
                term = row * taps_ref[9 * role + 3 * b + c, :, lanes]
                sums[c] = term if sums[c] is None else sums[c] + term
    before, here, after = (s.astype(F32).reshape(depth, width) for s in sums)
    position = lax.broadcasted_iota(jnp.int32, (depth, width), 0)
    before = jnp.where(position == 0, 0.0, pltpu.roll(before, 1, 0))
    after = jnp.where(position == depth - 1, 0.0, pltpu.roll(after, depth - 1, 0))
    return here + before + after


def conv_plane(planes, taps_ref, put):
    height, channels = planes[0][1].shape[1], planes[0][1].shape[3]

    def row(y, lanes):
        sources = []
        for role, ref, index in planes:
            rows = [None if isinstance(y, int) and not 0 <= y + b < height else ref[index, y + b, :, lanes]
                    for b in (-1, 0, 1)]
            sources.append((role, rows))
        put(y, lanes, conv_row(sources, taps_ref, lanes))

    blocks = [slice(i, i + BLOCK) for i in range(0, channels, BLOCK)]
    for y in (0, height - 1):
        for lanes in blocks:
            row(y, lanes)

    def pair(i, carry):
        for lanes in blocks:
            row(2 * i + 1, lanes)
            row(2 * i + 2, lanes)
        return carry

    lax.fori_loop(0, (height - 2) // 2, pair, 0)


def cells_of(y, depth):
    return pl.ds(y * depth if isinstance(y, int) else pl.multiple_of(y * depth, depth), depth)


def nt_dot(a, b):
    return lax.dot_general(a, b, (((1,), (1,)), ((), ())), preferred_element_type=F32)


def identity(size):
    row = lax.broadcasted_iota(jnp.int32, (size, size), 0)
    return (row == lax.broadcasted_iota(jnp.int32, (size, size), 1)).astype(BF16)


def assign(hid, map_ref, mass_ref):
    cells = hid.shape[0]
    slices = map_ref.shape[0] - TILE
    raw = nt_dot(map_ref[...], hid)
    soft = raw[slices : slices + 8]
    temperature = 0.25 + jnp.maximum(soft, 0.0) + jnp.log(1.0 + jnp.exp(-jnp.abs(soft)))
    scale = (1.0 / math.log(2.0)) / temperature
    raw = raw[:slices].reshape(slices // 8, 8, cells)
    top = jnp.max(jnp.max(raw, axis=0), axis=0, keepdims=True)
    powers = jnp.exp2((raw - top[None]) * scale[None])
    total = jnp.sum(jnp.sum(powers, axis=0), axis=0, keepdims=True)
    probs = (powers * (1.0 / total)[None]).reshape(slices, cells)
    mass = probs[:, :LANES]
    for start in range(LANES, cells, LANES):
        mass = mass + probs[:, start : start + LANES]
    mass_ref[...] += mass
    by_slice = probs.astype(BF16)
    by_cell = nt_dot(identity(cells), by_slice).astype(BF16)
    return by_slice, by_cell


def assign_plane(hid_ref, map_ref, by_slice_ref, probs_ref, plane, sums_ref, mass_ref):
    cells = hid_ref.shape[0]

    def group(i, carry):
        at = pl.ds(pl.multiple_of(i * GROUP, GROUP), GROUP)
        by_slice, by_cell = assign(hid_ref[at, :], map_ref, mass_ref)
        probs_ref[plane, at, :] = by_cell
        by_slice_ref[:, at] = by_slice
        return carry

    lax.fori_loop(0, cells // GROUP, group, 0)
    sums_ref[...] += dot(by_slice_ref[...], hid_ref[...])


def pack_kernel(meta_ref, x_ref, far_ref, near_ref, held_ref, sem):
    loads = [
        pltpu.make_async_copy(x_ref.at[pl.ds(meta_ref[i], 1)], held_ref.at[pl.ds(i, 1)], sem.at[i])
        for i in range(2)
    ]
    stores = [
        pltpu.make_async_copy(held_ref.at[pl.ds(i, 1)], ref, sem.at[2 + i])
        for i, ref in enumerate((far_ref, near_ref))
    ]
    for load in loads:
        load.start()
    for load, store in zip(loads, stores):
        load.wait()
        store.start()
    for store in stores:
        store.wait()


def pack_call(x, meta):
    plane = jax.ShapeDtypeStruct((1, *x.shape[1:]), BF16)
    return pl.pallas_call(
        pack_kernel,
        in_specs=[SMEM, HBM],
        out_specs=[HBM, HBM],
        out_shape=[plane, plane],
        scratch_shapes=[pltpu.VMEM((2, *x.shape[1:]), BF16), pltpu.SemaphoreType.DMA((4,))],
        cost_estimate=pl.CostEstimate(flops=0, bytes_accessed=2**22, transcendentals=0),
        compiler_params=pltpu.CompilerParams(vmem_limit_bytes=58 * MIB),
        name="pack",
    )(meta, x)


def inside_kernel(run, x_ref, k_ref, affinity_ref, softness_ref, probs_ref, partial_ref, sums_ref,
                  mass_ref, map_ref, taps_ref, hid_ref, by_slice_ref):
    planes, height, depth, channels = x_ref.shape
    slices = affinity_ref.shape[1]
    spread_taps(k_ref, range(3), taps_ref)
    sums_ref[...] = jnp.zeros(sums_ref.shape, F32)
    mass_ref[...] = jnp.zeros(mass_ref.shape, F32)
    new = lax.broadcasted_iota(jnp.int32, (slices, slices), 0)
    old = lax.broadcasted_iota(jnp.int32, (slices, slices), 1)
    half = (new >= slices // 2).astype(jnp.int32)
    rest = new - half * (slices // 2)
    place = rest & (run - 1)
    order = (old == 2 * (rest - place) + half * run + place).astype(BF16)
    map_ref[:slices] = nt_dot(order, affinity_ref[...]).astype(BF16)
    map_ref[slices:] = jnp.broadcast_to(softness_ref[...], (TILE, channels)).astype(BF16)

    def plane(p, carry):
        def put(y, lanes, total):
            hid_ref[cells_of(y, depth), lanes] = gelu(total).astype(BF16)

        conv_plane([(role, x_ref, p + role) for role in range(3)], taps_ref, put)
        assign_plane(hid_ref, map_ref, by_slice_ref, probs_ref, p, sums_ref, mass_ref)
        return carry

    lax.fori_loop(0, planes - 2, plane, 0)

    for which, known in enumerate((((1, 0), (2, 1)), ((0, planes - 2), (1, planes - 1)))):
        def put(y, lanes, total, which=which):
            partial_ref[which, cells_of(y, depth), lanes] = total.astype(BF16)

        conv_plane([(role, x_ref, p) for role, p in known], taps_ref, put)


def inside_call(x, taps, affinity, softness, run):
    planes, height, depth, channels = x.shape
    slices = affinity.shape[1]
    cells = height * depth
    work = planes * cells * channels
    return pl.pallas_call(
        functools.partial(inside_kernel, run),
        in_specs=[VMEM] * 4,
        out_specs=[VMEM] * 5,
        out_shape=[
            jax.ShapeDtypeStruct((planes - 2, cells, slices), BF16),
            jax.ShapeDtypeStruct((2, cells, channels), BF16),
            jax.ShapeDtypeStruct((slices, channels), F32),
            jax.ShapeDtypeStruct((slices, LANES), F32),
            jax.ShapeDtypeStruct((slices + TILE, channels), BF16),
        ],
        scratch_shapes=[
            pltpu.VMEM((27, TILE, channels), CONV),
            pltpu.VMEM((cells, channels), BF16),
            pltpu.VMEM((slices, cells), BF16),
        ],
        cost_estimate=pl.CostEstimate(
            flops=work * 9000, bytes_accessed=2 * work, transcendentals=2 * work
        ),
        compiler_params=pltpu.CompilerParams(vmem_limit_bytes=LIMIT),
        name="inside",
    )(x, taps, affinity, softness)


def edge_kernel(meta_ref, halo_ref, partial_ref, k_ref, map_ref, sums_in_ref, mass_in_ref,
                probs_ref, *rest):
    last = len(rest) == 9
    if last:
        send_ref, keep_ref, *rest = rest
    sums_ref, mass_ref, taps_ref, hid_ref, by_slice_ref, *rest = rest
    _, height, depth, channels = halo_ref.shape
    slices = sums_in_ref.shape[0]
    spread_taps(k_ref, [meta_ref[1]], taps_ref)
    sums_ref[...] = sums_in_ref[...]
    mass_ref[...] = mass_in_ref[...]
    which = meta_ref[0]

    def put(y, lanes, total):
        at = cells_of(y, depth)
        total = total + partial_ref[which, at, lanes].astype(F32)
        hid_ref[at, lanes] = gelu(total).astype(BF16)

    conv_plane([(0, halo_ref, 0)], taps_ref, put)
    assign_plane(hid_ref, map_ref, by_slice_ref, probs_ref, 0, sums_ref, mass_ref)
    if not last:
        return
    split_ref, lane_ref = rest
    mass = lax.dot_general(
        jnp.ones((8, LANES), F32), mass_ref[...], (((1,), (1,)), ((), ())),
        preferred_element_type=F32, precision=lax.Precision.HIGHEST,
    )
    split_ref[...] = split(mass)
    owners, rows, _ = send_ref.shape
    held = channels // LANES
    rows = (rows - 8) // held
    odd = meta_ref[2]
    for ref, half in ((send_ref, 1 - odd), (keep_ref, odd)):
        start = pl.multiple_of(half * (slices // 2), slices // 2)
        for i in range(held):
            part = sums_ref[pl.ds(start, slices // 2), i * LANES : (i + 1) * LANES].astype(BF16)
            ref[:, i * rows : (i + 1) * rows, :] = part.reshape(owners, rows, LANES)
        for owner in range(owners):
            lane = pl.multiple_of(start + owner * rows // LANES * LANES, LANES)
            ref[owner, held * rows :, :] = split_ref[:, pl.ds(lane, LANES)].astype(BF16)


def split(mass):
    high = mass.astype(BF16).astype(F32)
    row = lax.broadcasted_iota(jnp.int32, mass.shape, mass.ndim - 2)
    return jnp.where(row == 0, high, jnp.where(row == 1, mass - high, 0.0))


def edge_call(halo, meta, taps, maps, partial, sums, mass, owners, last):
    _, height, depth, channels = halo.shape
    slices = sums.shape[0]
    cells = height * depth
    carry = [(s.shape, F32) for s in (sums, mass)]
    scratch = [
        pltpu.VMEM((9, TILE, channels), CONV),
        pltpu.VMEM((cells, channels), BF16),
        pltpu.VMEM((slices, cells), BF16),
    ]
    if last:
        rows = channels // LANES * (slices // 2 // owners) + 8
        outs = [((owners, rows, LANES), BF16)] * 2
        scratch = [pltpu.VMEM(*c) for c in carry] + scratch + [
            pltpu.VMEM((8, slices), F32), pltpu.VMEM((8, LANES), F32)]
    else:
        outs = carry
    return pl.pallas_call(
        edge_kernel,
        in_specs=[SMEM] + [VMEM] * 6,
        out_specs=[VMEM] * (1 + len(outs)),
        out_shape=[jax.ShapeDtypeStruct((1, cells, slices), BF16)]
        + [jax.ShapeDtypeStruct(*o) for o in outs],
        scratch_shapes=scratch,
        cost_estimate=pl.CostEstimate(
            flops=cells * channels * 16000, bytes_accessed=4 * cells * channels,
            transcendentals=2 * cells * channels,
        ),
        compiler_params=pltpu.CompilerParams(vmem_limit_bytes=LIMIT),
        name="edge",
    )(meta, halo, partial, taps, maps, sums, mass)


def merge_kernel(keep_ref, other_ref, out_ref):
    total = keep_ref[...].astype(F32) + other_ref[...].astype(F32)
    rows = total.shape[1] - 8
    out_ref[:, :rows] = total[:, :rows].astype(BF16)
    tail = total[:, rows:]
    mass = jnp.broadcast_to(tail[:, 0:1] + tail[:, 1:2], tail.shape)
    out_ref[:, rows:] = split(mass).astype(BF16)


def merge_call(keep, other):
    return pl.pallas_call(
        merge_kernel,
        in_specs=[VMEM, VMEM],
        out_specs=VMEM,
        out_shape=jax.ShapeDtypeStruct(keep.shape, BF16),
        compiler_params=pltpu.CompilerParams(vmem_limit_bytes=LIMIT),
        name="merge",
    )(keep, other)


def owner_kernel(meta_ref, parts_ref, gain_ref, content, widening, narrowing, final, out_ref, spread_ref):
    channels = content.shape[0]
    held = channels // LANES
    rows = out_ref.shape[0]
    total = jnp.sum(parts_ref[...].astype(F32), axis=0)
    pooled = jnp.concatenate([total[i * rows : (i + 1) * rows] for i in range(held)], axis=1)
    mass = total[held * rows : held * rows + 1] + total[held * rows + 1 : held * rows + 2]
    lane = lax.broadcasted_iota(jnp.int32, (rows, LANES), 1)
    row = lax.broadcasted_iota(jnp.int32, (rows, LANES), 0)
    mass = jnp.sum(jnp.where(lane == row + meta_ref[0], mass, 0.0), axis=1, keepdims=True)
    pooled = pooled / (mass + epsilon)
    high = pooled.astype(BF16)
    low = (pooled - high.astype(F32)).astype(BF16)
    tokens = dot(high, content[...]) + dot(low, content[...])
    center = jnp.mean(tokens, axis=-1, keepdims=True)
    spread = jnp.mean((tokens - center) ** 2, axis=-1, keepdims=True)
    normed = ((tokens - center) * (1.0 / jnp.sqrt(spread + epsilon)) * gain_ref[...]).astype(BF16)
    inner = gelu(dot(normed, widening[...])).astype(BF16)
    out = (tokens + dot(inner, narrowing[...])).astype(BF16)
    out_ref[...] = out
    mapped = dot(out, final[...]).astype(BF16)
    spread_ref[...] = jnp.broadcast_to(mapped[None], spread_ref.shape)


def owner_call(meta, parts, gain, *weights):
    channels = weights[0].shape[0]
    owners = parts.shape[0]
    rows = (parts.shape[1] - 8) // (channels // LANES)
    return pl.pallas_call(
        owner_kernel,
        in_specs=[SMEM] + [VMEM] * 6,
        out_specs=[VMEM, VMEM],
        out_shape=[
            jax.ShapeDtypeStruct((rows, channels), BF16),
            jax.ShapeDtypeStruct((owners, rows, channels), BF16),
        ],
        compiler_params=pltpu.CompilerParams(vmem_limit_bytes=LIMIT),
        name="owner",
    )(meta, parts, gain, *weights)


def update_kernel(meta_ref, x_ref, inside_ref, near_ref, far_ref, own_ref, other_ref, out_ref,
                  done_ref, mapped_ref, sem):
    planes, cells, channels = x_ref.shape
    half = own_ref.shape[0]
    rows = math.gcd(cells, 512)
    pieces = cells // rows
    odd = meta_ref[2]
    mapped_ref[pl.ds(pl.multiple_of(odd * half, half), half)] = own_ref[...]
    mapped_ref[pl.ds(pl.multiple_of((1 - odd) * half, half), half)] = other_ref[...]

    def place(i):
        return pl.ds(pl.multiple_of(lax.rem(i, pieces) * rows, rows), rows)

    def store(plane, i):
        at = place(i)
        index = plane * pieces + lax.rem(i, pieces)
        return pltpu.make_async_copy(done_ref.at[plane, at], out_ref.at[plane, at], sem.at[index])

    for probs_ref, base in ((inside_ref, 1), (near_ref, meta_ref[1]), (far_ref, meta_ref[0])):
        def step(i, carry, probs_ref=probs_ref, base=base):
            part, at = i // pieces, place(i)
            change = dot(probs_ref[part, at, :], mapped_ref[...])
            done_ref[base + part, at, :] = (x_ref[base + part, at, :].astype(F32) + change).astype(BF16)
            store(base + part, i).start()
            return carry

        lax.fori_loop(0, probs_ref.shape[0] * pieces, step, 0)

    def finish(i, carry):
        store(i // pieces, i).wait()
        return carry

    lax.fori_loop(0, planes * pieces, finish, 0)


def update_call(meta, x, inside, near, far, own, other):
    planes, cells, channels = x.shape
    return pl.pallas_call(
        update_kernel,
        in_specs=[SMEM] + [VMEM] * 6,
        out_specs=HBM,
        out_shape=jax.ShapeDtypeStruct(x.shape, BF16),
        scratch_shapes=[
            pltpu.VMEM(x.shape, BF16),
            pltpu.VMEM((2 * own.shape[0], channels), BF16),
            pltpu.SemaphoreType.DMA((planes * cells // math.gcd(cells, 512),)),
        ],
        compiler_params=pltpu.CompilerParams(vmem_limit_bytes=LIMIT),
        name="update",
    )(meta, x, inside, near, far, own, other)


def per_device(
    mesh_feature_array,
    stencil_coefficients,
    partition_affinity_matrix,
    softness_mapping_matrix,
    content_mapping_matrix,
    layernorm_multiplier,
    widening_matrix,
    narrowing_matrix,
    final_mapping_matrix,
):
    x = mesh_feature_array
    planes, height, depth, channels = x.shape
    slices = partition_affinity_matrix.shape[1]
    n, me = lax.axis_size("gx"), lax.axis_index("gx")
    odd = lax.rem(me, 2)
    near = (planes - 1) * (1 - odd)
    far = (planes - 1) * odd
    ends = jnp.stack([far, near, odd]).astype(jnp.int32)
    far_pairs = [p for i in range(1, n - 1, 2) for p in ((i, i + 1), (i + 1, i))]
    near_pairs = [p for i in range(0, n, 2) for p in ((i, i + 1), (i + 1, i))]
    far_plane, near_plane = pack_call(x, ends)
    far_halo = lax.ppermute(far_plane, "gx", far_pairs)
    near_halo = lax.ppermute(near_plane, "gx", near_pairs)

    taps = stencil_coefficients.reshape(3, 9, channels)
    near_meta = jnp.stack([1 - odd, 2 * (1 - odd), odd]).astype(jnp.int32)
    far_meta = jnp.stack([odd, 2 * odd, odd]).astype(jnp.int32)

    owners = min(n // 2, slices // 2 // TILE)
    share = n // 2 // owners
    groups = [[2 * (share * j + s) + h for j in range(owners)] for h in range(2) for s in range(share)]
    owner = me // 2 // share
    rows = slices // 2 // owners
    inside_probs, partial, sums, mass, maps = inside_call(
        x, taps, partition_affinity_matrix, softness_mapping_matrix[None], slices // n
    )
    near_probs, sums, mass = edge_call(
        near_halo, near_meta, taps, maps, partial, sums, mass, owners, False
    )
    far_probs, send, keep = edge_call(
        far_halo, far_meta, taps, maps, partial, sums, mass, owners, True
    )

    parts = merge_call(keep, lax.ppermute(send, "gx", near_pairs))
    parts = lax.all_to_all(parts, "gx", 0, 0, axis_index_groups=groups)
    if share > 1:
        sharers = [[2 * (share * j + s) + h for s in range(share)]
                   for h in range(2) for j in range(owners)]
        parts = lax.psum(parts, "gx", axis_index_groups=sharers)
    own_out, mapped = owner_call(
        lax.rem(owner * rows, LANES).astype(jnp.int32)[None], parts, layernorm_multiplier[None],
        content_mapping_matrix, widening_matrix, narrowing_matrix, final_mapping_matrix,
    )
    if share > 1:
        place = lax.rem(me // 2, share) * (slices // n)
        own_out = lax.dynamic_slice_in_dim(own_out, place, slices // n)
    mapped = lax.all_to_all(mapped, "gx", 0, 0, axis_index_groups=groups)
    mapped = mapped.reshape(slices // 2, channels)
    updated = update_call(
        ends, x.reshape(planes, height * depth, channels), inside_probs, near_probs, far_probs,
        mapped, lax.ppermute(mapped, "gx", near_pairs),
    )
    return updated.reshape(x.shape), own_out


def solution(mesh):
    return jax.shard_map(
        per_device,
        mesh=mesh,
        in_specs=(P(("grp", "gx"), None, None, None), P(), P(), P(), P(), P(), P(), P(), P()),
        out_specs=(P(("grp", "gx"), None, None, None), P(("grp", "gx"), None)),
        check_vma=False,
    )
```

```python
import functools
import math

import jax
import jax.numpy as jnp
from jax import lax
from jax.experimental import pallas as pl
from jax.experimental.pallas import tpu as pltpu
from jax.sharding import PartitionSpec as P

epsilon = 1e-05
LANES = 128
BLOCK = 256
GROUP = 8
TILE = 16
MIB = 2**20
LIMIT = 32 * MIB
F32, BF16 = jnp.float32, jnp.bfloat16
CONV = BF16
VMEM = pl.BlockSpec(memory_space=pltpu.VMEM)
SMEM = pl.BlockSpec(memory_space=pltpu.SMEM)
HBM = pl.BlockSpec(memory_space=pltpu.HBM)


def dot(a, b):
    return jnp.dot(a, b, preferred_element_type=F32)


def gelu(x):
    inner = x * (x * x * (0.044715 * math.sqrt(2 / math.pi)) + math.sqrt(2 / math.pi))
    half = 0.5 * x
    return half + half * jnp.tanh(inner)


def spread_taps(k_ref, planes, taps_ref):
    for role, plane in enumerate(planes):
        for tap in range(9):
            row = k_ref[pl.ds(9 * plane + tap, 1), :]
            taps_ref[9 * role + tap] = jnp.broadcast_to(row, taps_ref.shape[1:]).astype(CONV)


def conv_row(sources, taps_ref, lanes):
    sums = [None] * 3
    for role, rows in sources:
        for b, row in enumerate(rows):
            if row is None:
                continue
            depth, width = row.shape
            row = row.astype(CONV).reshape(depth // TILE, TILE, width)
            for c in range(3):
                term = row * taps_ref[9 * role + 3 * b + c, :, lanes]
                sums[c] = term if sums[c] is None else sums[c] + term
    before, here, after = (s.astype(F32).reshape(depth, width) for s in sums)
    position = lax.broadcasted_iota(jnp.int32, (depth, width), 0)
    before = jnp.where(position == 0, 0.0, pltpu.roll(before, 1, 0))
    after = jnp.where(position == depth - 1, 0.0, pltpu.roll(after, depth - 1, 0))
    return here + before + after


def channel_blocks(channels):
    return [slice(i, i + BLOCK) for i in range(0, channels, BLOCK)]


def inner_row(ref, plane, y, lanes, inside=None):
    if inside is None:
        return ref[plane, y, :, lanes]
    row = ref[plane, jnp.clip(y, 0, ref.shape[1] - 1), :, lanes].astype(F32)
    return (row * jnp.where(inside, 1.0, 0.0)).astype(BF16)


def nt_dot(a, b):
    return lax.dot_general(a, b, (((1,), (1,)), ((), ())), preferred_element_type=F32)


def identity(size):
    row = lax.broadcasted_iota(jnp.int32, (size, size), 0)
    return (row == lax.broadcasted_iota(jnp.int32, (size, size), 1)).astype(BF16)


def assign(hid, map_ref, mass_ref):
    cells = hid.shape[0]
    slices = map_ref.shape[0] - TILE
    raw = nt_dot(map_ref[...], hid)
    soft = raw[slices : slices + 8]
    temperature = 0.25 + jnp.maximum(soft, 0.0) + jnp.log(1.0 + jnp.exp(-jnp.abs(soft)))
    scale = (1.0 / math.log(2.0)) / temperature
    raw = raw[:slices].reshape(slices // 8, 8, cells)
    top = jnp.max(jnp.max(raw, axis=0), axis=0, keepdims=True)
    powers = jnp.exp2((raw - top[None]) * scale[None])
    total = jnp.sum(jnp.sum(powers, axis=0), axis=0, keepdims=True)
    probs = (powers * (1.0 / total)[None]).reshape(slices, cells)
    mass = probs[:, :LANES]
    for start in range(LANES, cells, LANES):
        mass = mass + probs[:, start : start + LANES]
    mass_ref[...] += mass
    by_slice = probs.astype(BF16)
    by_cell = nt_dot(identity(cells), by_slice).astype(BF16)
    return by_slice, by_cell


def pack_kernel(me_ref, x_ref, far_ref, near_ref):
    planes, height = x_ref.shape[:2]
    odd = me_ref[0] & 1

    def row(y, carry):
        far_ref[0, y] = x_ref[(planes - 1) * odd, y]
        near_ref[0, y] = x_ref[(planes - 1) * (1 - odd), y]
        return carry

    lax.fori_loop(0, height, row, 0)


def pack_call(me, x):
    plane = jax.ShapeDtypeStruct((1, *x.shape[1:]), BF16)
    return pl.pallas_call(
        pack_kernel,
        in_specs=[SMEM, VMEM],
        out_specs=[VMEM, VMEM],
        out_shape=[plane, plane],
        cost_estimate=pl.CostEstimate(flops=0, bytes_accessed=2**22, transcendentals=0),
        compiler_params=pltpu.CompilerParams(vmem_limit_bytes=LIMIT),
        name="pack",
    )(me, x)


def reverse_bits(value, bits):
    result = jnp.zeros_like(value)
    for bit in range(bits):
        result = result * 2 + ((value >> bit) & 1)
    return result


def inside_kernel(bits, x_ref, k_ref, affinity_ref, softness_ref, probs_ref, partial_ref, sums_ref,
                  mass_ref, map_ref, taps_ref, even_ref, odd_ref, hid_ref, by_slice_ref):
    planes, height, depth, channels = x_ref.shape
    slices = affinity_ref.shape[1]
    spread_taps(k_ref, range(3), taps_ref)
    sums_ref[...] = jnp.zeros(sums_ref.shape, F32)
    mass_ref[...] = jnp.zeros(mass_ref.shape, F32)
    run = slices >> bits
    new = lax.broadcasted_iota(jnp.int32, (slices, 1), 0)
    old = lax.broadcasted_iota(jnp.int32, (slices, slices), 1)
    place = new & (run - 1)
    owner = reverse_bits(new >> (run.bit_length() - 1), bits)
    order = (old == owner * run + place).astype(BF16)
    map_ref[:slices] = nt_dot(order, affinity_ref[...]).astype(BF16)
    map_ref[slices:] = jnp.broadcast_to(softness_ref[...], (TILE, channels)).astype(BF16)

    for which, known in enumerate((((1, 0), (2, 1)), ((0, planes - 2), (1, planes - 1)))):
        def put(y, lanes, rows, known=known, which=which):
            sources = [(role, [None if b is None else x_ref[p, y + b, :, lanes] for b in rows])
                       for role, p in known]
            start = y * depth if isinstance(y, int) else pl.multiple_of(y * depth, depth)
            total = conv_row(sources, taps_ref, lanes).astype(BF16)
            partial_ref[which, pl.ds(start, depth), lanes] = total

        for lanes in channel_blocks(channels):
            put(0, lanes, (None, 0, 1))
            put(height - 1, lanes, (-1, 0, None))

        def pair(i, carry, put=put):
            for lanes in channel_blocks(channels):
                put(2 * i + 1, lanes, (-1, 0, 1))
                put(2 * i + 2, lanes, (-1, 0, 1))
            return carry

        lax.fori_loop(0, (height - 2) // 2, pair, 0)

    groups = height // GROUP
    cells = GROUP * depth

    def conv(t, pre_ref):
        plane, first = t // groups, lax.rem(t, groups) * GROUP
        for lanes in channel_blocks(channels):
            for j in range(GROUP):
                sources = []
                for role in range(3):
                    rows = []
                    for b in (-1, 0, 1):
                        y, ok = first + j + b, None
                        if j + b < 0:
                            ok = first > 0
                        elif j + b >= GROUP:
                            ok = first + GROUP < height
                        rows.append(inner_row(x_ref, plane + role, y, lanes, ok))
                    sources.append((role, rows))
                pre_ref[j * depth : (j + 1) * depth, lanes] = conv_row(sources, taps_ref, lanes)

    def share(t, pre_ref, at):
        hid = gelu(pre_ref[...]).astype(BF16)
        by_slice, by_cell = assign(hid, map_ref, mass_ref)
        start = pl.multiple_of(lax.rem(t, groups) * cells, cells)
        probs_ref[t // groups, pl.ds(start, cells), :] = by_cell
        hid_ref[at, :] = hid
        by_slice_ref[:, at] = by_slice

    count = (planes - 2) * groups
    conv(jnp.int32(0), even_ref)

    def two(s, carry):
        t = 2 * s
        share(t, even_ref, slice(0, cells))
        conv(t + 1, odd_ref)
        share(t + 1, odd_ref, slice(cells, 2 * cells))
        sums_ref[...] += dot(by_slice_ref[...], hid_ref[...])
        conv(jnp.minimum(t + 2, count - 1), even_ref)
        return carry

    lax.fori_loop(0, count // 2, two, 0)


def inside_call(x, taps, affinity, softness, bits):
    planes, height, depth, channels = x.shape
    slices = affinity.shape[1]
    cells = height * depth
    work = planes * cells * channels
    return pl.pallas_call(
        functools.partial(inside_kernel, bits),
        in_specs=[VMEM] * 4,
        out_specs=[VMEM] * 5,
        out_shape=[
            jax.ShapeDtypeStruct((planes - 2, cells, slices), BF16),
            jax.ShapeDtypeStruct((2, cells, channels), BF16),
            jax.ShapeDtypeStruct((slices, channels), F32),
            jax.ShapeDtypeStruct((slices, LANES), F32),
            jax.ShapeDtypeStruct((slices + TILE, channels), BF16),
        ],
        scratch_shapes=[
            pltpu.VMEM((27, TILE, channels), CONV),
            pltpu.VMEM((GROUP * depth, channels), F32),
            pltpu.VMEM((GROUP * depth, channels), F32),
            pltpu.VMEM((2 * GROUP * depth, channels), BF16),
            pltpu.VMEM((slices, 2 * GROUP * depth), BF16),
        ],
        cost_estimate=pl.CostEstimate(
            flops=work * 9000, bytes_accessed=2 * work, transcendentals=2 * work
        ),
        compiler_params=pltpu.CompilerParams(vmem_limit_bytes=LIMIT),
        name="inside",
    )(x, taps, affinity, softness)


def edge_kernel(is_far, me_ref, halo_ref, partial_ref, k_ref, map_ref, sums_in_ref, mass_in_ref,
                probs_ref, *rest):
    if is_far:
        send_ref, keep_ref, *rest = rest
    sums_ref, mass_ref, taps_ref, pre_ref, hid_ref, by_slice_ref, *rest = rest
    _, height, depth, channels = halo_ref.shape
    slices = sums_in_ref.shape[0]
    odd = me_ref[0] & 1
    side = odd if is_far else 1 - odd
    spread_taps(k_ref, [2 * side], taps_ref)
    mass_ref[...] = mass_in_ref[...]
    cells = GROUP * depth
    for first in range(0, height, GROUP):
        group = slice(first * depth, first * depth + cells)
        for lanes in channel_blocks(channels):
            for y in range(first, first + GROUP):
                rows = [halo_ref[0, y + b, :, lanes] if 0 <= y + b < height else None
                        for b in (-1, 0, 1)]
                at = slice(y * depth, (y + 1) * depth)
                total = conv_row([(0, rows)], taps_ref, lanes)
                pre_ref[at, lanes] = total + partial_ref[side, at, lanes].astype(F32)
        hid = gelu(pre_ref[group]).astype(BF16)
        by_slice, by_cell = assign(hid, map_ref, mass_ref)
        probs_ref[0, group] = by_cell
        hid_ref[group] = hid
        by_slice_ref[:, group] = by_slice
    sums_ref[...] = sums_in_ref[...] + dot(by_slice_ref[...], hid_ref[...])
    if not is_far:
        return
    split_ref, = rest
    mass = lax.dot_general(
        jnp.ones((8, LANES), F32), mass_ref[...], (((1,), (1,)), ((), ())),
        preferred_element_type=F32, precision=lax.Precision.HIGHEST,
    )
    split_ref[...] = split(mass)
    owners, rows, _ = send_ref.shape
    held = channels // LANES
    rows = (rows - 8) // held
    for ref, half in ((send_ref, 1 - odd), (keep_ref, odd)):
        start = pl.multiple_of(half * (slices // 2), slices // 2)
        for i in range(held):
            part = sums_ref[pl.ds(start, slices // 2), i * LANES : (i + 1) * LANES].astype(BF16)
            ref[:, i * rows : (i + 1) * rows, :] = part.reshape(owners, rows, LANES)
        for owner in range(owners):
            lane = pl.multiple_of(start + owner * rows // LANES * LANES, LANES)
            ref[owner, held * rows :, :] = split_ref[:, pl.ds(lane, LANES)].astype(BF16)


def split(mass):
    high = mass.astype(BF16).astype(F32)
    row = lax.broadcasted_iota(jnp.int32, mass.shape, mass.ndim - 2)
    return jnp.where(row == 0, high, jnp.where(row == 1, mass - high, 0.0))


def edge_call(is_far, me, halo, taps, maps, partial, sums, mass, owners):
    _, height, depth, channels = halo.shape
    slices = sums.shape[0]
    cells = height * depth
    carry = [(s.shape, F32) for s in (sums, mass)]
    scratch = [
        pltpu.VMEM((9, TILE, channels), CONV),
        pltpu.VMEM((cells, channels), F32),
        pltpu.VMEM((cells, channels), BF16),
        pltpu.VMEM((slices, cells), BF16),
    ]
    if is_far:
        rows = channels // LANES * (slices // owners) + 8
        outs = [((owners // 2, rows, LANES), BF16)] * 2
        scratch = [pltpu.VMEM(*c) for c in carry] + scratch + [pltpu.VMEM((8, slices), F32)]
    else:
        outs = carry
    return pl.pallas_call(
        functools.partial(edge_kernel, is_far),
        in_specs=[SMEM] + [VMEM] * 6,
        out_specs=[VMEM] * (1 + len(outs)),
        out_shape=[jax.ShapeDtypeStruct((1, cells, slices), BF16)]
        + [jax.ShapeDtypeStruct(*o) for o in outs],
        scratch_shapes=scratch,
        cost_estimate=pl.CostEstimate(
            flops=cells * channels * 16000, bytes_accessed=4 * cells * channels,
            transcendentals=2 * cells * channels,
        ),
        compiler_params=pltpu.CompilerParams(vmem_limit_bytes=LIMIT),
        name="far" if is_far else "near",
    )(me, halo, partial, taps, maps, sums, mass)


def merge_kernel(bit, me_ref, keep_ref, other_ref, *outs):
    def total(at):
        both = keep_ref[at].astype(F32) + other_ref[at].astype(F32)
        rows = both.shape[1] - 8
        tail = both[:, rows:]
        mass = jnp.broadcast_to(tail[:, 0:1] + tail[:, 1:2], tail.shape)
        return rows, both[:, :rows].astype(BF16), split(mass).astype(BF16)

    if len(outs) == 1:
        parts = [(outs[0], slice(None))]
    else:
        half = keep_ref.shape[0] // 2
        mine = (me_ref[0] >> bit) & 1
        parts = [(ref, pl.ds(side * half, half)) for ref, side in zip(outs, (1 - mine, mine))]
    for ref, at in parts:
        rows, body, tail = total(at)
        ref[:, :rows] = body
        ref[:, rows:] = tail


def merge_call(bit, me, keep, other, halve):
    shape = (keep.shape[0] // 2, *keep.shape[1:]) if halve else keep.shape
    outs = [jax.ShapeDtypeStruct(shape, BF16)] * (2 if halve else 1)
    return pl.pallas_call(
        functools.partial(merge_kernel, bit),
        in_specs=[SMEM, VMEM, VMEM],
        out_specs=[VMEM] * len(outs),
        out_shape=outs,
        compiler_params=pltpu.CompilerParams(vmem_limit_bytes=LIMIT),
        name="merge",
    )(me, keep, other)


def join_kernel(bit, me_ref, own_ref, other_ref, out_ref):
    mine = (me_ref[0] >> bit) & 1
    out_ref[mine] = own_ref[...]
    out_ref[1 - mine] = other_ref[...]


def join_call(bit, me, own, other):
    rows, channels = own.shape
    return pl.pallas_call(
        functools.partial(join_kernel, bit),
        in_specs=[SMEM, VMEM, VMEM],
        out_specs=VMEM,
        out_shape=jax.ShapeDtypeStruct((2, rows, channels), BF16),
        compiler_params=pltpu.CompilerParams(vmem_limit_bytes=LIMIT),
        name="join",
    )(me, own, other).reshape(2 * rows, channels)


def owner_kernel(bits, me_ref, keep_ref, other_ref, gain_ref, content_ref, widening_ref,
                 narrowing_ref, final_ref, out_ref, mapped_ref):
    channels = content_ref.shape[0]
    held = channels // LANES
    rows = out_ref.shape[0]
    total = keep_ref[0].astype(F32) + other_ref[0].astype(F32)
    pooled = jnp.concatenate([total[i * rows : (i + 1) * rows] for i in range(held)], axis=1)
    mass = total[held * rows : held * rows + 1] + total[held * rows + 1 : held * rows + 2]
    lane = lax.broadcasted_iota(jnp.int32, (rows, LANES), 1)
    row = lax.broadcasted_iota(jnp.int32, (rows, LANES), 0)
    first = (reverse_bits(me_ref[0], bits) * rows) & (LANES - 1)
    mass = jnp.sum(jnp.where(lane == row + first, mass, 0.0), axis=1, keepdims=True)
    pooled = pooled / (mass + epsilon)
    high = pooled.astype(BF16)
    low = (pooled - high.astype(F32)).astype(BF16)
    tokens = dot(high, content_ref[...]) + dot(low, content_ref[...])
    center = jnp.mean(tokens, axis=-1, keepdims=True)
    spread = jnp.mean((tokens - center) ** 2, axis=-1, keepdims=True)
    normed = ((tokens - center) * (1.0 / jnp.sqrt(spread + epsilon)) * gain_ref[...]).astype(BF16)
    inner = gelu(dot(normed, widening_ref[...])).astype(BF16)
    out = (tokens + dot(inner, narrowing_ref[...])).astype(BF16)
    out_ref[...] = out
    mapped_ref[...] = dot(out, final_ref[...]).astype(BF16)


def owner_call(bits, me, keep, other, gain, *weights):
    channels = weights[0].shape[0]
    rows = (keep.shape[1] - 8) // (channels // LANES)
    return pl.pallas_call(
        functools.partial(owner_kernel, bits),
        in_specs=[SMEM] + [VMEM] * 7,
        out_specs=[VMEM, VMEM],
        out_shape=[jax.ShapeDtypeStruct((rows, channels), BF16)] * 2,
        compiler_params=pltpu.CompilerParams(vmem_limit_bytes=LIMIT),
        name="owner",
    )(me, keep, other, gain, *weights)


def update_kernel(me_ref, x_ref, inside_ref, near_ref, far_ref, own_ref, other_ref, out_ref,
                  done_ref, mapped_ref, sem):
    planes, cells, channels = x_ref.shape
    half = own_ref.shape[0]
    rows = math.gcd(cells, 512)
    pieces = cells // rows
    odd = me_ref[0] & 1
    mapped_ref[pl.ds(pl.multiple_of(odd * half, half), half)] = own_ref[...]
    mapped_ref[pl.ds(pl.multiple_of((1 - odd) * half, half), half)] = other_ref[...]

    def place(i):
        return pl.ds(pl.multiple_of(lax.rem(i, pieces) * rows, rows), rows)

    def store(plane, i):
        at = place(i)
        index = plane * pieces + lax.rem(i, pieces)
        return pltpu.make_async_copy(done_ref.at[plane, at], out_ref.at[plane, at], sem.at[index])

    for probs_ref, base in (
        (inside_ref, 1), (near_ref, (planes - 1) * (1 - odd)), (far_ref, (planes - 1) * odd)
    ):
        def step(i, carry, probs_ref=probs_ref, base=base):
            part, at = i // pieces, place(i)
            change = dot(probs_ref[part, at, :], mapped_ref[...])
            done_ref[base + part, at, :] = (x_ref[base + part, at, :].astype(F32) + change).astype(BF16)
            store(base + part, i).start()
            return carry

        lax.fori_loop(0, probs_ref.shape[0] * pieces, step, 0)

    def finish(i, carry):
        store(i // pieces, i).wait()
        return carry

    lax.fori_loop(0, planes * pieces, finish, 0)


def update_call(me, x, inside, near, far, own, other):
    planes, cells, channels = x.shape
    return pl.pallas_call(
        update_kernel,
        in_specs=[SMEM] + [VMEM] * 6,
        out_specs=HBM,
        out_shape=jax.ShapeDtypeStruct(x.shape, BF16),
        scratch_shapes=[
            pltpu.VMEM(x.shape, BF16),
            pltpu.VMEM((2 * own.shape[0], channels), BF16),
            pltpu.SemaphoreType.DMA((planes * cells // math.gcd(cells, 512),)),
        ],
        compiler_params=pltpu.CompilerParams(vmem_limit_bytes=LIMIT),
        name="update",
    )(me, x, inside, near, far, own, other)


def per_device(
    mesh_feature_array,
    stencil_coefficients,
    partition_affinity_matrix,
    softness_mapping_matrix,
    content_mapping_matrix,
    layernorm_multiplier,
    widening_matrix,
    narrowing_matrix,
    final_mapping_matrix,
):
    x = mesh_feature_array
    planes, height, depth, channels = x.shape
    slices = partition_affinity_matrix.shape[1]
    n = lax.axis_size("gx")
    me = lax.axis_index("gx").astype(jnp.int32)[None]
    far_pairs = [p for i in range(1, n - 1, 2) for p in ((i, i + 1), (i + 1, i))]
    near_pairs = [p for i in range(0, n, 2) for p in ((i, i + 1), (i + 1, i))]
    far_plane, near_plane = pack_call(me, x)
    far_halo = lax.ppermute(far_plane, "gx", far_pairs)
    near_halo = lax.ppermute(near_plane, "gx", near_pairs)

    bits = n.bit_length() - 1
    owners = min(n, slices // TILE)
    halvings = owners.bit_length() - 1
    taps = stencil_coefficients
    inside_probs, partial, sums, mass, maps = inside_call(
        x, taps, partition_affinity_matrix, softness_mapping_matrix[None], bits
    )
    near_probs, sums, mass = edge_call(False, me, near_halo, taps, maps, partial, sums, mass, owners)
    far_probs, send, keep = edge_call(True, me, far_halo, taps, maps, partial, sums, mass, owners)

    across = lambda value, bit: lax.ppermute(value, "gx", [(i, i ^ (1 << bit)) for i in range(n)])
    other = across(send, 0)
    for bit in range(1, halvings):
        send, keep = merge_call(bit, me, keep, other, True)
        other = across(send, bit)
    for bit in range(halvings, bits):
        keep, = merge_call(bit, me, keep, other, False)
        other = across(keep, bit)
    own_out, mapped = owner_call(
        halvings, me, keep, other, layernorm_multiplier[None],
        content_mapping_matrix, widening_matrix, narrowing_matrix, final_mapping_matrix,
    )
    if halvings < bits:
        place = reverse_bits(me[0] >> halvings, bits - halvings) * (slices // n)
        own_out = lax.dynamic_slice_in_dim(own_out, place, slices // n)
    other = across(mapped, halvings - 1)
    for bit in range(halvings - 1, 0, -1):
        mapped = join_call(bit, me, mapped, other)
        other = across(mapped, bit - 1)
    updated = update_call(
        me, x.reshape(planes, height * depth, channels), inside_probs, near_probs, far_probs,
        mapped, other,
    )
    return updated.reshape(x.shape), own_out


def solution(mesh):
    return jax.shard_map(
        per_device,
        mesh=mesh,
        in_specs=(P(("grp", "gx"), None, None, None), P(), P(), P(), P(), P(), P(), P(), P()),
        out_specs=(P(("grp", "gx"), None, None, None), P(("grp", "gx"), None)),
        check_vma=False,
    )
```

```python
import functools
import math

import jax
import jax.numpy as jnp
from jax import lax
from jax.experimental import pallas as pl
from jax.experimental.pallas import tpu as pltpu
from jax.sharding import PartitionSpec as P

epsilon = 1e-05
LANES = 128
BLOCK = 256
GROUP = 8
TILE = 16
REPEAT = 8
MIB = 2**20
LIMIT = 32 * MIB
F32, BF16 = jnp.float32, jnp.bfloat16
CONV = BF16
VMEM = pl.BlockSpec(memory_space=pltpu.VMEM)
SMEM = pl.BlockSpec(memory_space=pltpu.SMEM)
HBM = pl.BlockSpec(memory_space=pltpu.HBM)


def dot(a, b):
    return jnp.dot(a, b, preferred_element_type=F32)


def gelu(x):
    inner = x * (x * x * (0.044715 * math.sqrt(2 / math.pi)) + math.sqrt(2 / math.pi))
    half = 0.5 * x
    return half + half * jnp.tanh(inner)


def spread_taps(k_ref, planes, taps_ref):
    for role, plane in enumerate(planes):
        for tap in range(9):
            row = k_ref[pl.ds(9 * plane + tap, 1), :]
            taps_ref[9 * role + tap] = jnp.broadcast_to(row, taps_ref.shape[1:]).astype(CONV)


def conv_rows(sources, taps_ref, lanes, count):
    sums = [[None] * 3 for _ in range(count)]
    for role, rows in sources:
        taps = [taps_ref[9 * role + i, :, lanes] for i in range(9)]
        for j, row in enumerate(rows):
            if row is None:
                continue
            depth, width = row.shape
            row = row.astype(CONV).reshape(depth // REPEAT, REPEAT, width)
            for out in range(max(0, j - 2), min(count, j + 1)):
                for c in range(3):
                    term = row * taps[3 * (j - out) + c]
                    sums[out][c] = term if sums[out][c] is None else sums[out][c] + term
    position = lax.broadcasted_iota(jnp.int32, (depth, width), 0)
    results = []
    for out in range(count):
        before, here, after = (s.astype(F32).reshape(depth, width) for s in sums[out])
        before = jnp.where(position == 0, 0.0, pltpu.roll(before, 1, 0))
        after = jnp.where(position == depth - 1, 0.0, pltpu.roll(after, depth - 1, 0))
        results.append(here + before + after)
    return results


def channel_blocks(channels):
    return [slice(i, i + BLOCK) for i in range(0, channels, BLOCK)]


def inner_row(ref, plane, y, lanes, inside=None):
    if inside is None:
        return ref[plane, y, :, lanes]
    row = ref[plane, jnp.clip(y, 0, ref.shape[1] - 1), :, lanes].astype(F32)
    return (row * jnp.where(inside, 1.0, 0.0)).astype(BF16)


def nt_dot(a, b):
    return lax.dot_general(a, b, (((1,), (1,)), ((), ())), preferred_element_type=F32)


def identity(size):
    row = lax.broadcasted_iota(jnp.int32, (size, size), 0)
    return (row == lax.broadcasted_iota(jnp.int32, (size, size), 1)).astype(BF16)


def assign(hid, map_ref, mass_ref):
    cells = hid.shape[0]
    slices = map_ref.shape[0] - TILE
    raw = nt_dot(map_ref[...], hid)
    soft = raw[slices : slices + 8]
    temperature = 0.25 + jnp.maximum(soft, 0.0) + jnp.log(1.0 + jnp.exp(-jnp.abs(soft)))
    scale = (1.0 / math.log(2.0)) / temperature
    raw = raw[:slices].reshape(slices // 8, 8, cells)
    top = jnp.max(jnp.max(raw, axis=0), axis=0, keepdims=True)
    powers = jnp.exp2((raw - top[None]) * scale[None])
    total = jnp.sum(jnp.sum(powers, axis=0), axis=0, keepdims=True)
    probs = (powers * (1.0 / total)[None]).reshape(slices, cells)
    mass = probs[:, :LANES]
    for start in range(LANES, cells, LANES):
        mass = mass + probs[:, start : start + LANES]
    mass_ref[...] += mass
    by_slice = probs.astype(BF16)
    by_cell = nt_dot(identity(cells), by_slice).astype(BF16)
    return by_slice, by_cell


def pack_kernel(me_ref, x_ref, far_ref):
    planes, height = x_ref.shape[:2]

    def row(y, carry):
        far_ref[0, y] = x_ref[(planes - 1) * (me_ref[0] & 1), y]
        return carry

    lax.fori_loop(0, height, row, 0)


def pack_call(me, x):
    return pl.pallas_call(
        pack_kernel,
        in_specs=[SMEM, VMEM],
        out_specs=VMEM,
        out_shape=jax.ShapeDtypeStruct((1, *x.shape[1:]), BF16),
        cost_estimate=pl.CostEstimate(flops=0, bytes_accessed=2**22, transcendentals=0),
        compiler_params=pltpu.CompilerParams(vmem_limit_bytes=LIMIT),
        name="pack",
    )(me, x)


def ends_kernel(bits, me_ref, x_ref, k_ref, affinity_ref, softness_ref, near_ref, partial_ref, map_ref,
                taps_ref):
    planes, height, depth, channels = x_ref.shape
    slices = affinity_ref.shape[1]
    odd = me_ref[0] & 1

    def row(y, carry):
        near_ref[0, y] = x_ref[(planes - 1) * (1 - odd), y]
        return carry

    lax.fori_loop(0, height, row, 0)
    spread_taps(k_ref, range(3), taps_ref)
    run = slices >> bits
    new = lax.broadcasted_iota(jnp.int32, (slices, 1), 0)
    old = lax.broadcasted_iota(jnp.int32, (slices, slices), 1)
    place = new & (run - 1)
    owner = reverse_lowest(new >> (run.bit_length() - 1), bits)
    order = (old == owner * run + place).astype(BF16)
    map_ref[:slices] = nt_dot(order, affinity_ref[...]).astype(BF16)
    map_ref[slices:] = jnp.broadcast_to(softness_ref[...], (TILE, channels)).astype(BF16)

    for which, known in enumerate((((1, 0), (2, 1)), ((0, planes - 2), (1, planes - 1)))):
        def put(y, lanes, rows, known=known, which=which):
            sources = [(role, [None if b is None else x_ref[p, y + b, :, lanes] for b in rows])
                       for role, p in known]
            totals = conv_rows(sources, taps_ref, lanes, len(rows) - 2)
            for i, total in enumerate(totals):
                start = (y + i) * depth
                start = start if isinstance(y, int) else pl.multiple_of(start, depth)
                partial_ref[which, pl.ds(start, depth), lanes] = total.astype(BF16)

        for lanes in channel_blocks(channels):
            put(0, lanes, (None, 0, 1))
            put(height - 1, lanes, (-1, 0, None))

        def pair(i, carry, put=put):
            for lanes in channel_blocks(channels):
                put(2 * i + 1, lanes, (-1, 0, 1, 2))
            return carry

        lax.fori_loop(0, (height - 2) // 2, pair, 0)


def ends_call(me, x, taps, affinity, softness, bits):
    planes, height, depth, channels = x.shape
    slices = affinity.shape[1]
    cells = height * depth
    return pl.pallas_call(
        functools.partial(ends_kernel, bits),
        in_specs=[SMEM] + [VMEM] * 4,
        out_specs=[VMEM] * 3,
        out_shape=[
            jax.ShapeDtypeStruct((1, height, depth, channels), BF16),
            jax.ShapeDtypeStruct((2, cells, channels), BF16),
            jax.ShapeDtypeStruct((slices + TILE, channels), BF16),
        ],
        scratch_shapes=[pltpu.VMEM((27, REPEAT, channels), CONV)],
        cost_estimate=pl.CostEstimate(
            flops=cells * channels * 12000, bytes_accessed=8 * cells * channels, transcendentals=0
        ),
        compiler_params=pltpu.CompilerParams(vmem_limit_bytes=LIMIT),
        name="ends",
    )(me, x, taps, affinity, softness)


def reverse_lowest(value, bits):
    return ((value & ((1 << (bits - 1)) - 1)) << 1) | (value >> (bits - 1))


def inside_kernel(x_ref, k_ref, map_ref, probs_ref, sums_ref, mass_ref,
                  taps_ref, even_ref, odd_ref, hid_ref, by_slice_ref):
    planes, height, depth, channels = x_ref.shape
    spread_taps(k_ref, range(3), taps_ref)
    sums_ref[...] = jnp.zeros(sums_ref.shape, F32)
    mass_ref[...] = jnp.zeros(mass_ref.shape, F32)
    groups = height // GROUP
    cells = GROUP * depth

    def conv(t, hid_ref):
        plane, first = t // groups, lax.rem(t, groups) * GROUP
        for lanes in channel_blocks(channels):
            for j in range(0, GROUP, 2):
                sources = []
                for role in range(3):
                    rows = []
                    for b in (-1, 0, 1, 2):
                        y, ok = first + j + b, None
                        if j + b < 0:
                            ok = first > 0
                        elif j + b >= GROUP:
                            ok = first + GROUP < height
                        rows.append(inner_row(x_ref, plane + role, y, lanes, ok))
                    sources.append((role, rows))
                for i, total in enumerate(conv_rows(sources, taps_ref, lanes, 2)):
                    hid_ref[(j + i) * depth : (j + i + 1) * depth, lanes] = gelu(total).astype(BF16)

    def share(t, source_ref, at):
        hid = source_ref[...]
        by_slice, by_cell = assign(hid, map_ref, mass_ref)
        start = pl.multiple_of(lax.rem(t, groups) * cells, cells)
        probs_ref[t // groups, pl.ds(start, cells), :] = by_cell
        hid_ref[at, :] = hid
        by_slice_ref[:, at] = by_slice

    count = (planes - 2) * groups
    conv(jnp.int32(0), even_ref)

    def two(s, carry):
        t = 2 * s
        share(t, even_ref, slice(0, cells))
        conv(t + 1, odd_ref)
        share(t + 1, odd_ref, slice(cells, 2 * cells))
        sums_ref[...] += dot(by_slice_ref[...], hid_ref[...])
        conv(jnp.minimum(t + 2, count - 1), even_ref)
        return carry

    lax.fori_loop(0, count // 2, two, 0)


def inside_call(x, taps, maps):
    planes, height, depth, channels = x.shape
    slices = maps.shape[0] - TILE
    cells = height * depth
    work = planes * cells * channels
    return pl.pallas_call(
        inside_kernel,
        in_specs=[VMEM] * 3,
        out_specs=[VMEM] * 3,
        out_shape=[
            jax.ShapeDtypeStruct((planes - 2, cells, slices), BF16),
            jax.ShapeDtypeStruct((slices, channels), F32),
            jax.ShapeDtypeStruct((slices, LANES), F32),
        ],
        scratch_shapes=[
            pltpu.VMEM((27, REPEAT, channels), CONV),
            pltpu.VMEM((GROUP * depth, channels), BF16),
            pltpu.VMEM((GROUP * depth, channels), BF16),
            pltpu.VMEM((2 * GROUP * depth, channels), BF16),
            pltpu.VMEM((slices, 2 * GROUP * depth), BF16),
        ],
        cost_estimate=pl.CostEstimate(
            flops=work * 7000, bytes_accessed=2 * work, transcendentals=2 * work
        ),
        compiler_params=pltpu.CompilerParams(vmem_limit_bytes=LIMIT),
        name="inside",
    )(x, taps, maps)


def edge_kernel(is_far, me_ref, halo_ref, partial_ref, k_ref, map_ref, sums_in_ref, mass_in_ref,
                probs_ref, *rest):
    if is_far:
        send_ref, keep_ref, *rest = rest
    sums_ref, mass_ref, taps_ref, hid_ref, by_slice_ref, *rest = rest
    _, height, depth, channels = halo_ref.shape
    slices = sums_in_ref.shape[0]
    odd = me_ref[0] & 1
    side = odd if is_far else 1 - odd
    spread_taps(k_ref, [2 * side], taps_ref)
    mass_ref[...] = mass_in_ref[...]
    cells = GROUP * depth
    for first in range(0, height, GROUP):
        group = slice(first * depth, first * depth + cells)
        for lanes in channel_blocks(channels):
            for y in range(first, first + GROUP, 2):
                rows = [halo_ref[0, y + b, :, lanes] if 0 <= y + b < height else None
                        for b in (-1, 0, 1, 2)]
                for i, total in enumerate(conv_rows([(0, rows)], taps_ref, lanes, 2)):
                    at = slice((y + i) * depth, (y + i + 1) * depth)
                    total = total + partial_ref[side, at, lanes].astype(F32)
                    hid_ref[at, lanes] = gelu(total).astype(BF16)
        by_slice, by_cell = assign(hid_ref[group], map_ref, mass_ref)
        probs_ref[0, group] = by_cell
        by_slice_ref[:, group] = by_slice
    sums_ref[...] = sums_in_ref[...] + dot(by_slice_ref[...], hid_ref[...])
    if not is_far:
        return
    split_ref, = rest
    mass = lax.dot_general(
        jnp.ones((8, LANES), F32), mass_ref[...], (((1,), (1,)), ((), ())),
        preferred_element_type=F32, precision=lax.Precision.HIGHEST,
    )
    split_ref[...] = split(mass)
    owners, rows, _ = send_ref.shape
    held = channels // LANES
    rows = (rows - 8) // held
    for ref, half in ((send_ref, 1 - odd), (keep_ref, odd)):
        start = pl.multiple_of(half * (slices // 2), slices // 2)
        for i in range(held):
            part = sums_ref[pl.ds(start, slices // 2), i * LANES : (i + 1) * LANES].astype(BF16)
            ref[:, i * rows : (i + 1) * rows, :] = part.reshape(owners, rows, LANES)
        for owner in range(owners):
            lane = pl.multiple_of(start + owner * rows // LANES * LANES, LANES)
            ref[owner, held * rows :, :] = split_ref[:, pl.ds(lane, LANES)].astype(BF16)


def split(mass):
    high = mass.astype(BF16).astype(F32)
    row = lax.broadcasted_iota(jnp.int32, mass.shape, mass.ndim - 2)
    return jnp.where(row == 0, high, jnp.where(row == 1, mass - high, 0.0))


def edge_call(is_far, me, halo, taps, maps, partial, sums, mass, owners):
    _, height, depth, channels = halo.shape
    slices = sums.shape[0]
    cells = height * depth
    carry = [(s.shape, F32) for s in (sums, mass)]
    scratch = [
        pltpu.VMEM((9, REPEAT, channels), CONV),
        pltpu.VMEM((cells, channels), BF16),
        pltpu.VMEM((slices, cells), BF16),
    ]
    if is_far:
        rows = channels // LANES * (slices // owners) + 8
        outs = [((owners // 2, rows, LANES), BF16)] * 2
        scratch = [pltpu.VMEM(*c) for c in carry] + scratch + [pltpu.VMEM((8, slices), F32)]
    else:
        outs = carry
    return pl.pallas_call(
        functools.partial(edge_kernel, is_far),
        in_specs=[SMEM] + [VMEM] * 6,
        out_specs=[VMEM] * (1 + len(outs)),
        out_shape=[jax.ShapeDtypeStruct((1, cells, slices), BF16)]
        + [jax.ShapeDtypeStruct(*o) for o in outs],
        scratch_shapes=scratch,
        cost_estimate=pl.CostEstimate(
            flops=cells * channels * 16000, bytes_accessed=4 * cells * channels,
            transcendentals=2 * cells * channels,
        ),
        compiler_params=pltpu.CompilerParams(vmem_limit_bytes=LIMIT),
        name="far" if is_far else "near",
    )(me, halo, partial, taps, maps, sums, mass)


def merge_kernel(keep_ref, other_ref, out_ref):
    both = keep_ref[...].astype(F32) + other_ref[...].astype(F32)
    rows = both.shape[1] - 8
    tail = both[:, rows:]
    out_ref[:, :rows] = both[:, :rows].astype(BF16)
    out_ref[:, rows:] = split(jnp.broadcast_to(tail[:, 0:1] + tail[:, 1:2], tail.shape)).astype(BF16)


def merge_call(keep, other):
    return pl.pallas_call(
        merge_kernel,
        in_specs=[VMEM, VMEM],
        out_specs=VMEM,
        out_shape=jax.ShapeDtypeStruct(keep.shape, BF16),
        compiler_params=pltpu.CompilerParams(vmem_limit_bytes=LIMIT),
        name="merge",
    )(keep, other)


def owner_kernel(share, me_ref, parts_ref, gain_ref, content_ref, widening_ref,
                 narrowing_ref, final_ref, out_ref, mapped_ref):
    channels = content_ref.shape[0]
    held = channels // LANES
    rows = out_ref.shape[0]
    total = jnp.sum(parts_ref[...].astype(F32), axis=0)
    pooled = jnp.concatenate([total[i * rows : (i + 1) * rows] for i in range(held)], axis=1)
    mass = total[held * rows : held * rows + 1] + total[held * rows + 1 : held * rows + 2]
    lane = lax.broadcasted_iota(jnp.int32, (rows, LANES), 1)
    row = lax.broadcasted_iota(jnp.int32, (rows, LANES), 0)
    first = ((me_ref[0] >> 1) // share * rows) & (LANES - 1)
    mass = jnp.sum(jnp.where(lane == row + first, mass, 0.0), axis=1, keepdims=True)
    pooled = pooled / (mass + epsilon)
    high = pooled.astype(BF16)
    low = (pooled - high.astype(F32)).astype(BF16)
    tokens = dot(high, content_ref[...]) + dot(low, content_ref[...])
    center = jnp.mean(tokens, axis=-1, keepdims=True)
    spread = jnp.mean((tokens - center) ** 2, axis=-1, keepdims=True)
    normed = ((tokens - center) * (1.0 / jnp.sqrt(spread + epsilon)) * gain_ref[...]).astype(BF16)
    inner = gelu(dot(normed, widening_ref[...])).astype(BF16)
    out = (tokens + dot(inner, narrowing_ref[...])).astype(BF16)
    out_ref[...] = out
    mapped = dot(out, final_ref[...]).astype(BF16)
    mapped_ref[...] = jnp.broadcast_to(mapped[None], mapped_ref.shape)


def owner_call(share, me, parts, gain, *weights):
    channels = weights[0].shape[0]
    owners = parts.shape[0]
    rows = (parts.shape[1] - 8) // (channels // LANES)
    return pl.pallas_call(
        functools.partial(owner_kernel, share),
        in_specs=[SMEM] + [VMEM] * 6,
        out_specs=[VMEM, VMEM],
        out_shape=[
            jax.ShapeDtypeStruct((rows, channels), BF16),
            jax.ShapeDtypeStruct((owners, rows, channels), BF16),
        ],
        compiler_params=pltpu.CompilerParams(vmem_limit_bytes=LIMIT),
        name="owner",
    )(me, parts, gain, *weights)


def update_kernel(me_ref, x_ref, inside_ref, near_ref, far_ref, own_ref, other_ref, out_ref,
                  done_ref, mapped_ref, sem):
    planes, cells, channels = x_ref.shape
    half = own_ref.shape[0]
    rows = math.gcd(cells, 512)
    pieces = cells // rows
    odd = me_ref[0] & 1
    mapped_ref[pl.ds(pl.multiple_of(odd * half, half), half)] = own_ref[...]
    mapped_ref[pl.ds(pl.multiple_of((1 - odd) * half, half), half)] = other_ref[...]

    def place(i):
        return pl.ds(pl.multiple_of(lax.rem(i, pieces) * rows, rows), rows)

    def store(plane, i):
        at = place(i)
        index = plane * pieces + lax.rem(i, pieces)
        return pltpu.make_async_copy(done_ref.at[plane, at], out_ref.at[plane, at], sem.at[index])

    for probs_ref, base in (
        (inside_ref, 1), (near_ref, (planes - 1) * (1 - odd)), (far_ref, (planes - 1) * odd)
    ):
        def step(i, carry, probs_ref=probs_ref, base=base):
            part, at = i // pieces, place(i)
            change = dot(probs_ref[part, at, :], mapped_ref[...])
            done_ref[base + part, at, :] = (x_ref[base + part, at, :].astype(F32) + change).astype(BF16)
            store(base + part, i).start()
            return carry

        lax.fori_loop(0, probs_ref.shape[0] * pieces, step, 0)

    def finish(i, carry):
        store(i // pieces, i).wait()
        return carry

    lax.fori_loop(0, planes * pieces, finish, 0)


def update_call(me, x, inside, near, far, own, other):
    planes, cells, channels = x.shape
    return pl.pallas_call(
        update_kernel,
        in_specs=[SMEM] + [VMEM] * 6,
        out_specs=HBM,
        out_shape=jax.ShapeDtypeStruct(x.shape, BF16),
        scratch_shapes=[
            pltpu.VMEM(x.shape, BF16),
            pltpu.VMEM((2 * own.shape[0], channels), BF16),
            pltpu.SemaphoreType.DMA((planes * cells // math.gcd(cells, 512),)),
        ],
        compiler_params=pltpu.CompilerParams(vmem_limit_bytes=LIMIT),
        name="update",
    )(me, x, inside, near, far, own, other)


def per_device(
    mesh_feature_array,
    stencil_coefficients,
    partition_affinity_matrix,
    softness_mapping_matrix,
    content_mapping_matrix,
    layernorm_multiplier,
    widening_matrix,
    narrowing_matrix,
    final_mapping_matrix,
):
    x = mesh_feature_array
    planes, height, depth, channels = x.shape
    slices = partition_affinity_matrix.shape[1]
    n = lax.axis_size("gx")
    me = lax.axis_index("gx").astype(jnp.int32)[None]
    far_pairs = [p for i in range(1, n - 1, 2) for p in ((i, i + 1), (i + 1, i))]
    near_pairs = [p for i in range(0, n, 2) for p in ((i, i + 1), (i + 1, i))]
    far_halo = lax.ppermute(pack_call(me, x), "gx", far_pairs)

    owners = min(n // 2, slices // 2 // TILE)
    share = n // 2 // owners
    groups = [[2 * (share * j + s) + h for j in range(owners)] for h in range(2) for s in range(share)]
    taps = stencil_coefficients
    near_plane, partial, maps = ends_call(
        me, x, taps, partition_affinity_matrix, softness_mapping_matrix[None], n.bit_length() - 1
    )
    near_halo = lax.ppermute(near_plane, "gx", near_pairs)
    inside_probs, sums, mass = inside_call(x, taps, maps)
    near_probs, sums, mass = edge_call(
        False, me, near_halo, taps, maps, partial, sums, mass, 2 * owners
    )
    far_probs, send, keep = edge_call(True, me, far_halo, taps, maps, partial, sums, mass, 2 * owners)

    parts = merge_call(keep, lax.ppermute(send, "gx", near_pairs))
    parts = lax.all_to_all(parts, "gx", 0, 0, axis_index_groups=groups)
    if share > 1:
        sharers = [[2 * (share * j + s) + h for s in range(share)]
                   for h in range(2) for j in range(owners)]
        parts = lax.psum(parts, "gx", axis_index_groups=sharers)
    own_out, mapped = owner_call(
        share, me, parts, layernorm_multiplier[None],
        content_mapping_matrix, widening_matrix, narrowing_matrix, final_mapping_matrix,
    )
    if share > 1:
        place = lax.rem(me[0] // 2, share) * (slices // n)
        own_out = lax.dynamic_slice_in_dim(own_out, place, slices // n)
    mapped = lax.all_to_all(mapped, "gx", 0, 0, axis_index_groups=groups).reshape(slices // 2, channels)
    updated = update_call(
        me, x.reshape(planes, height * depth, channels), inside_probs, near_probs, far_probs,
        mapped, lax.ppermute(mapped, "gx", near_pairs),
    )
    return updated.reshape(x.shape), own_out


def solution(mesh):
    return jax.shard_map(
        per_device,
        mesh=mesh,
        in_specs=(P(("grp", "gx"), None, None, None), P(), P(), P(), P(), P(), P(), P(), P()),
        out_specs=(P(("grp", "gx"), None, None, None), P(("grp", "gx"), None)),
        check_vma=False,
    )
```

```python
import functools
import math

import jax
import jax.numpy as jnp
from jax import lax
from jax.experimental import pallas as pl
from jax.experimental.pallas import tpu as pltpu
from jax.sharding import PartitionSpec as P

epsilon = 1e-05
LANES = 128
BLOCK = 256
GROUP = 8
TILE = 16
REPEAT = 8
MIB = 2**20
LIMIT = 32 * MIB
F32, BF16 = jnp.float32, jnp.bfloat16
CONV = BF16
VMEM = pl.BlockSpec(memory_space=pltpu.VMEM)
SMEM = pl.BlockSpec(memory_space=pltpu.SMEM)
HBM = pl.BlockSpec(memory_space=pltpu.HBM)


def dot(a, b):
    return jnp.dot(a, b, preferred_element_type=F32)


def gelu(x):
    inner = x * (x * x * (0.044715 * math.sqrt(2 / math.pi)) + math.sqrt(2 / math.pi))
    return x + x * jnp.tanh(inner)


def spread_taps(k_ref, planes, taps_ref):
    for role, plane in enumerate(planes):
        for tap in range(9):
            row = k_ref[pl.ds(9 * plane + tap, 1), :]
            taps_ref[9 * role + tap] = jnp.broadcast_to(row, taps_ref.shape[1:]).astype(CONV)


def conv_rows(sources, taps_ref, lanes, count):
    sums = [[None] * 3 for _ in range(count)]
    for role, rows in sources:
        taps = [taps_ref[9 * role + i, :, lanes] for i in range(9)]
        for j, row in enumerate(rows):
            if row is None:
                continue
            depth, width = row.shape
            row = row.astype(CONV).reshape(depth // REPEAT, REPEAT, width)
            for out in range(max(0, j - 2), min(count, j + 1)):
                for c in range(3):
                    term = row * taps[3 * (j - out) + c]
                    sums[out][c] = term if sums[out][c] is None else sums[out][c] + term
    position = lax.broadcasted_iota(jnp.int32, (8, width), 0)
    results = []
    for out in range(count):
        before, here, after = (s.astype(F32).reshape(depth, width) for s in sums[out])
        before, after = pltpu.roll(before, 1, 0), pltpu.roll(after, depth - 1, 0)
        low = jnp.where(position == 0, 0.0, before[:8])
        high = jnp.where(position == 7, 0.0, after[depth - 8 :])
        before = jnp.concatenate([low, before[8:]], axis=0)
        after = jnp.concatenate([after[: depth - 8], high], axis=0)
        results.append(here + before + after)
    return results


def channel_blocks(channels):
    return [slice(i, i + BLOCK) for i in range(0, channels, BLOCK)]


def inner_row(ref, plane, y, lanes, inside=None):
    if inside is None:
        return ref[plane, y, :, lanes]
    row = ref[plane, jnp.clip(y, 0, ref.shape[1] - 1), :, lanes].astype(F32)
    return (row * jnp.where(inside, 1.0, 0.0)).astype(BF16)


def nt_dot(a, b):
    return lax.dot_general(a, b, (((1,), (1,)), ((), ())), preferred_element_type=F32)


def assign(hid, map_ref, mass_ref):
    cells = hid.shape[0]
    slices = map_ref.shape[0] - TILE
    raw = nt_dot(map_ref[...], hid)
    soft = raw[slices : slices + 8]
    temperature = 0.25 + jnp.maximum(soft, 0.0) + jnp.log(1.0 + jnp.exp(-jnp.abs(soft)))
    scale = (1.0 / math.log(2.0)) / temperature
    raw = raw[:slices].reshape(slices // 8, 8, cells)
    top = jnp.max(jnp.max(raw, axis=0), axis=0, keepdims=True)
    powers = jnp.exp2((raw - top[None]) * scale[None])
    total = jnp.sum(jnp.sum(powers, axis=0), axis=0, keepdims=True)
    probs = (powers * (1.0 / total)[None]).reshape(slices, cells)
    mass = probs[:, :LANES]
    for start in range(LANES, cells, LANES):
        mass = mass + probs[:, start : start + LANES]
    mass_ref[...] += mass
    return probs.astype(BF16)


def pack_kernel(me_ref, x_ref, far_ref, after_ref, sem):
    plane = (x_ref.shape[0] - 1) * (me_ref[0] & 1)
    load = pltpu.make_async_copy(x_ref.at[pl.ds(plane, 1)], far_ref, sem)
    load.start()
    after_ref[...] = jnp.zeros(after_ref.shape, F32)
    load.wait()


def pack_call(me, x):
    return pl.pallas_call(
        pack_kernel,
        in_specs=[SMEM, HBM],
        out_specs=[VMEM, VMEM],
        out_shape=[
            jax.ShapeDtypeStruct((1, *x.shape[1:]), BF16),
            jax.ShapeDtypeStruct((8, LANES), F32),
        ],
        scratch_shapes=[pltpu.SemaphoreType.DMA],
        cost_estimate=pl.CostEstimate(flops=0, bytes_accessed=2**22, transcendentals=0),
        compiler_params=pltpu.CompilerParams(vmem_limit_bytes=58 * MIB),
        name="pack",
    )(me, x)


def ends_kernel(bits, me_ref, _, x_ref, k_ref, affinity_ref, softness_ref, near_ref, partial_ref, map_ref,
                taps_ref):
    planes, height, depth, channels = x_ref.shape
    slices = affinity_ref.shape[1]
    odd = me_ref[0] & 1

    def row(y, carry):
        near_ref[0, y] = x_ref[(planes - 1) * (1 - odd), y]
        return carry

    lax.fori_loop(0, height, row, 0)
    spread_taps(k_ref, range(3), taps_ref)
    run = slices >> bits
    new = lax.broadcasted_iota(jnp.int32, (slices, 1), 0)
    old = lax.broadcasted_iota(jnp.int32, (slices, slices), 1)
    place = new & (run - 1)
    owner = reverse_lowest(new >> (run.bit_length() - 1), bits)
    order = (old == owner * run + place).astype(BF16)
    map_ref[:slices] = (0.5 * nt_dot(order, affinity_ref[...])).astype(BF16)
    softness = softness_ref[...].astype(BF16).astype(F32)
    map_ref[slices:] = jnp.broadcast_to(0.5 * softness, (TILE, channels)).astype(BF16)

    for which, known in enumerate((((1, 0), (2, 1)), ((0, planes - 2), (1, planes - 1)))):
        def put(y, lanes, rows, known=known, which=which):
            sources = [(role, [None if b is None else x_ref[p, y + b, :, lanes] for b in rows])
                       for role, p in known]
            totals = conv_rows(sources, taps_ref, lanes, len(rows) - 2)
            for i, total in enumerate(totals):
                start = (y + i) * depth
                start = start if isinstance(y, int) else pl.multiple_of(start, depth)
                partial_ref[which, pl.ds(start, depth), lanes] = total.astype(BF16)

        for lanes in channel_blocks(channels):
            put(0, lanes, (None, 0, 1))
            put(height - 1, lanes, (-1, 0, None))

        def pair(i, carry, put=put):
            for lanes in channel_blocks(channels):
                put(2 * i + 1, lanes, (-1, 0, 1, 2))
            return carry

        lax.fori_loop(0, (height - 2) // 2, pair, 0)


def ends_call(me, after, x, taps, affinity, softness, bits):
    planes, height, depth, channels = x.shape
    slices = affinity.shape[1]
    cells = height * depth
    return pl.pallas_call(
        functools.partial(ends_kernel, bits),
        in_specs=[SMEM] + [VMEM] * 5,
        out_specs=[VMEM] * 3,
        out_shape=[
            jax.ShapeDtypeStruct((1, height, depth, channels), BF16),
            jax.ShapeDtypeStruct((2, cells, channels), BF16),
            jax.ShapeDtypeStruct((slices + TILE, channels), BF16),
        ],
        scratch_shapes=[pltpu.VMEM((27, REPEAT, channels), CONV)],
        cost_estimate=pl.CostEstimate(
            flops=cells * channels * 12000, bytes_accessed=8 * cells * channels, transcendentals=0
        ),
        compiler_params=pltpu.CompilerParams(vmem_limit_bytes=LIMIT),
        name="ends",
    )(me, after, x, taps, affinity, softness)


def reverse_lowest(value, bits):
    return ((value & ((1 << (bits - 1)) - 1)) << 1) | (value >> (bits - 1))


def inside_kernel(x_ref, k_ref, map_ref, probs_ref, sums_ref, mass_ref,
                  taps_ref, even_ref, odd_ref, hid_ref, by_slice_ref):
    planes, height, depth, channels = x_ref.shape
    spread_taps(k_ref, range(3), taps_ref)
    sums_ref[...] = jnp.zeros(sums_ref.shape, F32)
    mass_ref[...] = jnp.zeros(mass_ref.shape, F32)
    groups = height // GROUP
    cells = GROUP * depth

    def conv(t, hid_ref):
        plane, first = t // groups, lax.rem(t, groups) * GROUP
        for lanes in channel_blocks(channels):
            for j in range(0, GROUP, 2):
                sources = []
                for role in range(3):
                    rows = []
                    for b in (-1, 0, 1, 2):
                        y, ok = first + j + b, None
                        if j + b < 0:
                            ok = first > 0
                        elif j + b >= GROUP:
                            ok = first + GROUP < height
                        rows.append(inner_row(x_ref, plane + role, y, lanes, ok))
                    sources.append((role, rows))
                for i, total in enumerate(conv_rows(sources, taps_ref, lanes, 2)):
                    hid_ref[(j + i) * depth : (j + i + 1) * depth, lanes] = gelu(total).astype(BF16)

    def share(t, source_ref, at):
        hid = source_ref[...]
        by_slice = assign(hid, map_ref, mass_ref)
        start = pl.multiple_of(lax.rem(t, groups) * cells, cells)
        probs_ref[t // groups, pl.ds(start, cells), :] = by_slice.T
        hid_ref[at, :] = hid
        by_slice_ref[:, at] = by_slice

    count = (planes - 2) * groups
    conv(jnp.int32(0), even_ref)

    def two(s, carry):
        t = 2 * s
        share(t, even_ref, slice(0, cells))
        conv(t + 1, odd_ref)
        share(t + 1, odd_ref, slice(cells, 2 * cells))
        sums_ref[...] += dot(by_slice_ref[...], hid_ref[...])
        conv(jnp.minimum(t + 2, count - 1), even_ref)
        return carry

    lax.fori_loop(0, count // 2, two, 0)


def inside_call(x, taps, maps):
    planes, height, depth, channels = x.shape
    slices = maps.shape[0] - TILE
    cells = height * depth
    work = planes * cells * channels
    return pl.pallas_call(
        inside_kernel,
        in_specs=[VMEM] * 3,
        out_specs=[VMEM] * 3,
        out_shape=[
            jax.ShapeDtypeStruct((planes - 2, cells, slices), BF16),
            jax.ShapeDtypeStruct((slices, channels), F32),
            jax.ShapeDtypeStruct((slices, LANES), F32),
        ],
        scratch_shapes=[
            pltpu.VMEM((27, REPEAT, channels), CONV),
            pltpu.VMEM((GROUP * depth, channels), BF16),
            pltpu.VMEM((GROUP * depth, channels), BF16),
            pltpu.VMEM((2 * GROUP * depth, channels), BF16),
            pltpu.VMEM((slices, 2 * GROUP * depth), BF16),
        ],
        cost_estimate=pl.CostEstimate(
            flops=work * 7000, bytes_accessed=2 * work, transcendentals=2 * work
        ),
        compiler_params=pltpu.CompilerParams(vmem_limit_bytes=LIMIT),
        name="inside",
    )(x, taps, maps)


def edge_kernel(is_far, me_ref, halo_ref, partial_ref, k_ref, map_ref, sums_in_ref, mass_in_ref,
                probs_ref, *rest):
    if is_far:
        by_slice_ref, (send_ref, keep_ref, *rest) = probs_ref, rest
    sums_ref, mass_ref, taps_ref, hid_ref, scratch_ref = rest
    if is_far:
        split_ref = scratch_ref
    else:
        by_slice_ref = scratch_ref
    _, height, depth, channels = halo_ref.shape
    slices = sums_in_ref.shape[0]
    odd = me_ref[0] & 1
    side = odd if is_far else 1 - odd
    spread_taps(k_ref, [2 * side], taps_ref)
    mass_ref[...] = mass_in_ref[...]
    cells = GROUP * depth
    for first in range(0, height, GROUP):
        group = slice(first * depth, first * depth + cells)
        for lanes in channel_blocks(channels):
            for y in range(first, first + GROUP, 2):
                rows = [halo_ref[0, y + b, :, lanes] if 0 <= y + b < height else None
                        for b in (-1, 0, 1, 2)]
                for i, total in enumerate(conv_rows([(0, rows)], taps_ref, lanes, 2)):
                    at = slice((y + i) * depth, (y + i + 1) * depth)
                    total = total + partial_ref[side, at, lanes].astype(F32)
                    hid_ref[at, lanes] = gelu(total).astype(BF16)
        by_slice = assign(hid_ref[group], map_ref, mass_ref)
        if not is_far:
            probs_ref[0, group] = by_slice.T
        by_slice_ref[:, group] = by_slice
        if first + GROUP == height // 2:
            done = slice(0, first * depth + cells)
            sums_ref[...] = sums_in_ref[...] + dot(by_slice_ref[:, done], hid_ref[done])
    rest_of = slice(height * depth // 2, height * depth)
    sums_ref[...] += dot(by_slice_ref[:, rest_of], hid_ref[rest_of])
    if not is_far:
        return
    mass = lax.dot_general(
        jnp.ones((8, LANES), F32), mass_ref[...], (((1,), (1,)), ((), ())),
        preferred_element_type=F32, precision=lax.Precision.HIGHEST,
    )
    split_ref[...] = split(mass)
    owners, rows, _ = send_ref.shape
    held = channels // LANES
    rows = (rows - 8) // held
    for ref, half in ((send_ref, 1 - odd), (keep_ref, odd)):
        start = pl.multiple_of(half * (slices // 2), slices // 2)
        for i in range(held):
            part = sums_ref[pl.ds(start, slices // 2), i * LANES : (i + 1) * LANES].astype(BF16)
            ref[:, i * rows : (i + 1) * rows, :] = part.reshape(owners, rows, LANES)
        for owner in range(owners):
            lane = pl.multiple_of(start + owner * rows // LANES * LANES, LANES)
            ref[owner, held * rows :, :] = split_ref[:, pl.ds(lane, LANES)].astype(BF16)


def split(mass):
    high = mass.astype(BF16).astype(F32)
    row = lax.broadcasted_iota(jnp.int32, mass.shape, mass.ndim - 2)
    return jnp.where(row == 0, high, jnp.where(row == 1, mass - high, 0.0))


def edge_call(is_far, me, halo, taps, maps, partial, sums, mass, owners):
    _, height, depth, channels = halo.shape
    slices = sums.shape[0]
    cells = height * depth
    carry = [(s.shape, F32) for s in (sums, mass)]
    scratch = [
        pltpu.VMEM((9, REPEAT, channels), CONV),
        pltpu.VMEM((cells, channels), BF16),
    ]
    if is_far:
        rows = channels // LANES * (slices // owners) + 8
        outs = [((owners // 2, rows, LANES), BF16)] * 2
        scratch = [pltpu.VMEM(*c) for c in carry] + scratch + [pltpu.VMEM((8, slices), F32)]
    else:
        outs = carry
        scratch += [pltpu.VMEM((slices, cells), BF16)]
    probs = (slices, cells) if is_far else (1, cells, slices)
    return pl.pallas_call(
        functools.partial(edge_kernel, is_far),
        in_specs=[SMEM] + [VMEM] * 6,
        out_specs=[VMEM] * (1 + len(outs)),
        out_shape=[jax.ShapeDtypeStruct(probs, BF16)]
        + [jax.ShapeDtypeStruct(*o) for o in outs],
        scratch_shapes=scratch,
        cost_estimate=pl.CostEstimate(
            flops=cells * channels * 16000, bytes_accessed=4 * cells * channels,
            transcendentals=2 * cells * channels,
        ),
        compiler_params=pltpu.CompilerParams(vmem_limit_bytes=LIMIT),
        name="far" if is_far else "near",
    )(me, halo, partial, taps, maps, sums, mass)


def turn_kernel(by_slice_ref, probs_ref):
    probs_ref[0] = by_slice_ref[...].T


def turn_call(by_slice):
    slices, cells = by_slice.shape
    return pl.pallas_call(
        turn_kernel,
        in_specs=[VMEM],
        out_specs=VMEM,
        out_shape=jax.ShapeDtypeStruct((1, cells, slices), BF16),
        cost_estimate=pl.CostEstimate(flops=0, bytes_accessed=4 * cells * slices, transcendentals=0),
        compiler_params=pltpu.CompilerParams(vmem_limit_bytes=LIMIT),
        name="turn",
    )(by_slice)


def merge_kernel(keep_ref, other_ref, out_ref):
    both = keep_ref[...].astype(F32) + other_ref[...].astype(F32)
    rows = both.shape[1] - 8
    tail = both[:, rows:]
    out_ref[:, :rows] = both[:, :rows].astype(BF16)
    out_ref[:, rows:] = split(jnp.broadcast_to(tail[:, 0:1] + tail[:, 1:2], tail.shape)).astype(BF16)


def merge_call(keep, other):
    return pl.pallas_call(
        merge_kernel,
        in_specs=[VMEM, VMEM],
        out_specs=VMEM,
        out_shape=jax.ShapeDtypeStruct(keep.shape, BF16),
        compiler_params=pltpu.CompilerParams(vmem_limit_bytes=LIMIT),
        name="merge",
    )(keep, other)


def owner_kernel(share, me_ref, parts_ref, gain_ref, content_ref, widening_ref,
                 narrowing_ref, final_ref, out_ref, mapped_ref):
    channels = content_ref.shape[0]
    held = channels // LANES
    rows = out_ref.shape[0]
    total = jnp.sum(parts_ref[...].astype(F32), axis=0)
    pooled = jnp.concatenate([total[i * rows : (i + 1) * rows] for i in range(held)], axis=1)
    mass = total[held * rows : held * rows + 1] + total[held * rows + 1 : held * rows + 2]
    lane = lax.broadcasted_iota(jnp.int32, (rows, LANES), 1)
    row = lax.broadcasted_iota(jnp.int32, (rows, LANES), 0)
    first = ((me_ref[0] >> 1) // share * rows) & (LANES - 1)
    mass = jnp.sum(jnp.where(lane == row + first, mass, 0.0), axis=1, keepdims=True)
    pooled = 0.5 * pooled / (mass + epsilon)
    high = pooled.astype(BF16)
    low = (pooled - high.astype(F32)).astype(BF16)
    tokens = dot(high, content_ref[...]) + dot(low, content_ref[...])
    center = jnp.mean(tokens, axis=-1, keepdims=True)
    spread = jnp.mean((tokens - center) ** 2, axis=-1, keepdims=True)
    normed = ((tokens - center) * (1.0 / jnp.sqrt(spread + epsilon)) * gain_ref[...]).astype(BF16)
    inner = (0.5 * gelu(dot(normed, widening_ref[...]))).astype(BF16)
    out = (tokens + dot(inner, narrowing_ref[...])).astype(BF16)
    out_ref[...] = out
    mapped_ref[...] = dot(out, final_ref[...]).astype(BF16)


def owner_call(share, me, parts, gain, *weights):
    channels = weights[0].shape[0]
    rows = (parts.shape[1] - 8) // (channels // LANES)
    return pl.pallas_call(
        functools.partial(owner_kernel, share),
        in_specs=[SMEM] + [VMEM] * 6,
        out_specs=[VMEM, VMEM],
        out_shape=[jax.ShapeDtypeStruct((rows, channels), BF16)] * 2,
        compiler_params=pltpu.CompilerParams(vmem_limit_bytes=LIMIT),
        name="owner",
    )(me, parts, gain, *weights)


def update_kernel(me_ref, x_ref, inside_ref, near_ref, far_ref, own_ref, other_ref, out_ref,
                  done_ref, mapped_ref, sem):
    planes, cells, channels = x_ref.shape
    half = own_ref.shape[0]
    rows = cells
    pieces = cells // rows
    odd = me_ref[0] & 1
    mapped_ref[pl.ds(pl.multiple_of(odd * half, half), half)] = own_ref[...]
    mapped_ref[pl.ds(pl.multiple_of((1 - odd) * half, half), half)] = other_ref[...]

    def place(i):
        return pl.ds(pl.multiple_of(lax.rem(i, pieces) * rows, rows), rows)

    def store(plane, i):
        at = place(i)
        index = plane * pieces + lax.rem(i, pieces)
        return pltpu.make_async_copy(done_ref.at[plane, at], out_ref.at[plane, at], sem.at[index])

    for probs_ref, base in (
        (inside_ref, 1), (near_ref, (planes - 1) * (1 - odd)), (far_ref, (planes - 1) * odd)
    ):
        def step(i, carry, probs_ref=probs_ref, base=base):
            part, at = i // pieces, place(i)
            change = dot(probs_ref[part, at, :], mapped_ref[...])
            done_ref[base + part, at, :] = (x_ref[base + part, at, :].astype(F32) + change).astype(BF16)
            store(base + part, i).start()
            return carry

        lax.fori_loop(0, probs_ref.shape[0] * pieces, step, 0)

    def finish(i, carry):
        store(i // pieces, i).wait()
        return carry

    lax.fori_loop(0, planes * pieces, finish, 0)


def update_call(me, x, inside, near, far, own, other):
    planes, cells, channels = x.shape
    return pl.pallas_call(
        update_kernel,
        in_specs=[SMEM] + [VMEM] * 6,
        out_specs=HBM,
        out_shape=jax.ShapeDtypeStruct(x.shape, BF16),
        scratch_shapes=[
            pltpu.VMEM(x.shape, BF16),
            pltpu.VMEM((2 * own.shape[0], channels), BF16),
            pltpu.SemaphoreType.DMA((planes,)),
        ],
        compiler_params=pltpu.CompilerParams(vmem_limit_bytes=LIMIT),
        name="update",
    )(me, x, inside, near, far, own, other)


def per_device(
    mesh_feature_array,
    stencil_coefficients,
    partition_affinity_matrix,
    softness_mapping_matrix,
    content_mapping_matrix,
    layernorm_multiplier,
    widening_matrix,
    narrowing_matrix,
    final_mapping_matrix,
):
    x = mesh_feature_array
    planes, height, depth, channels = x.shape
    slices = partition_affinity_matrix.shape[1]
    n = lax.axis_size("gx")
    me = lax.axis_index("gx").astype(jnp.int32)[None]
    far_pairs = [p for i in range(1, n - 1, 2) for p in ((i, i + 1), (i + 1, i))]
    near_pairs = [p for i in range(0, n, 2) for p in ((i, i + 1), (i + 1, i))]
    far_plane, after = pack_call(me, x)
    far_halo = lax.ppermute(far_plane, "gx", far_pairs)

    owners = min(n // 2, slices // 2 // TILE)
    share = n // 2 // owners
    groups = [[2 * (share * j + s) + h for j in range(owners)] for h in range(2) for s in range(share)]
    taps = stencil_coefficients
    near_plane, partial, maps = ends_call(
        me, after, x, taps, partition_affinity_matrix, softness_mapping_matrix[None],
        n.bit_length() - 1,
    )
    near_halo = lax.ppermute(near_plane, "gx", near_pairs)
    inside_probs, sums, mass = inside_call(x, taps, maps)
    near_probs, sums, mass = edge_call(
        False, me, near_halo, taps, maps, partial, sums, mass, 2 * owners
    )
    far_by_slice, send, keep = edge_call(True, me, far_halo, taps, maps, partial, sums, mass, 2 * owners)

    received = lax.ppermute(send, "gx", near_pairs)
    far_probs = turn_call(far_by_slice)
    parts = merge_call(keep, received)
    parts = lax.all_to_all(parts, "gx", 0, 0, axis_index_groups=groups)
    if share > 1:
        sharers = [[2 * (share * j + s) + h for s in range(share)]
                   for h in range(2) for j in range(owners)]
        parts = lax.psum(parts, "gx", axis_index_groups=sharers)
    own_out, mapped = owner_call(
        share, me, parts, layernorm_multiplier[None],
        content_mapping_matrix, widening_matrix, narrowing_matrix, final_mapping_matrix,
    )
    if share > 1:
        place = lax.rem(me[0] // 2, share) * (slices // n)
        own_out = lax.dynamic_slice_in_dim(own_out, place, slices // n)
    mapped = lax.all_gather(mapped, "gx", axis_index_groups=groups, tiled=True)
    updated = update_call(
        me, x.reshape(planes, height * depth, channels), inside_probs, near_probs, far_probs,
        mapped, lax.ppermute(mapped, "gx", near_pairs),
    )
    return updated.reshape(x.shape), own_out


def solution(mesh):
    return jax.shard_map(
        per_device,
        mesh=mesh,
        in_specs=(P(("grp", "gx"), None, None, None), P(), P(), P(), P(), P(), P(), P(), P()),
        out_specs=(P(("grp", "gx"), None, None, None), P(("grp", "gx"), None)),
        check_vma=False,
    )
```

```python
import functools
import math

import jax
import jax.numpy as jnp
from jax import lax
from jax.experimental import pallas as pl
from jax.experimental.pallas import tpu as pltpu
from jax.sharding import PartitionSpec as P

epsilon = 1e-05
LANES = 128
BLOCK = 256
GROUP = 8
TILE = 16
REPEAT = 8
MIB = 2**20
LIMIT = 32 * MIB
F32, BF16 = jnp.float32, jnp.bfloat16
CONV = BF16
VMEM = pl.BlockSpec(memory_space=pltpu.VMEM)
SMEM = pl.BlockSpec(memory_space=pltpu.SMEM)
HBM = pl.BlockSpec(memory_space=pltpu.HBM)


def dot(a, b):
    return jnp.dot(a, b, preferred_element_type=F32)


def gelu(x):
    inner = x * (x * x * (0.044715 * math.sqrt(2 / math.pi)) + math.sqrt(2 / math.pi))
    return x + x * jnp.tanh(inner)


def spread_taps(k_ref, planes, taps_ref):
    for role, plane in enumerate(planes):
        for tap in range(9):
            row = k_ref[pl.ds(9 * plane + tap, 1), :]
            taps_ref[9 * role + tap] = jnp.broadcast_to(row, taps_ref.shape[1:]).astype(CONV)


def conv_rows(sources, taps_ref, lanes, count):
    sums = [[None] * 3 for _ in range(count)]
    for role, rows in sources:
        taps = [taps_ref[9 * role + i, :, lanes] for i in range(9)]
        for j, row in enumerate(rows):
            if row is None:
                continue
            depth, width = row.shape
            row = row.astype(CONV).reshape(depth // REPEAT, REPEAT, width)
            for out in range(max(0, j - 2), min(count, j + 1)):
                for c in range(3):
                    term = row * taps[3 * (j - out) + c]
                    sums[out][c] = term if sums[out][c] is None else sums[out][c] + term
    position = lax.broadcasted_iota(jnp.int32, (8, width), 0)
    results = []
    for out in range(count):
        before, here, after = (s.astype(F32).reshape(depth, width) for s in sums[out])
        before, after = pltpu.roll(before, 1, 0), pltpu.roll(after, depth - 1, 0)
        low = jnp.where(position == 0, 0.0, before[:8])
        high = jnp.where(position == 7, 0.0, after[depth - 8 :])
        before = jnp.concatenate([low, before[8:]], axis=0)
        after = jnp.concatenate([after[: depth - 8], high], axis=0)
        results.append(here + before + after)
    return results


def channel_blocks(channels):
    return [slice(i, i + BLOCK) for i in range(0, channels, BLOCK)]


def inner_row(ref, plane, y, lanes, inside=None):
    if inside is None:
        return ref[plane, y, :, lanes]
    row = ref[plane, jnp.clip(y, 0, ref.shape[1] - 1), :, lanes].astype(F32)
    return (row * jnp.where(inside, 1.0, 0.0)).astype(BF16)


def nt_dot(a, b):
    return lax.dot_general(a, b, (((1,), (1,)), ((), ())), preferred_element_type=F32)


def assign(hid, map_ref, mass_ref):
    cells = hid.shape[0]
    slices = map_ref.shape[0] - TILE
    raw = nt_dot(map_ref[...], hid)
    soft = raw[slices : slices + 8]
    temperature = 0.25 + jnp.maximum(soft, 0.0) + jnp.log(1.0 + jnp.exp(-jnp.abs(soft)))
    scale = (1.0 / math.log(2.0)) / temperature
    raw = raw[:slices].reshape(slices // 8, 8, cells)
    top = jnp.max(jnp.max(raw, axis=0), axis=0, keepdims=True)
    powers = jnp.exp2((raw - top[None]) * scale[None])
    total = jnp.sum(jnp.sum(powers, axis=0), axis=0, keepdims=True)
    probs = (powers * (1.0 / total)[None]).reshape(slices, cells)
    mass = probs[:, :LANES]
    for start in range(LANES, cells, LANES):
        mass = mass + probs[:, start : start + LANES]
    mass_ref[...] += mass
    return probs.astype(BF16)


def pack_kernel(me_ref, x_ref, rows_ref, me_out_ref, sem):
    plane = (x_ref.shape[0] - 1) * (me_ref[0] & 1)
    rows = pl.ds(0, rows_ref.shape[1])
    load = pltpu.make_async_copy(x_ref.at[pl.ds(plane, 1), rows], rows_ref, sem)
    load.start()
    me_out_ref[0] = me_ref[0]
    load.wait()


def pack_call(me, x, rows):
    _, _, depth, channels = x.shape
    return pl.pallas_call(
        pack_kernel,
        in_specs=[SMEM, HBM],
        out_specs=[VMEM, SMEM],
        out_shape=[
            jax.ShapeDtypeStruct((1, rows, depth, channels), BF16),
            jax.ShapeDtypeStruct((1,), jnp.int32),
        ],
        scratch_shapes=[pltpu.SemaphoreType.DMA],
        cost_estimate=pl.CostEstimate(flops=0, bytes_accessed=2**22, transcendentals=0),
        compiler_params=pltpu.CompilerParams(vmem_limit_bytes=60 * MIB + 400 * 2**10),
        name="pack",
    )(me, x)


def ends_kernel(bits, me_ref, x_ref, k_ref, affinity_ref, softness_ref, late_ref, near_ref, partial_ref,
                map_ref, taps_ref):
    planes, height, depth, channels = x_ref.shape
    slices = affinity_ref.shape[1]
    odd = me_ref[0] & 1

    late = late_ref.shape[1]

    def row(y, carry):
        near_ref[0, y] = x_ref[(planes - 1) * (1 - odd), y]
        return carry

    def late_row(y, carry):
        late_ref[0, y] = x_ref[(planes - 1) * odd, height - late + y]
        return carry

    lax.fori_loop(0, height, row, 0)
    lax.fori_loop(0, late, late_row, 0)
    spread_taps(k_ref, range(3), taps_ref)
    run = slices >> bits
    new = lax.broadcasted_iota(jnp.int32, (slices, 1), 0)
    old = lax.broadcasted_iota(jnp.int32, (slices, slices), 1)
    place = new & (run - 1)
    owner = reverse_lowest(new >> (run.bit_length() - 1), bits)
    order = (old == owner * run + place).astype(BF16)
    map_ref[:slices] = (0.5 * nt_dot(order, affinity_ref[...])).astype(BF16)
    softness = softness_ref[...].astype(BF16).astype(F32)
    map_ref[slices:] = jnp.broadcast_to(0.5 * softness, (TILE, channels)).astype(BF16)

    for which, known in enumerate((((1, 0), (2, 1)), ((0, planes - 2), (1, planes - 1)))):
        def put(y, lanes, rows, known=known, which=which):
            sources = [(role, [None if b is None else x_ref[p, y + b, :, lanes] for b in rows])
                       for role, p in known]
            totals = conv_rows(sources, taps_ref, lanes, len(rows) - 2)
            for i, total in enumerate(totals):
                start = (y + i) * depth
                start = start if isinstance(y, int) else pl.multiple_of(start, depth)
                partial_ref[which, pl.ds(start, depth), lanes] = total.astype(BF16)

        for lanes in channel_blocks(channels):
            put(0, lanes, (None, 0, 1))
            put(height - 1, lanes, (-1, 0, None))

        def pair(i, carry, put=put):
            for lanes in channel_blocks(channels):
                put(2 * i + 1, lanes, (-1, 0, 1, 2))
            return carry

        lax.fori_loop(0, (height - 2) // 2, pair, 0)


def ends_call(me, x, taps, affinity, softness, bits, late):
    planes, height, depth, channels = x.shape
    slices = affinity.shape[1]
    cells = height * depth
    return pl.pallas_call(
        functools.partial(ends_kernel, bits),
        in_specs=[SMEM] + [VMEM] * 4,
        out_specs=[VMEM] * 4,
        out_shape=[
            jax.ShapeDtypeStruct((1, late, depth, channels), BF16),
            jax.ShapeDtypeStruct((1, height, depth, channels), BF16),
            jax.ShapeDtypeStruct((2, cells, channels), BF16),
            jax.ShapeDtypeStruct((slices + TILE, channels), BF16),
        ],
        scratch_shapes=[pltpu.VMEM((27, REPEAT, channels), CONV)],
        cost_estimate=pl.CostEstimate(
            flops=cells * channels * 12000, bytes_accessed=8 * cells * channels, transcendentals=0
        ),
        compiler_params=pltpu.CompilerParams(vmem_limit_bytes=LIMIT),
        name="ends",
    )(me, x, taps, affinity, softness)


def reverse_lowest(value, bits):
    return ((value & ((1 << (bits - 1)) - 1)) << 1) | (value >> (bits - 1))


def inside_kernel(x_ref, k_ref, map_ref, probs_ref, sums_ref, mass_ref,
                  taps_ref, even_ref, odd_ref, hid_ref, by_slice_ref):
    planes, height, depth, channels = x_ref.shape
    spread_taps(k_ref, range(3), taps_ref)
    sums_ref[...] = jnp.zeros(sums_ref.shape, F32)
    mass_ref[...] = jnp.zeros(mass_ref.shape, F32)
    groups = height // GROUP
    cells = GROUP * depth

    def conv(t, hid_ref):
        plane, first = t // groups, lax.rem(t, groups) * GROUP
        for lanes in channel_blocks(channels):
            for j in range(0, GROUP, 2):
                sources = []
                for role in range(3):
                    rows = []
                    for b in (-1, 0, 1, 2):
                        y, ok = first + j + b, None
                        if j + b < 0:
                            ok = first > 0
                        elif j + b >= GROUP:
                            ok = first + GROUP < height
                        rows.append(inner_row(x_ref, plane + role, y, lanes, ok))
                    sources.append((role, rows))
                for i, total in enumerate(conv_rows(sources, taps_ref, lanes, 2)):
                    hid_ref[(j + i) * depth : (j + i + 1) * depth, lanes] = gelu(total).astype(BF16)

    def share(t, source_ref, at):
        hid = source_ref[...]
        by_slice = assign(hid, map_ref, mass_ref)
        start = pl.multiple_of(lax.rem(t, groups) * cells, cells)
        probs_ref[t // groups, pl.ds(start, cells), :] = by_slice.T
        hid_ref[at, :] = hid
        by_slice_ref[:, at] = by_slice

    count = (planes - 2) * groups
    conv(jnp.int32(0), even_ref)

    def two(s, carry):
        t = 2 * s
        share(t, even_ref, slice(0, cells))
        conv(t + 1, odd_ref)
        share(t + 1, odd_ref, slice(cells, 2 * cells))
        sums_ref[...] += dot(by_slice_ref[...], hid_ref[...])
        conv(jnp.minimum(t + 2, count - 1), even_ref)
        return carry

    lax.fori_loop(0, count // 2, two, 0)


def inside_call(x, taps, maps):
    planes, height, depth, channels = x.shape
    slices = maps.shape[0] - TILE
    cells = height * depth
    work = planes * cells * channels
    return pl.pallas_call(
        inside_kernel,
        in_specs=[VMEM] * 3,
        out_specs=[VMEM] * 3,
        out_shape=[
            jax.ShapeDtypeStruct((planes - 2, cells, slices), BF16),
            jax.ShapeDtypeStruct((slices, channels), F32),
            jax.ShapeDtypeStruct((slices, LANES), F32),
        ],
        scratch_shapes=[
            pltpu.VMEM((27, REPEAT, channels), CONV),
            pltpu.VMEM((GROUP * depth, channels), BF16),
            pltpu.VMEM((GROUP * depth, channels), BF16),
            pltpu.VMEM((2 * GROUP * depth, channels), BF16),
            pltpu.VMEM((slices, 2 * GROUP * depth), BF16),
        ],
        cost_estimate=pl.CostEstimate(
            flops=work * 7000, bytes_accessed=2 * work, transcendentals=2 * work
        ),
        compiler_params=pltpu.CompilerParams(vmem_limit_bytes=LIMIT),
        name="inside",
    )(x, taps, maps)


def edge_kernel(stage, me_ref, *refs):
    halos = 2 if stage == "late" else 1
    halo_refs, refs = refs[:halos], refs[halos:]
    partial_ref, k_ref, map_ref, sums_in_ref, mass_in_ref, probs_ref, *rest = refs
    if stage == "late":
        send_ref, keep_ref, *rest = rest
    sums_ref, mass_ref, taps_ref, hid_ref, scratch_ref = rest
    by_slice_ref = scratch_ref if stage == "near" else probs_ref
    depth, channels = halo_refs[0].shape[2:]
    height = partial_ref.shape[1] // depth
    slices = sums_in_ref.shape[0]
    odd = me_ref[0] & 1
    side = 1 - odd if stage == "near" else odd
    spread_taps(k_ref, [2 * side], taps_ref)
    mass_ref[...] = mass_in_ref[...]
    start = height // 2 if stage == "late" else 0
    stop = height // 2 if stage == "early" else height

    def halo(y, lanes):
        if not 0 <= y < height:
            return None
        for ref in halo_refs:
            if y < ref.shape[1]:
                return ref[0, y, :, lanes]
            y -= ref.shape[1]

    cells = GROUP * depth
    for first in range(start, stop, GROUP):
        group = slice((first - start) * depth, (first - start) * depth + cells)
        for lanes in channel_blocks(channels):
            for y in range(first, first + GROUP, 2):
                rows = [halo(y + b, lanes) for b in (-1, 0, 1, 2)]
                for i, total in enumerate(conv_rows([(0, rows)], taps_ref, lanes, 2)):
                    at = slice((y + i) * depth, (y + i + 1) * depth)
                    total = total + partial_ref[side, at, lanes].astype(F32)
                    at = slice((y + i - start) * depth, (y + i - start + 1) * depth)
                    hid_ref[at, lanes] = gelu(total).astype(BF16)
        by_slice = assign(hid_ref[group], map_ref, mass_ref)
        if stage == "near":
            probs_ref[0, group] = by_slice.T
        by_slice_ref[:, group] = by_slice
    sums_ref[...] = sums_in_ref[...] + dot(by_slice_ref[...], hid_ref[...])
    if stage != "late":
        return
    split_ref = scratch_ref
    mass = lax.dot_general(
        jnp.ones((8, LANES), F32), mass_ref[...], (((1,), (1,)), ((), ())),
        preferred_element_type=F32, precision=lax.Precision.HIGHEST,
    )
    split_ref[...] = split(mass)
    owners, rows, _ = send_ref.shape
    held = channels // LANES
    rows = (rows - 8) // held
    for ref, half in ((send_ref, 1 - odd), (keep_ref, odd)):
        start = pl.multiple_of(half * (slices // 2), slices // 2)
        for i in range(held):
            part = sums_ref[pl.ds(start, slices // 2), i * LANES : (i + 1) * LANES].astype(BF16)
            ref[:, i * rows : (i + 1) * rows, :] = part.reshape(owners, rows, LANES)
        for owner in range(owners):
            lane = pl.multiple_of(start + owner * rows // LANES * LANES, LANES)
            ref[owner, held * rows :, :] = split_ref[:, pl.ds(lane, LANES)].astype(BF16)


def split(mass):
    high = mass.astype(BF16).astype(F32)
    row = lax.broadcasted_iota(jnp.int32, mass.shape, mass.ndim - 2)
    return jnp.where(row == 0, high, jnp.where(row == 1, mass - high, 0.0))


def edge_call(stage, me, halos, taps, maps, partial, sums, mass, owners):
    channels = taps.shape[1]
    slices = sums.shape[0]
    cells = partial.shape[1] // (1 if stage == "near" else 2)
    carry = [(s.shape, F32) for s in (sums, mass)]
    scratch = [
        pltpu.VMEM((9, REPEAT, channels), CONV),
        pltpu.VMEM((cells, channels), BF16),
    ]
    outs = [((1, cells, slices) if stage == "near" else (slices, cells), BF16)]
    if stage == "late":
        rows = channels // LANES * (slices // owners) + 8
        outs += [((owners // 2, rows, LANES), BF16)] * 2
        scratch = [pltpu.VMEM(*c) for c in carry] + scratch
    else:
        outs += carry
    scratch += [pltpu.VMEM(*{
        "near": ((slices, cells), BF16), "early": ((8, LANES), F32), "late": ((8, slices), F32)
    }[stage])]
    return pl.pallas_call(
        functools.partial(edge_kernel, stage),
        in_specs=[SMEM] + [VMEM] * (len(halos) + 5),
        out_specs=[VMEM] * len(outs),
        out_shape=[jax.ShapeDtypeStruct(*o) for o in outs],
        scratch_shapes=scratch,
        cost_estimate=pl.CostEstimate(
            flops=cells * channels * 16000, bytes_accessed=4 * cells * channels,
            transcendentals=2 * cells * channels,
        ),
        compiler_params=pltpu.CompilerParams(vmem_limit_bytes=LIMIT),
        name=stage,
    )(me, *halos, partial, taps, maps, sums, mass)


def turn_kernel(early_ref, late_ref, probs_ref):
    cells = early_ref.shape[1]
    probs_ref[0, :cells] = early_ref[...].T
    probs_ref[0, cells:] = late_ref[...].T


def turn_call(early, late):
    slices, cells = early.shape
    return pl.pallas_call(
        turn_kernel,
        in_specs=[VMEM, VMEM],
        out_specs=VMEM,
        out_shape=jax.ShapeDtypeStruct((1, 2 * cells, slices), BF16),
        cost_estimate=pl.CostEstimate(flops=0, bytes_accessed=8 * cells * slices, transcendentals=0),
        compiler_params=pltpu.CompilerParams(vmem_limit_bytes=LIMIT),
        name="turn",
    )(early, late)


def merge_kernel(keep_ref, other_ref, out_ref):
    both = keep_ref[...].astype(F32) + other_ref[...].astype(F32)
    rows = both.shape[1] - 8
    tail = both[:, rows:]
    out_ref[:, :rows] = both[:, :rows].astype(BF16)
    out_ref[:, rows:] = split(jnp.broadcast_to(tail[:, 0:1] + tail[:, 1:2], tail.shape)).astype(BF16)


def merge_call(keep, other):
    return pl.pallas_call(
        merge_kernel,
        in_specs=[VMEM, VMEM],
        out_specs=VMEM,
        out_shape=jax.ShapeDtypeStruct(keep.shape, BF16),
        compiler_params=pltpu.CompilerParams(vmem_limit_bytes=LIMIT),
        name="merge",
    )(keep, other)


def owner_kernel(share, me_ref, parts_ref, gain_ref, content_ref, widening_ref,
                 narrowing_ref, final_ref, out_ref, mapped_ref):
    channels = content_ref.shape[0]
    held = channels // LANES
    rows = out_ref.shape[0]
    total = jnp.sum(parts_ref[...].astype(F32), axis=0)
    pooled = jnp.concatenate([total[i * rows : (i + 1) * rows] for i in range(held)], axis=1)
    mass = total[held * rows : held * rows + 1] + total[held * rows + 1 : held * rows + 2]
    lane = lax.broadcasted_iota(jnp.int32, (rows, LANES), 1)
    row = lax.broadcasted_iota(jnp.int32, (rows, LANES), 0)
    first = ((me_ref[0] >> 1) // share * rows) & (LANES - 1)
    mass = jnp.sum(jnp.where(lane == row + first, mass, 0.0), axis=1, keepdims=True)
    pooled = 0.5 * pooled / (mass + epsilon)
    high = pooled.astype(BF16)
    low = (pooled - high.astype(F32)).astype(BF16)
    tokens = dot(high, content_ref[...]) + dot(low, content_ref[...])
    center = jnp.mean(tokens, axis=-1, keepdims=True)
    spread = jnp.mean((tokens - center) ** 2, axis=-1, keepdims=True)
    normed = ((tokens - center) * (1.0 / jnp.sqrt(spread + epsilon)) * gain_ref[...]).astype(BF16)
    inner = (0.5 * gelu(dot(normed, widening_ref[...]))).astype(BF16)
    out = (tokens + dot(inner, narrowing_ref[...])).astype(BF16)
    out_ref[...] = out
    mapped = dot(out, final_ref[...]).astype(BF16)
    mapped_ref[...] = jnp.broadcast_to(mapped[None], mapped_ref.shape)


def owner_call(share, me, parts, gain, *weights):
    channels = weights[0].shape[0]
    owners = parts.shape[0]
    rows = (parts.shape[1] - 8) // (channels // LANES)
    return pl.pallas_call(
        functools.partial(owner_kernel, share),
        in_specs=[SMEM] + [VMEM] * 6,
        out_specs=[VMEM, VMEM],
        out_shape=[
            jax.ShapeDtypeStruct((rows, channels), BF16),
            jax.ShapeDtypeStruct((owners, rows, channels), BF16),
        ],
        compiler_params=pltpu.CompilerParams(vmem_limit_bytes=LIMIT),
        name="owner",
    )(me, parts, gain, *weights)


def update_kernel(me_ref, x_ref, inside_ref, near_ref, far_ref, own_ref, other_ref, out_ref,
                  done_ref, mapped_ref, sem):
    planes, cells, channels = x_ref.shape
    half = own_ref.shape[0]
    rows = cells
    pieces = cells // rows
    odd = me_ref[0] & 1
    mapped_ref[pl.ds(pl.multiple_of(odd * half, half), half)] = own_ref[...]
    mapped_ref[pl.ds(pl.multiple_of((1 - odd) * half, half), half)] = other_ref[...]

    def place(i):
        return pl.ds(pl.multiple_of(lax.rem(i, pieces) * rows, rows), rows)

    def store(plane, i):
        at = place(i)
        index = plane * pieces + lax.rem(i, pieces)
        return pltpu.make_async_copy(done_ref.at[plane, at], out_ref.at[plane, at], sem.at[index])

    for probs_ref, base in (
        (inside_ref, 1), (near_ref, (planes - 1) * (1 - odd)), (far_ref, (planes - 1) * odd)
    ):
        def step(i, carry, probs_ref=probs_ref, base=base):
            part, at = i // pieces, place(i)
            change = dot(probs_ref[part, at, :], mapped_ref[...])
            done_ref[base + part, at, :] = (x_ref[base + part, at, :].astype(F32) + change).astype(BF16)
            store(base + part, i).start()
            return carry

        lax.fori_loop(0, probs_ref.shape[0] * pieces, step, 0)

    def finish(i, carry):
        store(i // pieces, i).wait()
        return carry

    lax.fori_loop(0, planes * pieces, finish, 0)


def update_call(me, x, inside, near, far, own, other):
    planes, cells, channels = x.shape
    return pl.pallas_call(
        update_kernel,
        in_specs=[SMEM] + [VMEM] * 6,
        out_specs=HBM,
        out_shape=jax.ShapeDtypeStruct(x.shape, BF16),
        scratch_shapes=[
            pltpu.VMEM(x.shape, BF16),
            pltpu.VMEM((2 * own.shape[0], channels), BF16),
            pltpu.SemaphoreType.DMA((planes,)),
        ],
        compiler_params=pltpu.CompilerParams(vmem_limit_bytes=LIMIT),
        name="update",
    )(me, x, inside, near, far, own, other)


def per_device(
    mesh_feature_array,
    stencil_coefficients,
    partition_affinity_matrix,
    softness_mapping_matrix,
    content_mapping_matrix,
    layernorm_multiplier,
    widening_matrix,
    narrowing_matrix,
    final_mapping_matrix,
):
    x = mesh_feature_array
    planes, height, depth, channels = x.shape
    slices = partition_affinity_matrix.shape[1]
    n = lax.axis_size("gx")
    me = lax.axis_index("gx").astype(jnp.int32)[None]
    far_pairs = [p for i in range(1, n - 1, 2) for p in ((i, i + 1), (i + 1, i))]
    near_pairs = [p for i in range(0, n, 2) for p in ((i, i + 1), (i + 1, i))]
    first = height // 2 + 1
    rows, me = pack_call(me, x, first)
    early_halo = lax.ppermute(rows, "gx", far_pairs)

    owners = min(n // 2, slices // 2 // TILE)
    share = n // 2 // owners
    groups = [[2 * (share * j + s) + h for j in range(owners)] for h in range(2) for s in range(share)]
    taps = stencil_coefficients
    late_rows, near_plane, partial, maps = ends_call(
        me, x, taps, partition_affinity_matrix, softness_mapping_matrix[None],
        n.bit_length() - 1, height - first,
    )
    late_halo = lax.ppermute(late_rows, "gx", far_pairs)
    near_halo = lax.ppermute(near_plane, "gx", near_pairs)
    inside_probs, sums, mass = inside_call(x, taps, maps)
    fixed = (taps, maps, partial)
    near_probs, sums, mass = edge_call("near", me, (near_halo,), *fixed, sums, mass, 2 * owners)
    early, sums, mass = edge_call("early", me, (early_halo,), *fixed, sums, mass, 2 * owners)
    late, send, keep = edge_call(
        "late", me, (early_halo, late_halo), *fixed, sums, mass, 2 * owners
    )

    received = lax.ppermute(send, "gx", near_pairs)
    far_probs = turn_call(early, late)
    parts = merge_call(keep, received)
    parts = lax.all_to_all(parts, "gx", 0, 0, axis_index_groups=groups)
    if share > 1:
        sharers = [[2 * (share * j + s) + h for s in range(share)]
                   for h in range(2) for j in range(owners)]
        parts = lax.psum(parts, "gx", axis_index_groups=sharers)
    own_out, mapped = owner_call(
        share, me, parts, layernorm_multiplier[None],
        content_mapping_matrix, widening_matrix, narrowing_matrix, final_mapping_matrix,
    )
    if share > 1:
        place = lax.rem(me[0] // 2, share) * (slices // n)
        own_out = lax.dynamic_slice_in_dim(own_out, place, slices // n)
    mapped = lax.all_to_all(mapped, "gx", 0, 0, axis_index_groups=groups).reshape(slices // 2, channels)
    updated = update_call(
        me, x.reshape(planes, height * depth, channels), inside_probs, near_probs, far_probs,
        mapped, lax.ppermute(mapped, "gx", near_pairs),
    )
    return updated.reshape(x.shape), own_out


def solution(mesh):
    return jax.shard_map(
        per_device,
        mesh=mesh,
        in_specs=(P(("grp", "gx"), None, None, None), P(), P(), P(), P(), P(), P(), P(), P()),
        out_specs=(P(("grp", "gx"), None, None, None), P(("grp", "gx"), None)),
        check_vma=False,
    )
```

```python
import functools
import math

import jax
import jax.numpy as jnp
from jax import lax
from jax.experimental import pallas as pl
from jax.experimental.pallas import tpu as pltpu
from jax.sharding import PartitionSpec as P

epsilon = 1e-05
LANES = 128
BLOCK = 256
GROUP = 8
TILE = 16
REPEAT = 8
MIB = 2**20
LIMIT = 32 * MIB
F32, BF16 = jnp.float32, jnp.bfloat16
CONV = BF16
VMEM = pl.BlockSpec(memory_space=pltpu.VMEM)
SMEM = pl.BlockSpec(memory_space=pltpu.SMEM)
HBM = pl.BlockSpec(memory_space=pltpu.HBM)


def dot(a, b):
    return jnp.dot(a, b, preferred_element_type=F32)


def gelu(x):
    inner = x * (x * x * (0.044715 * math.sqrt(2 / math.pi)) + math.sqrt(2 / math.pi))
    return x + x * jnp.tanh(inner)


def spread_taps(k_ref, planes, taps_ref):
    for role, plane in enumerate(planes):
        for tap in range(9):
            row = k_ref[pl.ds(9 * plane + tap, 1), :]
            taps_ref[9 * role + tap] = jnp.broadcast_to(row, taps_ref.shape[1:]).astype(CONV)


def conv_rows(sources, taps_ref, lanes, count, known=()):
    sums = [[None] * 3 for _ in range(count)]
    for role, rows in sources:
        taps = [taps_ref[9 * role + i, :, lanes] for i in range(9)]
        for j, row in enumerate(rows):
            if row is None:
                continue
            depth, width = row.shape
            row = row.astype(CONV).reshape(depth // REPEAT, REPEAT, width)
            for out in range(max(0, j - 2), min(count, j + 1)):
                for c in range(3):
                    term = row * taps[3 * (j - out) + c]
                    sums[out][c] = term if sums[out][c] is None else sums[out][c] + term
    for out, row in enumerate(known):
        sums[out][1] = sums[out][1] + row.astype(CONV).reshape(sums[out][1].shape)
    position = lax.broadcasted_iota(jnp.int32, (8, width), 0)
    results = []
    for out in range(count):
        before, here, after = (s.astype(F32).reshape(depth, width) for s in sums[out])
        before, after = pltpu.roll(before, 1, 0), pltpu.roll(after, depth - 1, 0)
        low = jnp.where(position == 0, 0.0, before[:8])
        high = jnp.where(position == 7, 0.0, after[depth - 8 :])
        before = jnp.concatenate([low, before[8:]], axis=0)
        after = jnp.concatenate([after[: depth - 8], high], axis=0)
        results.append(here + before + after)
    return results


def channel_blocks(channels):
    return [slice(i, i + BLOCK) for i in range(0, channels, BLOCK)]


def inner_row(ref, plane, y, lanes, inside=None):
    if inside is None:
        return ref[plane, y, :, lanes]
    row = ref[plane, jnp.clip(y, 0, ref.shape[1] - 1), :, lanes].astype(F32)
    return (row * jnp.where(inside, 1.0, 0.0)).astype(BF16)


def nt_dot(a, b):
    return lax.dot_general(a, b, (((1,), (1,)), ((), ())), preferred_element_type=F32)


def assign(hid, map_ref, mass_ref):
    cells = hid.shape[0]
    slices = map_ref.shape[0] - TILE
    raw = nt_dot(map_ref[...], hid)
    soft = raw[slices : slices + 8]
    temperature = 0.25 + jnp.maximum(soft, 0.0) + jnp.log(1.0 + jnp.exp(-jnp.abs(soft)))
    scale = (1.0 / math.log(2.0)) / temperature
    raw = raw[:slices].reshape(slices // 8, 8, cells)
    top = jnp.max(jnp.max(raw, axis=0), axis=0, keepdims=True)
    powers = jnp.exp2((raw - top[None]) * scale[None])
    total = jnp.sum(jnp.sum(powers, axis=0), axis=0, keepdims=True)
    probs = (powers * (1.0 / total)[None]).reshape(slices, cells)
    mass = probs[:, :LANES]
    for start in range(LANES, cells, LANES):
        mass = mass + probs[:, start : start + LANES]
    mass_ref[...] += mass
    return probs.astype(BF16)


def pack_kernel(me_ref, x_ref, far_ref):
    planes, height = x_ref.shape[:2]

    def row(y, carry):
        far_ref[0, y] = x_ref[(planes - 1) * (me_ref[0] & 1), y]
        return carry

    lax.fori_loop(0, height, row, 0)


def pack_call(me, x):
    return pl.pallas_call(
        pack_kernel,
        in_specs=[SMEM, VMEM],
        out_specs=VMEM,
        out_shape=jax.ShapeDtypeStruct((1, *x.shape[1:]), BF16),
        cost_estimate=pl.CostEstimate(flops=0, bytes_accessed=2**22, transcendentals=0),
        compiler_params=pltpu.CompilerParams(vmem_limit_bytes=LIMIT),
        name="pack",
    )(me, x)


def ends_kernel(bits, me_ref, _, x_ref, k_ref, affinity_ref, softness_ref, near_ref, partial_ref, map_ref,
                taps_ref):
    planes, height, depth, channels = x_ref.shape
    slices = affinity_ref.shape[1]
    odd = me_ref[0] & 1

    def row(y, carry):
        near_ref[0, y] = x_ref[(planes - 1) * (1 - odd), y]
        return carry

    lax.fori_loop(0, height, row, 0)
    spread_taps(k_ref, range(3), taps_ref)
    run = slices >> bits
    new = lax.broadcasted_iota(jnp.int32, (slices, 1), 0)
    old = lax.broadcasted_iota(jnp.int32, (slices, slices), 1)
    place = new & (run - 1)
    owner = reverse_lowest(new >> (run.bit_length() - 1), bits)
    order = (old == owner * run + place).astype(BF16)
    map_ref[:slices] = (0.5 * nt_dot(order, affinity_ref[...])).astype(BF16)
    softness = softness_ref[...].astype(BF16).astype(F32)
    map_ref[slices:] = jnp.broadcast_to(0.5 * softness, (TILE, channels)).astype(BF16)

    for which, known in enumerate((((1, 0), (2, 1)), ((0, planes - 2), (1, planes - 1)))):
        def put(y, lanes, rows, known=known, which=which):
            sources = [(role, [None if b is None else x_ref[p, y + b, :, lanes] for b in rows])
                       for role, p in known]
            totals = conv_rows(sources, taps_ref, lanes, len(rows) - 2)
            for i, total in enumerate(totals):
                start = (y + i) * depth
                start = start if isinstance(y, int) else pl.multiple_of(start, depth)
                partial_ref[which, pl.ds(start, depth), lanes] = total.astype(BF16)

        for lanes in channel_blocks(channels):
            put(0, lanes, (None, 0, 1))
            put(height - 1, lanes, (-1, 0, None))

        def pair(i, carry, put=put):
            for lanes in channel_blocks(channels):
                put(2 * i + 1, lanes, (-1, 0, 1, 2))
            return carry

        lax.fori_loop(0, (height - 2) // 2, pair, 0)


def ends_call(me, after, x, taps, affinity, softness, bits):
    planes, height, depth, channels = x.shape
    slices = affinity.shape[1]
    cells = height * depth
    return pl.pallas_call(
        functools.partial(ends_kernel, bits),
        in_specs=[SMEM, pl.BlockSpec(memory_space=pl.ANY)] + [VMEM] * 4,
        out_specs=[VMEM] * 3,
        out_shape=[
            jax.ShapeDtypeStruct((1, height, depth, channels), BF16),
            jax.ShapeDtypeStruct((2, cells, channels), BF16),
            jax.ShapeDtypeStruct((slices + TILE, channels), BF16),
        ],
        scratch_shapes=[pltpu.VMEM((27, REPEAT, channels), CONV)],
        cost_estimate=pl.CostEstimate(
            flops=cells * channels * 12000, bytes_accessed=8 * cells * channels, transcendentals=0
        ),
        compiler_params=pltpu.CompilerParams(vmem_limit_bytes=LIMIT),
        name="ends",
    )(me, after, x, taps, affinity, softness)


def reverse_lowest(value, bits):
    return ((value & ((1 << (bits - 1)) - 1)) << 1) | (value >> (bits - 1))


def inside_kernel(x_ref, k_ref, map_ref, probs_ref, sums_ref, mass_ref,
                  taps_ref, even_ref, odd_ref, hid_ref, by_slice_ref):
    planes, height, depth, channels = x_ref.shape
    spread_taps(k_ref, range(3), taps_ref)
    sums_ref[...] = jnp.zeros(sums_ref.shape, F32)
    mass_ref[...] = jnp.zeros(mass_ref.shape, F32)
    groups = height // GROUP
    cells = GROUP * depth

    def conv(t, hid_ref):
        plane, first = t // groups, lax.rem(t, groups) * GROUP
        for lanes in channel_blocks(channels):
            for j in range(0, GROUP, 2):
                sources = []
                for role in range(3):
                    rows = []
                    for b in (-1, 0, 1, 2):
                        y, ok = first + j + b, None
                        if j + b < 0:
                            ok = first > 0
                        elif j + b >= GROUP:
                            ok = first + GROUP < height
                        rows.append(inner_row(x_ref, plane + role, y, lanes, ok))
                    sources.append((role, rows))
                for i, total in enumerate(conv_rows(sources, taps_ref, lanes, 2)):
                    hid_ref[(j + i) * depth : (j + i + 1) * depth, lanes] = gelu(total).astype(BF16)

    def share(t, source_ref, at):
        hid = source_ref[...]
        by_slice = assign(hid, map_ref, mass_ref)
        start = pl.multiple_of(lax.rem(t, groups) * cells, cells)
        probs_ref[t // groups, pl.ds(start, cells), :] = by_slice.T
        hid_ref[at, :] = hid
        by_slice_ref[:, at] = by_slice

    count = (planes - 2) * groups
    conv(jnp.int32(0), even_ref)

    def two(s, carry):
        t = 2 * s
        share(t, even_ref, slice(0, cells))
        conv(t + 1, odd_ref)
        share(t + 1, odd_ref, slice(cells, 2 * cells))
        sums_ref[...] += dot(by_slice_ref[...], hid_ref[...])
        conv(jnp.minimum(t + 2, count - 1), even_ref)
        return carry

    lax.fori_loop(0, count // 2, two, 0)


def inside_call(x, taps, maps):
    planes, height, depth, channels = x.shape
    slices = maps.shape[0] - TILE
    cells = height * depth
    work = planes * cells * channels
    return pl.pallas_call(
        inside_kernel,
        in_specs=[VMEM] * 3,
        out_specs=[VMEM] * 3,
        out_shape=[
            jax.ShapeDtypeStruct((planes - 2, cells, slices), BF16),
            jax.ShapeDtypeStruct((slices, channels), F32),
            jax.ShapeDtypeStruct((slices, LANES), F32),
        ],
        scratch_shapes=[
            pltpu.VMEM((27, REPEAT, channels), CONV),
            pltpu.VMEM((GROUP * depth, channels), BF16),
            pltpu.VMEM((GROUP * depth, channels), BF16),
            pltpu.VMEM((2 * GROUP * depth, channels), BF16),
            pltpu.VMEM((slices, 2 * GROUP * depth), BF16),
        ],
        cost_estimate=pl.CostEstimate(
            flops=work * 7000, bytes_accessed=2 * work, transcendentals=2 * work
        ),
        compiler_params=pltpu.CompilerParams(vmem_limit_bytes=LIMIT),
        name="inside",
    )(x, taps, maps)


def edge_kernel(is_far, me_ref, halo_ref, partial_ref, k_ref, map_ref, sums_in_ref, mass_in_ref, *rest):
    if is_far:
        by_slice_ref, send_ref, sums_ref, hid_ref, split_ref, taps_ref, mass_ref = rest
    else:
        probs_ref, sums_ref, mass_ref, taps_ref, hid_ref, by_slice_ref = rest
    _, height, depth, channels = halo_ref.shape
    slices = sums_in_ref.shape[0]
    odd = me_ref[0] & 1
    side = odd if is_far else 1 - odd
    spread_taps(k_ref, [2 * side], taps_ref)
    mass_ref[...] = mass_in_ref[...]
    cells = GROUP * depth
    half = height * depth // 2
    for first in range(0, height, GROUP):
        group = slice(first * depth, first * depth + cells)
        for lanes in channel_blocks(channels):
            for y in range(first, first + GROUP, 2):
                rows = [halo_ref[0, y + b, :, lanes] if 0 <= y + b < height else None
                        for b in (-1, 0, 1, 2)]
                ats = [slice((y + i) * depth, (y + i + 1) * depth) for i in range(2)]
                known = [partial_ref[side, at, lanes] for at in ats]
                for at, total in zip(ats, conv_rows([(0, rows)], taps_ref, lanes, 2, known)):
                    hid_ref[at, lanes] = gelu(total).astype(BF16)
        by_slice = assign(hid_ref[group], map_ref, mass_ref)
        if not is_far:
            probs_ref[0, group] = by_slice.T
        by_slice_ref[:, group] = by_slice
        if group.stop == half:
            sums_ref[...] = sums_in_ref[...] + dot(by_slice_ref[:, :half], hid_ref[:half])
    if not is_far:
        sums_ref[...] += dot(by_slice_ref[:, half:], hid_ref[half:])
        return
    mass = lax.dot_general(
        jnp.ones((8, LANES), F32), mass_ref[...], (((1,), (1,)), ((), ())),
        preferred_element_type=F32, precision=lax.Precision.HIGHEST,
    )
    split_ref[...] = split(mass)
    write_share(1 - odd, by_slice_ref, hid_ref, sums_ref, split_ref, send_ref)


def write_share(side, by_slice_ref, hid_ref, sums_ref, split_ref, share_ref):
    slices, channels = sums_ref.shape
    half = hid_ref.shape[0] // 2
    owners, rows, _ = share_ref.shape
    held = channels // LANES
    rows = (rows - 8) // held
    start = pl.multiple_of(side * (slices // 2), slices // 2)
    mine = pl.ds(start, slices // 2)
    total = sums_ref[mine, :] + dot(by_slice_ref[mine, half:], hid_ref[half:])
    for i in range(held):
        part = total[:, i * LANES : (i + 1) * LANES].astype(share_ref.dtype)
        share_ref[:, i * rows : (i + 1) * rows, :] = part.reshape(owners, rows, LANES)
    for owner in range(owners):
        lane = pl.multiple_of(start + owner * rows // LANES * LANES, LANES)
        share_ref[owner, held * rows :, :] = split_ref[:, pl.ds(lane, LANES)].astype(share_ref.dtype)


def keep_kernel(me_ref, by_slice_ref, hid_ref, sums_ref, split_ref, keep_ref):
    write_share(me_ref[0] & 1, by_slice_ref, hid_ref, sums_ref, split_ref, keep_ref)


def keep_call(me, by_slice, hid, sums, split_mass, shape):
    return pl.pallas_call(
        keep_kernel,
        in_specs=[SMEM] + [VMEM] * 4,
        out_specs=VMEM,
        out_shape=jax.ShapeDtypeStruct(shape, F32),
        cost_estimate=pl.CostEstimate(flops=2**28, bytes_accessed=2**21, transcendentals=0),
        compiler_params=pltpu.CompilerParams(vmem_limit_bytes=LIMIT),
        name="keep",
    )(me, by_slice, hid, sums, split_mass)


def split(mass):
    high = mass.astype(BF16).astype(F32)
    row = lax.broadcasted_iota(jnp.int32, mass.shape, mass.ndim - 2)
    return jnp.where(row == 0, high, jnp.where(row == 1, mass - high, 0.0))


def edge_call(is_far, me, halo, taps, maps, partial, sums, mass, owners):
    _, height, depth, channels = halo.shape
    slices = sums.shape[0]
    cells = height * depth
    hidden, by_slice = ((cells, channels), BF16), ((slices, cells), BF16)
    carry = [(s.shape, F32) for s in (sums, mass)]
    scratch = [((9, REPEAT, channels), CONV)]
    if is_far:
        rows = channels // LANES * (slices // owners) + 8
        outs = [by_slice, ((owners // 2, rows, LANES), BF16), carry[0], hidden, ((8, slices), F32)]
        scratch += [carry[1]]
    else:
        outs = [((1, cells, slices), BF16)] + carry
        scratch += [hidden, by_slice]
    return pl.pallas_call(
        functools.partial(edge_kernel, is_far),
        in_specs=[SMEM] + [VMEM] * 6,
        out_specs=[VMEM] * len(outs),
        out_shape=[jax.ShapeDtypeStruct(*o) for o in outs],
        scratch_shapes=[pltpu.VMEM(*o) for o in scratch],
        cost_estimate=pl.CostEstimate(
            flops=cells * channels * 16000, bytes_accessed=4 * cells * channels,
            transcendentals=2 * cells * channels,
        ),
        compiler_params=pltpu.CompilerParams(vmem_limit_bytes=LIMIT),
        name="far" if is_far else "near",
    )(me, halo, partial, taps, maps, sums, mass)


def turn_kernel(by_slice_ref, probs_ref):
    probs_ref[0] = by_slice_ref[...].T


def turn_call(by_slice):
    slices, cells = by_slice.shape
    return pl.pallas_call(
        turn_kernel,
        in_specs=[VMEM],
        out_specs=VMEM,
        out_shape=jax.ShapeDtypeStruct((1, cells, slices), BF16),
        cost_estimate=pl.CostEstimate(flops=0, bytes_accessed=4 * cells * slices, transcendentals=0),
        compiler_params=pltpu.CompilerParams(vmem_limit_bytes=LIMIT),
        name="turn",
    )(by_slice)


def merge_kernel(keep_ref, other_ref, out_ref):
    both = keep_ref[...] + other_ref[...].astype(F32)
    rows = both.shape[1] - 8
    tail = both[:, rows:]
    out_ref[:, :rows] = both[:, :rows].astype(BF16)
    out_ref[:, rows:] = split(jnp.broadcast_to(tail[:, 0:1] + tail[:, 1:2], tail.shape)).astype(BF16)


def merge_call(keep, other):
    return pl.pallas_call(
        merge_kernel,
        in_specs=[VMEM, VMEM],
        out_specs=VMEM,
        out_shape=jax.ShapeDtypeStruct(keep.shape, BF16),
        compiler_params=pltpu.CompilerParams(vmem_limit_bytes=LIMIT),
        name="merge",
    )(keep, other)


def owner_kernel(share, me_ref, parts_ref, gain_ref, content_ref, widening_ref,
                 narrowing_ref, final_ref, out_ref, mapped_ref):
    channels = content_ref.shape[0]
    held = channels // LANES
    rows = out_ref.shape[0]
    total = jnp.sum(parts_ref[...].astype(F32), axis=0)
    pooled = jnp.concatenate([total[i * rows : (i + 1) * rows] for i in range(held)], axis=1)
    mass = total[held * rows : held * rows + 1] + total[held * rows + 1 : held * rows + 2]
    lane = lax.broadcasted_iota(jnp.int32, (rows, LANES), 1)
    row = lax.broadcasted_iota(jnp.int32, (rows, LANES), 0)
    first = ((me_ref[0] >> 1) // share * rows) & (LANES - 1)
    mass = jnp.sum(jnp.where(lane == row + first, mass, 0.0), axis=1, keepdims=True)
    pooled = 0.5 * pooled / (mass + epsilon)
    high = pooled.astype(BF16)
    low = (pooled - high.astype(F32)).astype(BF16)
    tokens = dot(jnp.concatenate([high, low], axis=0), content_ref[...])
    tokens = tokens[:rows] + tokens[rows:]
    center = jnp.mean(tokens, axis=-1, keepdims=True)
    spread = jnp.mean((tokens - center) ** 2, axis=-1, keepdims=True)
    normed = ((tokens - center) * (1.0 / jnp.sqrt(spread + epsilon)) * gain_ref[...]).astype(BF16)
    inner = (0.5 * gelu(dot(normed, widening_ref[...]))).astype(BF16)
    out = (tokens + dot(inner, narrowing_ref[...])).astype(BF16)
    out_ref[...] = out
    mapped = dot(out, final_ref[...]).astype(BF16)
    mapped_ref[...] = jnp.broadcast_to(mapped[None], mapped_ref.shape)


def owner_call(share, me, parts, gain, *weights):
    channels = weights[0].shape[0]
    owners = parts.shape[0]
    rows = (parts.shape[1] - 8) // (channels // LANES)
    return pl.pallas_call(
        functools.partial(owner_kernel, share),
        in_specs=[SMEM] + [VMEM] * 6,
        out_specs=[VMEM, VMEM],
        out_shape=[
            jax.ShapeDtypeStruct((rows, channels), BF16),
            jax.ShapeDtypeStruct((owners, rows, channels), BF16),
        ],
        compiler_params=pltpu.CompilerParams(vmem_limit_bytes=LIMIT),
        name="owner",
    )(me, parts, gain, *weights)


def update_kernel(me_ref, x_ref, inside_ref, near_ref, far_ref, own_ref, other_ref, out_ref,
                  done_ref, mapped_ref, sem):
    planes, cells, channels = x_ref.shape
    half = own_ref.shape[0]
    rows = cells
    pieces = cells // rows
    odd = me_ref[0] & 1
    mapped_ref[pl.ds(pl.multiple_of(odd * half, half), half)] = own_ref[...]
    mapped_ref[pl.ds(pl.multiple_of((1 - odd) * half, half), half)] = other_ref[...]

    def place(i):
        return pl.ds(pl.multiple_of(lax.rem(i, pieces) * rows, rows), rows)

    def store(plane, i):
        at = place(i)
        index = plane * pieces + lax.rem(i, pieces)
        return pltpu.make_async_copy(done_ref.at[plane, at], out_ref.at[plane, at], sem.at[index])

    for probs_ref, base in (
        (inside_ref, 1), (near_ref, (planes - 1) * (1 - odd)), (far_ref, (planes - 1) * odd)
    ):
        def step(i, carry, probs_ref=probs_ref, base=base):
            part, at = i // pieces, place(i)
            change = dot(probs_ref[part, at, :], mapped_ref[...])
            done_ref[base + part, at, :] = (x_ref[base + part, at, :].astype(F32) + change).astype(BF16)
            store(base + part, i).start()
            return carry

        lax.fori_loop(0, probs_ref.shape[0] * pieces, step, 0)

    def finish(i, carry):
        store(i // pieces, i).wait()
        return carry

    lax.fori_loop(0, planes * pieces, finish, 0)


def update_call(me, x, inside, near, far, own, other):
    planes, cells, channels = x.shape
    return pl.pallas_call(
        update_kernel,
        in_specs=[SMEM] + [VMEM] * 6,
        out_specs=HBM,
        out_shape=jax.ShapeDtypeStruct(x.shape, BF16),
        scratch_shapes=[
            pltpu.VMEM(x.shape, BF16),
            pltpu.VMEM((2 * own.shape[0], channels), BF16),
            pltpu.SemaphoreType.DMA((planes,)),
        ],
        compiler_params=pltpu.CompilerParams(vmem_limit_bytes=LIMIT),
        name="update",
    )(me, x, inside, near, far, own, other)


def per_device(
    mesh_feature_array,
    stencil_coefficients,
    partition_affinity_matrix,
    softness_mapping_matrix,
    content_mapping_matrix,
    layernorm_multiplier,
    widening_matrix,
    narrowing_matrix,
    final_mapping_matrix,
):
    x = mesh_feature_array
    planes, height, depth, channels = x.shape
    slices = partition_affinity_matrix.shape[1]
    n = lax.axis_size("gx")
    me = lax.axis_index("gx").astype(jnp.int32)[None]
    far_pairs = [p for i in range(1, n - 1, 2) for p in ((i, i + 1), (i + 1, i))]
    near_pairs = [p for i in range(0, n, 2) for p in ((i, i + 1), (i + 1, i))]
    far_plane = pack_call(me, x)
    far_halo = lax.ppermute(far_plane, "gx", far_pairs)

    owners = min(n // 2, slices // 2 // TILE)
    share = n // 2 // owners
    groups = [[2 * (share * j + s) + h for j in range(owners)] for h in range(2) for s in range(share)]
    taps = stencil_coefficients
    near_plane, partial, maps = ends_call(
        me, far_plane, x, taps, partition_affinity_matrix, softness_mapping_matrix[None],
        n.bit_length() - 1,
    )
    near_halo = lax.ppermute(near_plane, "gx", near_pairs)
    inside_probs, sums, mass = inside_call(x, taps, maps)
    near_probs, sums, mass = edge_call(
        False, me, near_halo, taps, maps, partial, sums, mass, 2 * owners
    )
    by_slice, send, sums, hid, split_mass = edge_call(
        True, me, far_halo, taps, maps, partial, sums, mass, 2 * owners
    )

    received = lax.ppermute(send, "gx", near_pairs)
    keep = keep_call(me, by_slice, hid, sums, split_mass, send.shape)
    far_probs = turn_call(by_slice)
    parts = merge_call(keep, received)
    parts = lax.all_to_all(parts, "gx", 0, 0, axis_index_groups=groups)
    if share > 1:
        sharers = [[2 * (share * j + s) + h for s in range(share)]
                   for h in range(2) for j in range(owners)]
        parts = lax.psum(parts, "gx", axis_index_groups=sharers)
    own_out, mapped = owner_call(
        share, me, parts, layernorm_multiplier[None],
        content_mapping_matrix, widening_matrix, narrowing_matrix, final_mapping_matrix,
    )
    if share > 1:
        place = lax.rem(me[0] // 2, share) * (slices // n)
        own_out = lax.dynamic_slice_in_dim(own_out, place, slices // n)
    mapped = lax.all_to_all(mapped, "gx", 0, 0, axis_index_groups=groups).reshape(slices // 2, channels)
    updated = update_call(
        me, x.reshape(planes, height * depth, channels), inside_probs, near_probs, far_probs,
        mapped, lax.ppermute(mapped, "gx", near_pairs),
    )
    return updated.reshape(x.shape), own_out


def solution(mesh):
    return jax.shard_map(
        per_device,
        mesh=mesh,
        in_specs=(P(("grp", "gx"), None, None, None), P(), P(), P(), P(), P(), P(), P(), P()),
        out_specs=(P(("grp", "gx"), None, None, None), P(("grp", "gx"), None)),
        check_vma=False,
    )
```

```python
import functools
import math

import jax
import jax.numpy as jnp
from jax import lax
from jax.experimental import pallas as pl
from jax.experimental.pallas import tpu as pltpu
from jax.sharding import PartitionSpec as P

epsilon = 1e-05
LANES = 128
BLOCK = 256
GROUP = 8
TILE = 16
REPEAT = 8
MIB = 2**20
LIMIT = 32 * MIB
F32, BF16 = jnp.float32, jnp.bfloat16
CONV = BF16
VMEM = pl.BlockSpec(memory_space=pltpu.VMEM)
SMEM = pl.BlockSpec(memory_space=pltpu.SMEM)
HBM = pl.BlockSpec(memory_space=pltpu.HBM)


def dot(a, b):
    return jnp.dot(a, b, preferred_element_type=F32)


def gelu(x):
    inner = x * (x * x * (0.044715 * math.sqrt(2 / math.pi)) + math.sqrt(2 / math.pi))
    return x + x * jnp.tanh(inner)


def spread_taps(k_ref, planes, taps_ref):
    for role, plane in enumerate(planes):
        for tap in range(9):
            row = k_ref[pl.ds(9 * plane + tap, 1), :]
            taps_ref[9 * role + tap] = jnp.broadcast_to(row, taps_ref.shape[1:]).astype(CONV)


def conv_rows(sources, taps_ref, lanes, count, known=()):
    sums = [[None] * 3 for _ in range(count)]
    for role, rows in sources:
        taps = [taps_ref[9 * role + i, :, lanes] for i in range(9)]
        for j, row in enumerate(rows):
            if row is None:
                continue
            depth, width = row.shape
            row = row.astype(CONV).reshape(depth // REPEAT, REPEAT, width)
            for out in range(max(0, j - 2), min(count, j + 1)):
                for c in range(3):
                    term = row * taps[3 * (j - out) + c]
                    sums[out][c] = term if sums[out][c] is None else sums[out][c] + term
    for out, row in enumerate(known):
        sums[out][1] = sums[out][1] + row.astype(CONV).reshape(sums[out][1].shape)
    position = lax.broadcasted_iota(jnp.int32, (8, width), 0)
    results = []
    for out in range(count):
        before, here, after = (s.astype(F32).reshape(depth, width) for s in sums[out])
        before, after = pltpu.roll(before, 1, 0), pltpu.roll(after, depth - 1, 0)
        low = jnp.where(position == 0, 0.0, before[:8])
        high = jnp.where(position == 7, 0.0, after[depth - 8 :])
        before = jnp.concatenate([low, before[8:]], axis=0)
        after = jnp.concatenate([after[: depth - 8], high], axis=0)
        results.append(here + before + after)
    return results


def channel_blocks(channels):
    return [slice(i, i + BLOCK) for i in range(0, channels, BLOCK)]


def inner_row(ref, plane, y, lanes, inside=None):
    if inside is None:
        return ref[plane, y, :, lanes]
    row = ref[plane, jnp.clip(y, 0, ref.shape[1] - 1), :, lanes].astype(F32)
    return (row * jnp.where(inside, 1.0, 0.0)).astype(BF16)


def nt_dot(a, b):
    return lax.dot_general(a, b, (((1,), (1,)), ((), ())), preferred_element_type=F32)


def assign(hid, map_ref, mass_ref):
    cells = hid.shape[0]
    slices = map_ref.shape[0] - TILE
    raw = nt_dot(map_ref[...], hid)
    soft = raw[slices : slices + 8]
    temperature = 0.25 + jnp.maximum(soft, 0.0) + jnp.log(1.0 + jnp.exp(-jnp.abs(soft)))
    scale = (1.0 / math.log(2.0)) / temperature
    raw = raw[:slices].reshape(slices // 8, 8, cells)
    top = jnp.max(jnp.max(raw, axis=0), axis=0, keepdims=True)
    powers = jnp.exp2((raw - top[None]) * scale[None])
    total = jnp.sum(jnp.sum(powers, axis=0), axis=0, keepdims=True)
    probs = (powers * (1.0 / total)[None]).reshape(slices, cells)
    mass = probs[:, :LANES]
    for start in range(LANES, cells, LANES):
        mass = mass + probs[:, start : start + LANES]
    mass_ref[...] += mass
    return probs.astype(BF16)


def pack_kernel(me_ref, x_ref, far_ref):
    planes, height = x_ref.shape[:2]

    def row(y, carry):
        far_ref[0, y] = x_ref[(planes - 1) * (me_ref[0] & 1), y]
        return carry

    lax.fori_loop(0, height, row, 0)


def pack_call(me, x):
    return pl.pallas_call(
        pack_kernel,
        in_specs=[SMEM, VMEM],
        out_specs=VMEM,
        out_shape=jax.ShapeDtypeStruct((1, *x.shape[1:]), BF16),
        cost_estimate=pl.CostEstimate(flops=0, bytes_accessed=2**22, transcendentals=0),
        compiler_params=pltpu.CompilerParams(vmem_limit_bytes=LIMIT),
        name="pack",
    )(me, x)


def ends_kernel(bits, me_ref, _, x_ref, k_ref, affinity_ref, softness_ref, near_ref, partial_ref, map_ref,
                taps_ref):
    planes, height, depth, channels = x_ref.shape
    slices = affinity_ref.shape[1]
    odd = me_ref[0] & 1

    def row(y, carry):
        near_ref[0, y] = x_ref[(planes - 1) * (1 - odd), y]
        return carry

    lax.fori_loop(0, height, row, 0)
    spread_taps(k_ref, range(3), taps_ref)
    run = slices >> bits
    new = lax.broadcasted_iota(jnp.int32, (slices, 1), 0)
    old = lax.broadcasted_iota(jnp.int32, (slices, slices), 1)
    place = new & (run - 1)
    owner = reverse_lowest(new >> (run.bit_length() - 1), bits)
    order = (old == owner * run + place).astype(BF16)
    map_ref[:slices] = (0.5 * nt_dot(order, affinity_ref[...])).astype(BF16)
    softness = softness_ref[...].astype(BF16).astype(F32)
    map_ref[slices:] = jnp.broadcast_to(0.5 * softness, (TILE, channels)).astype(BF16)

    for which, known in enumerate((((1, 0), (2, 1)), ((0, planes - 2), (1, planes - 1)))):
        def put(y, lanes, rows, known=known, which=which):
            sources = [(role, [None if b is None else x_ref[p, y + b, :, lanes] for b in rows])
                       for role, p in known]
            totals = conv_rows(sources, taps_ref, lanes, len(rows) - 2)
            for i, total in enumerate(totals):
                start = (y + i) * depth
                start = start if isinstance(y, int) else pl.multiple_of(start, depth)
                partial_ref[which, pl.ds(start, depth), lanes] = total.astype(BF16)

        for lanes in channel_blocks(channels):
            put(0, lanes, (None, 0, 1))
            put(height - 1, lanes, (-1, 0, None))

        def pair(i, carry, put=put):
            for lanes in channel_blocks(channels):
                put(2 * i + 1, lanes, (-1, 0, 1, 2))
            return carry

        lax.fori_loop(0, (height - 2) // 2, pair, 0)


def ends_call(me, after, x, taps, affinity, softness, bits):
    planes, height, depth, channels = x.shape
    slices = affinity.shape[1]
    cells = height * depth
    return pl.pallas_call(
        functools.partial(ends_kernel, bits),
        in_specs=[SMEM, pl.BlockSpec(memory_space=pl.ANY)] + [VMEM] * 4,
        out_specs=[VMEM] * 3,
        out_shape=[
            jax.ShapeDtypeStruct((1, height, depth, channels), BF16),
            jax.ShapeDtypeStruct((2, cells, channels), BF16),
            jax.ShapeDtypeStruct((slices + TILE, channels), BF16),
        ],
        scratch_shapes=[pltpu.VMEM((27, REPEAT, channels), CONV)],
        cost_estimate=pl.CostEstimate(
            flops=cells * channels * 12000, bytes_accessed=8 * cells * channels, transcendentals=0
        ),
        compiler_params=pltpu.CompilerParams(vmem_limit_bytes=LIMIT),
        name="ends",
    )(me, after, x, taps, affinity, softness)


def reverse_lowest(value, bits):
    return ((value & ((1 << (bits - 1)) - 1)) << 1) | (value >> (bits - 1))


def inside_kernel(x_ref, k_ref, map_ref, probs_ref, sums_ref, mass_ref,
                  taps_ref, even_ref, odd_ref, hid_ref, by_slice_ref):
    planes, height, depth, channels = x_ref.shape
    spread_taps(k_ref, range(3), taps_ref)
    sums_ref[...] = jnp.zeros(sums_ref.shape, F32)
    mass_ref[...] = jnp.zeros(mass_ref.shape, F32)
    groups = height // GROUP
    cells = GROUP * depth

    def conv(t, hid_ref):
        plane, first = t // groups, lax.rem(t, groups) * GROUP
        for lanes in channel_blocks(channels):
            for j in range(0, GROUP, 2):
                sources = []
                for role in range(3):
                    rows = []
                    for b in (-1, 0, 1, 2):
                        y, ok = first + j + b, None
                        if j + b < 0:
                            ok = first > 0
                        elif j + b >= GROUP:
                            ok = first + GROUP < height
                        rows.append(inner_row(x_ref, plane + role, y, lanes, ok))
                    sources.append((role, rows))
                for i, total in enumerate(conv_rows(sources, taps_ref, lanes, 2)):
                    hid_ref[(j + i) * depth : (j + i + 1) * depth, lanes] = gelu(total.astype(BF16))

    def share(t, source_ref, at):
        hid = source_ref[...]
        by_slice = assign(hid, map_ref, mass_ref)
        start = pl.multiple_of(lax.rem(t, groups) * cells, cells)
        probs_ref[t // groups, pl.ds(start, cells), :] = by_slice.T
        hid_ref[at, :] = hid
        by_slice_ref[:, at] = by_slice

    count = (planes - 2) * groups
    conv(jnp.int32(0), even_ref)

    def two(s, carry):
        t = 2 * s
        share(t, even_ref, slice(0, cells))
        conv(t + 1, odd_ref)
        share(t + 1, odd_ref, slice(cells, 2 * cells))
        sums_ref[...] += dot(by_slice_ref[...], hid_ref[...])
        conv(jnp.minimum(t + 2, count - 1), even_ref)
        return carry

    lax.fori_loop(0, count // 2, two, 0)


def inside_call(x, taps, maps):
    planes, height, depth, channels = x.shape
    slices = maps.shape[0] - TILE
    cells = height * depth
    work = planes * cells * channels
    return pl.pallas_call(
        inside_kernel,
        in_specs=[VMEM] * 3,
        out_specs=[VMEM] * 3,
        out_shape=[
            jax.ShapeDtypeStruct((planes - 2, cells, slices), BF16),
            jax.ShapeDtypeStruct((slices, channels), F32),
            jax.ShapeDtypeStruct((slices, LANES), F32),
        ],
        scratch_shapes=[
            pltpu.VMEM((27, REPEAT, channels), CONV),
            pltpu.VMEM((GROUP * depth, channels), BF16),
            pltpu.VMEM((GROUP * depth, channels), BF16),
            pltpu.VMEM((2 * GROUP * depth, channels), BF16),
            pltpu.VMEM((slices, 2 * GROUP * depth), BF16),
        ],
        cost_estimate=pl.CostEstimate(
            flops=work * 7000, bytes_accessed=2 * work, transcendentals=2 * work
        ),
        compiler_params=pltpu.CompilerParams(vmem_limit_bytes=LIMIT),
        name="inside",
    )(x, taps, maps)


def edge_kernel(is_far, me_ref, halo_ref, partial_ref, k_ref, map_ref, sums_in_ref, mass_in_ref, *rest):
    if is_far:
        by_slice_ref, send_ref, sums_ref, mass_ref, hid_ref, taps_ref = rest
    else:
        probs_ref, sums_ref, mass_ref, taps_ref, hid_ref, by_slice_ref = rest
    _, height, depth, channels = halo_ref.shape
    slices = sums_in_ref.shape[0]
    odd = me_ref[0] & 1
    side = odd if is_far else 1 - odd
    spread_taps(k_ref, [2 * side], taps_ref)
    mass_ref[...] = mass_in_ref[...]
    cells = GROUP * depth
    half = height * depth // 2
    for first in range(0, height, GROUP):
        group = slice(first * depth, first * depth + cells)
        for lanes in channel_blocks(channels):
            for y in range(first, first + GROUP, 2):
                rows = [halo_ref[0, y + b, :, lanes] if 0 <= y + b < height else None
                        for b in (-1, 0, 1, 2)]
                ats = [slice((y + i) * depth, (y + i + 1) * depth) for i in range(2)]
                known = [partial_ref[side, at, lanes] for at in ats]
                for at, total in zip(ats, conv_rows([(0, rows)], taps_ref, lanes, 2, known)):
                    hid_ref[at, lanes] = gelu(total.astype(BF16))
        by_slice = assign(hid_ref[group], map_ref, mass_ref)
        if not is_far:
            probs_ref[0, group] = by_slice.T
        by_slice_ref[:, group] = by_slice
        if group.stop == half:
            sums_ref[...] = sums_in_ref[...] + dot(by_slice_ref[:, :half], hid_ref[:half])
    if not is_far:
        sums_ref[...] += dot(by_slice_ref[:, half:], hid_ref[half:])
        return
    write_share(1 - odd, by_slice_ref, hid_ref, sums_ref, mass_ref, send_ref)


def write_share(side, by_slice_ref, hid_ref, sums_ref, mass_ref, share_ref):
    slices, channels = sums_ref.shape
    half = hid_ref.shape[0] // 2
    owners, rows, _ = share_ref.shape
    held = channels // LANES
    rows = (rows - 8) // held
    start = pl.multiple_of(side * (slices // 2), slices // 2)
    mine = pl.ds(start, slices // 2)
    total = sums_ref[mine, :] + dot(by_slice_ref[mine, half:], hid_ref[half:])
    for i in range(held):
        part = total[:, i * LANES : (i + 1) * LANES].astype(share_ref.dtype)
        share_ref[:, i * rows : (i + 1) * rows, :] = part.reshape(owners, rows, LANES)
    tiles = rows // 8
    lane = lax.broadcasted_iota(jnp.int32, (8, LANES), 1)
    mass = mass_ref[mine, :]
    for owner in range(owners):
        tail = None
        for g in range(tiles):
            tile = mass[owner * rows + 8 * g : owner * rows + 8 * (g + 1)]
            width = LANES
            while width > LANES // tiles:
                width //= 2
                tile = tile + pltpu.roll(tile, width, 1)
            tail = tile if tail is None else jnp.where(lane >= g * width, tile, tail)
        share_ref[owner, held * rows :, :] = tail.astype(share_ref.dtype)


def keep_kernel(me_ref, by_slice_ref, hid_ref, sums_ref, mass_ref, keep_ref, probs_ref):
    write_share(me_ref[0] & 1, by_slice_ref, hid_ref, sums_ref, mass_ref, keep_ref)
    probs_ref[0] = by_slice_ref[...].T


def keep_call(me, by_slice, hid, sums, mass, shape):
    slices, cells = by_slice.shape
    return pl.pallas_call(
        keep_kernel,
        in_specs=[SMEM] + [VMEM] * 4,
        out_specs=[VMEM, VMEM],
        out_shape=[jax.ShapeDtypeStruct(shape, F32), jax.ShapeDtypeStruct((1, cells, slices), BF16)],
        cost_estimate=pl.CostEstimate(flops=2**28, bytes_accessed=2**21, transcendentals=0),
        compiler_params=pltpu.CompilerParams(vmem_limit_bytes=LIMIT),
        name="keep",
    )(me, by_slice, hid, sums, mass)


def edge_call(is_far, me, halo, taps, maps, partial, sums, mass, owners):
    _, height, depth, channels = halo.shape
    slices = sums.shape[0]
    cells = height * depth
    hidden, by_slice = ((cells, channels), BF16), ((slices, cells), BF16)
    carry = [(s.shape, F32) for s in (sums, mass)]
    scratch = [((9, REPEAT, channels), CONV)]
    if is_far:
        rows = channels // LANES * (slices // owners) + 8
        outs = [by_slice, ((owners // 2, rows, LANES), BF16)] + carry + [hidden]
    else:
        outs = [((1, cells, slices), BF16)] + carry
        scratch += [hidden, by_slice]
    return pl.pallas_call(
        functools.partial(edge_kernel, is_far),
        in_specs=[SMEM] + [VMEM] * 6,
        out_specs=[VMEM] * len(outs),
        out_shape=[jax.ShapeDtypeStruct(*o) for o in outs],
        scratch_shapes=[pltpu.VMEM(*o) for o in scratch],
        cost_estimate=pl.CostEstimate(
            flops=cells * channels * 16000, bytes_accessed=4 * cells * channels,
            transcendentals=2 * cells * channels,
        ),
        compiler_params=pltpu.CompilerParams(vmem_limit_bytes=LIMIT),
        name="far" if is_far else "near",
    )(me, halo, partial, taps, maps, sums, mass)


def merge_kernel(keep_ref, other_ref, out_ref):
    out_ref[...] = (keep_ref[...] + other_ref[...].astype(F32)).astype(BF16)


def merge_call(keep, other):
    return pl.pallas_call(
        merge_kernel,
        in_specs=[VMEM, VMEM],
        out_specs=VMEM,
        out_shape=jax.ShapeDtypeStruct(keep.shape, BF16),
        compiler_params=pltpu.CompilerParams(vmem_limit_bytes=LIMIT),
        name="merge",
    )(keep, other)


def owner_kernel(parts_ref, gain_ref, content_ref, widening_ref,
                 narrowing_ref, final_ref, out_ref, mapped_ref):
    channels = content_ref.shape[0]
    held = channels // LANES
    rows = out_ref.shape[0]
    total = jnp.sum(parts_ref[...].astype(F32), axis=0)
    pooled = jnp.concatenate([total[i * rows : (i + 1) * rows] for i in range(held)], axis=1)
    tail = total[held * rows :]
    lane = lax.broadcasted_iota(jnp.int32, (8, LANES), 1)
    width = LANES // (rows // 8)
    mass = jnp.concatenate([
        jnp.sum(jnp.where((lane >= g) & (lane < g + width), tail, 0.0), axis=1, keepdims=True)
        for g in range(0, LANES, width)
    ], axis=0)
    pooled = 0.5 * pooled / (mass + epsilon)
    high = pooled.astype(BF16)
    low = (pooled - high.astype(F32)).astype(BF16)
    tokens = dot(jnp.concatenate([high, low], axis=0), content_ref[...])
    tokens = tokens[:rows] + tokens[rows:]
    center = jnp.mean(tokens, axis=-1, keepdims=True)
    spread = jnp.mean((tokens - center) ** 2, axis=-1, keepdims=True)
    normed = ((tokens - center) * (1.0 / jnp.sqrt(spread + epsilon)) * gain_ref[...]).astype(BF16)
    inner = (0.5 * gelu(dot(normed, widening_ref[...]))).astype(BF16)
    out = (tokens + dot(inner, narrowing_ref[...])).astype(BF16)
    out_ref[...] = out
    mapped = dot(out, final_ref[...]).astype(BF16)
    mapped_ref[...] = jnp.broadcast_to(mapped[None], mapped_ref.shape)


def owner_call(parts, gain, *weights):
    channels = weights[0].shape[0]
    owners = parts.shape[0]
    rows = (parts.shape[1] - 8) // (channels // LANES)
    return pl.pallas_call(
        owner_kernel,
        in_specs=[VMEM] * 6,
        out_specs=[VMEM, VMEM],
        out_shape=[
            jax.ShapeDtypeStruct((rows, channels), BF16),
            jax.ShapeDtypeStruct((owners, rows, channels), BF16),
        ],
        compiler_params=pltpu.CompilerParams(vmem_limit_bytes=LIMIT),
        name="owner",
    )(parts, gain, *weights)


def ahead_kernel(me_ref, x_ref, inside_ref, own_ref, out_ref):
    half = own_ref.shape[0]
    columns = pl.ds(pl.multiple_of((me_ref[0] & 1) * half, half), half)

    def step(i, carry):
        change = dot(inside_ref[i, :, columns], own_ref[...])
        out_ref[i] = x_ref[i + 1].astype(F32) + change
        return carry

    lax.fori_loop(0, inside_ref.shape[0], step, 0)


def ahead_call(me, x, inside, own):
    planes, cells, channels = x.shape
    return pl.pallas_call(
        ahead_kernel,
        in_specs=[SMEM] + [VMEM] * 3,
        out_specs=VMEM,
        out_shape=jax.ShapeDtypeStruct((planes - 2, cells, channels), F32),
        cost_estimate=pl.CostEstimate(flops=2**30, bytes_accessed=2**23, transcendentals=0),
        compiler_params=pltpu.CompilerParams(vmem_limit_bytes=LIMIT),
        name="ahead",
    )(me, x, inside, own)


def update_kernel(me_ref, x_ref, ahead_ref, inside_ref, near_ref, far_ref, own_ref, other_ref, out_ref,
                  done_ref, mapped_ref, sem):
    planes, cells, channels = x_ref.shape
    half = own_ref.shape[0]
    odd = me_ref[0] & 1
    mine = pl.ds(pl.multiple_of(odd * half, half), half)
    others = pl.ds(pl.multiple_of((1 - odd) * half, half), half)
    mapped_ref[mine] = own_ref[...]
    mapped_ref[others] = other_ref[...]

    def store(plane):
        return pltpu.make_async_copy(done_ref.at[plane], out_ref.at[plane], sem.at[plane])

    def step(i, carry):
        total = ahead_ref[i] + dot(inside_ref[i, :, others], other_ref[...])
        done_ref[i + 1] = total.astype(BF16)
        store(i + 1).start()
        return carry

    lax.fori_loop(0, planes - 2, step, 0)
    for probs_ref, plane in ((near_ref, (planes - 1) * (1 - odd)), (far_ref, (planes - 1) * odd)):
        change = dot(probs_ref[0], mapped_ref[...])
        done_ref[plane] = (x_ref[plane].astype(F32) + change).astype(BF16)
        store(plane).start()

    def finish(plane, carry):
        store(plane).wait()
        return carry

    lax.fori_loop(0, planes, finish, 0)


def update_call(me, x, ahead, inside, near, far, own, other):
    planes, cells, channels = x.shape
    return pl.pallas_call(
        update_kernel,
        in_specs=[SMEM] + [VMEM] * 7,
        out_specs=HBM,
        out_shape=jax.ShapeDtypeStruct(x.shape, BF16),
        scratch_shapes=[
            pltpu.VMEM(x.shape, BF16),
            pltpu.VMEM((2 * own.shape[0], channels), BF16),
            pltpu.SemaphoreType.DMA((planes,)),
        ],
        compiler_params=pltpu.CompilerParams(vmem_limit_bytes=LIMIT),
        name="update",
    )(me, x, ahead, inside, near, far, own, other)


def per_device(
    mesh_feature_array,
    stencil_coefficients,
    partition_affinity_matrix,
    softness_mapping_matrix,
    content_mapping_matrix,
    layernorm_multiplier,
    widening_matrix,
    narrowing_matrix,
    final_mapping_matrix,
):
    x = mesh_feature_array
    planes, height, depth, channels = x.shape
    slices = partition_affinity_matrix.shape[1]
    n = lax.axis_size("gx")
    me = lax.axis_index("gx").astype(jnp.int32)[None]
    far_pairs = [p for i in range(1, n - 1, 2) for p in ((i, i + 1), (i + 1, i))]
    near_pairs = [p for i in range(0, n, 2) for p in ((i, i + 1), (i + 1, i))]
    far_plane = pack_call(me, x)
    far_halo = lax.ppermute(far_plane, "gx", far_pairs)

    owners = min(n // 2, slices // 2 // TILE)
    share = n // 2 // owners
    groups = [[2 * (share * j + s) + h for j in range(owners)] for h in range(2) for s in range(share)]
    taps = stencil_coefficients
    near_plane, partial, maps = ends_call(
        me, far_plane, x, taps, partition_affinity_matrix, softness_mapping_matrix[None],
        n.bit_length() - 1,
    )
    near_halo = lax.ppermute(near_plane, "gx", near_pairs)
    inside_probs, sums, mass = inside_call(x, taps, maps)
    near_probs, sums, mass = edge_call(
        False, me, near_halo, taps, maps, partial, sums, mass, 2 * owners
    )
    by_slice, send, sums, mass, hid = edge_call(
        True, me, far_halo, taps, maps, partial, sums, mass, 2 * owners
    )

    received = lax.ppermute(send, "gx", near_pairs)
    keep, far_probs = keep_call(me, by_slice, hid, sums, mass, send.shape)
    parts = merge_call(keep, received)
    parts = lax.all_to_all(parts, "gx", 0, 0, axis_index_groups=groups)
    if share > 1:
        sharers = [[2 * (share * j + s) + h for s in range(share)]
                   for h in range(2) for j in range(owners)]
        parts = lax.psum(parts, "gx", axis_index_groups=sharers)
    own_out, mapped = owner_call(
        parts, layernorm_multiplier[None],
        content_mapping_matrix, widening_matrix, narrowing_matrix, final_mapping_matrix,
    )
    if share > 1:
        place = lax.rem(me[0] // 2, share) * (slices // n)
        own_out = lax.dynamic_slice_in_dim(own_out, place, slices // n)
    mapped = lax.all_to_all(mapped, "gx", 0, 0, axis_index_groups=groups).reshape(slices // 2, channels)
    other = lax.ppermute(mapped, "gx", near_pairs)
    planes_of_cells = x.reshape(planes, height * depth, channels)
    ahead = ahead_call(me, planes_of_cells, inside_probs, mapped)
    updated = update_call(
        me, planes_of_cells, ahead, inside_probs, near_probs, far_probs, mapped, other
    )
    return updated.reshape(x.shape), own_out


def solution(mesh):
    return jax.shard_map(
        per_device,
        mesh=mesh,
        in_specs=(P(("grp", "gx"), None, None, None), P(), P(), P(), P(), P(), P(), P(), P()),
        out_specs=(P(("grp", "gx"), None, None, None), P(("grp", "gx"), None)),
        check_vma=False,
    )
```

```python
import functools
import math

import jax
import jax.numpy as jnp
from jax import lax
from jax.experimental import pallas as pl
from jax.experimental.pallas import tpu as pltpu
from jax.sharding import PartitionSpec as P

epsilon = 1e-05
LANES = 128
BLOCK = 256
GROUP = 8
TILE = 16
REPEAT = 8
MIB = 2**20
LIMIT = 32 * MIB
F32, BF16 = jnp.float32, jnp.bfloat16
CONV = BF16
VMEM = pl.BlockSpec(memory_space=pltpu.VMEM)
SMEM = pl.BlockSpec(memory_space=pltpu.SMEM)
HBM = pl.BlockSpec(memory_space=pltpu.HBM)


def dot(a, b):
    return jnp.dot(a, b, preferred_element_type=F32)


def gelu(x):
    inner = x * (x * x * (0.044715 * math.sqrt(2 / math.pi)) + math.sqrt(2 / math.pi))
    return x + x * jnp.tanh(inner)


def spread_taps(k_ref, planes, taps_ref):
    for role, plane in enumerate(planes):
        for tap in range(9):
            row = k_ref[pl.ds(9 * plane + tap, 1), :]
            taps_ref[9 * role + tap] = jnp.broadcast_to(row, taps_ref.shape[1:]).astype(CONV)


def conv_rows(sources, taps_ref, lanes, count, known=()):
    sums = [[None] * 3 for _ in range(count)]
    for role, rows in sources:
        taps = [taps_ref[9 * role + i, :, lanes] for i in range(9)]
        for j, row in enumerate(rows):
            if row is None:
                continue
            depth, width = row.shape
            row = row.astype(CONV).reshape(depth // REPEAT, REPEAT, width)
            for out in range(max(0, j - 2), min(count, j + 1)):
                for c in range(3):
                    term = row * taps[3 * (j - out) + c]
                    sums[out][c] = term if sums[out][c] is None else sums[out][c] + term
    for out, row in enumerate(known):
        sums[out][1] = sums[out][1] + row.astype(CONV).reshape(sums[out][1].shape)
    position = lax.broadcasted_iota(jnp.int32, (8, width), 0)
    results = []
    for out in range(count):
        before, here, after = (s.astype(F32).reshape(depth, width) for s in sums[out])
        before, after = pltpu.roll(before, 1, 0), pltpu.roll(after, depth - 1, 0)
        low = jnp.where(position == 0, 0.0, before[:8])
        high = jnp.where(position == 7, 0.0, after[depth - 8 :])
        before = jnp.concatenate([low, before[8:]], axis=0)
        after = jnp.concatenate([after[: depth - 8], high], axis=0)
        results.append(here + before + after)
    return results


def channel_blocks(channels):
    return [slice(i, i + BLOCK) for i in range(0, channels, BLOCK)]


def inner_row(ref, plane, y, lanes, inside=None):
    if inside is None:
        return ref[plane, y, :, lanes]
    row = ref[plane, jnp.clip(y, 0, ref.shape[1] - 1), :, lanes].astype(F32)
    return (row * jnp.where(inside, 1.0, 0.0)).astype(BF16)


def nt_dot(a, b):
    return lax.dot_general(a, b, (((1,), (1,)), ((), ())), preferred_element_type=F32)


def assign(hid, map_ref, mass_ref):
    cells = hid.shape[0]
    slices = map_ref.shape[0] - TILE
    raw = nt_dot(map_ref[...], hid)
    soft = raw[slices : slices + 8]
    temperature = 0.25 + jnp.maximum(soft, 0.0) + jnp.log(1.0 + jnp.exp(-jnp.abs(soft)))
    scale = (1.0 / math.log(2.0)) / temperature
    raw = raw[:slices].reshape(slices // 8, 8, cells)
    top = jnp.max(jnp.max(raw, axis=0), axis=0, keepdims=True)
    powers = jnp.exp2((raw - top[None]) * scale[None])
    total = jnp.sum(jnp.sum(powers, axis=0), axis=0, keepdims=True)
    probs = (powers * (1.0 / total)[None]).reshape(slices, cells)
    mass = probs[:, :LANES]
    for start in range(LANES, cells, LANES):
        mass = mass + probs[:, start : start + LANES]
    mass_ref[...] += mass
    return probs.astype(BF16)


def ends_kernel(bits, me_ref, _, x_ref, k_ref, affinity_ref, softness_ref, near_ref, partial_ref, map_ref,
                taps_ref):
    planes, height, depth, channels = x_ref.shape
    slices = affinity_ref.shape[1]
    odd = me_ref[0] & 1

    def row(y, carry):
        near_ref[0, y] = x_ref[(planes - 1) * (1 - odd), y]
        return carry

    lax.fori_loop(0, height, row, 0)
    spread_taps(k_ref, range(3), taps_ref)
    run = slices >> bits
    new = lax.broadcasted_iota(jnp.int32, (slices, 1), 0)
    old = lax.broadcasted_iota(jnp.int32, (slices, slices), 1)
    place = new & (run - 1)
    owner = reverse_lowest(new >> (run.bit_length() - 1), bits)
    order = (old == owner * run + place).astype(BF16)
    map_ref[:slices] = (0.5 * nt_dot(order, affinity_ref[...])).astype(BF16)
    softness = softness_ref[...].astype(BF16).astype(F32)
    map_ref[slices:] = jnp.broadcast_to(0.5 * softness, (TILE, channels)).astype(BF16)

    for which, known in enumerate((((1, 0), (2, 1)), ((0, planes - 2), (1, planes - 1)))):
        def put(y, lanes, rows, known=known, which=which):
            sources = [(role, [None if b is None else x_ref[p, y + b, :, lanes] for b in rows])
                       for role, p in known]
            totals = conv_rows(sources, taps_ref, lanes, len(rows) - 2)
            for i, total in enumerate(totals):
                start = (y + i) * depth
                start = start if isinstance(y, int) else pl.multiple_of(start, depth)
                partial_ref[which, pl.ds(start, depth), lanes] = total.astype(BF16)

        for lanes in channel_blocks(channels):
            put(0, lanes, (None, 0, 1))
            put(height - 1, lanes, (-1, 0, None))

        def pair(i, carry, put=put):
            for lanes in channel_blocks(channels):
                put(2 * i + 1, lanes, (-1, 0, 1, 2))
            return carry

        lax.fori_loop(0, (height - 2) // 2, pair, 0)


def ends_call(me, after, x, taps, affinity, softness, bits):
    planes, height, depth, channels = x.shape
    slices = affinity.shape[1]
    cells = height * depth
    return pl.pallas_call(
        functools.partial(ends_kernel, bits),
        in_specs=[SMEM, pl.BlockSpec(memory_space=pl.ANY)] + [VMEM] * 4,
        out_specs=[VMEM] * 3,
        out_shape=[
            jax.ShapeDtypeStruct((1, height, depth, channels), BF16),
            jax.ShapeDtypeStruct((2, cells, channels), BF16),
            jax.ShapeDtypeStruct((slices + TILE, channels), BF16),
        ],
        scratch_shapes=[pltpu.VMEM((27, REPEAT, channels), CONV)],
        cost_estimate=pl.CostEstimate(
            flops=cells * channels * 12000, bytes_accessed=8 * cells * channels, transcendentals=0
        ),
        compiler_params=pltpu.CompilerParams(vmem_limit_bytes=LIMIT),
        name="ends",
    )(me, after, x, taps, affinity, softness)


def reverse_lowest(value, bits):
    return ((value & ((1 << (bits - 1)) - 1)) << 1) | (value >> (bits - 1))


def inside_kernel(x_ref, k_ref, map_ref, probs_ref, sums_ref, mass_ref,
                  taps_ref, even_ref, odd_ref, hid_ref, by_slice_ref):
    planes, height, depth, channels = x_ref.shape
    spread_taps(k_ref, range(3), taps_ref)
    sums_ref[...] = jnp.zeros(sums_ref.shape, F32)
    mass_ref[...] = jnp.zeros(mass_ref.shape, F32)
    groups = height // GROUP
    cells = GROUP * depth

    def conv(t, hid_ref):
        plane, first = t // groups, lax.rem(t, groups) * GROUP
        for lanes in channel_blocks(channels):
            for j in range(0, GROUP, 2):
                sources = []
                for role in range(3):
                    rows = []
                    for b in (-1, 0, 1, 2):
                        y, ok = first + j + b, None
                        if j + b < 0:
                            ok = first > 0
                        elif j + b >= GROUP:
                            ok = first + GROUP < height
                        rows.append(inner_row(x_ref, plane + role, y, lanes, ok))
                    sources.append((role, rows))
                for i, total in enumerate(conv_rows(sources, taps_ref, lanes, 2)):
                    hid_ref[(j + i) * depth : (j + i + 1) * depth, lanes] = gelu(total.astype(BF16))

    def share(t, source_ref, at):
        hid = source_ref[...]
        by_slice = assign(hid, map_ref, mass_ref)
        start = pl.multiple_of(lax.rem(t, groups) * cells, cells)
        probs_ref[t // groups, pl.ds(start, cells), :] = by_slice.T
        hid_ref[at, :] = hid
        by_slice_ref[:, at] = by_slice

    count = (planes - 2) * groups
    conv(jnp.int32(0), even_ref)

    def two(s, carry):
        t = 2 * s
        share(t, even_ref, slice(0, cells))
        conv(t + 1, odd_ref)
        share(t + 1, odd_ref, slice(cells, 2 * cells))
        sums_ref[...] += dot(by_slice_ref[...], hid_ref[...])
        conv(jnp.minimum(t + 2, count - 1), even_ref)
        return carry

    lax.fori_loop(0, count // 2, two, 0)


def inside_call(x, taps, maps):
    planes, height, depth, channels = x.shape
    slices = maps.shape[0] - TILE
    cells = height * depth
    work = planes * cells * channels
    return pl.pallas_call(
        inside_kernel,
        in_specs=[VMEM] * 3,
        out_specs=[VMEM] * 3,
        out_shape=[
            jax.ShapeDtypeStruct((planes - 2, cells, slices), BF16),
            jax.ShapeDtypeStruct((slices, channels), F32),
            jax.ShapeDtypeStruct((slices, LANES), F32),
        ],
        scratch_shapes=[
            pltpu.VMEM((27, REPEAT, channels), CONV),
            pltpu.VMEM((GROUP * depth, channels), BF16),
            pltpu.VMEM((GROUP * depth, channels), BF16),
            pltpu.VMEM((2 * GROUP * depth, channels), BF16),
            pltpu.VMEM((slices, 2 * GROUP * depth), BF16),
        ],
        cost_estimate=pl.CostEstimate(
            flops=work * 7000, bytes_accessed=2 * work, transcendentals=2 * work
        ),
        compiler_params=pltpu.CompilerParams(vmem_limit_bytes=LIMIT),
        name="inside",
    )(x, taps, maps)


def edge_kernel(is_far, me_ref, halo_ref, partial_ref, k_ref, map_ref, sums_in_ref, mass_in_ref, *rest):
    if is_far:
        by_slice_ref, send_ref, sums_ref, mass_ref, hid_ref, taps_ref = rest
    else:
        probs_ref, sums_ref, mass_ref, taps_ref, hid_ref, by_slice_ref = rest
    _, height, depth, channels = halo_ref.shape
    slices = sums_in_ref.shape[0]
    odd = me_ref[0] & 1
    side = odd if is_far else 1 - odd
    spread_taps(k_ref, [2 * side], taps_ref)
    mass_ref[...] = mass_in_ref[...]
    cells = GROUP * depth
    half = height * depth // 2
    for first in range(0, height, GROUP):
        group = slice(first * depth, first * depth + cells)
        for lanes in channel_blocks(channels):
            for y in range(first, first + GROUP, 2):
                rows = [halo_ref[0, y + b, :, lanes] if 0 <= y + b < height else None
                        for b in (-1, 0, 1, 2)]
                ats = [slice((y + i) * depth, (y + i + 1) * depth) for i in range(2)]
                known = [partial_ref[side, at, lanes] for at in ats]
                for at, total in zip(ats, conv_rows([(0, rows)], taps_ref, lanes, 2, known)):
                    hid_ref[at, lanes] = gelu(total.astype(BF16))
        by_slice = assign(hid_ref[group], map_ref, mass_ref)
        if not is_far:
            probs_ref[0, group] = by_slice.T
        by_slice_ref[:, group] = by_slice
        if group.stop == half:
            sums_ref[...] = sums_in_ref[...] + dot(by_slice_ref[:, :half], hid_ref[:half])
    if not is_far:
        sums_ref[...] += dot(by_slice_ref[:, half:], hid_ref[half:])
        return
    write_share(1 - odd, by_slice_ref, hid_ref, sums_ref, mass_ref, send_ref)


def write_share(side, by_slice_ref, hid_ref, sums_ref, mass_ref, share_ref):
    slices, channels = sums_ref.shape
    half = hid_ref.shape[0] // 2
    owners, rows, _ = share_ref.shape
    held = channels // LANES
    rows = (rows - 8) // held
    start = pl.multiple_of(side * (slices // 2), slices // 2)
    mine = pl.ds(start, slices // 2)
    total = sums_ref[mine, :] + dot(by_slice_ref[mine, half:], hid_ref[half:])
    for i in range(held):
        part = total[:, i * LANES : (i + 1) * LANES].astype(share_ref.dtype)
        share_ref[:, i * rows : (i + 1) * rows, :] = part.reshape(owners, rows, LANES)
    tiles = rows // 8
    lane = lax.broadcasted_iota(jnp.int32, (8, LANES), 1)
    mass = mass_ref[mine, :]
    for owner in range(owners):
        tail = None
        for g in range(tiles):
            tile = mass[owner * rows + 8 * g : owner * rows + 8 * (g + 1)]
            width = LANES
            while width > LANES // tiles:
                width //= 2
                tile = tile + pltpu.roll(tile, width, 1)
            tail = tile if tail is None else jnp.where(lane >= g * width, tile, tail)
        share_ref[owner, held * rows :, :] = tail.astype(share_ref.dtype)


def keep_kernel(me_ref, by_slice_ref, hid_ref, sums_ref, mass_ref, keep_ref, probs_ref):
    write_share(me_ref[0] & 1, by_slice_ref, hid_ref, sums_ref, mass_ref, keep_ref)
    probs_ref[0] = by_slice_ref[...].T


def keep_call(me, by_slice, hid, sums, mass, shape):
    slices, cells = by_slice.shape
    return pl.pallas_call(
        keep_kernel,
        in_specs=[SMEM] + [VMEM] * 4,
        out_specs=[VMEM, VMEM],
        out_shape=[jax.ShapeDtypeStruct(shape, F32), jax.ShapeDtypeStruct((1, cells, slices), BF16)],
        cost_estimate=pl.CostEstimate(flops=2**28, bytes_accessed=2**21, transcendentals=0),
        compiler_params=pltpu.CompilerParams(vmem_limit_bytes=LIMIT),
        name="keep",
    )(me, by_slice, hid, sums, mass)


def edge_call(is_far, me, halo, taps, maps, partial, sums, mass, owners):
    _, height, depth, channels = halo.shape
    slices = sums.shape[0]
    cells = height * depth
    hidden, by_slice = ((cells, channels), BF16), ((slices, cells), BF16)
    carry = [(s.shape, F32) for s in (sums, mass)]
    scratch = [((9, REPEAT, channels), CONV)]
    if is_far:
        rows = channels // LANES * (slices // owners) + 8
        outs = [by_slice, ((owners // 2, rows, LANES), BF16)] + carry + [hidden]
    else:
        outs = [((1, cells, slices), BF16)] + carry
        scratch += [hidden, by_slice]
    return pl.pallas_call(
        functools.partial(edge_kernel, is_far),
        in_specs=[SMEM] + [VMEM] * 6,
        out_specs=[VMEM] * len(outs),
        out_shape=[jax.ShapeDtypeStruct(*o) for o in outs],
        scratch_shapes=[pltpu.VMEM(*o) for o in scratch],
        cost_estimate=pl.CostEstimate(
            flops=cells * channels * 16000, bytes_accessed=4 * cells * channels,
            transcendentals=2 * cells * channels,
        ),
        compiler_params=pltpu.CompilerParams(vmem_limit_bytes=LIMIT),
        name="far" if is_far else "near",
    )(me, halo, partial, taps, maps, sums, mass)


def merge_kernel(keep_ref, other_ref, out_ref):
    out_ref[...] = (keep_ref[...] + other_ref[...].astype(F32)).astype(BF16)


def merge_call(keep, other):
    return pl.pallas_call(
        merge_kernel,
        in_specs=[VMEM, VMEM],
        out_specs=VMEM,
        out_shape=jax.ShapeDtypeStruct(keep.shape, BF16),
        compiler_params=pltpu.CompilerParams(vmem_limit_bytes=LIMIT),
        name="merge",
    )(keep, other)


def owner_kernel(parts_ref, gain_ref, content_ref, widening_ref,
                 narrowing_ref, final_ref, out_ref, mapped_ref):
    channels = content_ref.shape[0]
    held = channels // LANES
    rows = out_ref.shape[0]
    total = jnp.sum(parts_ref[...].astype(F32), axis=0)
    pooled = jnp.concatenate([total[i * rows : (i + 1) * rows] for i in range(held)], axis=1)
    tail = total[held * rows :]
    lane = lax.broadcasted_iota(jnp.int32, (8, LANES), 1)
    width = LANES // (rows // 8)
    mass = jnp.concatenate([
        jnp.sum(jnp.where((lane >= g) & (lane < g + width), tail, 0.0), axis=1, keepdims=True)
        for g in range(0, LANES, width)
    ], axis=0)
    pooled = 0.5 * pooled / (mass + epsilon)
    high = pooled.astype(BF16)
    low = (pooled - high.astype(F32)).astype(BF16)
    tokens = dot(jnp.concatenate([high, low], axis=0), content_ref[...])
    tokens = tokens[:rows] + tokens[rows:]
    center = jnp.mean(tokens, axis=-1, keepdims=True)
    spread = jnp.mean((tokens - center) ** 2, axis=-1, keepdims=True)
    normed = ((tokens - center) * (1.0 / jnp.sqrt(spread + epsilon)) * gain_ref[...]).astype(BF16)
    inner = (0.5 * gelu(dot(normed, widening_ref[...]))).astype(BF16)
    out = (tokens + dot(inner, narrowing_ref[...])).astype(BF16)
    out_ref[...] = out
    mapped = dot(out, final_ref[...]).astype(BF16)
    mapped_ref[...] = jnp.broadcast_to(mapped[None], mapped_ref.shape)


def owner_call(parts, gain, *weights):
    channels = weights[0].shape[0]
    owners = parts.shape[0]
    rows = (parts.shape[1] - 8) // (channels // LANES)
    return pl.pallas_call(
        owner_kernel,
        in_specs=[VMEM] * 6,
        out_specs=[VMEM, VMEM],
        out_shape=[
            jax.ShapeDtypeStruct((rows, channels), BF16),
            jax.ShapeDtypeStruct((owners, rows, channels), BF16),
        ],
        compiler_params=pltpu.CompilerParams(vmem_limit_bytes=LIMIT),
        name="owner",
    )(parts, gain, *weights)


def ahead_kernel(me_ref, x_ref, inside_ref, near_ref, own_ref, out_ref):
    planes = x_ref.shape[0]
    half = own_ref.shape[0]
    odd = me_ref[0] & 1
    columns = pl.ds(pl.multiple_of(odd * half, half), half)

    def step(i, carry):
        change = dot(inside_ref[i, :, columns], own_ref[...])
        out_ref[i] = x_ref[i + 1].astype(F32) + change
        return carry

    lax.fori_loop(0, planes - 2, step, 0)
    change = dot(near_ref[0, :, columns], own_ref[...])
    out_ref[planes - 2] = x_ref[(planes - 1) * (1 - odd)].astype(F32) + change


def ahead_call(me, x, inside, near, own):
    planes, cells, channels = x.shape
    return pl.pallas_call(
        ahead_kernel,
        in_specs=[SMEM] + [VMEM] * 4,
        out_specs=VMEM,
        out_shape=jax.ShapeDtypeStruct((planes - 1, cells, channels), F32),
        cost_estimate=pl.CostEstimate(flops=2**30, bytes_accessed=2**23, transcendentals=0),
        compiler_params=pltpu.CompilerParams(vmem_limit_bytes=LIMIT),
        name="ahead",
    )(me, x, inside, near, own)


def update_kernel(me_ref, x_ref, ahead_ref, inside_ref, near_ref, far_ref, own_ref, other_ref, out_ref,
                  done_ref, mapped_ref, sem):
    planes, cells, channels = x_ref.shape
    half = own_ref.shape[0]
    odd = me_ref[0] & 1
    mine = pl.ds(pl.multiple_of(odd * half, half), half)
    others = pl.ds(pl.multiple_of((1 - odd) * half, half), half)
    mapped_ref[mine] = own_ref[...]
    mapped_ref[others] = other_ref[...]

    def store(plane):
        return pltpu.make_async_copy(done_ref.at[plane], out_ref.at[plane], sem.at[plane])

    def step(i, carry):
        total = ahead_ref[i] + dot(inside_ref[i, :, others], other_ref[...])
        done_ref[i + 1] = total.astype(BF16)
        store(i + 1).start()
        return carry

    lax.fori_loop(0, planes - 2, step, 0)
    near, far = (planes - 1) * (1 - odd), (planes - 1) * odd
    total = ahead_ref[planes - 2] + dot(near_ref[0, :, others], other_ref[...])
    done_ref[near] = total.astype(BF16)
    store(near).start()
    change = dot(far_ref[0], mapped_ref[...])
    done_ref[far] = (x_ref[far].astype(F32) + change).astype(BF16)
    store(far).start()

    def finish(plane, carry):
        store(plane).wait()
        return carry

    lax.fori_loop(0, planes, finish, 0)


def update_call(me, x, ahead, inside, near, far, own, other):
    planes, cells, channels = x.shape
    return pl.pallas_call(
        update_kernel,
        in_specs=[SMEM] + [VMEM] * 7,
        out_specs=HBM,
        out_shape=jax.ShapeDtypeStruct(x.shape, BF16),
        scratch_shapes=[
            pltpu.VMEM(x.shape, BF16),
            pltpu.VMEM((2 * own.shape[0], channels), BF16),
            pltpu.SemaphoreType.DMA((planes,)),
        ],
        compiler_params=pltpu.CompilerParams(vmem_limit_bytes=LIMIT),
        name="update",
    )(me, x, ahead, inside, near, far, own, other)


def per_device(
    mesh_feature_array,
    stencil_coefficients,
    partition_affinity_matrix,
    softness_mapping_matrix,
    content_mapping_matrix,
    layernorm_multiplier,
    widening_matrix,
    narrowing_matrix,
    final_mapping_matrix,
):
    x = mesh_feature_array
    planes, height, depth, channels = x.shape
    slices = partition_affinity_matrix.shape[1]
    n = lax.axis_size("gx")
    me = lax.axis_index("gx").astype(jnp.int32)[None]
    far_pairs = [p for i in range(1, n - 1, 2) for p in ((i, i + 1), (i + 1, i))]
    near_pairs = [p for i in range(0, n, 2) for p in ((i, i + 1), (i + 1, i))]
    far_plane = lax.dynamic_slice_in_dim(x, (planes - 1) * (me[0] & 1), 1)
    far_halo = lax.ppermute(far_plane, "gx", far_pairs)

    owners = min(n // 2, slices // 2 // TILE)
    share = n // 2 // owners
    groups = [[2 * (share * j + s) + h for j in range(owners)] for h in range(2) for s in range(share)]
    taps = stencil_coefficients
    near_plane, partial, maps = ends_call(
        me, far_plane, x, taps, partition_affinity_matrix, softness_mapping_matrix[None],
        n.bit_length() - 1,
    )
    near_halo = lax.ppermute(near_plane, "gx", near_pairs)
    inside_probs, sums, mass = inside_call(x, taps, maps)
    near_probs, sums, mass = edge_call(
        False, me, near_halo, taps, maps, partial, sums, mass, 2 * owners
    )
    by_slice, send, sums, mass, hid = edge_call(
        True, me, far_halo, taps, maps, partial, sums, mass, 2 * owners
    )

    received = lax.ppermute(send, "gx", near_pairs)
    keep, far_probs = keep_call(me, by_slice, hid, sums, mass, send.shape)
    parts = merge_call(keep, received)
    parts = lax.all_to_all(parts, "gx", 0, 0, axis_index_groups=groups)
    if share > 1:
        sharers = [[2 * (share * j + s) + h for s in range(share)]
                   for h in range(2) for j in range(owners)]
        parts = lax.psum(parts, "gx", axis_index_groups=sharers)
    own_out, mapped = owner_call(
        parts, layernorm_multiplier[None],
        content_mapping_matrix, widening_matrix, narrowing_matrix, final_mapping_matrix,
    )
    if share > 1:
        place = lax.rem(me[0] // 2, share) * (slices // n)
        own_out = lax.dynamic_slice_in_dim(own_out, place, slices // n)
    mapped = lax.all_to_all(mapped, "gx", 0, 0, axis_index_groups=groups).reshape(slices // 2, channels)
    other = lax.ppermute(mapped, "gx", near_pairs)
    planes_of_cells = x.reshape(planes, height * depth, channels)
    ahead = ahead_call(me, planes_of_cells, inside_probs, near_probs, mapped)
    updated = update_call(
        me, planes_of_cells, ahead, inside_probs, near_probs, far_probs, mapped, other
    )
    return updated.reshape(x.shape), own_out


def solution(mesh):
    return jax.shard_map(
        per_device,
        mesh=mesh,
        in_specs=(P(("grp", "gx"), None, None, None), P(), P(), P(), P(), P(), P(), P(), P()),
        out_specs=(P(("grp", "gx"), None, None, None), P(("grp", "gx"), None)),
        check_vma=False,
    )
```

```python
import functools
import math

import jax
import jax.numpy as jnp
from jax import lax
from jax.experimental import pallas as pl
from jax.experimental.pallas import tpu as pltpu
from jax.sharding import PartitionSpec as P

epsilon = 1e-05
LANES = 128
BLOCK = 256
GROUP = 8
TILE = 16
REPEAT = 8
MIB = 2**20
LIMIT = 32 * MIB
F32, BF16 = jnp.float32, jnp.bfloat16
CONV = BF16
VMEM = pl.BlockSpec(memory_space=pltpu.VMEM)
SMEM = pl.BlockSpec(memory_space=pltpu.SMEM)
HBM = pl.BlockSpec(memory_space=pltpu.HBM)


def dot(a, b):
    return jnp.dot(a, b, preferred_element_type=F32)


def gelu(x):
    inner = x * (x * x * (0.044715 * math.sqrt(2 / math.pi)) + math.sqrt(2 / math.pi))
    return x + x * jnp.tanh(inner)


def spread_taps(k_ref, planes, taps_ref):
    for role, plane in enumerate(planes):
        for tap in range(9):
            row = k_ref[pl.ds(9 * plane + tap, 1), :]
            taps_ref[9 * role + tap] = jnp.broadcast_to(row, taps_ref.shape[1:]).astype(CONV)


def conv_rows(sources, taps_ref, lanes, count, known=()):
    sums = [[None] * 3 for _ in range(count)]
    for role, rows in sources:
        taps = [taps_ref[9 * role + i, :, lanes] for i in range(9)]
        for j, row in enumerate(rows):
            if row is None:
                continue
            depth, width = row.shape
            row = row.astype(CONV).reshape(depth // REPEAT, REPEAT, width)
            for out in range(max(0, j - 2), min(count, j + 1)):
                for c in range(3):
                    term = row * taps[3 * (j - out) + c]
                    sums[out][c] = term if sums[out][c] is None else sums[out][c] + term
    for out, row in enumerate(known):
        sums[out][1] = sums[out][1] + row.astype(CONV).reshape(sums[out][1].shape)
    position = lax.broadcasted_iota(jnp.int32, (8, width), 0)
    results = []
    for out in range(count):
        before, here, after = (s.astype(F32).reshape(depth, width) for s in sums[out])
        before, after = pltpu.roll(before, 1, 0), pltpu.roll(after, depth - 1, 0)
        low = jnp.where(position == 0, 0.0, before[:8])
        high = jnp.where(position == 7, 0.0, after[depth - 8 :])
        before = jnp.concatenate([low, before[8:]], axis=0)
        after = jnp.concatenate([after[: depth - 8], high], axis=0)
        results.append(here + before + after)
    return results


def channel_blocks(channels):
    return [slice(i, i + BLOCK) for i in range(0, channels, BLOCK)]


def inner_row(ref, plane, y, lanes, inside=None):
    if inside is None:
        return ref[plane, y, :, lanes]
    row = ref[plane, jnp.clip(y, 0, ref.shape[1] - 1), :, lanes].astype(F32)
    return (row * jnp.where(inside, 1.0, 0.0)).astype(BF16)


def nt_dot(a, b):
    return lax.dot_general(a, b, (((1,), (1,)), ((), ())), preferred_element_type=F32)


def assign(hid, map_ref, mass_ref):
    cells = hid.shape[0]
    slices = map_ref.shape[0] - TILE
    raw = nt_dot(map_ref[...], hid)
    soft = raw[slices : slices + 8]
    temperature = 0.25 + jnp.maximum(soft, 0.0) + jnp.log(1.0 + jnp.exp(-jnp.abs(soft)))
    scale = (1.0 / math.log(2.0)) / temperature
    raw = raw[:slices].reshape(slices // 8, 8, cells)
    top = jnp.max(jnp.max(raw, axis=0), axis=0, keepdims=True)
    powers = jnp.exp2((raw - top[None]) * scale[None])
    total = jnp.sum(jnp.sum(powers, axis=0), axis=0, keepdims=True)
    probs = (powers * (1.0 / total)[None]).reshape(slices, cells)
    mass = probs[:, :LANES]
    for start in range(LANES, cells, LANES):
        mass = mass + probs[:, start : start + LANES]
    mass_ref[...] += mass
    return probs.astype(BF16)


def ends_kernel(me_ref, _, x_ref, k_ref, near_ref, partial_ref, taps_ref):
    planes, height, depth, channels = x_ref.shape
    odd = me_ref[0] & 1

    def row(y, carry):
        near_ref[0, y] = x_ref[(planes - 1) * (1 - odd), y]
        return carry

    lax.fori_loop(0, height, row, 0)
    spread_taps(k_ref, range(3), taps_ref)
    for which, known in enumerate((((1, 0), (2, 1)), ((0, planes - 2), (1, planes - 1)))):
        def put(y, lanes, rows, known=known, which=which):
            sources = [(role, [None if b is None else x_ref[p, y + b, :, lanes] for b in rows])
                       for role, p in known]
            totals = conv_rows(sources, taps_ref, lanes, len(rows) - 2)
            for i, total in enumerate(totals):
                start = (y + i) * depth
                start = start if isinstance(y, int) else pl.multiple_of(start, depth)
                partial_ref[which, pl.ds(start, depth), lanes] = total.astype(BF16)

        for lanes in channel_blocks(channels):
            put(0, lanes, (None, 0, 1))
            put(height - 1, lanes, (-1, 0, None))

        def pair(i, carry, put=put):
            for lanes in channel_blocks(channels):
                put(2 * i + 1, lanes, (-1, 0, 1, 2))
            return carry

        lax.fori_loop(0, (height - 2) // 2, pair, 0)


def ends_call(me, after, x, taps):
    planes, height, depth, channels = x.shape
    cells = height * depth
    return pl.pallas_call(
        ends_kernel,
        in_specs=[SMEM, pl.BlockSpec(memory_space=pl.ANY)] + [VMEM] * 2,
        out_specs=[VMEM] * 2,
        out_shape=[
            jax.ShapeDtypeStruct((1, height, depth, channels), BF16),
            jax.ShapeDtypeStruct((2, cells, channels), BF16),
        ],
        scratch_shapes=[pltpu.VMEM((27, REPEAT, channels), CONV)],
        cost_estimate=pl.CostEstimate(
            flops=cells * channels * 12000, bytes_accessed=8 * cells * channels, transcendentals=0
        ),
        compiler_params=pltpu.CompilerParams(vmem_limit_bytes=LIMIT),
        name="ends",
    )(me, after, x, taps)


def reverse_lowest(value, bits):
    return ((value & ((1 << (bits - 1)) - 1)) << 1) | (value >> (bits - 1))


def inside_kernel(bits, x_ref, k_ref, affinity_ref, softness_ref, probs_ref, sums_ref, mass_ref, map_ref,
                  taps_ref, even_ref, odd_ref, hid_ref, by_slice_ref):
    planes, height, depth, channels = x_ref.shape
    slices = affinity_ref.shape[1]
    spread_taps(k_ref, range(3), taps_ref)
    run = slices >> bits
    new = lax.broadcasted_iota(jnp.int32, (slices, 1), 0)
    old = lax.broadcasted_iota(jnp.int32, (slices, slices), 1)
    place = new & (run - 1)
    owner = reverse_lowest(new >> (run.bit_length() - 1), bits)
    order = (old == owner * run + place).astype(BF16)
    map_ref[:slices] = (0.5 * nt_dot(order, affinity_ref[...])).astype(BF16)
    softness = softness_ref[...].astype(BF16).astype(F32)
    map_ref[slices:] = jnp.broadcast_to(0.5 * softness, (TILE, channels)).astype(BF16)

    sums_ref[...] = jnp.zeros(sums_ref.shape, F32)
    mass_ref[...] = jnp.zeros(mass_ref.shape, F32)
    groups = height // GROUP
    cells = GROUP * depth

    def conv(t, hid_ref):
        plane, first = t // groups, lax.rem(t, groups) * GROUP
        for lanes in channel_blocks(channels):
            for j in range(0, GROUP, 2):
                sources = []
                for role in range(3):
                    rows = []
                    for b in (-1, 0, 1, 2):
                        y, ok = first + j + b, None
                        if j + b < 0:
                            ok = first > 0
                        elif j + b >= GROUP:
                            ok = first + GROUP < height
                        rows.append(inner_row(x_ref, plane + role, y, lanes, ok))
                    sources.append((role, rows))
                for i, total in enumerate(conv_rows(sources, taps_ref, lanes, 2)):
                    hid_ref[(j + i) * depth : (j + i + 1) * depth, lanes] = gelu(total.astype(BF16))

    def share(t, source_ref, at):
        hid = source_ref[...]
        by_slice = assign(hid, map_ref, mass_ref)
        start = pl.multiple_of(lax.rem(t, groups) * cells, cells)
        probs_ref[t // groups, pl.ds(start, cells), :] = by_slice.T
        hid_ref[at, :] = hid
        by_slice_ref[:, at] = by_slice

    count = (planes - 2) * groups
    conv(jnp.int32(0), even_ref)

    def two(s, carry):
        t = 2 * s
        share(t, even_ref, slice(0, cells))
        conv(t + 1, odd_ref)
        share(t + 1, odd_ref, slice(cells, 2 * cells))
        sums_ref[...] += dot(by_slice_ref[...], hid_ref[...])
        conv(jnp.minimum(t + 2, count - 1), even_ref)
        return carry

    lax.fori_loop(0, count // 2, two, 0)


def inside_call(x, taps, affinity, softness, bits):
    planes, height, depth, channels = x.shape
    slices = affinity.shape[1]
    cells = height * depth
    work = planes * cells * channels
    return pl.pallas_call(
        functools.partial(inside_kernel, bits),
        in_specs=[VMEM] * 4,
        out_specs=[VMEM] * 4,
        out_shape=[
            jax.ShapeDtypeStruct((planes - 2, cells, slices), BF16),
            jax.ShapeDtypeStruct((slices, channels), F32),
            jax.ShapeDtypeStruct((slices, LANES), F32),
            jax.ShapeDtypeStruct((slices + TILE, channels), BF16),
        ],
        scratch_shapes=[
            pltpu.VMEM((27, REPEAT, channels), CONV),
            pltpu.VMEM((GROUP * depth, channels), BF16),
            pltpu.VMEM((GROUP * depth, channels), BF16),
            pltpu.VMEM((2 * GROUP * depth, channels), BF16),
            pltpu.VMEM((slices, 2 * GROUP * depth), BF16),
        ],
        cost_estimate=pl.CostEstimate(
            flops=work * 7000, bytes_accessed=2 * work, transcendentals=2 * work
        ),
        compiler_params=pltpu.CompilerParams(vmem_limit_bytes=LIMIT),
        name="inside",
    )(x, taps, affinity, softness)


def edge_kernel(is_far, me_ref, halo_ref, partial_ref, k_ref, map_ref, sums_in_ref, mass_in_ref, *rest):
    if is_far:
        by_slice_ref, send_ref, sums_ref, mass_ref, hid_ref, taps_ref = rest
    else:
        probs_ref, sums_ref, mass_ref, taps_ref, hid_ref, by_slice_ref = rest
    _, height, depth, channels = halo_ref.shape
    slices = sums_in_ref.shape[0]
    odd = me_ref[0] & 1
    side = odd if is_far else 1 - odd
    spread_taps(k_ref, [2 * side], taps_ref)
    mass_ref[...] = mass_in_ref[...]
    cells = GROUP * depth
    half = height * depth // 2

    def conv(first):
        for lanes in channel_blocks(channels):
            for y in range(first, first + GROUP, 2):
                rows = [halo_ref[0, y + b, :, lanes] if 0 <= y + b < height else None
                        for b in (-1, 0, 1, 2)]
                ats = [slice((y + i) * depth, (y + i + 1) * depth) for i in range(2)]
                known = [partial_ref[side, at, lanes] for at in ats]
                for at, total in zip(ats, conv_rows([(0, rows)], taps_ref, lanes, 2, known)):
                    hid_ref[at, lanes] = gelu(total.astype(BF16))

    conv(0)
    for first in range(0, height, GROUP):
        if first + GROUP < height:
            conv(first + GROUP)
        group = slice(first * depth, first * depth + cells)
        by_slice = assign(hid_ref[group], map_ref, mass_ref)
        if not is_far:
            probs_ref[0, group] = by_slice.T
        by_slice_ref[:, group] = by_slice
        if group.stop == half:
            sums_ref[...] = sums_in_ref[...] + dot(by_slice_ref[:, :half], hid_ref[:half])
    if not is_far:
        sums_ref[...] += dot(by_slice_ref[:, half:], hid_ref[half:])
        return
    write_share(1 - odd, by_slice_ref, hid_ref, sums_ref, mass_ref, send_ref)


def write_share(side, by_slice_ref, hid_ref, sums_ref, mass_ref, share_ref):
    slices, channels = sums_ref.shape
    half = hid_ref.shape[0] // 2
    owners, rows, _ = share_ref.shape
    held = channels // LANES
    rows = (rows - 8) // held
    start = pl.multiple_of(side * (slices // 2), slices // 2)
    mine = pl.ds(start, slices // 2)
    total = sums_ref[mine, :] + dot(by_slice_ref[mine, half:], hid_ref[half:])
    for i in range(held):
        part = total[:, i * LANES : (i + 1) * LANES].astype(share_ref.dtype)
        share_ref[:, i * rows : (i + 1) * rows, :] = part.reshape(owners, rows, LANES)
    tiles = rows // 8
    lane = lax.broadcasted_iota(jnp.int32, (8, LANES), 1)
    mass = mass_ref[mine, :]
    for owner in range(owners):
        tail = None
        for g in range(tiles):
            tile = mass[owner * rows + 8 * g : owner * rows + 8 * (g + 1)]
            width = LANES
            while width > LANES // tiles:
                width //= 2
                tile = tile + pltpu.roll(tile, width, 1)
            tail = tile if tail is None else jnp.where(lane >= g * width, tile, tail)
        share_ref[owner, held * rows :, :] = tail.astype(share_ref.dtype)


def keep_kernel(me_ref, by_slice_ref, hid_ref, sums_ref, mass_ref, keep_ref, probs_ref):
    write_share(me_ref[0] & 1, by_slice_ref, hid_ref, sums_ref, mass_ref, keep_ref)
    probs_ref[0] = by_slice_ref[...].T


def keep_call(me, by_slice, hid, sums, mass, shape):
    slices, cells = by_slice.shape
    return pl.pallas_call(
        keep_kernel,
        in_specs=[SMEM] + [VMEM] * 4,
        out_specs=[VMEM, VMEM],
        out_shape=[jax.ShapeDtypeStruct(shape, F32), jax.ShapeDtypeStruct((1, cells, slices), BF16)],
        cost_estimate=pl.CostEstimate(flops=2**28, bytes_accessed=2**21, transcendentals=0),
        compiler_params=pltpu.CompilerParams(vmem_limit_bytes=LIMIT),
        name="keep",
    )(me, by_slice, hid, sums, mass)


def edge_call(is_far, me, halo, taps, maps, partial, sums, mass, owners):
    _, height, depth, channels = halo.shape
    slices = sums.shape[0]
    cells = height * depth
    hidden, by_slice = ((cells, channels), BF16), ((slices, cells), BF16)
    carry = [(s.shape, F32) for s in (sums, mass)]
    scratch = [((9, REPEAT, channels), CONV)]
    if is_far:
        rows = channels // LANES * (slices // owners) + 8
        outs = [by_slice, ((owners // 2, rows, LANES), BF16)] + carry + [hidden]
    else:
        outs = [((1, cells, slices), BF16)] + carry
        scratch += [hidden, by_slice]
    return pl.pallas_call(
        functools.partial(edge_kernel, is_far),
        in_specs=[SMEM] + [VMEM] * 6,
        out_specs=[VMEM] * len(outs),
        out_shape=[jax.ShapeDtypeStruct(*o) for o in outs],
        scratch_shapes=[pltpu.VMEM(*o) for o in scratch],
        cost_estimate=pl.CostEstimate(
            flops=cells * channels * 16000, bytes_accessed=4 * cells * channels,
            transcendentals=2 * cells * channels,
        ),
        compiler_params=pltpu.CompilerParams(vmem_limit_bytes=LIMIT),
        name="far" if is_far else "near",
    )(me, halo, partial, taps, maps, sums, mass)


def merge_kernel(keep_ref, other_ref, out_ref):
    out_ref[...] = (keep_ref[...] + other_ref[...].astype(F32)).astype(BF16)


def merge_call(keep, other):
    return pl.pallas_call(
        merge_kernel,
        in_specs=[VMEM, VMEM],
        out_specs=VMEM,
        out_shape=jax.ShapeDtypeStruct(keep.shape, BF16),
        compiler_params=pltpu.CompilerParams(vmem_limit_bytes=LIMIT),
        name="merge",
    )(keep, other)


def owner_kernel(parts_ref, gain_ref, content_ref, widening_ref,
                 narrowing_ref, final_ref, out_ref, mapped_ref):
    channels = content_ref.shape[0]
    held = channels // LANES
    rows = out_ref.shape[0]
    total = jnp.sum(parts_ref[...].astype(F32), axis=0)
    pooled = jnp.concatenate([total[i * rows : (i + 1) * rows] for i in range(held)], axis=1)
    tail = total[held * rows :]
    lane = lax.broadcasted_iota(jnp.int32, (8, LANES), 1)
    width = LANES // (rows // 8)
    mass = jnp.concatenate([
        jnp.sum(jnp.where((lane >= g) & (lane < g + width), tail, 0.0), axis=1, keepdims=True)
        for g in range(0, LANES, width)
    ], axis=0)
    pooled = 0.5 * pooled / (mass + epsilon)
    high = pooled.astype(BF16)
    low = (pooled - high.astype(F32)).astype(BF16)
    tokens = dot(jnp.concatenate([high, low], axis=0), content_ref[...])
    tokens = tokens[:rows] + tokens[rows:]
    center = jnp.mean(tokens, axis=-1, keepdims=True)
    spread = jnp.mean((tokens - center) ** 2, axis=-1, keepdims=True)
    normed = ((tokens - center) * (1.0 / jnp.sqrt(spread + epsilon)) * gain_ref[...]).astype(BF16)
    inner = (0.5 * gelu(dot(normed, widening_ref[...]))).astype(BF16)
    out = (tokens + dot(inner, narrowing_ref[...])).astype(BF16)
    out_ref[...] = out
    mapped = dot(out, final_ref[...]).astype(BF16)
    mapped_ref[...] = jnp.broadcast_to(mapped[None], mapped_ref.shape)


def owner_call(parts, gain, *weights):
    channels = weights[0].shape[0]
    owners = parts.shape[0]
    rows = (parts.shape[1] - 8) // (channels // LANES)
    return pl.pallas_call(
        owner_kernel,
        in_specs=[VMEM] * 6,
        out_specs=[VMEM, VMEM],
        out_shape=[
            jax.ShapeDtypeStruct((rows, channels), BF16),
            jax.ShapeDtypeStruct((owners, rows, channels), BF16),
        ],
        compiler_params=pltpu.CompilerParams(vmem_limit_bytes=LIMIT),
        name="owner",
    )(parts, gain, *weights)


def ahead_kernel(me_ref, x_ref, inside_ref, near_ref, own_ref, out_ref):
    planes = x_ref.shape[0]
    half = own_ref.shape[0]
    odd = me_ref[0] & 1
    columns = pl.ds(pl.multiple_of(odd * half, half), half)

    def step(i, carry):
        change = dot(inside_ref[i, :, columns], own_ref[...])
        out_ref[i] = x_ref[i + 1].astype(F32) + change
        return carry

    lax.fori_loop(0, planes - 2, step, 0)
    change = dot(near_ref[0, :, columns], own_ref[...])
    out_ref[planes - 2] = x_ref[(planes - 1) * (1 - odd)].astype(F32) + change


def ahead_call(me, x, inside, near, own):
    planes, cells, channels = x.shape
    return pl.pallas_call(
        ahead_kernel,
        in_specs=[SMEM] + [VMEM] * 4,
        out_specs=VMEM,
        out_shape=jax.ShapeDtypeStruct((planes - 1, cells, channels), F32),
        cost_estimate=pl.CostEstimate(flops=2**30, bytes_accessed=2**23, transcendentals=0),
        compiler_params=pltpu.CompilerParams(vmem_limit_bytes=LIMIT),
        name="ahead",
    )(me, x, inside, near, own)


def update_kernel(me_ref, x_ref, ahead_ref, inside_ref, near_ref, far_ref, own_ref, other_ref, out_ref,
                  done_ref, mapped_ref, sem):
    planes, cells, channels = x_ref.shape
    half = own_ref.shape[0]
    odd = me_ref[0] & 1
    mine = pl.ds(pl.multiple_of(odd * half, half), half)
    others = pl.ds(pl.multiple_of((1 - odd) * half, half), half)
    mapped_ref[mine] = own_ref[...]
    mapped_ref[others] = other_ref[...]

    def store(plane, at, sem_ref):
        return pltpu.make_async_copy(done_ref.at[plane, at], out_ref.at[plane, at], sem_ref)

    def whole(plane):
        return store(plane, pl.ds(0, cells), sem.at[plane])

    near, far = (planes - 1) * (1 - odd), (planes - 1) * odd
    change = dot(far_ref[0], mapped_ref[...])
    done_ref[far] = (x_ref[far].astype(F32) + change).astype(BF16)
    whole(far).start()

    def step(i, carry):
        total = ahead_ref[i] + dot(inside_ref[i, :, others], other_ref[...])
        done_ref[i + 1] = total.astype(BF16)
        whole(i + 1).start()
        return carry

    lax.fori_loop(0, planes - 2, step, 0)
    parts = [pl.ds(0, cells // 2), pl.ds(cells // 2, cells // 2)]
    ends = [store(near, at, sem.at[planes + i]) for i, at in enumerate(parts)]
    for at, end in zip(parts, ends):
        total = ahead_ref[planes - 2, at, :] + dot(near_ref[0, at, others], other_ref[...])
        done_ref[near, at, :] = total.astype(BF16)
        end.start()
    whole(far).wait()
    for i in range(planes - 2):
        whole(i + 1).wait()
    for end in ends:
        end.wait()


def update_call(me, x, ahead, inside, near, far, own, other):
    planes, cells, channels = x.shape
    return pl.pallas_call(
        update_kernel,
        in_specs=[SMEM] + [VMEM] * 7,
        out_specs=HBM,
        out_shape=jax.ShapeDtypeStruct(x.shape, BF16),
        scratch_shapes=[
            pltpu.VMEM(x.shape, BF16),
            pltpu.VMEM((2 * own.shape[0], channels), BF16),
            pltpu.SemaphoreType.DMA((planes + 2,)),
        ],
        compiler_params=pltpu.CompilerParams(vmem_limit_bytes=LIMIT),
        name="update",
    )(me, x, ahead, inside, near, far, own, other)


def per_device(
    mesh_feature_array,
    stencil_coefficients,
    partition_affinity_matrix,
    softness_mapping_matrix,
    content_mapping_matrix,
    layernorm_multiplier,
    widening_matrix,
    narrowing_matrix,
    final_mapping_matrix,
):
    x = mesh_feature_array
    planes, height, depth, channels = x.shape
    slices = partition_affinity_matrix.shape[1]
    n = lax.axis_size("gx")
    me = lax.axis_index("gx").astype(jnp.int32)[None]
    far_pairs = [p for i in range(1, n - 1, 2) for p in ((i, i + 1), (i + 1, i))]
    near_pairs = [p for i in range(0, n, 2) for p in ((i, i + 1), (i + 1, i))]
    far_plane = lax.dynamic_slice_in_dim(x, (planes - 1) * (me[0] & 1), 1)
    far_halo = lax.ppermute(far_plane, "gx", far_pairs)

    owners = min(n // 2, slices // 2 // TILE)
    share = n // 2 // owners
    groups = [[2 * (share * j + s) + h for j in range(owners)] for h in range(2) for s in range(share)]
    taps = stencil_coefficients
    near_plane, partial = ends_call(me, far_plane, x, taps)
    near_halo = lax.ppermute(near_plane, "gx", near_pairs)
    inside_probs, sums, mass, maps = inside_call(
        x, taps, partition_affinity_matrix, softness_mapping_matrix[None], n.bit_length() - 1
    )
    near_probs, sums, mass = edge_call(
        False, me, near_halo, taps, maps, partial, sums, mass, 2 * owners
    )
    by_slice, send, sums, mass, hid = edge_call(
        True, me, far_halo, taps, maps, partial, sums, mass, 2 * owners
    )

    received = lax.ppermute(send, "gx", near_pairs)
    keep, far_probs = keep_call(me, by_slice, hid, sums, mass, send.shape)
    parts = merge_call(keep, received)
    parts = lax.all_to_all(parts, "gx", 0, 0, axis_index_groups=groups)
    if share > 1:
        sharers = [[2 * (share * j + s) + h for s in range(share)]
                   for h in range(2) for j in range(owners)]
        parts = lax.psum(parts, "gx", axis_index_groups=sharers)
    own_out, mapped = owner_call(
        parts, layernorm_multiplier[None],
        content_mapping_matrix, widening_matrix, narrowing_matrix, final_mapping_matrix,
    )
    if share > 1:
        place = lax.rem(me[0] // 2, share) * (slices // n)
        own_out = lax.dynamic_slice_in_dim(own_out, place, slices // n)
    mapped = lax.all_to_all(mapped, "gx", 0, 0, axis_index_groups=groups).reshape(slices // 2, channels)
    other = lax.ppermute(mapped, "gx", near_pairs)
    planes_of_cells = x.reshape(planes, height * depth, channels)
    ahead = ahead_call(me, planes_of_cells, inside_probs, near_probs, mapped)
    updated = update_call(
        me, planes_of_cells, ahead, inside_probs, near_probs, far_probs, mapped, other
    )
    return updated.reshape(x.shape), own_out


def solution(mesh):
    return jax.shard_map(
        per_device,
        mesh=mesh,
        in_specs=(P(("grp", "gx"), None, None, None), P(), P(), P(), P(), P(), P(), P(), P()),
        out_specs=(P(("grp", "gx"), None, None, None), P(("grp", "gx"), None)),
        check_vma=False,
    )
```

```python
import functools
import math

import jax
import jax.numpy as jnp
from jax import lax
from jax.experimental import pallas as pl
from jax.experimental.pallas import tpu as pltpu
from jax.sharding import PartitionSpec as P

epsilon = 1e-05
LANES = 128
BLOCK = 256
GROUP = 8
TILE = 16
REPEAT = 8
MIB = 2**20
LIMIT = 32 * MIB
F32, BF16 = jnp.float32, jnp.bfloat16
CONV = BF16
VMEM = pl.BlockSpec(memory_space=pltpu.VMEM)
SMEM = pl.BlockSpec(memory_space=pltpu.SMEM)
HBM = pl.BlockSpec(memory_space=pltpu.HBM)


def dot(a, b):
    return jnp.dot(a, b, preferred_element_type=F32)


def gelu(x):
    inner = x * (x * x * (0.044715 * math.sqrt(2 / math.pi)) + math.sqrt(2 / math.pi))
    return x + x * jnp.tanh(inner)


def spread_taps(k_ref, planes, taps_ref):
    for role, plane in enumerate(planes):
        for tap in range(9):
            row = k_ref[pl.ds(9 * plane + tap, 1), :]
            taps_ref[9 * role + tap] = jnp.broadcast_to(row, taps_ref.shape[1:]).astype(CONV)


def conv_rows(sources, taps_ref, lanes, count, known=()):
    sums = [[None] * 3 for _ in range(count)]
    for role, rows in sources:
        taps = [taps_ref[9 * role + i, :, lanes] for i in range(9)]
        for j, row in enumerate(rows):
            if row is None:
                continue
            depth, width = row.shape
            row = row.astype(CONV).reshape(depth // REPEAT, REPEAT, width)
            for out in range(max(0, j - 2), min(count, j + 1)):
                for c in range(3):
                    term = row * taps[3 * (j - out) + c]
                    sums[out][c] = term if sums[out][c] is None else sums[out][c] + term
    for out, row in enumerate(known):
        sums[out][1] = sums[out][1] + row.astype(CONV).reshape(sums[out][1].shape)
    position = lax.broadcasted_iota(jnp.int32, (8, width), 0)
    results = []
    for out in range(count):
        before, here, after = (s.astype(F32).reshape(depth, width) for s in sums[out])
        before, after = pltpu.roll(before, 1, 0), pltpu.roll(after, depth - 1, 0)
        low = jnp.where(position == 0, 0.0, before[:8])
        high = jnp.where(position == 7, 0.0, after[depth - 8 :])
        before = jnp.concatenate([low, before[8:]], axis=0)
        after = jnp.concatenate([after[: depth - 8], high], axis=0)
        results.append(here + before + after)
    return results


def channel_blocks(channels):
    return [slice(i, i + BLOCK) for i in range(0, channels, BLOCK)]


def inner_row(ref, plane, y, lanes, inside=None):
    if inside is None:
        return ref[plane, y, :, lanes]
    row = ref[plane, jnp.clip(y, 0, ref.shape[1] - 1), :, lanes].astype(F32)
    return (row * jnp.where(inside, 1.0, 0.0)).astype(BF16)


def nt_dot(a, b):
    return lax.dot_general(a, b, (((1,), (1,)), ((), ())), preferred_element_type=F32)


def assign(hid, map_ref, mass_ref):
    cells = hid.shape[0]
    slices = map_ref.shape[0] - TILE
    raw = nt_dot(map_ref[...], hid)
    soft = raw[slices : slices + 8]
    temperature = 0.25 + jnp.maximum(soft, 0.0) + jnp.log(1.0 + jnp.exp(-jnp.abs(soft)))
    scale = (1.0 / math.log(2.0)) / temperature
    raw = raw[:slices].reshape(slices // 8, 8, cells)
    top = jnp.max(jnp.max(raw, axis=0), axis=0, keepdims=True)
    powers = jnp.exp2((raw - top[None]) * scale[None])
    total = jnp.sum(jnp.sum(powers, axis=0), axis=0, keepdims=True)
    probs = (powers * (1.0 / total)[None]).reshape(slices, cells)
    mass = probs[:, :LANES]
    for start in range(LANES, cells, LANES):
        mass = mass + probs[:, start : start + LANES]
    mass_ref[...] += mass
    return probs.astype(BF16)


def ends_kernel(me_ref, _, x_ref, k_ref, near_ref, partial_ref, taps_ref):
    planes, height, depth, channels = x_ref.shape
    odd = me_ref[0] & 1

    def row(y, carry):
        near_ref[0, y] = x_ref[(planes - 1) * (1 - odd), y]
        return carry

    lax.fori_loop(0, height, row, 0)
    spread_taps(k_ref, range(3), taps_ref)
    for which, known in enumerate((((1, 0), (2, 1)), ((0, planes - 2), (1, planes - 1)))):
        def put(y, lanes, rows, known=known, which=which):
            sources = [(role, [None if b is None else x_ref[p, y + b, :, lanes] for b in rows])
                       for role, p in known]
            totals = conv_rows(sources, taps_ref, lanes, len(rows) - 2)
            for i, total in enumerate(totals):
                start = (y + i) * depth
                start = start if isinstance(y, int) else pl.multiple_of(start, depth)
                partial_ref[which, pl.ds(start, depth), lanes] = total.astype(BF16)

        for lanes in channel_blocks(channels):
            put(0, lanes, (None, 0, 1))
            put(height - 1, lanes, (-1, 0, None))

        def pair(i, carry, put=put):
            for lanes in channel_blocks(channels):
                put(2 * i + 1, lanes, (-1, 0, 1, 2))
            return carry

        lax.fori_loop(0, (height - 2) // 2, pair, 0)


def ends_call(me, after, x, taps):
    planes, height, depth, channels = x.shape
    cells = height * depth
    return pl.pallas_call(
        ends_kernel,
        in_specs=[SMEM, pl.BlockSpec(memory_space=pl.ANY)] + [VMEM] * 2,
        out_specs=[VMEM] * 2,
        out_shape=[
            jax.ShapeDtypeStruct((1, height, depth, channels), BF16),
            jax.ShapeDtypeStruct((2, cells, channels), BF16),
        ],
        scratch_shapes=[pltpu.VMEM((27, REPEAT, channels), CONV)],
        cost_estimate=pl.CostEstimate(
            flops=cells * channels * 12000, bytes_accessed=8 * cells * channels, transcendentals=0
        ),
        compiler_params=pltpu.CompilerParams(vmem_limit_bytes=LIMIT),
        name="ends",
    )(me, after, x, taps)


def reverse_lowest(value, bits):
    return ((value & ((1 << (bits - 1)) - 1)) << 1) | (value >> (bits - 1))


def inside_kernel(bits, x_ref, k_ref, affinity_ref, softness_ref, probs_ref, sums_ref, mass_ref, map_ref,
                  taps_ref, even_ref, odd_ref, hid_ref, by_slice_ref):
    planes, height, depth, channels = x_ref.shape
    slices = affinity_ref.shape[1]
    spread_taps(k_ref, range(3), taps_ref)
    run = slices >> bits
    new = lax.broadcasted_iota(jnp.int32, (slices, 1), 0)
    old = lax.broadcasted_iota(jnp.int32, (slices, slices), 1)
    place = new & (run - 1)
    owner = reverse_lowest(new >> (run.bit_length() - 1), bits)
    order = (old == owner * run + place).astype(BF16)
    map_ref[:slices] = (0.5 * nt_dot(order, affinity_ref[...])).astype(BF16)
    softness = softness_ref[...].astype(BF16).astype(F32)
    map_ref[slices:] = jnp.broadcast_to(0.5 * softness, (TILE, channels)).astype(BF16)

    sums_ref[...] = jnp.zeros(sums_ref.shape, F32)
    mass_ref[...] = jnp.zeros(mass_ref.shape, F32)
    groups = height // GROUP
    cells = GROUP * depth

    def conv(t, hid_ref):
        plane, first = t // groups, lax.rem(t, groups) * GROUP
        for lanes in channel_blocks(channels):
            for j in range(0, GROUP, 2):
                sources = []
                for role in range(3):
                    rows = []
                    for b in (-1, 0, 1, 2):
                        y, ok = first + j + b, None
                        if j + b < 0:
                            ok = first > 0
                        elif j + b >= GROUP:
                            ok = first + GROUP < height
                        rows.append(inner_row(x_ref, plane + role, y, lanes, ok))
                    sources.append((role, rows))
                for i, total in enumerate(conv_rows(sources, taps_ref, lanes, 2)):
                    hid_ref[(j + i) * depth : (j + i + 1) * depth, lanes] = gelu(total.astype(BF16))

    def share(t, source_ref, at):
        hid = source_ref[...]
        by_slice = assign(hid, map_ref, mass_ref)
        start = pl.multiple_of(lax.rem(t, groups) * cells, cells)
        probs_ref[t // groups, pl.ds(start, cells), :] = by_slice.T
        hid_ref[at, :] = hid
        by_slice_ref[:, at] = by_slice

    count = (planes - 2) * groups
    conv(jnp.int32(0), even_ref)

    def two(s, carry):
        t = 2 * s
        share(t, even_ref, slice(0, cells))
        conv(t + 1, odd_ref)
        share(t + 1, odd_ref, slice(cells, 2 * cells))
        sums_ref[...] += dot(by_slice_ref[...], hid_ref[...])
        conv(jnp.minimum(t + 2, count - 1), even_ref)
        return carry

    lax.fori_loop(0, count // 2, two, 0)


def inside_call(x, taps, affinity, softness, bits):
    planes, height, depth, channels = x.shape
    slices = affinity.shape[1]
    cells = height * depth
    work = planes * cells * channels
    return pl.pallas_call(
        functools.partial(inside_kernel, bits),
        in_specs=[VMEM] * 4,
        out_specs=[VMEM] * 4,
        out_shape=[
            jax.ShapeDtypeStruct((planes - 2, cells, slices), BF16),
            jax.ShapeDtypeStruct((slices, channels), F32),
            jax.ShapeDtypeStruct((slices, LANES), F32),
            jax.ShapeDtypeStruct((slices + TILE, channels), BF16),
        ],
        scratch_shapes=[
            pltpu.VMEM((27, REPEAT, channels), CONV),
            pltpu.VMEM((GROUP * depth, channels), BF16),
            pltpu.VMEM((GROUP * depth, channels), BF16),
            pltpu.VMEM((2 * GROUP * depth, channels), BF16),
            pltpu.VMEM((slices, 2 * GROUP * depth), BF16),
        ],
        cost_estimate=pl.CostEstimate(
            flops=work * 7000, bytes_accessed=2 * work, transcendentals=2 * work
        ),
        compiler_params=pltpu.CompilerParams(vmem_limit_bytes=LIMIT),
        name="inside",
    )(x, taps, affinity, softness)


def edge_kernel(is_far, me_ref, halo_ref, partial_ref, k_ref, map_ref, sums_in_ref, mass_in_ref, *rest):
    if is_far:
        by_slice_ref, send_ref, sums_ref, mass_ref, hid_ref, taps_ref = rest
    else:
        probs_ref, sums_ref, mass_ref, taps_ref, hid_ref, by_slice_ref = rest
    _, height, depth, channels = halo_ref.shape
    slices = sums_in_ref.shape[0]
    odd = me_ref[0] & 1
    side = odd if is_far else 1 - odd
    spread_taps(k_ref, [2 * side], taps_ref)
    mass_ref[...] = mass_in_ref[...]
    cells = GROUP * depth
    most = height * depth - cells

    def conv(first):
        for lanes in channel_blocks(channels):
            for y in range(first, first + GROUP, 2):
                rows = [halo_ref[0, y + b, :, lanes] if 0 <= y + b < height else None
                        for b in (-1, 0, 1, 2)]
                ats = [slice((y + i) * depth, (y + i + 1) * depth) for i in range(2)]
                known = [partial_ref[side, at, lanes] for at in ats]
                for at, total in zip(ats, conv_rows([(0, rows)], taps_ref, lanes, 2, known)):
                    hid_ref[at, lanes] = gelu(total.astype(BF16))

    conv(0)
    for first in range(0, height, GROUP):
        if first + GROUP < height:
            conv(first + GROUP)
        group = slice(first * depth, first * depth + cells)
        by_slice = assign(hid_ref[group], map_ref, mass_ref)
        if not is_far:
            probs_ref[0, group] = by_slice.T
        by_slice_ref[:, group] = by_slice
        if group.stop == most:
            sums_ref[...] = sums_in_ref[...] + dot(by_slice_ref[:, :most], hid_ref[:most])
    if not is_far:
        sums_ref[...] += dot(by_slice_ref[:, most:], hid_ref[most:])
        return
    write_share(1 - odd, cells, by_slice_ref, hid_ref, sums_ref, mass_ref, send_ref)


def write_share(side, left, by_slice_ref, hid_ref, sums_ref, mass_ref, share_ref):
    slices, channels = sums_ref.shape
    most = hid_ref.shape[0] - left
    owners, rows, _ = share_ref.shape
    held = channels // LANES
    rows = (rows - 8) // held
    start = pl.multiple_of(side * (slices // 2), slices // 2)
    mine = pl.ds(start, slices // 2)
    total = sums_ref[mine, :] + dot(by_slice_ref[mine, most:], hid_ref[most:])
    for i in range(held):
        part = total[:, i * LANES : (i + 1) * LANES].astype(share_ref.dtype)
        share_ref[:, i * rows : (i + 1) * rows, :] = part.reshape(owners, rows, LANES)
    tiles = rows // 8
    lane = lax.broadcasted_iota(jnp.int32, (8, LANES), 1)
    mass = mass_ref[mine, :]
    for owner in range(owners):
        tail = None
        for g in range(tiles):
            tile = mass[owner * rows + 8 * g : owner * rows + 8 * (g + 1)]
            width = LANES
            while width > LANES // tiles:
                width //= 2
                tile = tile + pltpu.roll(tile, width, 1)
            tail = tile if tail is None else jnp.where(lane >= g * width, tile, tail)
        share_ref[owner, held * rows :, :] = tail.astype(share_ref.dtype)


def keep_kernel(left, me_ref, by_slice_ref, hid_ref, sums_ref, mass_ref, keep_ref, probs_ref):
    write_share(me_ref[0] & 1, left, by_slice_ref, hid_ref, sums_ref, mass_ref, keep_ref)
    probs_ref[0] = by_slice_ref[...].T


def keep_call(me, by_slice, hid, sums, mass, shape, left):
    slices, cells = by_slice.shape
    return pl.pallas_call(
        functools.partial(keep_kernel, left),
        in_specs=[SMEM] + [VMEM] * 4,
        out_specs=[VMEM, VMEM],
        out_shape=[jax.ShapeDtypeStruct(shape, F32), jax.ShapeDtypeStruct((1, cells, slices), BF16)],
        cost_estimate=pl.CostEstimate(flops=2**28, bytes_accessed=2**21, transcendentals=0),
        compiler_params=pltpu.CompilerParams(vmem_limit_bytes=LIMIT),
        name="keep",
    )(me, by_slice, hid, sums, mass)


def edge_call(is_far, me, halo, taps, maps, partial, sums, mass, owners):
    _, height, depth, channels = halo.shape
    slices = sums.shape[0]
    cells = height * depth
    hidden, by_slice = ((cells, channels), BF16), ((slices, cells), BF16)
    carry = [(s.shape, F32) for s in (sums, mass)]
    scratch = [((9, REPEAT, channels), CONV)]
    if is_far:
        rows = channels // LANES * (slices // owners) + 8
        outs = [by_slice, ((owners // 2, rows, LANES), BF16)] + carry + [hidden]
    else:
        outs = [((1, cells, slices), BF16)] + carry
        scratch += [hidden, by_slice]
    return pl.pallas_call(
        functools.partial(edge_kernel, is_far),
        in_specs=[SMEM] + [VMEM] * 6,
        out_specs=[VMEM] * len(outs),
        out_shape=[jax.ShapeDtypeStruct(*o) for o in outs],
        scratch_shapes=[pltpu.VMEM(*o) for o in scratch],
        cost_estimate=pl.CostEstimate(
            flops=cells * channels * 16000, bytes_accessed=4 * cells * channels,
            transcendentals=2 * cells * channels,
        ),
        compiler_params=pltpu.CompilerParams(vmem_limit_bytes=LIMIT),
        name="far" if is_far else "near",
    )(me, halo, partial, taps, maps, sums, mass)


def merge_kernel(keep_ref, other_ref, out_ref):
    out_ref[...] = (keep_ref[...] + other_ref[...].astype(F32)).astype(BF16)


def merge_call(keep, other):
    return pl.pallas_call(
        merge_kernel,
        in_specs=[VMEM, VMEM],
        out_specs=VMEM,
        out_shape=jax.ShapeDtypeStruct(keep.shape, BF16),
        compiler_params=pltpu.CompilerParams(vmem_limit_bytes=LIMIT),
        name="merge",
    )(keep, other)


def owner_kernel(parts_ref, gain_ref, content_ref, widening_ref,
                 narrowing_ref, final_ref, out_ref, mapped_ref):
    channels = content_ref.shape[0]
    held = channels // LANES
    rows = out_ref.shape[0]
    total = jnp.sum(parts_ref[...].astype(F32), axis=0)
    pooled = jnp.concatenate([total[i * rows : (i + 1) * rows] for i in range(held)], axis=1)
    tail = total[held * rows :]
    lane = lax.broadcasted_iota(jnp.int32, (8, LANES), 1)
    width = LANES // (rows // 8)
    mass = jnp.concatenate([
        jnp.sum(jnp.where((lane >= g) & (lane < g + width), tail, 0.0), axis=1, keepdims=True)
        for g in range(0, LANES, width)
    ], axis=0)
    pooled = 0.5 * pooled / (mass + epsilon)
    high = pooled.astype(BF16)
    low = (pooled - high.astype(F32)).astype(BF16)
    tokens = dot(jnp.concatenate([high, low], axis=0), content_ref[...])
    tokens = tokens[:rows] + tokens[rows:]
    center = jnp.mean(tokens, axis=-1, keepdims=True)
    spread = jnp.mean((tokens - center) ** 2, axis=-1, keepdims=True)
    normed = ((tokens - center) * (1.0 / jnp.sqrt(spread + epsilon)) * gain_ref[...]).astype(BF16)
    inner = (0.5 * gelu(dot(normed, widening_ref[...]))).astype(BF16)
    out = (tokens + dot(inner, narrowing_ref[...])).astype(BF16)
    out_ref[...] = out
    mapped = dot(out, final_ref[...]).astype(BF16)
    mapped_ref[...] = jnp.broadcast_to(mapped[None], mapped_ref.shape)


def owner_call(parts, gain, *weights):
    channels = weights[0].shape[0]
    owners = parts.shape[0]
    rows = (parts.shape[1] - 8) // (channels // LANES)
    return pl.pallas_call(
        owner_kernel,
        in_specs=[VMEM] * 6,
        out_specs=[VMEM, VMEM],
        out_shape=[
            jax.ShapeDtypeStruct((rows, channels), BF16),
            jax.ShapeDtypeStruct((owners, rows, channels), BF16),
        ],
        compiler_params=pltpu.CompilerParams(vmem_limit_bytes=LIMIT),
        name="owner",
    )(parts, gain, *weights)


def ahead_kernel(me_ref, x_ref, inside_ref, near_ref, own_ref, out_ref):
    planes = x_ref.shape[0]
    half = own_ref.shape[0]
    odd = me_ref[0] & 1
    columns = pl.ds(pl.multiple_of(odd * half, half), half)

    def step(i, carry):
        change = dot(inside_ref[i, :, columns], own_ref[...])
        out_ref[i] = x_ref[i + 1].astype(F32) + change
        return carry

    lax.fori_loop(0, planes - 2, step, 0)
    change = dot(near_ref[0, :, columns], own_ref[...])
    out_ref[planes - 2] = x_ref[(planes - 1) * (1 - odd)].astype(F32) + change


def ahead_call(me, x, inside, near, own):
    planes, cells, channels = x.shape
    return pl.pallas_call(
        ahead_kernel,
        in_specs=[SMEM] + [VMEM] * 4,
        out_specs=VMEM,
        out_shape=jax.ShapeDtypeStruct((planes - 1, cells, channels), F32),
        cost_estimate=pl.CostEstimate(flops=2**30, bytes_accessed=2**23, transcendentals=0),
        compiler_params=pltpu.CompilerParams(vmem_limit_bytes=LIMIT),
        name="ahead",
    )(me, x, inside, near, own)


def update_kernel(me_ref, x_ref, ahead_ref, inside_ref, near_ref, far_ref, own_ref, other_ref, out_ref,
                  done_ref, mapped_ref, sem):
    planes, cells, channels = x_ref.shape
    half = own_ref.shape[0]
    odd = me_ref[0] & 1
    mine = pl.ds(pl.multiple_of(odd * half, half), half)
    others = pl.ds(pl.multiple_of((1 - odd) * half, half), half)
    mapped_ref[mine] = own_ref[...]
    mapped_ref[others] = other_ref[...]

    pieces = 2
    rows = cells // pieces
    near, far = (planes - 1) * (1 - odd), (planes - 1) * odd

    def store(plane, piece):
        at = pl.ds(pl.multiple_of(piece * rows, rows), rows)
        return pltpu.make_async_copy(
            done_ref.at[plane, at], out_ref.at[plane, at], sem.at[plane * pieces + piece]
        )

    def step(i, carry):
        part, piece = i // pieces, lax.rem(i, pieces)
        at = pl.ds(pl.multiple_of(piece * rows, rows), rows)
        total = ahead_ref[part, at, :] + dot(inside_ref[part, at, others], other_ref[...])
        done_ref[part + 1, at, :] = total.astype(BF16)
        store(part + 1, piece).start()
        return carry

    lax.fori_loop(0, (planes - 2) * pieces, step, 0)
    for piece in range(pieces):
        at = pl.ds(piece * rows, rows)
        total = ahead_ref[planes - 2, at, :] + dot(near_ref[0, at, others], other_ref[...])
        done_ref[near, at, :] = total.astype(BF16)
        store(near, piece).start()
    for piece in range(pieces):
        at = pl.ds(piece * rows, rows)
        change = dot(far_ref[0, at], mapped_ref[...])
        done_ref[far, at, :] = (x_ref[far, at, :].astype(F32) + change).astype(BF16)
        store(far, piece).start()

    def finish(i, carry):
        store(i // pieces, lax.rem(i, pieces)).wait()
        return carry

    lax.fori_loop(0, planes * pieces, finish, 0)


def update_call(me, x, ahead, inside, near, far, own, other):
    planes, cells, channels = x.shape
    return pl.pallas_call(
        update_kernel,
        in_specs=[SMEM] + [VMEM] * 7,
        out_specs=HBM,
        out_shape=jax.ShapeDtypeStruct(x.shape, BF16),
        scratch_shapes=[
            pltpu.VMEM(x.shape, BF16),
            pltpu.VMEM((2 * own.shape[0], channels), BF16),
            pltpu.SemaphoreType.DMA((2 * planes,)),
        ],
        compiler_params=pltpu.CompilerParams(vmem_limit_bytes=LIMIT),
        name="update",
    )(me, x, ahead, inside, near, far, own, other)


def per_device(
    mesh_feature_array,
    stencil_coefficients,
    partition_affinity_matrix,
    softness_mapping_matrix,
    content_mapping_matrix,
    layernorm_multiplier,
    widening_matrix,
    narrowing_matrix,
    final_mapping_matrix,
):
    x = mesh_feature_array
    planes, height, depth, channels = x.shape
    slices = partition_affinity_matrix.shape[1]
    n = lax.axis_size("gx")
    me = lax.axis_index("gx").astype(jnp.int32)[None]
    far_pairs = [p for i in range(1, n - 1, 2) for p in ((i, i + 1), (i + 1, i))]
    near_pairs = [p for i in range(0, n, 2) for p in ((i, i + 1), (i + 1, i))]
    far_plane = lax.dynamic_slice_in_dim(x, (planes - 1) * (me[0] & 1), 1)
    far_halo = lax.ppermute(far_plane, "gx", far_pairs)

    owners = min(n // 2, slices // 2 // TILE)
    share = n // 2 // owners
    groups = [[2 * (share * j + s) + h for j in range(owners)] for h in range(2) for s in range(share)]
    taps = stencil_coefficients
    near_plane, partial = ends_call(me, far_plane, x, taps)
    near_halo = lax.ppermute(near_plane, "gx", near_pairs)
    inside_probs, sums, mass, maps = inside_call(
        x, taps, partition_affinity_matrix, softness_mapping_matrix[None], n.bit_length() - 1
    )
    near_probs, sums, mass = edge_call(
        False, me, near_halo, taps, maps, partial, sums, mass, 2 * owners
    )
    by_slice, send, sums, mass, hid = edge_call(
        True, me, far_halo, taps, maps, partial, sums, mass, 2 * owners
    )

    received = lax.ppermute(send, "gx", near_pairs)
    keep, far_probs = keep_call(me, by_slice, hid, sums, mass, send.shape, GROUP * depth)
    parts = merge_call(keep, received)
    parts = lax.all_to_all(parts, "gx", 0, 0, axis_index_groups=groups)
    if share > 1:
        sharers = [[2 * (share * j + s) + h for s in range(share)]
                   for h in range(2) for j in range(owners)]
        parts = lax.psum(parts, "gx", axis_index_groups=sharers)
    own_out, mapped = owner_call(
        parts, layernorm_multiplier[None],
        content_mapping_matrix, widening_matrix, narrowing_matrix, final_mapping_matrix,
    )
    if share > 1:
        place = lax.rem(me[0] // 2, share) * (slices // n)
        own_out = lax.dynamic_slice_in_dim(own_out, place, slices // n)
    mapped = lax.all_to_all(mapped, "gx", 0, 0, axis_index_groups=groups).reshape(slices // 2, channels)
    other = lax.ppermute(mapped, "gx", near_pairs)
    planes_of_cells = x.reshape(planes, height * depth, channels)
    ahead = ahead_call(me, planes_of_cells, inside_probs, near_probs, mapped)
    updated = update_call(
        me, planes_of_cells, ahead, inside_probs, near_probs, far_probs, mapped, other
    )
    return updated.reshape(x.shape), own_out


def solution(mesh):
    return jax.shard_map(
        per_device,
        mesh=mesh,
        in_specs=(P(("grp", "gx"), None, None, None), P(), P(), P(), P(), P(), P(), P(), P()),
        out_specs=(P(("grp", "gx"), None, None, None), P(("grp", "gx"), None)),
        check_vma=False,
    )
```

```python
import functools
import math

import jax
import jax.numpy as jnp
from jax import lax
from jax.experimental import pallas as pl
from jax.experimental.pallas import tpu as pltpu
from jax.sharding import PartitionSpec as P

epsilon = 1e-05
LANES = 128
BLOCK = 256
GROUP = 8
TILE = 16
REPEAT = 8
MIB = 2**20
LIMIT = 32 * MIB
F32, BF16 = jnp.float32, jnp.bfloat16
CONV = BF16
VMEM = pl.BlockSpec(memory_space=pltpu.VMEM)
SMEM = pl.BlockSpec(memory_space=pltpu.SMEM)
HBM = pl.BlockSpec(memory_space=pltpu.HBM)


def dot(a, b):
    return jnp.dot(a, b, preferred_element_type=F32)


def gelu(x):
    inner = x * (x * x * (0.044715 * math.sqrt(2 / math.pi)) + math.sqrt(2 / math.pi))
    return x + x * jnp.tanh(inner)


def spread_taps(k_ref, planes, taps_ref):
    for role, plane in enumerate(planes):
        for tap in range(9):
            row = k_ref[pl.ds(9 * plane + tap, 1), :]
            taps_ref[9 * role + tap] = jnp.broadcast_to(row, taps_ref.shape[1:]).astype(CONV)


def conv_rows(sources, taps_ref, lanes, count, known=()):
    sums = [[None] * 3 for _ in range(count)]
    for role, rows in sources:
        taps = [taps_ref[9 * role + i, :, lanes] for i in range(9)]
        for j, row in enumerate(rows):
            if row is None:
                continue
            depth, width = row.shape
            row = row.astype(CONV).reshape(depth // REPEAT, REPEAT, width)
            for out in range(max(0, j - 2), min(count, j + 1)):
                for c in range(3):
                    term = row * taps[3 * (j - out) + c]
                    sums[out][c] = term if sums[out][c] is None else sums[out][c] + term
    for out, row in enumerate(known):
        sums[out][1] = sums[out][1] + row.astype(CONV).reshape(sums[out][1].shape)
    position = lax.broadcasted_iota(jnp.int32, (8, width), 0)
    results = []
    for out in range(count):
        before, here, after = (s.astype(F32).reshape(depth, width) for s in sums[out])
        before, after = pltpu.roll(before, 1, 0), pltpu.roll(after, depth - 1, 0)
        low = jnp.where(position == 0, 0.0, before[:8])
        high = jnp.where(position == 7, 0.0, after[depth - 8 :])
        before = jnp.concatenate([low, before[8:]], axis=0)
        after = jnp.concatenate([after[: depth - 8], high], axis=0)
        results.append(here + before + after)
    return results


def channel_blocks(channels):
    return [slice(i, i + BLOCK) for i in range(0, channels, BLOCK)]


def inner_row(ref, plane, y, lanes, inside=None):
    if inside is None:
        return ref[plane, y, :, lanes]
    row = ref[plane, jnp.clip(y, 0, ref.shape[1] - 1), :, lanes].astype(F32)
    return (row * jnp.where(inside, 1.0, 0.0)).astype(BF16)


def nt_dot(a, b):
    return lax.dot_general(a, b, (((1,), (1,)), ((), ())), preferred_element_type=F32)


def assign_steps(hid, map_ref, mass_ref, result):
    cells = hid.shape[0]
    slices = map_ref.shape[0] - TILE
    raw = nt_dot(map_ref[...], hid)
    yield
    soft = raw[slices : slices + 8]
    temperature = 0.25 + jnp.maximum(soft, 0.0) + jnp.log(1.0 + jnp.exp(-jnp.abs(soft)))
    scale = (1.0 / math.log(2.0)) / temperature
    raw = raw[:slices].reshape(slices // 8, 8, cells)
    top = jnp.max(jnp.max(raw, axis=0), axis=0, keepdims=True)
    yield
    powers = jnp.exp2((raw - top[None]) * scale[None])
    total = jnp.sum(jnp.sum(powers, axis=0), axis=0, keepdims=True)
    yield
    probs = (powers * (1.0 / total)[None]).reshape(slices, cells)
    mass = probs[:, :LANES]
    for start in range(LANES, cells, LANES):
        mass = mass + probs[:, start : start + LANES]
    mass_ref[...] += mass
    result.append(probs.astype(BF16))


def assign(hid, map_ref, mass_ref):
    result = []
    for _ in assign_steps(hid, map_ref, mass_ref, result):
        pass
    return result[0]


def ends_kernel(me_ref, _, x_ref, k_ref, near_ref, partial_ref, taps_ref):
    planes, height, depth, channels = x_ref.shape
    odd = me_ref[0] & 1

    def row(y, carry):
        near_ref[0, y] = x_ref[(planes - 1) * (1 - odd), y]
        return carry

    lax.fori_loop(0, height, row, 0)
    spread_taps(k_ref, range(3), taps_ref)
    for which, known in enumerate((((1, 0), (2, 1)), ((0, planes - 2), (1, planes - 1)))):
        def put(y, lanes, rows, known=known, which=which):
            sources = [(role, [None if b is None else x_ref[p, y + b, :, lanes] for b in rows])
                       for role, p in known]
            totals = conv_rows(sources, taps_ref, lanes, len(rows) - 2)
            for i, total in enumerate(totals):
                start = (y + i) * depth
                start = start if isinstance(y, int) else pl.multiple_of(start, depth)
                partial_ref[which, pl.ds(start, depth), lanes] = total.astype(BF16)

        for lanes in channel_blocks(channels):
            put(0, lanes, (None, 0, 1))
            put(height - 1, lanes, (-1, 0, None))

        def pair(i, carry, put=put):
            for lanes in channel_blocks(channels):
                put(2 * i + 1, lanes, (-1, 0, 1, 2))
            return carry

        lax.fori_loop(0, (height - 2) // 2, pair, 0)


def ends_call(me, after, x, taps):
    planes, height, depth, channels = x.shape
    cells = height * depth
    return pl.pallas_call(
        ends_kernel,
        in_specs=[SMEM, pl.BlockSpec(memory_space=pl.ANY)] + [VMEM] * 2,
        out_specs=[VMEM] * 2,
        out_shape=[
            jax.ShapeDtypeStruct((1, height, depth, channels), BF16),
            jax.ShapeDtypeStruct((2, cells, channels), BF16),
        ],
        scratch_shapes=[pltpu.VMEM((27, REPEAT, channels), CONV)],
        cost_estimate=pl.CostEstimate(
            flops=cells * channels * 12000, bytes_accessed=8 * cells * channels, transcendentals=0
        ),
        compiler_params=pltpu.CompilerParams(vmem_limit_bytes=LIMIT),
        name="ends",
    )(me, after, x, taps)


def reverse_lowest(value, bits):
    return ((value & ((1 << (bits - 1)) - 1)) << 1) | (value >> (bits - 1))


def inside_kernel(bits, x_ref, k_ref, affinity_ref, softness_ref, probs_ref, sums_ref, mass_ref, map_ref,
                  taps_ref, even_ref, odd_ref, hid_ref, by_slice_ref):
    planes, height, depth, channels = x_ref.shape
    slices = affinity_ref.shape[1]
    spread_taps(k_ref, range(3), taps_ref)
    run = slices >> bits
    new = lax.broadcasted_iota(jnp.int32, (slices, 1), 0)
    old = lax.broadcasted_iota(jnp.int32, (slices, slices), 1)
    place = new & (run - 1)
    owner = reverse_lowest(new >> (run.bit_length() - 1), bits)
    order = (old == owner * run + place).astype(BF16)
    map_ref[:slices] = (0.5 * nt_dot(order, affinity_ref[...])).astype(BF16)
    softness = softness_ref[...].astype(BF16).astype(F32)
    map_ref[slices:] = jnp.broadcast_to(0.5 * softness, (TILE, channels)).astype(BF16)

    sums_ref[...] = jnp.zeros(sums_ref.shape, F32)
    mass_ref[...] = jnp.zeros(mass_ref.shape, F32)
    groups = height // GROUP
    cells = GROUP * depth

    def conv(t, hid_ref):
        plane, first = t // groups, lax.rem(t, groups) * GROUP
        for lanes in channel_blocks(channels):
            for j in range(0, GROUP, 2):
                sources = []
                for role in range(3):
                    rows = []
                    for b in (-1, 0, 1, 2):
                        y, ok = first + j + b, None
                        if j + b < 0:
                            ok = first > 0
                        elif j + b >= GROUP:
                            ok = first + GROUP < height
                        rows.append(inner_row(x_ref, plane + role, y, lanes, ok))
                    sources.append((role, rows))
                for i, total in enumerate(conv_rows(sources, taps_ref, lanes, 2)):
                    hid_ref[(j + i) * depth : (j + i + 1) * depth, lanes] = gelu(total.astype(BF16))

    def share(t, source_ref, at):
        hid = source_ref[...]
        by_slice = assign(hid, map_ref, mass_ref)
        start = pl.multiple_of(lax.rem(t, groups) * cells, cells)
        probs_ref[t // groups, pl.ds(start, cells), :] = by_slice.T
        hid_ref[at, :] = hid
        by_slice_ref[:, at] = by_slice

    count = (planes - 2) * groups
    conv(jnp.int32(0), even_ref)

    def two(s, carry):
        t = 2 * s
        share(t, even_ref, slice(0, cells))
        conv(t + 1, odd_ref)
        share(t + 1, odd_ref, slice(cells, 2 * cells))
        sums_ref[...] += dot(by_slice_ref[...], hid_ref[...])
        conv(jnp.minimum(t + 2, count - 1), even_ref)
        return carry

    lax.fori_loop(0, count // 2, two, 0)


def inside_call(x, taps, affinity, softness, bits):
    planes, height, depth, channels = x.shape
    slices = affinity.shape[1]
    cells = height * depth
    work = planes * cells * channels
    return pl.pallas_call(
        functools.partial(inside_kernel, bits),
        in_specs=[VMEM] * 4,
        out_specs=[VMEM] * 4,
        out_shape=[
            jax.ShapeDtypeStruct((planes - 2, cells, slices), BF16),
            jax.ShapeDtypeStruct((slices, channels), F32),
            jax.ShapeDtypeStruct((slices, LANES), F32),
            jax.ShapeDtypeStruct((slices + TILE, channels), BF16),
        ],
        scratch_shapes=[
            pltpu.VMEM((27, REPEAT, channels), CONV),
            pltpu.VMEM((GROUP * depth, channels), BF16),
            pltpu.VMEM((GROUP * depth, channels), BF16),
            pltpu.VMEM((2 * GROUP * depth, channels), BF16),
            pltpu.VMEM((slices, 2 * GROUP * depth), BF16),
        ],
        cost_estimate=pl.CostEstimate(
            flops=work * 7000, bytes_accessed=2 * work, transcendentals=2 * work
        ),
        compiler_params=pltpu.CompilerParams(vmem_limit_bytes=LIMIT),
        name="inside",
    )(x, taps, affinity, softness)


def edge_kernel(is_far, me_ref, halo_ref, partial_ref, k_ref, map_ref, sums_in_ref, mass_in_ref, *rest):
    if is_far:
        by_slice_ref, send_ref, sums_ref, mass_ref, hid_ref, taps_ref = rest
    else:
        probs_ref, sums_ref, mass_ref, taps_ref, hid_ref, by_slice_ref = rest
    _, height, depth, channels = halo_ref.shape
    slices = sums_in_ref.shape[0]
    odd = me_ref[0] & 1
    side = odd if is_far else 1 - odd
    spread_taps(k_ref, [2 * side], taps_ref)
    mass_ref[...] = mass_in_ref[...]
    cells = GROUP * depth
    most = height * depth - cells

    def conv_steps(first):
        for y in range(first, min(first + GROUP, height), 2):
            for lanes in channel_blocks(channels):
                rows = [halo_ref[0, y + b, :, lanes] if 0 <= y + b < height else None
                        for b in (-1, 0, 1, 2)]
                ats = [slice((y + i) * depth, (y + i + 1) * depth) for i in range(2)]
                known = [partial_ref[side, at, lanes] for at in ats]
                for at, total in zip(ats, conv_rows([(0, rows)], taps_ref, lanes, 2, known)):
                    hid_ref[at, lanes] = gelu(total.astype(BF16))
                yield

    for _ in conv_steps(0):
        pass
    for first in range(0, height, GROUP):
        group = slice(first * depth, first * depth + cells)
        result, conv = [], conv_steps(first + GROUP)
        for _ in assign_steps(hid_ref[group], map_ref, mass_ref, result):
            next(conv, None)
            next(conv, None)
        for _ in conv:
            pass
        by_slice, = result
        if not is_far:
            probs_ref[0, group] = by_slice.T
        by_slice_ref[:, group] = by_slice
        if group.stop == most:
            sums_ref[...] = sums_in_ref[...] + dot(by_slice_ref[:, :most], hid_ref[:most])
    if not is_far:
        sums_ref[...] += dot(by_slice_ref[:, most:], hid_ref[most:])
        return
    write_share(1 - odd, cells, by_slice_ref, hid_ref, sums_ref, mass_ref, send_ref)


def write_share(side, left, by_slice_ref, hid_ref, sums_ref, mass_ref, share_ref):
    slices, channels = sums_ref.shape
    most = hid_ref.shape[0] - left
    owners, rows, _ = share_ref.shape
    held = channels // LANES
    rows = (rows - 8) // held
    start = pl.multiple_of(side * (slices // 2), slices // 2)
    mine = pl.ds(start, slices // 2)
    total = sums_ref[mine, :] + dot(by_slice_ref[mine, most:], hid_ref[most:])
    for i in range(held):
        part = total[:, i * LANES : (i + 1) * LANES].astype(share_ref.dtype)
        share_ref[:, i * rows : (i + 1) * rows, :] = part.reshape(owners, rows, LANES)
    tiles = rows // 8
    lane = lax.broadcasted_iota(jnp.int32, (8, LANES), 1)
    mass = mass_ref[mine, :]
    for owner in range(owners):
        tail = None
        for g in range(tiles):
            tile = mass[owner * rows + 8 * g : owner * rows + 8 * (g + 1)]
            width = LANES
            while width > LANES // tiles:
                width //= 2
                tile = tile + pltpu.roll(tile, width, 1)
            tail = tile if tail is None else jnp.where(lane >= g * width, tile, tail)
        share_ref[owner, held * rows :, :] = tail.astype(share_ref.dtype)


def keep_kernel(left, me_ref, by_slice_ref, hid_ref, sums_ref, mass_ref, keep_ref, probs_ref):
    write_share(me_ref[0] & 1, left, by_slice_ref, hid_ref, sums_ref, mass_ref, keep_ref)
    probs_ref[0] = by_slice_ref[...].T


def keep_call(me, by_slice, hid, sums, mass, shape, left):
    slices, cells = by_slice.shape
    return pl.pallas_call(
        functools.partial(keep_kernel, left),
        in_specs=[SMEM] + [VMEM] * 4,
        out_specs=[VMEM, VMEM],
        out_shape=[jax.ShapeDtypeStruct(shape, F32), jax.ShapeDtypeStruct((1, cells, slices), BF16)],
        cost_estimate=pl.CostEstimate(flops=2**28, bytes_accessed=2**21, transcendentals=0),
        compiler_params=pltpu.CompilerParams(vmem_limit_bytes=LIMIT),
        name="keep",
    )(me, by_slice, hid, sums, mass)


def edge_call(is_far, me, halo, taps, maps, partial, sums, mass, owners):
    _, height, depth, channels = halo.shape
    slices = sums.shape[0]
    cells = height * depth
    hidden, by_slice = ((cells, channels), BF16), ((slices, cells), BF16)
    carry = [(s.shape, F32) for s in (sums, mass)]
    scratch = [((9, REPEAT, channels), CONV)]
    if is_far:
        rows = channels // LANES * (slices // owners) + 8
        outs = [by_slice, ((owners // 2, rows, LANES), BF16)] + carry + [hidden]
    else:
        outs = [((1, cells, slices), BF16)] + carry
        scratch += [hidden, by_slice]
    return pl.pallas_call(
        functools.partial(edge_kernel, is_far),
        in_specs=[SMEM] + [VMEM] * 6,
        out_specs=[VMEM] * len(outs),
        out_shape=[jax.ShapeDtypeStruct(*o) for o in outs],
        scratch_shapes=[pltpu.VMEM(*o) for o in scratch],
        cost_estimate=pl.CostEstimate(
            flops=cells * channels * 16000, bytes_accessed=4 * cells * channels,
            transcendentals=2 * cells * channels,
        ),
        compiler_params=pltpu.CompilerParams(vmem_limit_bytes=LIMIT),
        name="far" if is_far else "near",
    )(me, halo, partial, taps, maps, sums, mass)


def merge_kernel(keep_ref, other_ref, out_ref):
    out_ref[...] = (keep_ref[...] + other_ref[...].astype(F32)).astype(BF16)


def merge_call(keep, other):
    return pl.pallas_call(
        merge_kernel,
        in_specs=[VMEM, VMEM],
        out_specs=VMEM,
        out_shape=jax.ShapeDtypeStruct(keep.shape, BF16),
        compiler_params=pltpu.CompilerParams(vmem_limit_bytes=LIMIT),
        name="merge",
    )(keep, other)


def owner_kernel(parts_ref, gain_ref, content_ref, widening_ref,
                 narrowing_ref, final_ref, out_ref, mapped_ref):
    channels = content_ref.shape[0]
    held = channels // LANES
    rows = out_ref.shape[0]
    total = jnp.sum(parts_ref[...].astype(F32), axis=0)
    pooled = jnp.concatenate([total[i * rows : (i + 1) * rows] for i in range(held)], axis=1)
    tail = total[held * rows :]
    lane = lax.broadcasted_iota(jnp.int32, (8, LANES), 1)
    width = LANES // (rows // 8)
    mass = jnp.concatenate([
        jnp.sum(jnp.where((lane >= g) & (lane < g + width), tail, 0.0), axis=1, keepdims=True)
        for g in range(0, LANES, width)
    ], axis=0)
    pooled = 0.5 * pooled / (mass + epsilon)
    high = pooled.astype(BF16)
    low = (pooled - high.astype(F32)).astype(BF16)
    tokens = dot(jnp.concatenate([high, low], axis=0), content_ref[...])
    tokens = tokens[:rows] + tokens[rows:]
    center = jnp.mean(tokens, axis=-1, keepdims=True)
    spread = jnp.mean((tokens - center) ** 2, axis=-1, keepdims=True)
    normed = ((tokens - center) * (1.0 / jnp.sqrt(spread + epsilon)) * gain_ref[...]).astype(BF16)
    inner = (0.5 * gelu(dot(normed, widening_ref[...]))).astype(BF16)
    out = (tokens + dot(inner, narrowing_ref[...])).astype(BF16)
    out_ref[...] = out
    mapped = dot(out, final_ref[...]).astype(BF16)
    mapped_ref[...] = jnp.broadcast_to(mapped[None], mapped_ref.shape)


def owner_call(parts, gain, *weights):
    channels = weights[0].shape[0]
    owners = parts.shape[0]
    rows = (parts.shape[1] - 8) // (channels // LANES)
    return pl.pallas_call(
        owner_kernel,
        in_specs=[VMEM] * 6,
        out_specs=[VMEM, VMEM],
        out_shape=[
            jax.ShapeDtypeStruct((rows, channels), BF16),
            jax.ShapeDtypeStruct((owners, rows, channels), BF16),
        ],
        compiler_params=pltpu.CompilerParams(vmem_limit_bytes=LIMIT),
        name="owner",
    )(parts, gain, *weights)


def ahead_kernel(me_ref, x_ref, inside_ref, near_ref, own_ref, out_ref):
    planes = x_ref.shape[0]
    half = own_ref.shape[0]
    odd = me_ref[0] & 1
    columns = pl.ds(pl.multiple_of(odd * half, half), half)

    def step(i, carry):
        change = dot(inside_ref[i, :, columns], own_ref[...])
        out_ref[i] = x_ref[i + 1].astype(F32) + change
        return carry

    lax.fori_loop(0, planes - 2, step, 0)
    change = dot(near_ref[0, :, columns], own_ref[...])
    out_ref[planes - 2] = x_ref[(planes - 1) * (1 - odd)].astype(F32) + change


def ahead_call(me, x, inside, near, own):
    planes, cells, channels = x.shape
    return pl.pallas_call(
        ahead_kernel,
        in_specs=[SMEM] + [VMEM] * 4,
        out_specs=VMEM,
        out_shape=jax.ShapeDtypeStruct((planes - 1, cells, channels), F32),
        cost_estimate=pl.CostEstimate(flops=2**30, bytes_accessed=2**23, transcendentals=0),
        compiler_params=pltpu.CompilerParams(vmem_limit_bytes=LIMIT),
        name="ahead",
    )(me, x, inside, near, own)


def update_kernel(me_ref, x_ref, ahead_ref, inside_ref, near_ref, far_ref, own_ref, other_ref, out_ref,
                  done_ref, mapped_ref, sem):
    planes, cells, channels = x_ref.shape
    half = own_ref.shape[0]
    odd = me_ref[0] & 1
    mine = pl.ds(pl.multiple_of(odd * half, half), half)
    others = pl.ds(pl.multiple_of((1 - odd) * half, half), half)
    mapped_ref[mine] = own_ref[...]
    mapped_ref[others] = other_ref[...]

    pieces = 2
    rows = cells // pieces
    near, far = (planes - 1) * (1 - odd), (planes - 1) * odd

    def store(plane, piece):
        at = pl.ds(pl.multiple_of(piece * rows, rows), rows)
        return pltpu.make_async_copy(
            done_ref.at[plane, at], out_ref.at[plane, at], sem.at[plane * pieces + piece]
        )

    def step(i, carry):
        part, piece = i // pieces, lax.rem(i, pieces)
        at = pl.ds(pl.multiple_of(piece * rows, rows), rows)
        total = ahead_ref[part, at, :] + dot(inside_ref[part, at, others], other_ref[...])
        done_ref[part + 1, at, :] = total.astype(BF16)
        store(part + 1, piece).start()
        return carry

    lax.fori_loop(0, (planes - 2) * pieces, step, 0)
    for piece in range(pieces):
        at = pl.ds(piece * rows, rows)
        total = ahead_ref[planes - 2, at, :] + dot(near_ref[0, at, others], other_ref[...])
        done_ref[near, at, :] = total.astype(BF16)
        store(near, piece).start()
    for piece in range(pieces):
        at = pl.ds(piece * rows, rows)
        change = dot(far_ref[0, at], mapped_ref[...])
        done_ref[far, at, :] = (x_ref[far, at, :].astype(F32) + change).astype(BF16)
        store(far, piece).start()

    def finish(i, carry):
        store(i // pieces, lax.rem(i, pieces)).wait()
        return carry

    lax.fori_loop(0, planes * pieces, finish, 0)


def update_call(me, x, ahead, inside, near, far, own, other):
    planes, cells, channels = x.shape
    return pl.pallas_call(
        update_kernel,
        in_specs=[SMEM] + [VMEM] * 7,
        out_specs=HBM,
        out_shape=jax.ShapeDtypeStruct(x.shape, BF16),
        scratch_shapes=[
            pltpu.VMEM(x.shape, BF16),
            pltpu.VMEM((2 * own.shape[0], channels), BF16),
            pltpu.SemaphoreType.DMA((2 * planes,)),
        ],
        compiler_params=pltpu.CompilerParams(vmem_limit_bytes=LIMIT),
        name="update",
    )(me, x, ahead, inside, near, far, own, other)


def per_device(
    mesh_feature_array,
    stencil_coefficients,
    partition_affinity_matrix,
    softness_mapping_matrix,
    content_mapping_matrix,
    layernorm_multiplier,
    widening_matrix,
    narrowing_matrix,
    final_mapping_matrix,
):
    x = mesh_feature_array
    planes, height, depth, channels = x.shape
    slices = partition_affinity_matrix.shape[1]
    n = lax.axis_size("gx")
    me = lax.axis_index("gx").astype(jnp.int32)[None]
    far_pairs = [p for i in range(1, n - 1, 2) for p in ((i, i + 1), (i + 1, i))]
    near_pairs = [p for i in range(0, n, 2) for p in ((i, i + 1), (i + 1, i))]
    far_plane = lax.dynamic_slice_in_dim(x, (planes - 1) * (me[0] & 1), 1)
    far_halo = lax.ppermute(far_plane, "gx", far_pairs)

    owners = min(n // 2, slices // 2 // TILE)
    share = n // 2 // owners
    groups = [[2 * (share * j + s) + h for j in range(owners)] for h in range(2) for s in range(share)]
    taps = stencil_coefficients
    near_plane, partial = ends_call(me, far_plane, x, taps)
    near_halo = lax.ppermute(near_plane, "gx", near_pairs)
    inside_probs, sums, mass, maps = inside_call(
        x, taps, partition_affinity_matrix, softness_mapping_matrix[None], n.bit_length() - 1
    )
    near_probs, sums, mass = edge_call(
        False, me, near_halo, taps, maps, partial, sums, mass, 2 * owners
    )
    by_slice, send, sums, mass, hid = edge_call(
        True, me, far_halo, taps, maps, partial, sums, mass, 2 * owners
    )

    received = lax.ppermute(send, "gx", near_pairs)
    keep, far_probs = keep_call(me, by_slice, hid, sums, mass, send.shape, GROUP * depth)
    parts = merge_call(keep, received)
    parts = lax.all_to_all(parts, "gx", 0, 0, axis_index_groups=groups)
    if share > 1:
        sharers = [[2 * (share * j + s) + h for s in range(share)]
                   for h in range(2) for j in range(owners)]
        parts = lax.psum(parts, "gx", axis_index_groups=sharers)
    own_out, mapped = owner_call(
        parts, layernorm_multiplier[None],
        content_mapping_matrix, widening_matrix, narrowing_matrix, final_mapping_matrix,
    )
    if share > 1:
        place = lax.rem(me[0] // 2, share) * (slices // n)
        own_out = lax.dynamic_slice_in_dim(own_out, place, slices // n)
    mapped = lax.all_to_all(mapped, "gx", 0, 0, axis_index_groups=groups).reshape(slices // 2, channels)
    other = lax.ppermute(mapped, "gx", near_pairs)
    planes_of_cells = x.reshape(planes, height * depth, channels)
    ahead = ahead_call(me, planes_of_cells, inside_probs, near_probs, mapped)
    updated = update_call(
        me, planes_of_cells, ahead, inside_probs, near_probs, far_probs, mapped, other
    )
    return updated.reshape(x.shape), own_out


def solution(mesh):
    return jax.shard_map(
        per_device,
        mesh=mesh,
        in_specs=(P(("grp", "gx"), None, None, None), P(), P(), P(), P(), P(), P(), P(), P()),
        out_specs=(P(("grp", "gx"), None, None, None), P(("grp", "gx"), None)),
        check_vma=False,
    )
```

```python
import functools
import math

import jax
import jax.numpy as jnp
from jax import lax
from jax.experimental import pallas as pl
from jax.experimental.pallas import tpu as pltpu
from jax.sharding import PartitionSpec as P

epsilon = 1e-05
LANES = 128
BLOCK = 256
GROUP = 8
TILE = 16
REPEAT = 8
MIB = 2**20
LIMIT = 32 * MIB
F32, BF16 = jnp.float32, jnp.bfloat16
CONV = BF16
VMEM = pl.BlockSpec(memory_space=pltpu.VMEM)
SMEM = pl.BlockSpec(memory_space=pltpu.SMEM)
HBM = pl.BlockSpec(memory_space=pltpu.HBM)


def dot(a, b):
    return jnp.dot(a, b, preferred_element_type=F32)


def gelu(x):
    inner = x * (x * x * (0.044715 * math.sqrt(2 / math.pi)) + math.sqrt(2 / math.pi))
    return x + x * jnp.tanh(inner)


def spread_taps(k_ref, planes, taps_ref):
    for role, plane in enumerate(planes):
        for tap in range(9):
            row = k_ref[pl.ds(9 * plane + tap, 1), :]
            taps_ref[9 * role + tap] = jnp.broadcast_to(row, taps_ref.shape[1:]).astype(CONV)


def conv_rows(sources, taps_ref, lanes, count, known=()):
    sums = [[None] * 3 for _ in range(count)]
    for role, rows in sources:
        taps = [taps_ref[9 * role + i, :, lanes] for i in range(9)]
        for j, row in enumerate(rows):
            if row is None:
                continue
            depth, width = row.shape
            row = row.astype(CONV).reshape(depth // REPEAT, REPEAT, width)
            for out in range(max(0, j - 2), min(count, j + 1)):
                for c in range(3):
                    term = row * taps[3 * (j - out) + c]
                    sums[out][c] = term if sums[out][c] is None else sums[out][c] + term
    for out, row in enumerate(known):
        sums[out][1] = sums[out][1] + row.astype(CONV).reshape(sums[out][1].shape)
    position = lax.broadcasted_iota(jnp.int32, (8, width), 0)
    results = []
    for out in range(count):
        before, here, after = (s.astype(F32).reshape(depth, width) for s in sums[out])
        before, after = pltpu.roll(before, 1, 0), pltpu.roll(after, depth - 1, 0)
        low = jnp.where(position == 0, 0.0, before[:8])
        high = jnp.where(position == 7, 0.0, after[depth - 8 :])
        before = jnp.concatenate([low, before[8:]], axis=0)
        after = jnp.concatenate([after[: depth - 8], high], axis=0)
        results.append(here + before + after)
    return results


def channel_blocks(channels):
    return [slice(i, i + BLOCK) for i in range(0, channels, BLOCK)]


def inner_row(ref, plane, y, lanes, inside=None):
    if inside is None:
        return ref[plane, y, :, lanes]
    row = ref[plane, jnp.clip(y, 0, ref.shape[1] - 1), :, lanes].astype(F32)
    return (row * jnp.where(inside, 1.0, 0.0)).astype(BF16)


def nt_dot(a, b):
    return lax.dot_general(a, b, (((1,), (1,)), ((), ())), preferred_element_type=F32)


def assign_steps(hid, map_ref, mass_ref, result):
    cells = hid.shape[0]
    slices = map_ref.shape[0] - TILE
    raw = nt_dot(map_ref[...], hid)
    yield
    soft = raw[slices : slices + 8]
    temperature = 0.25 + jnp.maximum(soft, 0.0) + jnp.log(1.0 + jnp.exp(-jnp.abs(soft)))
    scale = (1.0 / math.log(2.0)) / temperature
    raw = raw[:slices].reshape(slices // 8, 8, cells)
    top = jnp.max(jnp.max(raw, axis=0), axis=0, keepdims=True)
    yield
    powers = jnp.exp2((raw - top[None]) * scale[None])
    total = jnp.sum(jnp.sum(powers, axis=0), axis=0, keepdims=True)
    yield
    probs = (powers * (1.0 / total)[None]).reshape(slices, cells)
    mass = probs[:, :LANES]
    for start in range(LANES, cells, LANES):
        mass = mass + probs[:, start : start + LANES]
    mass_ref[...] += mass
    result.append(probs.astype(BF16))


def assign(hid, map_ref, mass_ref):
    result = []
    for _ in assign_steps(hid, map_ref, mass_ref, result):
        pass
    return result[0]


def ends_kernel(me_ref, _, x_ref, k_ref, near_ref, partial_ref, taps_ref):
    planes, height, depth, channels = x_ref.shape
    odd = me_ref[0] & 1

    def row(y, carry):
        near_ref[0, y] = x_ref[(planes - 1) * (1 - odd), y]
        return carry

    lax.fori_loop(0, height, row, 0)
    spread_taps(k_ref, range(3), taps_ref)
    for which, known in enumerate((((1, 0), (2, 1)), ((0, planes - 2), (1, planes - 1)))):
        def put(y, lanes, rows, known=known, which=which):
            sources = [(role, [None if b is None else x_ref[p, y + b, :, lanes] for b in rows])
                       for role, p in known]
            totals = conv_rows(sources, taps_ref, lanes, len(rows) - 2)
            for i, total in enumerate(totals):
                start = (y + i) * depth
                start = start if isinstance(y, int) else pl.multiple_of(start, depth)
                partial_ref[which, pl.ds(start, depth), lanes] = total.astype(BF16)

        for lanes in channel_blocks(channels):
            put(0, lanes, (None, 0, 1))
            put(height - 1, lanes, (-1, 0, None))

        def pair(i, carry, put=put):
            for lanes in channel_blocks(channels):
                put(2 * i + 1, lanes, (-1, 0, 1, 2))
            return carry

        lax.fori_loop(0, (height - 2) // 2, pair, 0)


def ends_call(me, after, x, taps):
    planes, height, depth, channels = x.shape
    cells = height * depth
    return pl.pallas_call(
        ends_kernel,
        in_specs=[SMEM, pl.BlockSpec(memory_space=pl.ANY)] + [VMEM] * 2,
        out_specs=[VMEM] * 2,
        out_shape=[
            jax.ShapeDtypeStruct((1, height, depth, channels), BF16),
            jax.ShapeDtypeStruct((2, cells, channels), BF16),
        ],
        scratch_shapes=[pltpu.VMEM((27, REPEAT, channels), CONV)],
        cost_estimate=pl.CostEstimate(
            flops=cells * channels * 12000, bytes_accessed=8 * cells * channels, transcendentals=0
        ),
        compiler_params=pltpu.CompilerParams(vmem_limit_bytes=LIMIT),
        name="ends",
    )(me, after, x, taps)


def reverse_lowest(value, bits):
    return ((value & ((1 << (bits - 1)) - 1)) << 1) | (value >> (bits - 1))


def inside_kernel(bits, x_ref, k_ref, affinity_ref, softness_ref, probs_ref, sums_ref, mass_ref, map_ref,
                  taps_ref, even_ref, odd_ref, hid_ref, by_slice_ref):
    planes, height, depth, channels = x_ref.shape
    slices = affinity_ref.shape[1]
    spread_taps(k_ref, range(3), taps_ref)
    run = slices >> bits
    new = lax.broadcasted_iota(jnp.int32, (slices, 1), 0)
    old = lax.broadcasted_iota(jnp.int32, (slices, slices), 1)
    place = new & (run - 1)
    owner = reverse_lowest(new >> (run.bit_length() - 1), bits)
    order = (old == owner * run + place).astype(BF16)
    map_ref[:slices] = (0.5 * nt_dot(order, affinity_ref[...])).astype(BF16)
    softness = softness_ref[...].astype(BF16).astype(F32)
    map_ref[slices:] = jnp.broadcast_to(0.5 * softness, (TILE, channels)).astype(BF16)

    sums_ref[...] = jnp.zeros(sums_ref.shape, F32)
    mass_ref[...] = jnp.zeros(mass_ref.shape, F32)
    groups = height // GROUP
    cells = GROUP * depth

    def conv(t, hid_ref):
        plane, first = t // groups, lax.rem(t, groups) * GROUP
        for lanes in channel_blocks(channels):
            for j in range(0, GROUP, 2):
                sources = []
                for role in range(3):
                    rows = []
                    for b in (-1, 0, 1, 2):
                        y, ok = first + j + b, None
                        if j + b < 0:
                            ok = first > 0
                        elif j + b >= GROUP:
                            ok = first + GROUP < height
                        rows.append(inner_row(x_ref, plane + role, y, lanes, ok))
                    sources.append((role, rows))
                for i, total in enumerate(conv_rows(sources, taps_ref, lanes, 2)):
                    hid_ref[(j + i) * depth : (j + i + 1) * depth, lanes] = gelu(total.astype(BF16))

    def share(t, source_ref, at):
        hid = source_ref[...]
        by_slice = assign(hid, map_ref, mass_ref)
        start = pl.multiple_of(lax.rem(t, groups) * cells, cells)
        probs_ref[t // groups, pl.ds(start, cells), :] = by_slice.T
        hid_ref[at, :] = hid
        by_slice_ref[:, at] = by_slice

    count = (planes - 2) * groups
    conv(jnp.int32(0), even_ref)

    def two(s, carry):
        t = 2 * s
        share(t, even_ref, slice(0, cells))
        conv(t + 1, odd_ref)
        share(t + 1, odd_ref, slice(cells, 2 * cells))
        sums_ref[...] += dot(by_slice_ref[...], hid_ref[...])
        conv(jnp.minimum(t + 2, count - 1), even_ref)
        return carry

    lax.fori_loop(0, count // 2, two, 0)


def inside_call(x, taps, affinity, softness, bits):
    planes, height, depth, channels = x.shape
    slices = affinity.shape[1]
    cells = height * depth
    work = planes * cells * channels
    return pl.pallas_call(
        functools.partial(inside_kernel, bits),
        in_specs=[VMEM] * 4,
        out_specs=[VMEM] * 4,
        out_shape=[
            jax.ShapeDtypeStruct((planes - 2, cells, slices), BF16),
            jax.ShapeDtypeStruct((slices, channels), F32),
            jax.ShapeDtypeStruct((slices, LANES), F32),
            jax.ShapeDtypeStruct((slices + TILE, channels), BF16),
        ],
        scratch_shapes=[
            pltpu.VMEM((27, REPEAT, channels), CONV),
            pltpu.VMEM((GROUP * depth, channels), BF16),
            pltpu.VMEM((GROUP * depth, channels), BF16),
            pltpu.VMEM((2 * GROUP * depth, channels), BF16),
            pltpu.VMEM((slices, 2 * GROUP * depth), BF16),
        ],
        cost_estimate=pl.CostEstimate(
            flops=work * 7000, bytes_accessed=2 * work, transcendentals=2 * work
        ),
        compiler_params=pltpu.CompilerParams(vmem_limit_bytes=LIMIT),
        name="inside",
    )(x, taps, affinity, softness)


def edge_kernel(is_far, me_ref, halo_ref, partial_ref, k_ref, map_ref, sums_in_ref, mass_in_ref, *rest):
    if is_far:
        by_slice_ref, send_ref, sums_ref, mass_ref, hid_ref, taps_ref = rest
    else:
        probs_ref, sums_ref, mass_ref, taps_ref, hid_ref, by_slice_ref = rest
    _, height, depth, channels = halo_ref.shape
    slices = sums_in_ref.shape[0]
    odd = me_ref[0] & 1
    side = odd if is_far else 1 - odd
    spread_taps(k_ref, [2 * side], taps_ref)
    mass_ref[...] = mass_in_ref[...]
    cells = GROUP * depth
    most = height * depth - cells

    def conv_steps(first):
        for y in range(first, min(first + GROUP, height), 2):
            for lanes in channel_blocks(channels):
                rows = [halo_ref[0, y + b, :, lanes] if 0 <= y + b < height else None
                        for b in (-1, 0, 1, 2)]
                ats = [slice((y + i) * depth, (y + i + 1) * depth) for i in range(2)]
                known = [partial_ref[side, at, lanes] for at in ats]
                for at, total in zip(ats, conv_rows([(0, rows)], taps_ref, lanes, 2, known)):
                    hid_ref[at, lanes] = gelu(total.astype(BF16))
                yield

    for _ in conv_steps(0):
        pass
    for first in range(0, height, GROUP):
        group = slice(first * depth, first * depth + cells)
        result, conv = [], conv_steps(first + GROUP)
        for _ in assign_steps(hid_ref[group], map_ref, mass_ref, result):
            next(conv, None)
            next(conv, None)
        for _ in conv:
            pass
        by_slice, = result
        if not is_far:
            probs_ref[0, group] = by_slice.T
        by_slice_ref[:, group] = by_slice
        if group.stop == most:
            sums_ref[...] = sums_in_ref[...] + dot(by_slice_ref[:, :most], hid_ref[:most])
    if not is_far:
        sums_ref[...] += dot(by_slice_ref[:, most:], hid_ref[most:])
        return
    write_share(1 - odd, cells, by_slice_ref, hid_ref, sums_ref, mass_ref, send_ref)


def write_share(side, left, by_slice_ref, hid_ref, sums_ref, mass_ref, share_ref):
    slices, channels = sums_ref.shape
    most = hid_ref.shape[0] - left
    owners, rows, _ = share_ref.shape
    held = channels // LANES
    rows = (rows - 8) // held
    start = pl.multiple_of(side * (slices // 2), slices // 2)
    mine = pl.ds(start, slices // 2)
    total = sums_ref[mine, :] + dot(by_slice_ref[mine, most:], hid_ref[most:])
    for i in range(held):
        part = total[:, i * LANES : (i + 1) * LANES].astype(share_ref.dtype)
        share_ref[:, i * rows : (i + 1) * rows, :] = part.reshape(owners, rows, LANES)
    tiles = rows // 8
    lane = lax.broadcasted_iota(jnp.int32, (8, LANES), 1)
    mass = mass_ref[mine, :]
    for owner in range(owners):
        tail = None
        for g in range(tiles):
            tile = mass[owner * rows + 8 * g : owner * rows + 8 * (g + 1)]
            width = LANES
            while width > LANES // tiles:
                width //= 2
                tile = tile + pltpu.roll(tile, width, 1)
            tail = tile if tail is None else jnp.where(lane >= g * width, tile, tail)
        share_ref[owner, held * rows :, :] = tail.astype(share_ref.dtype)


def keep_kernel(left, me_ref, by_slice_ref, hid_ref, sums_ref, mass_ref, keep_ref, probs_ref):
    write_share(me_ref[0] & 1, left, by_slice_ref, hid_ref, sums_ref, mass_ref, keep_ref)
    probs_ref[0] = by_slice_ref[...].T


def keep_call(me, by_slice, hid, sums, mass, shape, left):
    slices, cells = by_slice.shape
    return pl.pallas_call(
        functools.partial(keep_kernel, left),
        in_specs=[SMEM] + [VMEM] * 4,
        out_specs=[VMEM, VMEM],
        out_shape=[jax.ShapeDtypeStruct(shape, F32), jax.ShapeDtypeStruct((1, cells, slices), BF16)],
        cost_estimate=pl.CostEstimate(flops=2**28, bytes_accessed=2**21, transcendentals=0),
        compiler_params=pltpu.CompilerParams(vmem_limit_bytes=LIMIT),
        name="keep",
    )(me, by_slice, hid, sums, mass)


def edge_call(is_far, me, halo, taps, maps, partial, sums, mass, owners):
    _, height, depth, channels = halo.shape
    slices = sums.shape[0]
    cells = height * depth
    hidden, by_slice = ((cells, channels), BF16), ((slices, cells), BF16)
    carry = [(s.shape, F32) for s in (sums, mass)]
    scratch = [((9, REPEAT, channels), CONV)]
    if is_far:
        rows = channels // LANES * (slices // owners) + 8
        outs = [by_slice, ((owners // 2, rows, LANES), BF16)] + carry + [hidden]
    else:
        outs = [((1, cells, slices), BF16)] + carry
        scratch += [hidden, by_slice]
    return pl.pallas_call(
        functools.partial(edge_kernel, is_far),
        in_specs=[SMEM] + [VMEM] * 6,
        out_specs=[VMEM] * len(outs),
        out_shape=[jax.ShapeDtypeStruct(*o) for o in outs],
        scratch_shapes=[pltpu.VMEM(*o) for o in scratch],
        cost_estimate=pl.CostEstimate(
            flops=cells * channels * 16000, bytes_accessed=4 * cells * channels,
            transcendentals=2 * cells * channels,
        ),
        compiler_params=pltpu.CompilerParams(vmem_limit_bytes=LIMIT),
        name="far" if is_far else "near",
    )(me, halo, partial, taps, maps, sums, mass)


def merge_kernel(keep_ref, other_ref, out_ref):
    out_ref[...] = (keep_ref[...] + other_ref[...].astype(F32)).astype(BF16)


def merge_call(keep, other):
    return pl.pallas_call(
        merge_kernel,
        in_specs=[VMEM, VMEM],
        out_specs=VMEM,
        out_shape=jax.ShapeDtypeStruct(keep.shape, BF16),
        compiler_params=pltpu.CompilerParams(vmem_limit_bytes=LIMIT),
        name="merge",
    )(keep, other)


def owner_kernel(parts_ref, gain_ref, content_ref, widening_ref,
                 narrowing_ref, final_ref, out_ref, mapped_ref):
    channels = content_ref.shape[0]
    held = channels // LANES
    rows = out_ref.shape[0]
    total = jnp.sum(parts_ref[...].astype(F32), axis=0)
    pooled = jnp.concatenate([total[i * rows : (i + 1) * rows] for i in range(held)], axis=1)
    tail = total[held * rows :]
    lane = lax.broadcasted_iota(jnp.int32, (8, LANES), 1)
    width = LANES // (rows // 8)
    mass = jnp.concatenate([
        jnp.sum(jnp.where((lane >= g) & (lane < g + width), tail, 0.0), axis=1, keepdims=True)
        for g in range(0, LANES, width)
    ], axis=0)
    pooled = 0.5 * pooled / (mass + epsilon)
    high = pooled.astype(BF16)
    low = (pooled - high.astype(F32)).astype(BF16)
    tokens = dot(jnp.concatenate([high, low], axis=0), content_ref[...])
    tokens = tokens[:rows] + tokens[rows:]
    center = jnp.mean(tokens, axis=-1, keepdims=True)
    spread = jnp.mean((tokens - center) ** 2, axis=-1, keepdims=True)
    normed = ((tokens - center) * (1.0 / jnp.sqrt(spread + epsilon)) * gain_ref[...]).astype(BF16)
    inner = (0.5 * gelu(dot(normed, widening_ref[...]))).astype(BF16)
    out = (tokens + dot(inner, narrowing_ref[...])).astype(BF16)
    out_ref[...] = out
    mapped = dot(out, final_ref[...]).astype(BF16)
    mapped_ref[...] = jnp.broadcast_to(mapped[None], mapped_ref.shape)


def owner_call(parts, gain, *weights):
    channels = weights[0].shape[0]
    owners = parts.shape[0]
    rows = (parts.shape[1] - 8) // (channels // LANES)
    return pl.pallas_call(
        owner_kernel,
        in_specs=[VMEM] * 6,
        out_specs=[VMEM, VMEM],
        out_shape=[
            jax.ShapeDtypeStruct((rows, channels), BF16),
            jax.ShapeDtypeStruct((owners, rows, channels), BF16),
        ],
        compiler_params=pltpu.CompilerParams(vmem_limit_bytes=LIMIT),
        name="owner",
    )(parts, gain, *weights)


def ahead_kernel(me_ref, x_ref, inside_ref, near_ref, own_ref, out_ref):
    planes = x_ref.shape[0]
    half = own_ref.shape[0]
    odd = me_ref[0] & 1
    columns = pl.ds(pl.multiple_of(odd * half, half), half)

    def step(i, carry):
        change = dot(inside_ref[i, :, columns], own_ref[...])
        out_ref[i] = x_ref[i + 1].astype(F32) + change
        return carry

    lax.fori_loop(0, planes - 2, step, 0)
    change = dot(near_ref[0, :, columns], own_ref[...])
    out_ref[planes - 2] = x_ref[(planes - 1) * (1 - odd)].astype(F32) + change


def ahead_call(me, x, inside, near, own):
    planes, cells, channels = x.shape
    return pl.pallas_call(
        ahead_kernel,
        in_specs=[SMEM] + [VMEM] * 4,
        out_specs=VMEM,
        out_shape=jax.ShapeDtypeStruct((planes - 1, cells, channels), F32),
        cost_estimate=pl.CostEstimate(flops=2**30, bytes_accessed=2**23, transcendentals=0),
        compiler_params=pltpu.CompilerParams(vmem_limit_bytes=LIMIT),
        name="ahead",
    )(me, x, inside, near, own)


def update_kernel(me_ref, x_ref, ahead_ref, inside_ref, near_ref, far_ref, own_ref, other_ref, out_ref,
                  done_ref, mapped_ref, sem):
    planes, cells, channels = x_ref.shape
    half = own_ref.shape[0]
    odd = me_ref[0] & 1
    mine = pl.ds(pl.multiple_of(odd * half, half), half)
    others = pl.ds(pl.multiple_of((1 - odd) * half, half), half)
    mapped_ref[mine] = own_ref[...]
    mapped_ref[others] = other_ref[...]

    near, far = (planes - 1) * (1 - odd), (planes - 1) * odd

    def store(plane, at, sem_ref):
        return pltpu.make_async_copy(done_ref.at[plane, at], out_ref.at[plane, at], sem_ref)

    def whole(plane):
        return store(plane, pl.ds(0, cells), sem.at[plane])

    def step(i, carry):
        total = ahead_ref[i] + dot(inside_ref[i, :, others], other_ref[...])
        done_ref[i + 1] = total.astype(BF16)
        whole(i + 1).start()
        return carry

    lax.fori_loop(0, planes - 2, step, 0)
    total = ahead_ref[planes - 2] + dot(near_ref[0, :, others], other_ref[...])
    done_ref[near] = total.astype(BF16)
    whole(near).start()
    parts = [pl.ds(0, cells // 2), pl.ds(cells // 2, cells // 2)]
    lasts = [store(far, at, sem.at[planes + i]) for i, at in enumerate(parts)]
    for at, last in zip(parts, lasts):
        change = dot(far_ref[0, at], mapped_ref[...])
        done_ref[far, at, :] = (x_ref[far, at, :].astype(F32) + change).astype(BF16)
        last.start()
    whole(near).wait()
    for i in range(planes - 2):
        whole(i + 1).wait()
    for last in lasts:
        last.wait()


def update_call(me, x, ahead, inside, near, far, own, other):
    planes, cells, channels = x.shape
    return pl.pallas_call(
        update_kernel,
        in_specs=[SMEM] + [VMEM] * 7,
        out_specs=HBM,
        out_shape=jax.ShapeDtypeStruct(x.shape, BF16),
        scratch_shapes=[
            pltpu.VMEM(x.shape, BF16),
            pltpu.VMEM((2 * own.shape[0], channels), BF16),
            pltpu.SemaphoreType.DMA((planes + 2,)),
        ],
        compiler_params=pltpu.CompilerParams(vmem_limit_bytes=LIMIT),
        name="update",
    )(me, x, ahead, inside, near, far, own, other)


def per_device(
    mesh_feature_array,
    stencil_coefficients,
    partition_affinity_matrix,
    softness_mapping_matrix,
    content_mapping_matrix,
    layernorm_multiplier,
    widening_matrix,
    narrowing_matrix,
    final_mapping_matrix,
):
    x = mesh_feature_array
    planes, height, depth, channels = x.shape
    slices = partition_affinity_matrix.shape[1]
    n = lax.axis_size("gx")
    me = lax.axis_index("gx").astype(jnp.int32)[None]
    far_pairs = [p for i in range(1, n - 1, 2) for p in ((i, i + 1), (i + 1, i))]
    near_pairs = [p for i in range(0, n, 2) for p in ((i, i + 1), (i + 1, i))]
    far_plane = lax.dynamic_slice_in_dim(x, (planes - 1) * (me[0] & 1), 1)
    far_halo = lax.ppermute(far_plane, "gx", far_pairs)

    owners = min(n // 2, slices // 2 // TILE)
    share = n // 2 // owners
    groups = [[2 * (share * j + s) + h for j in range(owners)] for h in range(2) for s in range(share)]
    taps = stencil_coefficients
    near_plane, partial = ends_call(me, far_plane, x, taps)
    near_halo = lax.ppermute(near_plane, "gx", near_pairs)
    inside_probs, sums, mass, maps = inside_call(
        x, taps, partition_affinity_matrix, softness_mapping_matrix[None], n.bit_length() - 1
    )
    near_probs, sums, mass = edge_call(
        False, me, near_halo, taps, maps, partial, sums, mass, 2 * owners
    )
    by_slice, send, sums, mass, hid = edge_call(
        True, me, far_halo, taps, maps, partial, sums, mass, 2 * owners
    )

    received = lax.ppermute(send, "gx", near_pairs)
    keep, far_probs = keep_call(me, by_slice, hid, sums, mass, send.shape, GROUP * depth)
    parts = merge_call(keep, received)
    parts = lax.all_to_all(parts, "gx", 0, 0, axis_index_groups=groups)
    if share > 1:
        sharers = [[2 * (share * j + s) + h for s in range(share)]
                   for h in range(2) for j in range(owners)]
        parts = lax.psum(parts, "gx", axis_index_groups=sharers)
    own_out, mapped = owner_call(
        parts, layernorm_multiplier[None],
        content_mapping_matrix, widening_matrix, narrowing_matrix, final_mapping_matrix,
    )
    if share > 1:
        place = lax.rem(me[0] // 2, share) * (slices // n)
        own_out = lax.dynamic_slice_in_dim(own_out, place, slices // n)
    mapped = lax.all_to_all(mapped, "gx", 0, 0, axis_index_groups=groups).reshape(slices // 2, channels)
    other = lax.ppermute(mapped, "gx", near_pairs)
    planes_of_cells = x.reshape(planes, height * depth, channels)
    ahead = ahead_call(me, planes_of_cells, inside_probs, near_probs, mapped)
    updated = update_call(
        me, planes_of_cells, ahead, inside_probs, near_probs, far_probs, mapped, other
    )
    return updated.reshape(x.shape), own_out


def solution(mesh):
    return jax.shard_map(
        per_device,
        mesh=mesh,
        in_specs=(P(("grp", "gx"), None, None, None), P(), P(), P(), P(), P(), P(), P(), P()),
        out_specs=(P(("grp", "gx"), None, None, None), P(("grp", "gx"), None)),
        check_vma=False,
    )
```

```python
import functools
import math

import jax
import jax.numpy as jnp
from jax import lax
from jax.experimental import pallas as pl
from jax.experimental.pallas import tpu as pltpu
from jax.sharding import PartitionSpec as P

epsilon = 1e-05
LANES = 128
BLOCK = 256
GROUP = 8
TILE = 16
REPEAT = 8
MIB = 2**20
LIMIT = 32 * MIB
F32, BF16 = jnp.float32, jnp.bfloat16
CONV = BF16
VMEM = pl.BlockSpec(memory_space=pltpu.VMEM)
SMEM = pl.BlockSpec(memory_space=pltpu.SMEM)
HBM = pl.BlockSpec(memory_space=pltpu.HBM)


def dot(a, b):
    return jnp.dot(a, b, preferred_element_type=F32)


def gelu(x):
    inner = x * (x * x * (0.044715 * math.sqrt(2 / math.pi)) + math.sqrt(2 / math.pi))
    return x + x * jnp.tanh(inner)


def spread_taps(k_ref, planes, taps_ref):
    for role, plane in enumerate(planes):
        for tap in range(9):
            row = k_ref[pl.ds(9 * plane + tap, 1), :]
            taps_ref[9 * role + tap] = jnp.broadcast_to(row, taps_ref.shape[1:]).astype(CONV)


def conv_rows(sources, taps_ref, lanes, count, known=()):
    sums = [[None] * 3 for _ in range(count)]
    for role, rows in sources:
        taps = [taps_ref[9 * role + i, :, lanes] for i in range(9)]
        for j, row in enumerate(rows):
            if row is None:
                continue
            depth, width = row.shape
            row = row.astype(CONV).reshape(depth // REPEAT, REPEAT, width)
            for out in range(max(0, j - 2), min(count, j + 1)):
                for c in range(3):
                    term = row * taps[3 * (j - out) + c]
                    sums[out][c] = term if sums[out][c] is None else sums[out][c] + term
    for out, row in enumerate(known):
        sums[out][1] = sums[out][1] + row.astype(CONV).reshape(sums[out][1].shape)
    position = lax.broadcasted_iota(jnp.int32, (8, width), 0)
    results = []
    for out in range(count):
        before, here, after = (s.astype(F32).reshape(depth, width) for s in sums[out])
        before, after = pltpu.roll(before, 1, 0), pltpu.roll(after, depth - 1, 0)
        low = jnp.where(position == 0, 0.0, before[:8])
        high = jnp.where(position == 7, 0.0, after[depth - 8 :])
        before = jnp.concatenate([low, before[8:]], axis=0)
        after = jnp.concatenate([after[: depth - 8], high], axis=0)
        results.append(here + before + after)
    return results


def channel_blocks(channels):
    return [slice(i, i + BLOCK) for i in range(0, channels, BLOCK)]


def inner_row(ref, plane, y, lanes, inside=None):
    if inside is None:
        return ref[plane, y, :, lanes]
    row = ref[plane, jnp.clip(y, 0, ref.shape[1] - 1), :, lanes].astype(F32)
    return (row * jnp.where(inside, 1.0, 0.0)).astype(BF16)


def nt_dot(a, b):
    return lax.dot_general(a, b, (((1,), (1,)), ((), ())), preferred_element_type=F32)


def assign_steps(hid, map_ref, mass_ref, result):
    cells = hid.shape[0]
    slices = map_ref.shape[0] - TILE
    raw = nt_dot(map_ref[...], hid)
    yield
    soft = raw[slices : slices + 8]
    temperature = 0.25 + jnp.maximum(soft, 0.0) + jnp.log(1.0 + jnp.exp(-jnp.abs(soft)))
    scale = (1.0 / math.log(2.0)) / temperature
    raw = raw[:slices].reshape(slices // 8, 8, cells)
    top = jnp.max(jnp.max(raw, axis=0), axis=0, keepdims=True)
    yield
    powers = jnp.exp2((raw - top[None]) * scale[None])
    total = jnp.sum(jnp.sum(powers, axis=0), axis=0, keepdims=True)
    yield
    probs = (powers * (1.0 / total)[None]).reshape(slices, cells)
    mass = probs[:, :LANES]
    for start in range(LANES, cells, LANES):
        mass = mass + probs[:, start : start + LANES]
    mass_ref[...] += mass
    result.append(probs.astype(BF16))


def assign(hid, map_ref, mass_ref):
    result = []
    for _ in assign_steps(hid, map_ref, mass_ref, result):
        pass
    return result[0]


def ends_kernel(me_ref, _, x_ref, k_ref, near_ref, partial_ref, taps_ref):
    planes, height, depth, channels = x_ref.shape
    odd = me_ref[0] & 1

    def row(y, carry):
        near_ref[0, y] = x_ref[(planes - 1) * (1 - odd), y]
        return carry

    lax.fori_loop(0, height, row, 0)
    spread_taps(k_ref, range(3), taps_ref)
    for which, known in enumerate((((1, 0), (2, 1)), ((0, planes - 2), (1, planes - 1)))):
        def put(y, lanes, rows, known=known, which=which):
            sources = [(role, [None if b is None else x_ref[p, y + b, :, lanes] for b in rows])
                       for role, p in known]
            totals = conv_rows(sources, taps_ref, lanes, len(rows) - 2)
            for i, total in enumerate(totals):
                start = (y + i) * depth
                start = start if isinstance(y, int) else pl.multiple_of(start, depth)
                partial_ref[which, pl.ds(start, depth), lanes] = total.astype(BF16)

        for lanes in channel_blocks(channels):
            put(0, lanes, (None, 0, 1))
            put(height - 1, lanes, (-1, 0, None))

        def pair(i, carry, put=put):
            for lanes in channel_blocks(channels):
                put(2 * i + 1, lanes, (-1, 0, 1, 2))
            return carry

        lax.fori_loop(0, (height - 2) // 2, pair, 0)


def ends_call(me, after, x, taps):
    planes, height, depth, channels = x.shape
    cells = height * depth
    return pl.pallas_call(
        ends_kernel,
        in_specs=[SMEM, pl.BlockSpec(memory_space=pl.ANY)] + [VMEM] * 2,
        out_specs=[VMEM] * 2,
        out_shape=[
            jax.ShapeDtypeStruct((1, height, depth, channels), BF16),
            jax.ShapeDtypeStruct((2, cells, channels), BF16),
        ],
        scratch_shapes=[pltpu.VMEM((27, REPEAT, channels), CONV)],
        cost_estimate=pl.CostEstimate(
            flops=cells * channels * 12000, bytes_accessed=8 * cells * channels, transcendentals=0
        ),
        compiler_params=pltpu.CompilerParams(vmem_limit_bytes=LIMIT),
        name="ends",
    )(me, after, x, taps)


def reverse_lowest(value, bits):
    return ((value & ((1 << (bits - 1)) - 1)) << 1) | (value >> (bits - 1))


def inside_kernel(bits, x_ref, k_ref, affinity_ref, softness_ref, probs_ref, sums_ref, mass_ref, map_ref,
                  taps_ref, even_ref, odd_ref, hid_ref, by_slice_ref):
    planes, height, depth, channels = x_ref.shape
    slices = affinity_ref.shape[1]
    spread_taps(k_ref, range(3), taps_ref)
    run = slices >> bits
    new = lax.broadcasted_iota(jnp.int32, (slices, 1), 0)
    old = lax.broadcasted_iota(jnp.int32, (slices, slices), 1)
    place = new & (run - 1)
    owner = reverse_lowest(new >> (run.bit_length() - 1), bits)
    order = (old == owner * run + place).astype(BF16)
    map_ref[:slices] = (0.5 * nt_dot(order, affinity_ref[...])).astype(BF16)
    softness = softness_ref[...].astype(BF16).astype(F32)
    map_ref[slices:] = jnp.broadcast_to(0.5 * softness, (TILE, channels)).astype(BF16)

    sums_ref[...] = jnp.zeros(sums_ref.shape, F32)
    mass_ref[...] = jnp.zeros(mass_ref.shape, F32)
    groups = height // GROUP
    cells = GROUP * depth

    def conv(t, hid_ref):
        plane, first = t // groups, lax.rem(t, groups) * GROUP
        for lanes in channel_blocks(channels):
            for j in range(0, GROUP, 2):
                sources = []
                for role in range(3):
                    rows = []
                    for b in (-1, 0, 1, 2):
                        y, ok = first + j + b, None
                        if j + b < 0:
                            ok = first > 0
                        elif j + b >= GROUP:
                            ok = first + GROUP < height
                        rows.append(inner_row(x_ref, plane + role, y, lanes, ok))
                    sources.append((role, rows))
                for i, total in enumerate(conv_rows(sources, taps_ref, lanes, 2)):
                    hid_ref[(j + i) * depth : (j + i + 1) * depth, lanes] = gelu(total.astype(BF16))

    def share(t, source_ref, at):
        hid = source_ref[...]
        by_slice = assign(hid, map_ref, mass_ref)
        start = pl.multiple_of(lax.rem(t, groups) * cells, cells)
        probs_ref[t // groups, pl.ds(start, cells), :] = by_slice.T
        hid_ref[at, :] = hid
        by_slice_ref[:, at] = by_slice

    count = (planes - 2) * groups
    conv(jnp.int32(0), even_ref)

    def two(s, carry):
        t = 2 * s
        share(t, even_ref, slice(0, cells))
        conv(t + 1, odd_ref)
        share(t + 1, odd_ref, slice(cells, 2 * cells))
        sums_ref[...] += dot(by_slice_ref[...], hid_ref[...])
        conv(jnp.minimum(t + 2, count - 1), even_ref)
        return carry

    lax.fori_loop(0, count // 2, two, 0)


def inside_call(x, taps, affinity, softness, bits):
    planes, height, depth, channels = x.shape
    slices = affinity.shape[1]
    cells = height * depth
    work = planes * cells * channels
    return pl.pallas_call(
        functools.partial(inside_kernel, bits),
        in_specs=[VMEM] * 4,
        out_specs=[VMEM] * 4,
        out_shape=[
            jax.ShapeDtypeStruct((planes - 2, cells, slices), BF16),
            jax.ShapeDtypeStruct((slices, channels), F32),
            jax.ShapeDtypeStruct((slices, LANES), F32),
            jax.ShapeDtypeStruct((slices + TILE, channels), BF16),
        ],
        scratch_shapes=[
            pltpu.VMEM((27, REPEAT, channels), CONV),
            pltpu.VMEM((GROUP * depth, channels), BF16),
            pltpu.VMEM((GROUP * depth, channels), BF16),
            pltpu.VMEM((2 * GROUP * depth, channels), BF16),
            pltpu.VMEM((slices, 2 * GROUP * depth), BF16),
        ],
        cost_estimate=pl.CostEstimate(
            flops=work * 7000, bytes_accessed=2 * work, transcendentals=2 * work
        ),
        compiler_params=pltpu.CompilerParams(vmem_limit_bytes=LIMIT),
        name="inside",
    )(x, taps, affinity, softness)


def edge_kernel(is_far, me_ref, halo_ref, partial_ref, k_ref, map_ref, sums_in_ref, mass_in_ref, *rest):
    if is_far:
        by_slice_ref, send_ref, mass_ref, hid_ref, taps_ref, sums_ref = rest
    else:
        probs_ref, sums_ref, mass_ref, taps_ref, hid_ref, by_slice_ref = rest
    _, height, depth, channels = halo_ref.shape
    odd = me_ref[0] & 1
    rows_of = half_of(1 - odd, sums_in_ref) if is_far else slice(None)
    side = odd if is_far else 1 - odd
    spread_taps(k_ref, [2 * side], taps_ref)
    mass_ref[...] = mass_in_ref[...]
    cells = GROUP * depth
    most = height * depth - cells

    def conv_steps(first):
        for y in range(first, min(first + GROUP, height), 2):
            for lanes in channel_blocks(channels):
                rows = [halo_ref[0, y + b, :, lanes] if 0 <= y + b < height else None
                        for b in (-1, 0, 1, 2)]
                ats = [slice((y + i) * depth, (y + i + 1) * depth) for i in range(2)]
                known = [partial_ref[side, at, lanes] for at in ats]
                for at, total in zip(ats, conv_rows([(0, rows)], taps_ref, lanes, 2, known)):
                    hid_ref[at, lanes] = gelu(total.astype(BF16))
                yield

    for _ in conv_steps(0):
        pass
    for first in range(0, height, GROUP):
        group = slice(first * depth, first * depth + cells)
        result, conv = [], conv_steps(first + GROUP)
        for _ in assign_steps(hid_ref[group], map_ref, mass_ref, result):
            next(conv, None)
            next(conv, None)
        for _ in conv:
            pass
        by_slice, = result
        if not is_far:
            probs_ref[0, group] = by_slice.T
        by_slice_ref[:, group] = by_slice
        if group.stop == most:
            sums_ref[...] = sums_in_ref[rows_of, :] + dot(by_slice_ref[rows_of, :most], hid_ref[:most])
    total = sums_ref[...] + dot(by_slice_ref[rows_of, most:], hid_ref[most:])
    if is_far:
        write_share(total, mass_ref[rows_of, :], send_ref)
    else:
        sums_ref[...] = total


def half_of(side, ref):
    half = ref.shape[0] // 2
    return pl.ds(pl.multiple_of(side * half, half), half)


def write_share(total, mass, share_ref):
    owners, rows, _ = share_ref.shape
    held = total.shape[1] // LANES
    rows = (rows - 8) // held
    for i in range(held):
        part = total[:, i * LANES : (i + 1) * LANES].astype(share_ref.dtype)
        share_ref[:, i * rows : (i + 1) * rows, :] = part.reshape(owners, rows, LANES)
    tiles = rows // 8
    lane = lax.broadcasted_iota(jnp.int32, (8, LANES), 1)
    for owner in range(owners):
        tail = None
        for g in range(tiles):
            tile = mass[owner * rows + 8 * g : owner * rows + 8 * (g + 1)]
            width = LANES
            while width > LANES // tiles:
                width //= 2
                tile = tile + pltpu.roll(tile, width, 1)
            tail = tile if tail is None else jnp.where(lane >= g * width, tile, tail)
        share_ref[owner, held * rows :, :] = tail.astype(share_ref.dtype)


def keep_kernel(me_ref, by_slice_ref, hid_ref, sums_ref, mass_ref, keep_ref, probs_ref):
    mine = half_of(me_ref[0] & 1, sums_ref)
    total = sums_ref[mine, :] + dot(by_slice_ref[mine, :], hid_ref[...])
    write_share(total, mass_ref[mine, :], keep_ref)
    probs_ref[0] = by_slice_ref[...].T


def keep_call(me, by_slice, hid, sums, mass, shape):
    slices, cells = by_slice.shape
    return pl.pallas_call(
        keep_kernel,
        in_specs=[SMEM] + [VMEM] * 4,
        out_specs=[VMEM, VMEM],
        out_shape=[jax.ShapeDtypeStruct(shape, F32), jax.ShapeDtypeStruct((1, cells, slices), BF16)],
        cost_estimate=pl.CostEstimate(flops=2**28, bytes_accessed=2**21, transcendentals=0),
        compiler_params=pltpu.CompilerParams(vmem_limit_bytes=LIMIT),
        name="keep",
    )(me, by_slice, hid, sums, mass)


def edge_call(is_far, me, halo, taps, maps, partial, sums, mass, owners):
    _, height, depth, channels = halo.shape
    slices = sums.shape[0]
    cells = height * depth
    hidden, by_slice = ((cells, channels), BF16), ((slices, cells), BF16)
    carry = [(s.shape, F32) for s in (sums, mass)]
    scratch = [((9, REPEAT, channels), CONV)]
    if is_far:
        rows = channels // LANES * (slices // owners) + 8
        outs = [by_slice, ((owners // 2, rows, LANES), BF16), carry[1], hidden]
        scratch += [((slices // 2, channels), F32)]
    else:
        outs = [((1, cells, slices), BF16)] + carry
        scratch += [hidden, by_slice]
    return pl.pallas_call(
        functools.partial(edge_kernel, is_far),
        in_specs=[SMEM] + [VMEM] * 6,
        out_specs=[VMEM] * len(outs),
        out_shape=[jax.ShapeDtypeStruct(*o) for o in outs],
        scratch_shapes=[pltpu.VMEM(*o) for o in scratch],
        cost_estimate=pl.CostEstimate(
            flops=cells * channels * 16000, bytes_accessed=4 * cells * channels,
            transcendentals=2 * cells * channels,
        ),
        compiler_params=pltpu.CompilerParams(vmem_limit_bytes=LIMIT),
        name="far" if is_far else "near",
    )(me, halo, partial, taps, maps, sums, mass)


def merge_kernel(keep_ref, other_ref, out_ref):
    out_ref[...] = (keep_ref[...] + other_ref[...].astype(F32)).astype(BF16)


def merge_call(keep, other):
    return pl.pallas_call(
        merge_kernel,
        in_specs=[VMEM, VMEM],
        out_specs=VMEM,
        out_shape=jax.ShapeDtypeStruct(keep.shape, BF16),
        compiler_params=pltpu.CompilerParams(vmem_limit_bytes=LIMIT),
        name="merge",
    )(keep, other)


def owner_kernel(parts_ref, gain_ref, content_ref, widening_ref,
                 narrowing_ref, final_ref, out_ref, mapped_ref):
    channels = content_ref.shape[0]
    held = channels // LANES
    rows = out_ref.shape[0]
    total = jnp.sum(parts_ref[...].astype(F32), axis=0)
    pooled = jnp.concatenate([total[i * rows : (i + 1) * rows] for i in range(held)], axis=1)
    tail = total[held * rows :]
    lane = lax.broadcasted_iota(jnp.int32, (8, LANES), 1)
    width = LANES // (rows // 8)
    mass = jnp.concatenate([
        jnp.sum(jnp.where((lane >= g) & (lane < g + width), tail, 0.0), axis=1, keepdims=True)
        for g in range(0, LANES, width)
    ], axis=0)
    pooled = 0.5 * pooled / (mass + epsilon)
    high = pooled.astype(BF16)
    low = (pooled - high.astype(F32)).astype(BF16)
    tokens = dot(jnp.concatenate([high, low], axis=0), content_ref[...])
    tokens = tokens[:rows] + tokens[rows:]
    center = jnp.mean(tokens, axis=-1, keepdims=True)
    spread = jnp.mean((tokens - center) ** 2, axis=-1, keepdims=True)
    normed = ((tokens - center) * (1.0 / jnp.sqrt(spread + epsilon)) * gain_ref[...]).astype(BF16)
    inner = (0.5 * gelu(dot(normed, widening_ref[...]))).astype(BF16)
    out = (tokens + dot(inner, narrowing_ref[...])).astype(BF16)
    out_ref[...] = out
    mapped = dot(out, final_ref[...]).astype(BF16)
    mapped_ref[...] = jnp.broadcast_to(mapped[None], mapped_ref.shape)


def owner_call(parts, gain, *weights):
    channels = weights[0].shape[0]
    owners = parts.shape[0]
    rows = (parts.shape[1] - 8) // (channels // LANES)
    return pl.pallas_call(
        owner_kernel,
        in_specs=[VMEM] * 6,
        out_specs=[VMEM, VMEM],
        out_shape=[
            jax.ShapeDtypeStruct((rows, channels), BF16),
            jax.ShapeDtypeStruct((owners, rows, channels), BF16),
        ],
        compiler_params=pltpu.CompilerParams(vmem_limit_bytes=LIMIT),
        name="owner",
    )(parts, gain, *weights)


def ahead_kernel(me_ref, x_ref, inside_ref, near_ref, own_ref, out_ref):
    planes = x_ref.shape[0]
    half = own_ref.shape[0]
    odd = me_ref[0] & 1
    columns = pl.ds(pl.multiple_of(odd * half, half), half)

    def step(i, carry):
        change = dot(inside_ref[i, :, columns], own_ref[...])
        out_ref[i] = x_ref[i + 1].astype(F32) + change
        return carry

    lax.fori_loop(0, planes - 2, step, 0)
    change = dot(near_ref[0, :, columns], own_ref[...])
    out_ref[planes - 2] = x_ref[(planes - 1) * (1 - odd)].astype(F32) + change


def ahead_call(me, x, inside, near, own):
    planes, cells, channels = x.shape
    return pl.pallas_call(
        ahead_kernel,
        in_specs=[SMEM] + [VMEM] * 4,
        out_specs=VMEM,
        out_shape=jax.ShapeDtypeStruct((planes - 1, cells, channels), F32),
        cost_estimate=pl.CostEstimate(flops=2**30, bytes_accessed=2**23, transcendentals=0),
        compiler_params=pltpu.CompilerParams(vmem_limit_bytes=LIMIT),
        name="ahead",
    )(me, x, inside, near, own)


def update_kernel(me_ref, x_ref, ahead_ref, inside_ref, near_ref, far_ref, own_ref, other_ref, out_ref,
                  done_ref, mapped_ref, sem):
    planes, cells, channels = x_ref.shape
    half = own_ref.shape[0]
    odd = me_ref[0] & 1
    mine = pl.ds(pl.multiple_of(odd * half, half), half)
    others = pl.ds(pl.multiple_of((1 - odd) * half, half), half)
    mapped_ref[mine] = own_ref[...]
    mapped_ref[others] = other_ref[...]

    near, far = (planes - 1) * (1 - odd), (planes - 1) * odd

    def store(plane, at, sem_ref):
        return pltpu.make_async_copy(done_ref.at[plane, at], out_ref.at[plane, at], sem_ref)

    def whole(plane):
        return store(plane, pl.ds(0, cells), sem.at[plane])

    def step(i, carry):
        total = ahead_ref[i] + dot(inside_ref[i, :, others], other_ref[...])
        done_ref[i + 1] = total.astype(BF16)
        whole(i + 1).start()
        return carry

    lax.fori_loop(0, planes - 2, step, 0)
    total = ahead_ref[planes - 2] + dot(near_ref[0, :, others], other_ref[...])
    done_ref[near] = total.astype(BF16)
    whole(near).start()
    parts = [pl.ds(0, cells // 2), pl.ds(cells // 2, cells // 2)]
    lasts = [store(far, at, sem.at[planes + i]) for i, at in enumerate(parts)]
    for at, last in zip(parts, lasts):
        change = dot(far_ref[0, at], mapped_ref[...])
        done_ref[far, at, :] = (x_ref[far, at, :].astype(F32) + change).astype(BF16)
        last.start()
    whole(near).wait()
    for i in range(planes - 2):
        whole(i + 1).wait()
    for last in lasts:
        last.wait()


def update_call(me, x, ahead, inside, near, far, own, other):
    planes, cells, channels = x.shape
    return pl.pallas_call(
        update_kernel,
        in_specs=[SMEM] + [VMEM] * 7,
        out_specs=HBM,
        out_shape=jax.ShapeDtypeStruct(x.shape, BF16),
        scratch_shapes=[
            pltpu.VMEM(x.shape, BF16),
            pltpu.VMEM((2 * own.shape[0], channels), BF16),
            pltpu.SemaphoreType.DMA((planes + 2,)),
        ],
        compiler_params=pltpu.CompilerParams(vmem_limit_bytes=LIMIT),
        name="update",
    )(me, x, ahead, inside, near, far, own, other)


def per_device(
    mesh_feature_array,
    stencil_coefficients,
    partition_affinity_matrix,
    softness_mapping_matrix,
    content_mapping_matrix,
    layernorm_multiplier,
    widening_matrix,
    narrowing_matrix,
    final_mapping_matrix,
):
    x = mesh_feature_array
    planes, height, depth, channels = x.shape
    slices = partition_affinity_matrix.shape[1]
    n = lax.axis_size("gx")
    me = lax.axis_index("gx").astype(jnp.int32)[None]
    far_pairs = [p for i in range(1, n - 1, 2) for p in ((i, i + 1), (i + 1, i))]
    near_pairs = [p for i in range(0, n, 2) for p in ((i, i + 1), (i + 1, i))]
    far_plane = lax.dynamic_slice_in_dim(x, (planes - 1) * (me[0] & 1), 1)
    far_halo = lax.ppermute(far_plane, "gx", far_pairs)

    owners = min(n // 2, slices // 2 // TILE)
    share = n // 2 // owners
    groups = [[2 * (share * j + s) + h for j in range(owners)] for h in range(2) for s in range(share)]
    taps = stencil_coefficients
    near_plane, partial = ends_call(me, far_plane, x, taps)
    near_halo = lax.ppermute(near_plane, "gx", near_pairs)
    inside_probs, sums, mass, maps = inside_call(
        x, taps, partition_affinity_matrix, softness_mapping_matrix[None], n.bit_length() - 1
    )
    near_probs, sums, mass = edge_call(
        False, me, near_halo, taps, maps, partial, sums, mass, 2 * owners
    )
    by_slice, send, mass, hid = edge_call(
        True, me, far_halo, taps, maps, partial, sums, mass, 2 * owners
    )

    received = lax.ppermute(send, "gx", near_pairs)
    keep, far_probs = keep_call(me, by_slice, hid, sums, mass, send.shape)
    parts = merge_call(keep, received)
    parts = lax.all_to_all(parts, "gx", 0, 0, axis_index_groups=groups)
    if share > 1:
        sharers = [[2 * (share * j + s) + h for s in range(share)]
                   for h in range(2) for j in range(owners)]
        parts = lax.psum(parts, "gx", axis_index_groups=sharers)
    own_out, mapped = owner_call(
        parts, layernorm_multiplier[None],
        content_mapping_matrix, widening_matrix, narrowing_matrix, final_mapping_matrix,
    )
    if share > 1:
        place = lax.rem(me[0] // 2, share) * (slices // n)
        own_out = lax.dynamic_slice_in_dim(own_out, place, slices // n)
    mapped = lax.all_to_all(mapped, "gx", 0, 0, axis_index_groups=groups).reshape(slices // 2, channels)
    other = lax.ppermute(mapped, "gx", near_pairs)
    planes_of_cells = x.reshape(planes, height * depth, channels)
    ahead = ahead_call(me, planes_of_cells, inside_probs, near_probs, mapped)
    updated = update_call(
        me, planes_of_cells, ahead, inside_probs, near_probs, far_probs, mapped, other
    )
    return updated.reshape(x.shape), own_out


def solution(mesh):
    return jax.shard_map(
        per_device,
        mesh=mesh,
        in_specs=(P(("grp", "gx"), None, None, None), P(), P(), P(), P(), P(), P(), P(), P()),
        out_specs=(P(("grp", "gx"), None, None, None), P(("grp", "gx"), None)),
        check_vma=False,
    )
```

```python
import functools
import math

import jax
import jax.numpy as jnp
from jax import lax
from jax.experimental import pallas as pl
from jax.experimental.pallas import tpu as pltpu
from jax.sharding import PartitionSpec as P

epsilon = 1e-05
LANES = 128
BLOCK = 256
GROUP = 8
TILE = 16
REPEAT = 8
MIB = 2**20
LIMIT = 32 * MIB
F32, BF16 = jnp.float32, jnp.bfloat16
CONV = BF16
VMEM = pl.BlockSpec(memory_space=pltpu.VMEM)
SMEM = pl.BlockSpec(memory_space=pltpu.SMEM)
HBM = pl.BlockSpec(memory_space=pltpu.HBM)


def dot(a, b):
    return jnp.dot(a, b, preferred_element_type=F32)


def gelu(x):
    inner = x * (x * x * (0.044715 * math.sqrt(2 / math.pi)) + math.sqrt(2 / math.pi))
    return x + x * jnp.tanh(inner)


def spread_taps(k_ref, planes, taps_ref):
    for role, plane in enumerate(planes):
        for tap in range(9):
            row = k_ref[pl.ds(9 * plane + tap, 1), :]
            taps_ref[9 * role + tap] = jnp.broadcast_to(row, taps_ref.shape[1:]).astype(CONV)


def conv_rows(sources, taps_ref, lanes, count, known=()):
    sums = [[None] * 3 for _ in range(count)]
    for role, rows in sources:
        taps = [taps_ref[9 * role + i, :, lanes] for i in range(9)]
        for j, row in enumerate(rows):
            if row is None:
                continue
            depth, width = row.shape
            row = row.astype(CONV).reshape(depth // REPEAT, REPEAT, width)
            for out in range(max(0, j - 2), min(count, j + 1)):
                for c in range(3):
                    term = row * taps[3 * (j - out) + c]
                    sums[out][c] = term if sums[out][c] is None else sums[out][c] + term
    for out, row in enumerate(known):
        sums[out][1] = sums[out][1] + row.astype(CONV).reshape(sums[out][1].shape)
    position = lax.broadcasted_iota(jnp.int32, (8, width), 0)
    results = []
    for out in range(count):
        before, after = (sums[out][c].astype(F32).reshape(depth, width) for c in (0, 2))
        here = sums[out][1].reshape(depth, width)
        before, after = pltpu.roll(before, 1, 0), pltpu.roll(after, depth - 1, 0)
        low = jnp.where(position == 0, 0.0, before[:8])
        high = jnp.where(position == 7, 0.0, after[depth - 8 :])
        before = jnp.concatenate([low, before[8:]], axis=0)
        after = jnp.concatenate([after[: depth - 8], high], axis=0)
        results.append(here + (before + after).astype(CONV))
    return results


def channel_blocks(channels):
    return [slice(i, i + BLOCK) for i in range(0, channels, BLOCK)]


def inner_row(ref, plane, y, lanes, inside=None):
    if inside is None:
        return ref[plane, y, :, lanes]
    row = ref[plane, jnp.clip(y, 0, ref.shape[1] - 1), :, lanes].astype(F32)
    return (row * jnp.where(inside, 1.0, 0.0)).astype(BF16)


def nt_dot(a, b):
    return lax.dot_general(a, b, (((1,), (1,)), ((), ())), preferred_element_type=F32)


def assign_steps(hid, map_ref, mass_ref, result):
    cells = hid.shape[0]
    slices = map_ref.shape[0] - TILE
    raw = nt_dot(map_ref[...], hid)
    yield
    soft = raw[slices : slices + 8]
    temperature = 0.25 + jnp.maximum(soft, 0.0) + jnp.log(1.0 + jnp.exp(-jnp.abs(soft)))
    scale = (1.0 / math.log(2.0)) / temperature
    raw = raw[:slices].reshape(slices // 8, 8, cells)
    top = jnp.max(jnp.max(raw, axis=0), axis=0, keepdims=True)
    yield
    powers = jnp.exp2((raw - top[None]) * scale[None])
    total = jnp.sum(jnp.sum(powers, axis=0), axis=0, keepdims=True)
    yield
    probs = (powers * (1.0 / total)[None]).reshape(slices, cells)
    mass = probs[:, :LANES]
    for start in range(LANES, cells, LANES):
        mass = mass + probs[:, start : start + LANES]
    mass_ref[...] += mass
    result.append(probs.astype(BF16))


def assign(hid, map_ref, mass_ref):
    result = []
    for _ in assign_steps(hid, map_ref, mass_ref, result):
        pass
    return result[0]


def ends_kernel(me_ref, _, x_ref, k_ref, near_ref, partial_ref, taps_ref):
    planes, height, depth, channels = x_ref.shape
    odd = me_ref[0] & 1

    def row(y, carry):
        near_ref[0, y] = x_ref[(planes - 1) * (1 - odd), y]
        return carry

    lax.fori_loop(0, height, row, 0)
    spread_taps(k_ref, range(3), taps_ref)
    for which, known in enumerate((((1, 0), (2, 1)), ((0, planes - 2), (1, planes - 1)))):
        def put(y, lanes, rows, known=known, which=which):
            sources = [(role, [None if b is None else x_ref[p, y + b, :, lanes] for b in rows])
                       for role, p in known]
            totals = conv_rows(sources, taps_ref, lanes, len(rows) - 2)
            for i, total in enumerate(totals):
                start = (y + i) * depth
                start = start if isinstance(y, int) else pl.multiple_of(start, depth)
                partial_ref[which, pl.ds(start, depth), lanes] = total.astype(BF16)

        for lanes in channel_blocks(channels):
            put(0, lanes, (None, 0, 1))
            put(height - 1, lanes, (-1, 0, None))

        def pair(i, carry, put=put):
            for lanes in channel_blocks(channels):
                put(2 * i + 1, lanes, (-1, 0, 1, 2))
            return carry

        lax.fori_loop(0, (height - 2) // 2, pair, 0)


def ends_call(me, after, x, taps):
    planes, height, depth, channels = x.shape
    cells = height * depth
    return pl.pallas_call(
        ends_kernel,
        in_specs=[SMEM, pl.BlockSpec(memory_space=pl.ANY)] + [VMEM] * 2,
        out_specs=[VMEM] * 2,
        out_shape=[
            jax.ShapeDtypeStruct((1, height, depth, channels), BF16),
            jax.ShapeDtypeStruct((2, cells, channels), BF16),
        ],
        scratch_shapes=[pltpu.VMEM((27, REPEAT, channels), CONV)],
        cost_estimate=pl.CostEstimate(
            flops=cells * channels * 12000, bytes_accessed=8 * cells * channels, transcendentals=0
        ),
        compiler_params=pltpu.CompilerParams(vmem_limit_bytes=LIMIT),
        name="ends",
    )(me, after, x, taps)


def reverse_lowest(value, bits):
    return ((value & ((1 << (bits - 1)) - 1)) << 1) | (value >> (bits - 1))


def inside_kernel(bits, x_ref, k_ref, affinity_ref, softness_ref, probs_ref, sums_ref, mass_ref, map_ref,
                  taps_ref, even_ref, odd_ref, hid_ref, by_slice_ref):
    planes, height, depth, channels = x_ref.shape
    slices = affinity_ref.shape[1]
    spread_taps(k_ref, range(3), taps_ref)
    run = slices >> bits
    new = lax.broadcasted_iota(jnp.int32, (slices, 1), 0)
    old = lax.broadcasted_iota(jnp.int32, (slices, slices), 1)
    place = new & (run - 1)
    owner = reverse_lowest(new >> (run.bit_length() - 1), bits)
    order = (old == owner * run + place).astype(BF16)
    map_ref[:slices] = (0.5 * nt_dot(order, affinity_ref[...])).astype(BF16)
    softness = softness_ref[...].astype(BF16).astype(F32)
    map_ref[slices:] = jnp.broadcast_to(0.5 * softness, (TILE, channels)).astype(BF16)

    sums_ref[...] = jnp.zeros(sums_ref.shape, F32)
    mass_ref[...] = jnp.zeros(mass_ref.shape, F32)
    groups = height // GROUP
    cells = GROUP * depth

    def conv(t, hid_ref):
        plane, first = t // groups, lax.rem(t, groups) * GROUP
        for lanes in channel_blocks(channels):
            for j in range(0, GROUP, 2):
                sources = []
                for role in range(3):
                    rows = []
                    for b in (-1, 0, 1, 2):
                        y, ok = first + j + b, None
                        if j + b < 0:
                            ok = first > 0
                        elif j + b >= GROUP:
                            ok = first + GROUP < height
                        rows.append(inner_row(x_ref, plane + role, y, lanes, ok))
                    sources.append((role, rows))
                for i, total in enumerate(conv_rows(sources, taps_ref, lanes, 2)):
                    hid_ref[(j + i) * depth : (j + i + 1) * depth, lanes] = gelu(total.astype(BF16))

    def share(t, source_ref, at):
        hid = source_ref[...]
        by_slice = assign(hid, map_ref, mass_ref)
        start = pl.multiple_of(lax.rem(t, groups) * cells, cells)
        probs_ref[t // groups, pl.ds(start, cells), :] = by_slice.T
        hid_ref[at, :] = hid
        by_slice_ref[:, at] = by_slice

    count = (planes - 2) * groups
    conv(jnp.int32(0), even_ref)

    def two(s, carry):
        t = 2 * s
        share(t, even_ref, slice(0, cells))
        conv(t + 1, odd_ref)
        share(t + 1, odd_ref, slice(cells, 2 * cells))
        sums_ref[...] += dot(by_slice_ref[...], hid_ref[...])
        conv(jnp.minimum(t + 2, count - 1), even_ref)
        return carry

    lax.fori_loop(0, count // 2, two, 0)


def inside_call(x, taps, affinity, softness, bits):
    planes, height, depth, channels = x.shape
    slices = affinity.shape[1]
    cells = height * depth
    work = planes * cells * channels
    return pl.pallas_call(
        functools.partial(inside_kernel, bits),
        in_specs=[VMEM] * 4,
        out_specs=[VMEM] * 4,
        out_shape=[
            jax.ShapeDtypeStruct((planes - 2, cells, slices), BF16),
            jax.ShapeDtypeStruct((slices, channels), F32),
            jax.ShapeDtypeStruct((slices, LANES), F32),
            jax.ShapeDtypeStruct((slices + TILE, channels), BF16),
        ],
        scratch_shapes=[
            pltpu.VMEM((27, REPEAT, channels), CONV),
            pltpu.VMEM((GROUP * depth, channels), BF16),
            pltpu.VMEM((GROUP * depth, channels), BF16),
            pltpu.VMEM((2 * GROUP * depth, channels), BF16),
            pltpu.VMEM((slices, 2 * GROUP * depth), BF16),
        ],
        cost_estimate=pl.CostEstimate(
            flops=work * 7000, bytes_accessed=2 * work, transcendentals=2 * work
        ),
        compiler_params=pltpu.CompilerParams(vmem_limit_bytes=LIMIT),
        name="inside",
    )(x, taps, affinity, softness)


def edge_kernel(is_far, me_ref, halo_ref, partial_ref, k_ref, map_ref, sums_in_ref, mass_in_ref, *rest):
    if is_far:
        by_slice_ref, send_ref, mass_ref, hid_ref, taps_ref, sums_ref = rest
    else:
        probs_ref, sums_ref, mass_ref, taps_ref, hid_ref, by_slice_ref = rest
    _, height, depth, channels = halo_ref.shape
    odd = me_ref[0] & 1
    rows_of = half_of(1 - odd, sums_in_ref) if is_far else slice(None)
    side = odd if is_far else 1 - odd
    spread_taps(k_ref, [2 * side], taps_ref)
    mass_ref[...] = mass_in_ref[...]
    cells = GROUP * depth
    most = height * depth - cells

    def conv_steps(first):
        for y in range(first, min(first + GROUP, height), 2):
            for lanes in channel_blocks(channels):
                rows = [halo_ref[0, y + b, :, lanes] if 0 <= y + b < height else None
                        for b in (-1, 0, 1, 2)]
                ats = [slice((y + i) * depth, (y + i + 1) * depth) for i in range(2)]
                known = [partial_ref[side, at, lanes] for at in ats]
                for at, total in zip(ats, conv_rows([(0, rows)], taps_ref, lanes, 2, known)):
                    hid_ref[at, lanes] = gelu(total.astype(BF16))
                yield

    for _ in conv_steps(0):
        pass
    for first in range(0, height, GROUP):
        group = slice(first * depth, first * depth + cells)
        result, conv = [], conv_steps(first + GROUP)
        for _ in assign_steps(hid_ref[group], map_ref, mass_ref, result):
            next(conv, None)
            next(conv, None)
        for _ in conv:
            pass
        by_slice, = result
        if not is_far:
            probs_ref[0, group] = by_slice.T
        by_slice_ref[:, group] = by_slice
        if group.stop == most:
            sums_ref[...] = sums_in_ref[rows_of, :] + dot(by_slice_ref[rows_of, :most], hid_ref[:most])
    total = sums_ref[...] + dot(by_slice_ref[rows_of, most:], hid_ref[most:])
    if is_far:
        write_share(total, mass_ref[rows_of, :], send_ref)
    else:
        sums_ref[...] = total


def half_of(side, ref):
    half = ref.shape[0] // 2
    return pl.ds(pl.multiple_of(side * half, half), half)


def write_share(total, mass, share_ref):
    owners, rows, _ = share_ref.shape
    held = total.shape[1] // LANES
    rows = (rows - 8) // held
    for i in range(held):
        part = total[:, i * LANES : (i + 1) * LANES].astype(share_ref.dtype)
        share_ref[:, i * rows : (i + 1) * rows, :] = part.reshape(owners, rows, LANES)
    tiles = rows // 8
    lane = lax.broadcasted_iota(jnp.int32, (8, LANES), 1)
    for owner in range(owners):
        tail = None
        for g in range(tiles):
            tile = mass[owner * rows + 8 * g : owner * rows + 8 * (g + 1)]
            width = LANES
            while width > LANES // tiles:
                width //= 2
                tile = tile + pltpu.roll(tile, width, 1)
            tail = tile if tail is None else jnp.where(lane >= g * width, tile, tail)
        share_ref[owner, held * rows :, :] = tail.astype(share_ref.dtype)


def keep_kernel(me_ref, by_slice_ref, hid_ref, sums_ref, mass_ref, keep_ref, probs_ref):
    mine = half_of(me_ref[0] & 1, sums_ref)
    total = sums_ref[mine, :] + dot(by_slice_ref[mine, :], hid_ref[...])
    write_share(total, mass_ref[mine, :], keep_ref)
    probs_ref[0] = by_slice_ref[...].T


def keep_call(me, by_slice, hid, sums, mass, shape):
    slices, cells = by_slice.shape
    return pl.pallas_call(
        keep_kernel,
        in_specs=[SMEM] + [VMEM] * 4,
        out_specs=[VMEM, VMEM],
        out_shape=[jax.ShapeDtypeStruct(shape, F32), jax.ShapeDtypeStruct((1, cells, slices), BF16)],
        cost_estimate=pl.CostEstimate(flops=2**28, bytes_accessed=2**21, transcendentals=0),
        compiler_params=pltpu.CompilerParams(vmem_limit_bytes=LIMIT),
        name="keep",
    )(me, by_slice, hid, sums, mass)


def edge_call(is_far, me, halo, taps, maps, partial, sums, mass, owners):
    _, height, depth, channels = halo.shape
    slices = sums.shape[0]
    cells = height * depth
    hidden, by_slice = ((cells, channels), BF16), ((slices, cells), BF16)
    carry = [(s.shape, F32) for s in (sums, mass)]
    scratch = [((9, REPEAT, channels), CONV)]
    if is_far:
        rows = channels // LANES * (slices // owners) + 8
        outs = [by_slice, ((owners // 2, rows, LANES), BF16), carry[1], hidden]
        scratch += [((slices // 2, channels), F32)]
    else:
        outs = [((1, cells, slices), BF16)] + carry
        scratch += [hidden, by_slice]
    return pl.pallas_call(
        functools.partial(edge_kernel, is_far),
        in_specs=[SMEM] + [VMEM] * 6,
        out_specs=[VMEM] * len(outs),
        out_shape=[jax.ShapeDtypeStruct(*o) for o in outs],
        scratch_shapes=[pltpu.VMEM(*o) for o in scratch],
        cost_estimate=pl.CostEstimate(
            flops=cells * channels * 16000, bytes_accessed=4 * cells * channels,
            transcendentals=2 * cells * channels,
        ),
        compiler_params=pltpu.CompilerParams(vmem_limit_bytes=LIMIT),
        name="far" if is_far else "near",
    )(me, halo, partial, taps, maps, sums, mass)


def merge_kernel(keep_ref, other_ref, out_ref):
    out_ref[...] = (keep_ref[...] + other_ref[...].astype(F32)).astype(BF16)


def merge_call(keep, other):
    return pl.pallas_call(
        merge_kernel,
        in_specs=[VMEM, VMEM],
        out_specs=VMEM,
        out_shape=jax.ShapeDtypeStruct(keep.shape, BF16),
        compiler_params=pltpu.CompilerParams(vmem_limit_bytes=LIMIT),
        name="merge",
    )(keep, other)


def owner_kernel(parts_ref, gain_ref, content_ref, widening_ref,
                 narrowing_ref, final_ref, out_ref, mapped_ref):
    channels = content_ref.shape[0]
    held = channels // LANES
    rows = out_ref.shape[0]
    total = jnp.sum(parts_ref[...].astype(F32), axis=0)
    pooled = jnp.concatenate([total[i * rows : (i + 1) * rows] for i in range(held)], axis=1)
    tail = total[held * rows :]
    lane = lax.broadcasted_iota(jnp.int32, (8, LANES), 1)
    width = LANES // (rows // 8)
    mass = jnp.concatenate([
        jnp.sum(jnp.where((lane >= g) & (lane < g + width), tail, 0.0), axis=1, keepdims=True)
        for g in range(0, LANES, width)
    ], axis=0)
    pooled = 0.5 * pooled / (mass + epsilon)
    high = pooled.astype(BF16)
    low = (pooled - high.astype(F32)).astype(BF16)
    tokens = dot(jnp.concatenate([high, low], axis=0), content_ref[...])
    tokens = tokens[:rows] + tokens[rows:]
    center = jnp.mean(tokens, axis=-1, keepdims=True)
    spread = jnp.mean((tokens - center) ** 2, axis=-1, keepdims=True)
    normed = ((tokens - center) * (1.0 / jnp.sqrt(spread + epsilon)) * gain_ref[...]).astype(BF16)
    inner = (0.5 * gelu(dot(normed, widening_ref[...]))).astype(BF16)
    out = (tokens + dot(inner, narrowing_ref[...])).astype(BF16)
    out_ref[...] = out
    mapped = dot(out, final_ref[...]).astype(BF16)
    mapped_ref[...] = jnp.broadcast_to(mapped[None], mapped_ref.shape)


def owner_call(parts, gain, *weights):
    channels = weights[0].shape[0]
    owners = parts.shape[0]
    rows = (parts.shape[1] - 8) // (channels // LANES)
    return pl.pallas_call(
        owner_kernel,
        in_specs=[VMEM] * 6,
        out_specs=[VMEM, VMEM],
        out_shape=[
            jax.ShapeDtypeStruct((rows, channels), BF16),
            jax.ShapeDtypeStruct((owners, rows, channels), BF16),
        ],
        compiler_params=pltpu.CompilerParams(vmem_limit_bytes=LIMIT),
        name="owner",
    )(parts, gain, *weights)


def ahead_kernel(me_ref, x_ref, inside_ref, near_ref, own_ref, out_ref):
    planes = x_ref.shape[0]
    half = own_ref.shape[0]
    odd = me_ref[0] & 1
    columns = pl.ds(pl.multiple_of(odd * half, half), half)

    def step(i, carry):
        change = dot(inside_ref[i, :, columns], own_ref[...])
        out_ref[i] = x_ref[i + 1].astype(F32) + change
        return carry

    lax.fori_loop(0, planes - 2, step, 0)
    change = dot(near_ref[0, :, columns], own_ref[...])
    out_ref[planes - 2] = x_ref[(planes - 1) * (1 - odd)].astype(F32) + change


def ahead_call(me, x, inside, near, own):
    planes, cells, channels = x.shape
    return pl.pallas_call(
        ahead_kernel,
        in_specs=[SMEM] + [VMEM] * 4,
        out_specs=VMEM,
        out_shape=jax.ShapeDtypeStruct((planes - 1, cells, channels), F32),
        cost_estimate=pl.CostEstimate(flops=2**30, bytes_accessed=2**23, transcendentals=0),
        compiler_params=pltpu.CompilerParams(vmem_limit_bytes=LIMIT),
        name="ahead",
    )(me, x, inside, near, own)


def update_kernel(me_ref, x_ref, ahead_ref, inside_ref, near_ref, far_ref, own_ref, other_ref, out_ref,
                  done_ref, mapped_ref, sem):
    planes, cells, channels = x_ref.shape
    half = own_ref.shape[0]
    odd = me_ref[0] & 1
    mine = pl.ds(pl.multiple_of(odd * half, half), half)
    others = pl.ds(pl.multiple_of((1 - odd) * half, half), half)
    mapped_ref[mine] = own_ref[...]
    mapped_ref[others] = other_ref[...]

    near, far = (planes - 1) * (1 - odd), (planes - 1) * odd

    def store(plane, at, sem_ref):
        return pltpu.make_async_copy(done_ref.at[plane, at], out_ref.at[plane, at], sem_ref)

    def whole(plane):
        return store(plane, pl.ds(0, cells), sem.at[plane])

    def step(i, carry):
        total = ahead_ref[i] + dot(inside_ref[i, :, others], other_ref[...])
        done_ref[i + 1] = total.astype(BF16)
        whole(i + 1).start()
        return carry

    lax.fori_loop(0, planes - 2, step, 0)
    total = ahead_ref[planes - 2] + dot(near_ref[0, :, others], other_ref[...])
    done_ref[near] = total.astype(BF16)
    whole(near).start()
    parts = [pl.ds(0, cells // 2), pl.ds(cells // 2, cells // 2)]
    lasts = [store(far, at, sem.at[planes + i]) for i, at in enumerate(parts)]
    for at, last in zip(parts, lasts):
        change = dot(far_ref[0, at], mapped_ref[...])
        done_ref[far, at, :] = (x_ref[far, at, :].astype(F32) + change).astype(BF16)
        last.start()
    whole(near).wait()
    for i in range(planes - 2):
        whole(i + 1).wait()
    for last in lasts:
        last.wait()


def update_call(me, x, ahead, inside, near, far, own, other):
    planes, cells, channels = x.shape
    return pl.pallas_call(
        update_kernel,
        in_specs=[SMEM] + [VMEM] * 7,
        out_specs=HBM,
        out_shape=jax.ShapeDtypeStruct(x.shape, BF16),
        scratch_shapes=[
            pltpu.VMEM(x.shape, BF16),
            pltpu.VMEM((2 * own.shape[0], channels), BF16),
            pltpu.SemaphoreType.DMA((planes + 2,)),
        ],
        compiler_params=pltpu.CompilerParams(vmem_limit_bytes=LIMIT),
        name="update",
    )(me, x, ahead, inside, near, far, own, other)


def per_device(
    mesh_feature_array,
    stencil_coefficients,
    partition_affinity_matrix,
    softness_mapping_matrix,
    content_mapping_matrix,
    layernorm_multiplier,
    widening_matrix,
    narrowing_matrix,
    final_mapping_matrix,
):
    x = mesh_feature_array
    planes, height, depth, channels = x.shape
    slices = partition_affinity_matrix.shape[1]
    n = lax.axis_size("gx")
    me = lax.axis_index("gx").astype(jnp.int32)[None]
    far_pairs = [p for i in range(1, n - 1, 2) for p in ((i, i + 1), (i + 1, i))]
    near_pairs = [p for i in range(0, n, 2) for p in ((i, i + 1), (i + 1, i))]
    far_plane = lax.dynamic_slice_in_dim(x, (planes - 1) * (me[0] & 1), 1)
    far_halo = lax.ppermute(far_plane, "gx", far_pairs)

    owners = min(n // 2, slices // 2 // TILE)
    share = n // 2 // owners
    groups = [[2 * (share * j + s) + h for j in range(owners)] for h in range(2) for s in range(share)]
    taps = stencil_coefficients
    near_plane, partial = ends_call(me, far_plane, x, taps)
    near_halo = lax.ppermute(near_plane, "gx", near_pairs)
    inside_probs, sums, mass, maps = inside_call(
        x, taps, partition_affinity_matrix, softness_mapping_matrix[None], n.bit_length() - 1
    )
    near_probs, sums, mass = edge_call(
        False, me, near_halo, taps, maps, partial, sums, mass, 2 * owners
    )
    by_slice, send, mass, hid = edge_call(
        True, me, far_halo, taps, maps, partial, sums, mass, 2 * owners
    )

    received = lax.ppermute(send, "gx", near_pairs)
    keep, far_probs = keep_call(me, by_slice, hid, sums, mass, send.shape)
    parts = merge_call(keep, received)
    parts = lax.all_to_all(parts, "gx", 0, 0, axis_index_groups=groups)
    if share > 1:
        sharers = [[2 * (share * j + s) + h for s in range(share)]
                   for h in range(2) for j in range(owners)]
        parts = lax.psum(parts, "gx", axis_index_groups=sharers)
    own_out, mapped = owner_call(
        parts, layernorm_multiplier[None],
        content_mapping_matrix, widening_matrix, narrowing_matrix, final_mapping_matrix,
    )
    if share > 1:
        place = lax.rem(me[0] // 2, share) * (slices // n)
        own_out = lax.dynamic_slice_in_dim(own_out, place, slices // n)
    mapped = lax.all_to_all(mapped, "gx", 0, 0, axis_index_groups=groups).reshape(slices // 2, channels)
    other = lax.ppermute(mapped, "gx", near_pairs)
    planes_of_cells = x.reshape(planes, height * depth, channels)
    ahead = ahead_call(me, planes_of_cells, inside_probs, near_probs, mapped)
    updated = update_call(
        me, planes_of_cells, ahead, inside_probs, near_probs, far_probs, mapped, other
    )
    return updated.reshape(x.shape), own_out


def solution(mesh):
    return jax.shard_map(
        per_device,
        mesh=mesh,
        in_specs=(P(("grp", "gx"), None, None, None), P(), P(), P(), P(), P(), P(), P(), P()),
        out_specs=(P(("grp", "gx"), None, None, None), P(("grp", "gx"), None)),
        check_vma=False,
    )
```
